32 devices in a mesh: dp: 4 (over y, x), row: 4 (over z), col: 2 (over core).
Axes of the slice: x: 2, y: 2, z: 4, core: 2. Of those that a mesh axis runs over, the one named last changes fastest.
Arguments:
- tokens_in: bfloat16 [6144, 768], P(('dp', 'row', 'col')), may hold values from -6 to 6
- lengths: int32 [16], P(('dp', 'row')), may hold values from 192 to 384, as said below
- cotangent: bfloat16 [6144, 768], P(('dp', 'row', 'col')), may hold values from -6 to 6
- norm_gain: float32 [2, 768], replicated, may hold values from 0.5 to 1.5
- norm_shift: float32 [2, 768], replicated, may hold values from -1.75 to 1.75
- w_fwd: float32 [2, 768, 1536], P(None, 'row', 'col'), may hold values from -0.21875 to 0.21875
- w_bwd: float32 [2, 768, 1536], P(None, 'row', 'col'), may hold values from -0.21875 to 0.21875
- w_value: float32 [2, 768, 3072], P(None, 'row', 'col'), may hold values from -0.21875 to 0.21875
- bias_fwd: float32 [2, 1536], P(None, 'col'), may hold values from -1.75 to 1.75
- bias_bwd: float32 [2, 1536], P(None, 'col'), may hold values from -1.75 to 1.75
- bias_value: float32 [2, 3072], P(None, 'col'), may hold values from -1.75 to 1.75
- decay_log: float32 [2, 2, 1536, 64], P(None, None, 'col'), may hold values from -2 to 3
- step_log: float32 [2, 2, 1536], P(None, None, 'col'), may hold values from -6.9 to -2.3
- b_input: float32 [2, 2, 1536, 64], P(None, None, 'col'), may hold values from -6 to 6
- c_output: float32 [2, 2, 1536, 64], P(None, None, 'col'), may hold values from -0.75 to 0.75
- skip_gain: float32 [2, 2, 1536], P(None, None, 'col'), may hold values from -6 to 6
- w_mix: float32 [2, 1536, 3072], P(None, 'row', 'col'), may hold values from -0.15625 to 0.15625
- bias_mix: float32 [2, 3072], P(None, 'col'), may hold values from -1.75 to 1.75
- w_output: float32 [2, 3072, 768], P(None, 'col', 'row'), may hold values from -0.4375 to 0.4375
- bias_output: float32 [2, 768], replicated, may hold values from -1.75 to 1.75
Outputs:
- tokens_out: bfloat16 [6144, 768], P(('dp', 'row', 'col'))
- grad_tokens: float32 [6144, 768], P(('dp', 'row', 'col'))
- grad_norm_gain: float32 [2, 768], replicated
- grad_norm_shift: float32 [2, 768], replicated
- grad_w_fwd: float32 [2, 768, 1536], P(None, 'row', 'col')
- grad_w_bwd: float32 [2, 768, 1536], P(None, 'row', 'col')
- grad_w_value: float32 [2, 768, 3072], P(None, 'row', 'col')
- grad_bias_fwd: float32 [2, 1536], P(None, 'col')
- grad_bias_bwd: float32 [2, 1536], P(None, 'col')
- grad_bias_value: float32 [2, 3072], P(None, 'col')
- grad_decay_log: float32 [2, 2, 1536, 64], P(None, None, 'col')
- grad_step_log: float32 [2, 2, 1536], P(None, None, 'col')
- grad_b_input: float32 [2, 2, 1536, 64], P(None, None, 'col')
- grad_c_output: float32 [2, 2, 1536, 64], P(None, None, 'col')
- grad_skip_gain: float32 [2, 2, 1536], P(None, None, 'col')
- grad_w_mix: float32 [2, 1536, 3072], P(None, 'row', 'col')
- grad_bias_mix: float32 [2, 3072], P(None, 'col')
- grad_w_output: float32 [2, 3072, 768], P(None, 'col', 'row')
- grad_bias_output: float32 [2, 768], replicated
The draws below stay inside these ranges and needn't reach their ends.
Inputs may be any that keep to these rules, and one draw needn't show every extreme that they name: `lengths`: each slot's sequence starts at the slot's first position and the rest of the slot is padding; some slot is full and some holds exactly 192 tokens.
All inputs are finite; a program needn't handle non-finite values.
Results may differ from the reference program's by a relative error of at most 0.025.
Values may be sent and summed in bfloat16 or wider, within the bound.
A program may use at most 448 MiB of HBM per device.

```python
import jax
import jax.numpy as jnp
from jax import lax

D = 768
HID = 3072
SW = 1536
NS = 64
LAYERS = 2
QB = 64
SLOT = 384
SEQ_GROUPS = 4
GROUP_SEQS = 4
SLOTS = 16
TOKENS = 6144


def draw_lengths(key, part):
    key_len = jax.random.fold_in(key, 11)
    key_full = jax.random.fold_in(key, 23)
    spread = jax.random.randint(key_len, (SEQ_GROUPS, GROUP_SEQS), SLOT // 2, SLOT + 1)
    chosen = jax.random.randint(key_full, (SEQ_GROUPS, 1), 0, GROUP_SEQS)
    places = jnp.arange(GROUP_SEQS, dtype=jnp.int32)[None, :]
    halved = (chosen + 1) % GROUP_SEQS
    filled = jnp.where(places == chosen, SLOT, spread)
    filled = jnp.where(places == halved, SLOT // 2, filled)
    return filled.reshape(SEQ_GROUPS * GROUP_SEQS).astype(jnp.int32)


def levels(rng, shape, split, low, high):
    gain = 1.0
    for position, blocks in split:
        steps = jax.random.uniform(jax.random.fold_in(jax.random.fold_in(rng, 6), position), (blocks,), jnp.float32, low / len(split), high / len(split))
        gain = gain * jnp.repeat(jnp.exp(steps), shape[position] // blocks).reshape((-1,) + (1,) * (len(shape) - 1 - position))
    return gain


def centred(key, shape, scale, reach, pieces=(), held_as=jnp.bfloat16):
    entries = jax.random.normal(key, shape, jnp.float32) * scale
    if len(pieces) > 0:
        entries = levels(key, shape, pieces, -0.22, 0.18) * entries
    return jnp.clip(entries, min=-reach, max=reach).astype(held_as)


def setup_inputs(seed: int = 0) -> dict:
    seeds = jax.random.split(jax.random.key(seed), 21)
    return {
        "tokens_in": centred(seeds[0], (TOKENS, D), 1.0, 6.0, ((0, 32),)),
        "lengths": draw_lengths(jax.random.fold_in(seeds[20], 71), 0),
        "cotangent": centred(seeds[2], (TOKENS, D), 1.0, 6.0, ((0, 32),)),
        "norm_gain": jnp.clip(1.0 + 0.1 * jax.random.normal(seeds[3], (LAYERS, D), jnp.float32), 0.5, 1.5),
        "norm_shift": centred(seeds[4], (LAYERS, D), 0.3, 1.75, (), jnp.float32),
        "w_fwd": centred(seeds[5], (LAYERS, D, SW), D ** -0.5, 0.21875, ((1, 4), (2, 2)), jnp.float32),
        "w_bwd": centred(seeds[6], (LAYERS, D, SW), D ** -0.5, 0.21875, ((1, 4), (2, 2)), jnp.float32),
        "w_value": centred(seeds[7], (LAYERS, D, HID), D ** -0.5, 0.21875, ((1, 4), (2, 2)), jnp.float32),
        "bias_fwd": centred(seeds[8], (LAYERS, SW), 0.3, 1.75, ((1, 2),), jnp.float32),
        "bias_bwd": centred(seeds[9], (LAYERS, SW), 0.3, 1.75, ((1, 2),), jnp.float32),
        "bias_value": centred(seeds[10], (LAYERS, HID), 0.3, 1.75, ((1, 2),), jnp.float32),
        "decay_log": jnp.clip(-2.0 + 5.0 * jax.random.uniform(seeds[11], (LAYERS, 2, SW, NS), jnp.float32) ** levels(seeds[11], (LAYERS, 2, SW, NS), ((2, 2),), -0.2, 0.2), -2.0, 3.0),
        "step_log": jnp.clip(-6.9 + 4.6000001430511475 * jax.random.uniform(seeds[12], (LAYERS, 2, SW), jnp.float32) ** levels(seeds[12], (LAYERS, 2, SW), ((2, 2),), -0.2, 0.2), -6.9, -2.3),
        "b_input": centred(seeds[13], (LAYERS, 2, SW, NS), 1.0, 6.0, ((2, 2),), jnp.float32),
        "c_output": centred(seeds[14], (LAYERS, 2, SW, NS), 0.125, 0.75, ((2, 2),), jnp.float32),
        "skip_gain": centred(seeds[15], (LAYERS, 2, SW), 1.0, 6.0, ((2, 2),), jnp.float32),
        "w_mix": centred(seeds[16], (LAYERS, SW, HID), SW ** -0.5, 0.15625, ((1, 4), (2, 2)), jnp.float32),
        "bias_mix": centred(seeds[17], (LAYERS, HID), 0.3, 1.75, ((1, 2),), jnp.float32),
        "w_output": centred(seeds[18], (LAYERS, HID, D), (HID // 16) ** -0.5, 0.4375, ((1, 2), (2, 4)), jnp.float32),
        "bias_output": centred(seeds[19], (LAYERS, D), 0.3, 1.75, (), jnp.float32),
    }


HIGH = lax.Precision.HIGHEST
EPS = 1e-05

@jax.custom_vjp
def low(v):
    return lax.optimization_barrier(v.astype(jnp.bfloat16)).astype(jnp.float32)

@jax.custom_vjp
def low_back(v):
    return v

def low_keep(v):
    return (low(v), None)

def low_pass(kept, grad):
    return (grad,)

def back_keep(v):
    return (v, None)

def back_low(kept, grad):
    return (low(grad),)
low.defvjp(low_keep, low_pass)
low_back.defvjp(back_keep, back_low)

def norm_rows(residual, gain_now, shift_now):
    row_mean = lax.optimization_barrier(jnp.mean(residual, axis=1, keepdims=True))
    centered = residual - row_mean
    variance = lax.optimization_barrier(jnp.mean(centered * centered, axis=1, keepdims=True))
    return centered * lax.rsqrt(variance + EPS) * gain_now + shift_now

def ssm_scan(signal, decay_now, step_now, b_now, c_now, skip_now):
    length_rows, channels = signal.shape
    blocks_count = length_rows // QB
    decay_rate = jnp.exp(step_now)[:, None] * jnp.exp(decay_now)
    b_disc = (1.0 - jnp.exp(-decay_rate)) * jnp.exp(-decay_now) * b_now
    offsets = jnp.arange(QB, dtype=jnp.float32)
    lag_int = jnp.arange(QB, dtype=jnp.int32)
    lag_index = jnp.clip(lag_int[:, None] - lag_int[None, :], 0, QB - 1)
    causal = lag_int[:, None] >= lag_int[None, :]
    powers = jnp.exp(-offsets[:, None, None] * decay_rate[None])
    kernel = lax.optimization_barrier(jnp.sum(powers * (c_now * b_disc)[None], axis=2))
    toeplitz = jnp.where(causal[:, :, None], jnp.take(kernel, lag_index, axis=0), 0.0)
    blocks = signal.reshape(blocks_count, QB, channels)
    inside = jnp.einsum('tsc,bsc->btc', toeplitz, blocks, precision=HIGH)
    tail = jnp.exp(-(QB - 1.0 - offsets)[:, None, None] * decay_rate[None]) * b_disc[None]
    block_ends = jnp.einsum('bsc,scn->bcn', blocks, tail, precision=HIGH)
    block_decay = jnp.exp(-QB * decay_rate)

    def advance(carry_state, block_end):
        return (block_decay * carry_state + block_end, carry_state)
    unused_state, block_starts = lax.scan(advance, jnp.zeros_like(decay_rate), block_ends)
    head = jnp.exp(-(offsets + 1.0)[:, None, None] * decay_rate[None]) * c_now[None]
    carried = jnp.einsum('bcn,tcn->btc', block_starts, head, precision=HIGH)
    return (inside + carried).reshape(length_rows, channels) + skip_now * signal

def both_scans(fwd_in, bwd_in, ssm_params):
    decay_now, step_now, b_now, c_now, skip_now = ssm_params
    fwd_out = ssm_scan(fwd_in, decay_now[0], step_now[0], b_now[0], c_now[0], skip_now[0])
    bwd_out = ssm_scan(bwd_in[::-1], decay_now[1], step_now[1], b_now[1], c_now[1], skip_now[1])[::-1]
    return (fwd_out, bwd_out)

def layer_pass(residual, live_mask, params):
    gain_now, shift_now, wf_now, wb_now, wv_now, bf_now, bb_now, bv_now, decay_now, step_now, b_now, c_now, skip_now, wm_now, bm_now, wo_now, bo_now = params
    normed = low(norm_rows(residual, gain_now, shift_now))
    pre_fwd = low_back(jnp.dot(normed, low(wf_now), precision=HIGH)) + bf_now
    pre_bwd = low_back(jnp.dot(normed, low(wb_now), precision=HIGH)) + bb_now
    pre_value = low_back(jnp.dot(normed, low(wv_now), precision=HIGH)) + bv_now
    fwd_in = jax.nn.gelu(pre_fwd) * live_mask[:, None]
    bwd_in = jax.nn.gelu(pre_bwd) * live_mask[:, None]
    value_act = jax.nn.gelu(pre_value)
    fwd_out, bwd_out = both_scans(fwd_in, bwd_in, (decay_now, step_now, b_now, c_now, skip_now))
    mixed_low = low(fwd_out * bwd_out)
    pre_mix = low_back(jnp.dot(mixed_low, low(wm_now), precision=HIGH)) + bm_now
    product = low(jax.nn.gelu(pre_mix) * value_act)
    branch = low_back(jnp.dot(product, low(wo_now), precision=HIGH))
    return residual + live_mask[:, None] * (branch + bo_now)

def whole_block(residual, live_mask, params):
    for depth_index in range(LAYERS):
        residual = layer_pass(residual, live_mask, tuple((stacked[depth_index] for stacked in params)))
    return residual

def reference(tokens_in, lengths, cotangent, norm_gain, norm_shift, w_fwd, w_bwd, w_value, bias_fwd, bias_bwd, bias_value, decay_log, step_log, b_input, c_output, skip_gain, w_mix, bias_mix, w_output, bias_output):
    params = (norm_gain, norm_shift, w_fwd, w_bwd, w_value, bias_fwd, bias_bwd, bias_value, decay_log, step_log, b_input, c_output, skip_gain, w_mix, bias_mix, w_output, bias_output)
    slot_tokens = tokens_in.astype(jnp.float32).reshape(SLOTS, SLOT, D)
    slot_cot = cotangent.astype(jnp.float32).reshape(SLOTS, SLOT, D)
    positions = jnp.arange(SLOT, dtype=jnp.int32)

    def one_slot(totals, entry):
        tokens_now, cot_now, length_now = entry
        live_mask = (positions < length_now).astype(jnp.float32)
        result, pull = jax.vjp(lambda tok_val, par_val: whole_block(tok_val, live_mask, par_val), tokens_now, params)
        grad_tok, grad_par = pull(cot_now)
        return (jax.tree.map(jnp.add, totals, grad_par), (result, grad_tok))
    zeros = jax.tree.map(jnp.zeros_like, params)
    grads, (results, grad_toks) = lax.scan(one_slot, zeros, (slot_tokens, slot_cot, lengths))
    return (results.reshape(TOKENS, D).astype(jnp.bfloat16), grad_toks.reshape(TOKENS, D), grads[0], grads[1], grads[2], grads[3], grads[4], grads[5], grads[6], grads[7], grads[8], grads[9], grads[10], grads[11], grads[12], grads[13], grads[14], grads[15], grads[16])
```

```python
import functools

import jax
import jax.numpy as jnp
import numpy as np
from jax import lax
from jax.experimental import pallas as pl
from jax.experimental.pallas import tpu as pltpu
from jax.sharding import PartitionSpec as P

LAYERS = 2
EPS = 1e-05
LAG = 64
BF = jnp.bfloat16
F32 = jnp.float32
MESH = pl.DeviceIdType.MESH
VMEM_LIMIT = 60 * 1024 * 1024
CHUNK = 32


def transform_matrix(length):
    k = np.arange(length)[:, None]
    t = np.arange(length)[None, :]
    angle = np.pi * (((2 * k + 1) * t) % (4 * length)) / (2 * length)
    return np.concatenate((np.cos(angle), -np.sin(angle)), axis=0)


def gelu_only(v):
    t = jnp.tanh(v * (0.7978845608 + 0.035677408 * v * v))
    return (0.5 * v) * (1.0 + t)


def gelu_parts(v):
    sq = v * v
    t = jnp.tanh(v * (0.7978845608 + 0.035677408 * sq))
    half = 0.5 + 0.5 * t
    slope = half + (v * half) * (1.0 - t) * (0.7978845608 + 0.107032225 * sq)
    return v * half, slope


def dot(a, b, ca, cb):
    return lax.dot_general(a, b, (((ca,), (cb,)), ((), ())), preferred_element_type=F32)


def over_rows(rows, step, work):
    def one(i, unused):
        work(pl.ds(pl.multiple_of(i * step, step), step))
        return unused

    lax.fori_loop(0, rows // step, one, 0)


class Place:
    def __init__(self, n):
        self.n = n
        self.d = lax.axis_index("dp")
        self.c = lax.axis_index("col")

    def greet(self):
        barrier = pltpu.get_barrier_semaphore()
        for k in range(1, self.n):
            pl.semaphore_signal(barrier, inc=1, device_id={"dp": self.ahead(k)}, device_id_type=MESH)
        pl.semaphore_signal(barrier, inc=1, device_id={"col": 1 - self.c}, device_id_type=MESH)
        pl.semaphore_wait(barrier, self.n)

    def ahead(self, k):
        return lax.rem(self.d + k, self.n)

    def behind(self, k):
        return lax.rem(self.d - k + self.n, self.n)

    def other(self, i):
        return i + (i + self.n - self.d) // self.n

    def to_dp(self, src, dst, send, recv, q):
        return pltpu.make_async_remote_copy(
            src, dst, send, recv, device_id={"dp": q}, device_id_type=MESH
        )

    def to_mate(self, src, dst, send, recv):
        return pltpu.make_async_remote_copy(
            src, dst, send, recv, device_id={"col": 1 - self.c}, device_id_type=MESH
        )


def gather_tokens(place, buf, rows, length, send_p, recv_p, send_m, recv_m):
    def region(slot):
        return buf.at[pl.ds(pl.multiple_of(slot * length + place.c * rows, rows), rows)]

    own = region(place.d)

    def peer(k):
        return place.to_dp(own, own, send_p.at[k], recv_p.at[k], place.ahead(k))

    def mate(k):
        part = region(place.behind(k))
        return place.to_mate(part, part, send_m.at[k], recv_m.at[k])

    def start():
        mate(0).start()
        for k in range(1, place.n):
            peer(k).start()

    def fetch(k):
        peer(k).wait_recv()
        forward = mate(k)
        forward.start()
        forward.wait_recv()

    def finish():
        def one(k, unused):
            peer(k).wait_send()
            mate(k).wait_send()
            return unused

        mate(0).wait_send()
        lax.fori_loop(1, place.n, one, 0)

    return start, lambda: mate(0).wait_recv(), fetch, finish


def norm_stats(residual):
    mean = jnp.mean(residual, axis=1, keepdims=True)
    centered = residual - mean
    variance = jnp.mean(centered * centered, axis=1, keepdims=True)
    inv = lax.rsqrt(variance + EPS)
    return centered * inv, inv


def sum_to_owner(place, rows, mate_out, mate_in, sum_out, sum_in, own, send_m, recv_m, send_p, recv_p):
    def to_mate(slot):
        return place.to_mate(mate_out.at[slot], mate_in.at[slot], send_m.at[slot], recv_m.at[slot])

    def to_owner(slot):
        k = lax.rem(slot - place.d + place.n, place.n)
        return place.to_dp(sum_out.at[slot], sum_in.at[k], send_p.at[k], recv_p.at[k], slot)

    def close(slot, mine):
        to_mate(slot).wait_recv()

        def work(r):
            own[mine, r] = own[mine, r] + mate_in[slot, r].astype(F32)

        over_rows(rows, 16, work)

        @pl.when(slot != place.d)
        def _():
            sum_out[slot] = own[mine].astype(BF)
            to_owner(slot).start()

    def receive():
        def one(k, unused):
            to_owner(place.ahead(k)).wait_recv()
            return unused

        lax.fori_loop(1, place.n, one, 0)

    def finish():
        def one(k, unused):
            to_owner(place.ahead(k)).wait_send()
            return unused

        lax.fori_loop(1, place.n, one, 0)

        def two(s, unused):
            to_mate(s).wait_send()
            return unused

        lax.fori_loop(0, place.n, two, 0)

    return to_mate, close, receive, finish


def fwd_kernel(
    n, res_ref, gain_ref, shift_ref, mask_ref, own_mask_ref, w_in_ref, w_mx_ref, w_out_ref, in_bias_ref,
    mix_bias_ref, out_bias_ref, kre_ref, kim_ref, ft_ref, f_ref,
    new_ref, g_out, mx_out, pre_out, u_out, y_out, pm_out, prod_out,
    w_in_t, w_mx_t, g, mx, pre, u_sp, y, pm, prod, act, spec, y_hat, prod_f, prod_t,
    own, mate_out, mate_in, sum_out, sum_in,
    send_a, recv_a, send_am, recv_am, send_b, recv_b, send_bm, recv_bm, send_c, recv_c, send_cm, recv_cm, save,
):
    place = Place(n)
    d, c = place.d, place.c
    rows, width = res_ref.shape
    length = mask_ref.shape[2]
    hid = w_mx_ref.shape[1]
    ch2 = kre_ref.shape[0]
    ch = ch2 // 2

    place.greet()
    start_a, own_a, fetch_a, finish_a = gather_tokens(place, g, rows, length, send_a, recv_a, send_am, recv_am)
    base = d * length + c * rows

    def norm(r):
        xhat, _ = norm_stats(res_ref[r])
        at = pl.ds(pl.multiple_of(base + r.start, 16), 16)
        g[at] = (xhat * gain_ref[...] + shift_ref[...]).astype(BF)

    over_rows(rows, 16, norm)
    start_a()

    def turn_in(r):
        w_in_t[r] = w_in_ref[:, r].astype(F32).T.astype(BF)

    over_rows(w_in_ref.shape[1], 128, turn_in)

    def turn_mx(r):
        w_mx_t[:, r] = w_mx_ref[r].astype(F32).T.astype(BF)

    over_rows(w_mx_ref.shape[0], 128, turn_mx)
    own_a()

    def chunk(owner, slot):
        at = pl.ds(pl.multiple_of((c * n + owner) * ch, ch), ch)
        return mx.at[at, pl.ds(pl.multiple_of(slot * length, length), length)]

    def peer_b(k, slot):
        part = chunk(d, slot)
        return place.to_dp(part, part, send_b.at[slot, k], recv_b.at[slot, k], place.ahead(k))

    def mate_b(k, slot):
        part = chunk(place.behind(k), slot)
        return place.to_mate(part, part, send_bm.at[slot, k], recv_bm.at[slot, k])

    def saves(slot, item):
        lanes = pl.ds(pl.multiple_of(slot * length, length), length)
        src, dst = (
            lambda: (g.at[lanes], g_out.at[lanes]),
            lambda: (u_sp.at[slot], u_out.at[slot]),
            lambda: (y.at[slot], y_out.at[slot]),
            lambda: (pre.at[slot], pre_out.at[slot]),
            lambda: (mx.at[:, lanes], mx_out.at[:, lanes]),
            lambda: (pm.at[slot], pm_out.at[slot]),
            lambda: (prod.at[:, lanes], prod_out.at[:, lanes]),
        )[item]()
        return pltpu.make_async_copy(src, dst, save.at[item, slot])

    def scan_slot(i, unused):
        slot = lax.select(i == 0, d, place.other(i - 1))

        @pl.when(i > 0)
        def _():
            fetch_a(lax.rem(d - slot + n, n))

        lanes = pl.ds(pl.multiple_of(slot * length, length), length)
        pre[slot] = dot(w_in_t[...], g[lanes], 1, 1)
        live = mask_ref[slot]

        def acts(r):
            v = pre[slot, r] + in_bias_ref[r]
            pre[slot, r] = v
            act[r] = (gelu_only(v) * live).astype(BF)

        over_rows(ch2, CHUNK, acts)

        def shift_value(r):
            at = pl.ds(pl.multiple_of(ch2 + r.start, CHUNK), CHUNK)
            pre[slot, at] = pre[slot, at] + in_bias_ref[at]

        over_rows(hid, CHUNK, shift_value)
        spec[...] = dot(act[...], ft_ref[...], 1, 0)

        def multiply(r):
            u_re, u_im = spec[r, :length], spec[r, length:]
            k_re, k_im = kre_ref[r], kim_ref[r]
            u_sp[slot, r, :length] = u_re.astype(BF)
            u_sp[slot, r, length:] = u_im.astype(BF)
            y_hat[r, :length] = (k_re * u_re - k_im * u_im).astype(BF)
            y_hat[r, length:] = (k_re * u_im + k_im * u_re).astype(BF)

        over_rows(ch2, 16, multiply)
        y[slot] = dot(y_hat[...], f_ref[...], 1, 0)
        mine = (c * n + d) * ch

        def mix(r):
            back = pl.ds(pl.multiple_of(ch + r.start, 16), 16)
            at = pl.ds(pl.multiple_of(mine + r.start, 16), 16)
            mx[at, lanes] = (y[slot, r] * y[slot, back]).astype(BF)

        over_rows(ch, 16, mix)
        mate_b(0, slot).start()
        for k in range(1, n):
            peer_b(k, slot).start()
        for item in range(4):
            saves(slot, item).start()
        return unused

    lax.fori_loop(0, n, scan_slot, 0)

    to_mate, close, receive, finish_c = sum_to_owner(
        place, rows, mate_out, mate_in, sum_out, sum_in, own, send_cm, recv_cm, send_c, recv_c
    )

    def order(i):
        return lax.select(i == n - 1, d, place.other(i))

    def hidden_slot(i, unused):
        slot = order(i)
        lanes = pl.ds(pl.multiple_of(slot * length, length), length)
        for k in range(1, n):
            peer_b(k, slot).wait_recv()
            mate_b(k, slot).start()
        for k in range(n):
            mate_b(k, slot).wait_recv()
        pm[slot] = dot(w_mx_t[...], mx[:, lanes], 1, 0)

        def gate(r):
            v = pm[slot, r] + mix_bias_ref[r]
            pm[slot, r] = v
            at = pl.ds(pl.multiple_of(ch2 + r.start, CHUNK), CHUNK)
            product = gelu_only(v) * gelu_only(pre[slot, at])
            prod_f[r] = product
            prod[r, lanes] = product.astype(BF)

        over_rows(hid, CHUNK, gate)
        prod_t[...] = prod_f[...].T.astype(BF)
        for item in range(4, 7):
            saves(slot, item).start()
        theirs = pl.ds(pl.multiple_of((1 - c) * rows, rows), rows)
        ours = pl.ds(pl.multiple_of(c * rows, rows), rows)
        mate_out[slot] = dot(prod_t[theirs], w_out_ref[...], 1, 0).astype(BF)
        to_mate(slot).start()

        @pl.when(i > 0)
        def _():
            close(order(i - 1), lax.rem(i - 1, 2))

        own[lax.rem(i, 2)] = dot(prod_t[ours], w_out_ref[...], 1, 0)
        return unused

    lax.fori_loop(0, n, hidden_slot, 0)
    last = (n - 1) % 2
    close(d, last)
    receive()

    def final(r):
        total = own[last, r]
        for k in range(1, n):
            total = total + sum_in[k, r].astype(F32)
        new_ref[r] = res_ref[r] + own_mask_ref[r] * (total + out_bias_ref[...])

    over_rows(rows, 16, final)
    finish_a()
    finish_c()

    def drain(slot, unused):
        for k in range(1, n):
            peer_b(k, slot).wait_send()
        for k in range(n):
            mate_b(k, slot).wait_send()
        for item in range(7):
            saves(slot, item).wait()
        return unused

    lax.fori_loop(0, n, drain, 0)


def bwd_kernel(
    n, grad_ref, res_ref, gain_ref, mask_ref, own_mask_ref, w_in_ref, w_mx_ref, w_out_ref, kre_ref, kim_ref,
    ft_ref, f_ref, g_in, mx_in, pre_in, u_in, y_in, pm_in, prod_in,
    new_ref, gw_in_ref, gw_mx_ref, gw_out_ref, in_sum_ref, mix_sum_ref, norm_sum_ref, dk_ref,
    gb, g, mx, pre, u_sp, y, pm, prod, gpre, gpre_f, gpm, gact, spec, hat, turned,
    mix_out, mix_mate, mix_own, mix_sum, mix_got,
    own, mate_out, mate_in, sum_out, sum_in,
    send_a, recv_a, send_am, recv_am, send_b, recv_b, send_bm, recv_bm, send_c, recv_c, send_cm, recv_cm, load,
):
    place = Place(n)
    d, c = place.d, place.c
    rows, width = res_ref.shape
    length = mask_ref.shape[2]
    hid = w_mx_ref.shape[1]
    ch2 = kre_ref.shape[0]
    ch = ch2 // 2
    half = n * ch

    def loads(slot, item):
        lanes = pl.ds(pl.multiple_of(slot * length, length), length)
        src, dst = (
            lambda: (pre_in.at[slot], pre.at[slot]),
            lambda: (pm_in.at[slot], pm.at[slot]),
            lambda: (y_in.at[slot], y.at[slot]),
            lambda: (u_in.at[slot], u_sp.at[slot]),
            lambda: (prod_in.at[:, lanes], prod.at[:, lanes]),
            lambda: (mx_in.at[:, lanes], mx.at[:, lanes]),
            lambda: (g_in.at[lanes], g.at[lanes]),
        )[item]()
        return pltpu.make_async_copy(src, dst, load.at[item, slot])

    for item in range(7):
        loads(d, item).start()

    def start_loads(i, unused):
        for item in range(7):
            loads(place.other(i), item).start()
        return unused

    lax.fori_loop(0, n - 1, start_loads, 0)

    place.greet()
    start_a, own_a, fetch_a, finish_a = gather_tokens(place, gb, rows, length, send_a, recv_a, send_am, recv_am)
    base = d * length + c * rows

    norm_sum_ref[...] = jnp.zeros_like(norm_sum_ref)

    def first(r):
        part = grad_ref[r] * own_mask_ref[r]
        at = pl.ds(pl.multiple_of(base + r.start, 16), 16)
        gb[at] = part.astype(BF)
        norm_sum_ref[2:3] = norm_sum_ref[2:3] + jnp.sum(part, axis=0, keepdims=True)

    over_rows(rows, 16, first)
    start_a()
    in_sum_ref[...] = jnp.zeros_like(in_sum_ref)
    mix_sum_ref[...] = jnp.zeros_like(mix_sum_ref)
    dk_ref[...] = jnp.zeros_like(dk_ref)
    own_a()

    def mate_b(slot):
        return place.to_mate(mix_out.at[slot], mix_mate.at[slot], send_bm.at[slot], recv_bm.at[slot])

    def peer_b(k, slot):
        q = place.ahead(k)
        part = mix_sum.at[slot, pl.ds(pl.multiple_of(q * ch, ch), ch)]
        return place.to_dp(part, mix_got.at[k, slot], send_b.at[slot, k], recv_b.at[slot, k], q)

    def hidden_slot(i, unused):
        slot = lax.select(i == 0, d, place.other(i - 1))

        @pl.when(i > 0)
        def _():
            fetch_a(lax.rem(d - slot + n, n))

        lanes = pl.ds(pl.multiple_of(slot * length, length), length)
        gact[...] = dot(w_out_ref[...], gb[lanes], 1, 1)
        for item in range(2):
            loads(slot, item).wait()

        def gates(r):
            at = pl.ds(pl.multiple_of(ch2 + r.start, 16), 16)
            gated, slope = gelu_parts(pm[slot, r])
            value, value_slope = gelu_parts(pre[slot, at])
            now = gact[r]
            to_value = now * gated * value_slope
            to_mix = now * value * slope
            gpre[at, lanes] = to_value.astype(BF)
            gpm[r, lanes] = to_mix.astype(BF)
            in_sum_ref[at] = in_sum_ref[at] + jnp.sum(to_value, axis=1, keepdims=True)
            mix_sum_ref[r] = mix_sum_ref[r] + jnp.sum(to_mix, axis=1, keepdims=True)

        over_rows(hid, 16, gates)
        theirs = pl.ds(pl.multiple_of((1 - c) * half, half), half)
        ours = pl.ds(pl.multiple_of(c * half, half), half)
        mix_out[slot] = dot(w_mx_ref[theirs], gpm[:, lanes], 1, 0).astype(BF)
        mate_b(slot).start()
        mix_own[...] = dot(w_mx_ref[ours], gpm[:, lanes], 1, 0)
        mate_b(slot).wait_recv()

        def add(r):
            mix_sum[slot, r] = (mix_own[r] + mix_mate[slot, r].astype(F32)).astype(BF)

        over_rows(half, 16, add)
        for k in range(1, n):
            peer_b(k, slot).start()
        return unused

    lax.fori_loop(0, n, hidden_slot, 0)

    def wait_loads(slot, unused):
        for item in range(2, 7):
            loads(slot, item).wait()
        return unused

    lax.fori_loop(0, n, wait_loads, 0)
    gw_out_ref[...] = dot(prod[...], gb[...], 1, 0).astype(BF)

    def grad_mix(r):
        gw_mx_ref[r] = dot(mx[r], gpm[...], 1, 1).astype(BF)

    over_rows(mx.shape[0], 256, grad_mix)

    to_mate, close, receive, finish_c = sum_to_owner(
        place, rows, mate_out, mate_in, sum_out, sum_in, own, send_cm, recv_cm, send_c, recv_c
    )

    def order(i):
        return lax.select(i == n - 1, d, place.other(i))

    def scan_slot(i, unused):
        slot = order(i)
        lanes = pl.ds(pl.multiple_of(slot * length, length), length)
        for k in range(1, n):
            peer_b(k, slot).wait_recv()

        def outer(r):
            at = pl.ds(pl.multiple_of(d * ch + r.start, 16), 16)
            back = pl.ds(pl.multiple_of(ch + r.start, 16), 16)
            total = mix_sum[slot, at].astype(F32)
            for k in range(1, n):
                total = total + mix_got[k, slot, r].astype(F32)
            hat[r, :length] = (total * y[slot, back]).astype(BF)
            hat[back, :length] = (total * y[slot, r]).astype(BF)

        over_rows(ch, 16, outer)
        spec[...] = dot(hat[:, :length], ft_ref[...], 1, 0)

        def multiply(r):
            g_re, g_im = spec[r, :length], spec[r, length:]
            k_re, k_im = kre_ref[r], kim_ref[r]
            hat[r, :length] = (k_re * g_re + k_im * g_im).astype(BF)
            hat[r, length:] = (k_re * g_im - k_im * g_re).astype(BF)
            u_re, u_im = u_sp[slot, r, :length].astype(F32), u_sp[slot, r, length:].astype(F32)
            dk_ref[r, :length] = dk_ref[r, :length] + (u_re * g_re + u_im * g_im)
            dk_ref[r, length:] = dk_ref[r, length:] + (u_re * g_im - u_im * g_re)

        over_rows(ch2, 16, multiply)
        spec[:, :length] = dot(hat[...], f_ref[...], 1, 0)
        live = mask_ref[slot]

        def inner(r):
            _, slope = gelu_parts(pre[slot, r])
            part = spec[r, :length] * slope * live
            gpre_f[r] = part
            gpre[r, lanes] = part.astype(BF)
            in_sum_ref[r] = in_sum_ref[r] + jnp.sum(part, axis=1, keepdims=True)

        over_rows(ch2, 16, inner)
        turned[:, :ch2] = gpre_f[...].T.astype(BF)
        gpre_f[...] = gpre[ch2:, lanes].astype(F32)
        turned[:, ch2:] = gpre_f[...].T.astype(BF)
        theirs = pl.ds(pl.multiple_of((1 - c) * rows, rows), rows)
        ours = pl.ds(pl.multiple_of(c * rows, rows), rows)
        mate_out[slot] = dot(turned[theirs], w_in_ref[...], 1, 1).astype(BF)
        to_mate(slot).start()

        @pl.when(i > 0)
        def _():
            close(order(i - 1), lax.rem(i - 1, 2))

        own[lax.rem(i, 2)] = dot(turned[ours], w_in_ref[...], 1, 1)
        return unused

    lax.fori_loop(0, n, scan_slot, 0)
    last = (n - 1) % 2
    close(d, last)

    def grad_in(r):
        gw_in_ref[:, r] = dot(gpre[r], g[...], 1, 0).T.astype(BF)

    over_rows(gpre.shape[0], 128, grad_in)
    receive()

    def final(r):
        total = own[last, r]
        for k in range(1, n):
            total = total + sum_in[k, r].astype(F32)
        xhat, inv = norm_stats(res_ref[r])
        h = total * gain_ref[...]
        middle = jnp.mean(h, axis=1, keepdims=True)
        along = jnp.mean(h * xhat, axis=1, keepdims=True)
        new_ref[r] = grad_ref[r] + inv * (h - middle - xhat * along)
        norm_sum_ref[0:1] = norm_sum_ref[0:1] + jnp.sum(total * xhat, axis=0, keepdims=True)
        norm_sum_ref[1:2] = norm_sum_ref[1:2] + jnp.sum(total, axis=0, keepdims=True)

    over_rows(rows, 16, final)
    finish_a()
    finish_c()

    def drain(slot, unused):
        mate_b(slot).wait_send()
        for k in range(1, n):
            peer_b(k, slot).wait_send()
        return unused

    lax.fori_loop(0, n, drain, 0)


def tables_kernel(decay_ref, step_ref, b_ref, c_ref, skip_ref, sign_ref, ft_ref, kre_ref, kim_ref, rate, lead):
    length = ft_ref.shape[0]
    blocks = length // LAG
    decay = decay_ref[0]
    rate[...] = jnp.exp(step_ref[0]) * jnp.exp(decay)
    weight = (1.0 - jnp.exp(-rate[...])) * jnp.exp(-decay) * b_ref[0] * c_ref[0]
    for b in range(blocks):
        lead[b] = weight * jnp.exp(-(LAG * b) * rate[...])
    lanes = rate.shape[1]
    offs = lax.broadcasted_iota(jnp.int32, (LAG, lanes), 0).astype(F32)

    def state(i, totals):
        powers = jnp.exp(-offs * rate[pl.ds(i, 1)])
        return tuple(totals[b] + powers * lead[b, pl.ds(i, 1)] for b in range(blocks))

    zero = jnp.zeros((LAG, lanes), F32)
    totals = list(lax.fori_loop(0, rate.shape[0], state, (zero,) * blocks))
    at_zero = lax.broadcasted_iota(jnp.int32, (LAG, lanes), 0) == 0
    totals[0] = totals[0] + jnp.where(at_zero, skip_ref[0], 0.0)
    kernel = jnp.concatenate(totals, axis=0)
    k_hat = dot(kernel.T.astype(BF), ft_ref[...], 1, 0) * (1.0 / length)
    kre_ref[0] = k_hat[:, :length]
    kim_ref[0] = k_hat[:, length:] * sign_ref[...]


def params_kernel(
    dk_ref, decay_ref, step_ref, b_ref, c_ref, sign_ref, ft_ref, g_decay, g_b, g_c, g_row, lag_sums
):
    length = ft_ref.shape[0]
    re = dk_ref[:, :length].astype(BF)
    im = (dk_ref[:, length:] * sign_ref[...]).astype(BF)
    lag_sums[...] = (dot(ft_ref[:, :length], re, 1, 1) + dot(ft_ref[:, length:], im, 1, 1)) * (1.0 / length)
    decay = decay_ref[...]
    rate = jnp.exp(step_ref[...]) * jnp.exp(decay)
    a = jnp.exp(-rate)

    def lag(i, carry):
        total, slope = carry
        row = lag_sums[pl.ds(length - 1 - i, 1)]
        return total * a + row, slope * a + total

    zero = jnp.zeros_like(a)
    total, slope = lax.fori_loop(0, length, lag, (zero, zero))
    inv_decay = jnp.exp(-decay)
    gain = (1.0 - a) * inv_decay
    b_in, c_out = b_ref[...], c_ref[...]
    b_disc = gain * b_in
    to_b = c_out * total
    to_rate = a * (to_b * inv_decay * b_in - (c_out * b_disc) * slope)
    through = to_rate * rate
    g_decay[...] = through - to_b * b_disc
    g_b[...] = to_b * gain
    g_c[...] = b_disc * total
    g_row[...] = jnp.zeros_like(g_row)
    g_row[0:1] = jnp.sum(through, axis=0, keepdims=True)
    g_row[1:2] = lag_sums[0:1]


VM = pl.BlockSpec(memory_space=pltpu.VMEM)
ANY = pl.BlockSpec(memory_space=pl.ANY)


def shape(dims, dtype):
    return jax.ShapeDtypeStruct(tuple(dims), dtype)


def sem(*dims):
    return pltpu.SemaphoreType.DMA(dims)


def body(
    tokens_in, lengths, cotangent, norm_gain, norm_shift, w_fwd, w_bwd, w_value, bias_fwd, bias_bwd,
    bias_value, decay_log, step_log, b_input, c_output, skip_gain, w_mix, bias_mix, w_output, bias_output,
):
    n = lax.axis_size("dp")
    cols = lax.axis_size("col")
    d = lax.axis_index("dp")
    rows, width = tokens_in.shape
    length = rows * cols
    ch = w_fwd.shape[2] // n
    ch2 = 2 * ch
    hid = w_mix.shape[2] // n
    wide = ch2 + hid
    chans = n * cols * ch
    tokens = n * length
    matrix = transform_matrix(length)
    f_mat = jnp.asarray(matrix, BF)
    ft_mat = jnp.asarray(np.ascontiguousarray(matrix.T), BF)

    def mine(x, size, axis):
        return lax.dynamic_slice_in_dim(x, d * size, size, axis)

    weights = []
    for l in range(LAYERS):
        w_in = jnp.concatenate(
            (mine(w_fwd[l], ch, 1), mine(w_bwd[l], ch, 1), mine(w_value[l], hid, 1)), axis=1
        ).astype(BF)
        w_in = lax.all_gather(w_in, "row", axis=0, tiled=True)
        w_mx = lax.all_gather(mine(w_mix[l], hid, 1).astype(BF), "row", axis=0, tiled=True)
        w_out = lax.all_gather(mine(w_output[l], hid, 0).astype(BF), "row", axis=1, tiled=True)
        in_bias = jnp.concatenate(
            (mine(bias_fwd[l], ch, 0), mine(bias_bwd[l], ch, 0), mine(bias_value[l], hid, 0))
        )[:, None]
        mix_bias = mine(bias_mix[l], hid, 0)[:, None]
        weights.append((w_in, w_mx, w_out, in_bias, mix_bias))

    all_lengths = lax.all_gather(lengths, "dp", axis=0, tiled=True)
    positions = jnp.arange(length, dtype=jnp.int32)
    mask = (positions[None, :] < all_lengths[:, None]).astype(F32)[:, None, :]
    own_mask = lax.dynamic_slice_in_dim(
        (positions < lengths[0]).astype(F32), lax.axis_index("col") * rows, rows, 0
    )[:, None]

    def states_first(x):
        part = mine(x, ch, 2)
        return part.transpose(0, 3, 1, 2).reshape(LAYERS, x.shape[3], ch2)

    def one_row(x):
        return mine(x, ch, 2).reshape(LAYERS, 1, ch2)

    decay_t, b_t, c_t = states_first(decay_log), states_first(b_input), states_first(c_output)
    step_t, skip_t = one_row(step_log), one_row(skip_gain)
    states = decay_t.shape[1]
    sign = jnp.where(jnp.arange(ch2) < ch, 1.0, -1.0).astype(F32)[:, None]
    lane = 128
    by_state = pl.BlockSpec((1, states, lane), lambda l, j: (l, 0, j))
    by_row = pl.BlockSpec((1, 1, lane), lambda l, j: (l, 0, j))
    by_sign = pl.BlockSpec((lane, 1), lambda l, j: (j, 0))
    by_chan = pl.BlockSpec((1, lane, length), lambda l, j: (l, j, 0))
    k_re, k_im = pl.pallas_call(
        tables_kernel,
        grid=(LAYERS, ch2 // lane),
        out_shape=(shape((LAYERS, ch2, length), F32),) * 2,
        in_specs=[by_state, by_row, by_state, by_state, by_row, by_sign,
                  pl.BlockSpec((length, 2 * length), lambda l, j: (0, 0))],
        out_specs=(by_chan, by_chan),
        scratch_shapes=[pltpu.VMEM((states, lane), F32), pltpu.VMEM((length // LAG, states, lane), F32)],
        name="tables",
    )(decay_t, step_t, b_t, c_t, skip_t, sign, ft_mat)

    comm = [
        sem(n), sem(n), sem(n), sem(n), sem(n, n), sem(n, n),
    ]
    sums = [
        pltpu.VMEM((2, rows, width), F32), pltpu.VMEM((n, rows, width), BF), pltpu.VMEM((n, rows, width), BF),
        pltpu.VMEM((n, rows, width), BF), pltpu.VMEM((n, rows, width), BF),
    ]
    saved_shapes = (
        shape((tokens, width), BF), shape((chans, tokens), BF), shape((n, wide, length), F32),
        shape((n, ch2, 2 * length), BF), shape((n, ch2, length), F32), shape((n, hid, length), F32),
        shape((hid, tokens), BF),
    )
    fwd = pl.pallas_call(
        functools.partial(fwd_kernel, n),
        out_shape=(shape((rows, width), F32), *saved_shapes),
        in_specs=[VM] * 15,
        out_specs=(VM, *([ANY] * 7)),
        scratch_shapes=[
            pltpu.VMEM((wide, width), BF), pltpu.VMEM((hid, chans), BF),
            *(pltpu.VMEM(s.shape, s.dtype) for s in saved_shapes),
            pltpu.VMEM((ch2, length), BF), pltpu.VMEM((ch2, 2 * length), F32), pltpu.VMEM((ch2, 2 * length), BF),
            pltpu.VMEM((hid, length), F32), pltpu.VMEM((length, hid), BF),
            *sums, *comm, sem(n, n), sem(n, n), sem(n), sem(n), sem(n), sem(n), sem(7, n),
        ],
        compiler_params=pltpu.CompilerParams(
            collective_id=0, has_side_effects=True, vmem_limit_bytes=VMEM_LIMIT
        ),
        name="forward_block",
    )
    bwd = pl.pallas_call(
        functools.partial(bwd_kernel, n),
        out_shape=(
            shape((rows, width), F32), shape((width, wide), BF), shape((chans, hid), BF), shape((hid, width), BF),
            shape((wide, 1), F32), shape((hid, 1), F32), shape((8, width), F32), shape((ch2, 2 * length), F32),
        ),
        in_specs=[VM] * 12 + [ANY] * 7,
        out_specs=(VM,) * 8,
        scratch_shapes=[
            pltpu.VMEM((tokens, width), BF),
            *(pltpu.VMEM(s.shape, s.dtype) for s in saved_shapes),
            pltpu.VMEM((wide, tokens), BF), pltpu.VMEM((ch2, length), F32), pltpu.VMEM((hid, tokens), BF),
            pltpu.VMEM((hid, length), F32), pltpu.VMEM((ch2, 2 * length), F32), pltpu.VMEM((ch2, 2 * length), BF),
            pltpu.VMEM((length, wide), BF),
            pltpu.VMEM((n, n * ch, length), BF), pltpu.VMEM((n, n * ch, length), BF),
            pltpu.VMEM((n * ch, length), F32), pltpu.VMEM((n, n * ch, length), BF),
            pltpu.VMEM((n, n, ch, length), BF),
            *sums, *comm, sem(n), sem(n), sem(n), sem(n), sem(n), sem(n), sem(7, n),
        ],
        compiler_params=pltpu.CompilerParams(
            collective_id=1, has_side_effects=True, vmem_limit_bytes=VMEM_LIMIT
        ),
        name="backward_block",
    )

    residual = tokens_in.astype(F32)
    stored = []
    for l in range(LAYERS):
        w_in, w_mx, w_out, in_bias, mix_bias = weights[l]
        new, *saved = fwd(
            residual, norm_gain[l][None], norm_shift[l][None], mask, own_mask, w_in, w_mx, w_out, in_bias,
            mix_bias, bias_output[l][None], k_re[l], k_im[l], ft_mat, f_mat,
        )
        stored.append((residual, saved))
        residual = new
    tokens_out = residual.astype(BF)

    by_all = pl.BlockSpec((states, lane), lambda j: (0, j))
    params = pl.pallas_call(
        params_kernel,
        grid=(ch2 // lane,),
        out_shape=(shape((states, ch2), F32),) * 3 + (shape((8, ch2), F32),),
        in_specs=[
            pl.BlockSpec((lane, 2 * length), lambda j: (j, 0)), by_all, pl.BlockSpec((1, lane), lambda j: (0, j)),
            by_all, by_all, pl.BlockSpec((lane, 1), lambda j: (j, 0)),
            pl.BlockSpec((length, 2 * length), lambda j: (0, 0)),
        ],
        out_specs=(by_all, by_all, by_all, pl.BlockSpec((8, lane), lambda j: (0, j))),
        scratch_shapes=[pltpu.VMEM((length, lane), F32)],
        name="state_gradients",
    )

    def spread(x, axis):
        return lax.all_gather(x, "dp", axis=axis, tiled=True).astype(F32)

    grad = cotangent.astype(F32)
    outs = []
    for l in reversed(range(LAYERS)):
        w_in, w_mx, w_out, _, _ = weights[l]
        resid_in, saved = stored[l]
        grad, gw_in, gw_mix, gw_out, in_sum, mix_sum, norm_part, dk = bwd(
            grad, resid_in, norm_gain[l][None], mask, own_mask, w_in, w_mx, w_out, k_re[l], k_im[l], ft_mat,
            f_mat, *saved,
        )
        row_in = lax.psum_scatter(gw_in, "row", scatter_dimension=0, tiled=True)
        row_mix = lax.psum_scatter(gw_mix, "row", scatter_dimension=0, tiled=True)
        row_out = lax.psum_scatter(gw_out, "row", scatter_dimension=1, tiled=True)
        g_decay, g_b, g_c, g_row = params(dk, decay_t[l], step_t[l], b_t[l], c_t[l], sign, ft_mat)
        small = jnp.concatenate((in_sum[:, 0], mix_sum[:, 0], g_row[0], g_row[1]))
        big = jnp.stack((g_decay, g_b, g_c))
        small, big = lax.psum((small, big), "row")
        small = lax.all_gather(small, "dp", axis=0, tiled=False)
        big = big.reshape(3, states, 2, ch).transpose(0, 2, 3, 1)
        big = lax.all_gather(big, "dp", axis=2, tiled=True)
        norm_sums = lax.psum(norm_part, ("dp", "row", "col"))
        cuts = np.cumsum([0, ch, ch, hid, hid, ch, ch, ch, ch])
        parts = [small[:, cuts[i] : cuts[i + 1]].reshape(-1) for i in range(8)]
        outs.append((
            norm_sums[0], norm_sums[1],
            spread(row_in[:, :ch], 1), spread(row_in[:, ch:ch2], 1), spread(row_in[:, ch2:], 1),
            parts[0], parts[1], parts[2],
            big[0], jnp.stack((parts[4], parts[5])), big[1], big[2], jnp.stack((parts[6], parts[7])),
            spread(row_mix, 1), parts[3], spread(row_out, 0), norm_sums[2],
        ))
    ordered = outs[::-1]
    stacked = [jnp.stack([entry[i] for entry in ordered]) for i in range(17)]
    return (tokens_out, grad, *stacked)


def solution(mesh):
    tokens = P(("dp", "row", "col"), None)
    weight = P(None, "row", "col")
    bias = P(None, "col")
    state = P(None, None, "col", None)
    chan = P(None, None, "col")
    in_specs = (
        tokens, P(("dp", "row")), tokens, P(), P(), weight, weight, weight, bias, bias, bias,
        state, chan, state, state, chan, weight, bias, P(None, "col", "row"), P(),
    )
    out_specs = (
        tokens, tokens, P(), P(), weight, weight, weight, bias, bias, bias,
        state, chan, state, state, chan, weight, bias, P(None, "col", "row"), P(),
    )
    return jax.shard_map(body, mesh=mesh, in_specs=in_specs, out_specs=out_specs, check_vma=False)
```

```python
import functools

import jax
import jax.numpy as jnp
import numpy as np
from jax import lax
from jax.experimental import pallas as pl
from jax.experimental.pallas import tpu as pltpu
from jax.sharding import PartitionSpec as P

LAYERS = 2
EPS = 1e-05
LAG = 64
BF = jnp.bfloat16
F32 = jnp.float32
MESH = pl.DeviceIdType.MESH
VMEM_LIMIT = 60 * 1024 * 1024


def transform_matrix(length):
    k = np.arange(length)[:, None]
    t = np.arange(length)[None, :]
    angle = np.pi * (((2 * k + 1) * t) % (4 * length)) / (2 * length)
    return np.concatenate((np.cos(angle), -np.sin(angle)), axis=0)


def gelu_only(v):
    t = jnp.tanh(v * (0.7978845608 + 0.035677408 * v * v))
    return (0.5 * v) * (1.0 + t)


def gelu_parts(v):
    sq = v * v
    t = jnp.tanh(v * (0.7978845608 + 0.035677408 * sq))
    half = 0.5 + 0.5 * t
    slope = half + (v * half) * (1.0 - t) * (0.7978845608 + 0.107032225 * sq)
    return v * half, slope


def dot(a, b, ca, cb):
    return lax.dot_general(a, b, (((ca,), (cb,)), ((), ())), preferred_element_type=F32)


def over_rows(rows, step, work):
    def one(i, unused):
        work(pl.ds(pl.multiple_of(i * step, step), step))
        return unused

    lax.fori_loop(0, rows // step, one, 0)


def lane_sums(x):
    total = x[:, :128]
    for i in range(1, x.shape[1] // 128):
        total = total + x[:, 128 * i : 128 * (i + 1)]
    return total


def as_row(partial):
    return lax.dot_general(
        jnp.ones((8, 128), F32), partial, (((1,), (1,)), ((), ())), precision=lax.Precision.HIGHEST,
        preferred_element_type=F32,
    )


class Place:
    def __init__(self, n, m):
        self.n = n
        self.m = m
        self.d = lax.axis_index("dp")
        self.c = lax.axis_index("col")
        self.r = lax.axis_index("row")

    def greet(self):
        barrier = pltpu.get_barrier_semaphore()

        def hail(device):
            pl.semaphore_signal(barrier, inc=1, device_id=device, device_id_type=MESH)

        for k in range(1, self.n):
            hail({"dp": self.ahead(k)})
        hail({"col": 1 - self.c})

        def one(j, unused):
            hail({"row": self.up(j)})
            return unused

        lax.fori_loop(1, self.m, one, 0)
        pl.semaphore_wait(barrier, self.n + self.m - 1)

    def ahead(self, k):
        return lax.rem(self.d + k, self.n)

    def behind(self, k):
        return lax.rem(self.d - k + self.n, self.n)

    def up(self, j):
        return lax.rem(self.r + j, self.m)

    def down(self, j):
        return lax.rem(self.r - j + self.m, self.m)

    def other(self, i):
        return i + (i + self.n - self.d) // self.n

    def to_dp(self, src, dst, send, recv, q):
        return pltpu.make_async_remote_copy(
            src, dst, send, recv, device_id={"dp": q}, device_id_type=MESH
        )

    def to_mate(self, src, dst, send, recv):
        return pltpu.make_async_remote_copy(
            src, dst, send, recv, device_id={"col": 1 - self.c}, device_id_type=MESH
        )

    def to_row(self, src, dst, send, recv, q):
        return pltpu.make_async_remote_copy(
            src, dst, send, recv, device_id={"row": q}, device_id_type=MESH
        )


class RowSum:
    def __init__(self, place, part, got, send, recv):
        self.place, self.part, self.got, self.send, self.recv = place, part, got, send, recv

    def copy(self, j):
        q = self.place.up(j)
        return self.place.to_row(self.part.at[q], self.got.at[j], self.send.at[j], self.recv.at[j], q)

    def each(self, act):
        def one(j, unused):
            act(self.copy(j))
            return unused

        lax.fori_loop(1, self.place.m, one, 0)

    def start(self):
        self.each(lambda copy: copy.start())

    def total(self):
        self.each(lambda copy: copy.wait_recv())
        total = self.part[self.place.r].astype(F32)
        if self.place.m <= 4:
            for j in range(1, self.place.m):
                total = total + self.got[j].astype(F32)
            return total
        return lax.fori_loop(1, self.place.m, lambda j, t: t + self.got[j].astype(F32), total)

    def finish(self):
        self.each(lambda copy: copy.wait_send())


def gather_tokens(place, buf, rows, length, send_p, recv_p, send_m, recv_m):
    def region(slot):
        return buf.at[pl.ds(pl.multiple_of(slot * length + place.c * rows, rows), rows)]

    own = region(place.d)

    def peer(k):
        return place.to_dp(own, own, send_p.at[k], recv_p.at[k], place.ahead(k))

    def mate(k):
        part = region(place.behind(k))
        return place.to_mate(part, part, send_m.at[k], recv_m.at[k])

    def start():
        mate(0).start()
        for k in range(1, place.n):
            peer(k).start()

    def fetch(k):
        peer(k).wait_recv()
        forward = mate(k)
        forward.start()
        forward.wait_recv()

    def finish():
        def one(k, unused):
            peer(k).wait_send()
            mate(k).wait_send()
            return unused

        mate(0).wait_send()
        lax.fori_loop(1, place.n, one, 0)

    return start, lambda: mate(0).wait_recv(), fetch, finish


def norm_stats(residual):
    mean = jnp.mean(residual, axis=1, keepdims=True)
    centered = residual - mean
    variance = jnp.mean(centered * centered, axis=1, keepdims=True)
    inv = lax.rsqrt(variance + EPS)
    return centered * inv, inv


def sum_to_owner(place, rows, mate_out, mate_in, sum_out, sum_in, own, send_m, recv_m, send_p, recv_p):
    def to_mate(slot):
        return place.to_mate(mate_out.at[slot], mate_in.at[slot], send_m.at[slot], recv_m.at[slot])

    def to_owner(slot):
        k = lax.rem(slot - place.d + place.n, place.n)
        return place.to_dp(sum_out.at[slot], sum_in.at[k], send_p.at[k], recv_p.at[k], slot)

    def close(slot, mine):
        to_mate(slot).wait_recv()

        own[mine] = own[mine] + mate_in[slot].astype(F32)

        @pl.when(slot != place.d)
        def _():
            sum_out[slot] = own[mine].astype(BF)
            to_owner(slot).start()

    def receive():
        def one(k, unused):
            to_owner(place.ahead(k)).wait_recv()
            return unused

        lax.fori_loop(1, place.n, one, 0)

    def finish():
        def one(k, unused):
            to_owner(place.ahead(k)).wait_send()
            return unused

        lax.fori_loop(1, place.n, one, 0)

        def two(s, unused):
            to_mate(s).wait_send()
            return unused

        lax.fori_loop(0, place.n, two, 0)

    return to_mate, close, receive, finish


class RowGather:
    def __init__(self, place, shard, land, send, recv):
        self.place, self.shard, self.land, self.send, self.recv = place, shard, land, send, recv

    def copy(self, j):
        place = self.place
        return place.to_row(self.shard, self.land.at[place.r], self.send.at[j], self.recv.at[j], place.up(j))

    def each(self, act):
        def one(j, unused):
            act(self.copy(j))
            return unused

        lax.fori_loop(1, self.place.m, one, 0)

    def start(self):
        self.each(lambda copy: copy.start())
        self.land[self.place.r] = self.shard[...]

    def whole(self):
        self.each(lambda copy: copy.wait_recv())
        m, rows, lanes = self.land.shape
        return self.land[...].astype(F32).reshape(m * rows, lanes)

    def finish(self):
        self.each(lambda copy: copy.wait_send())


def kernel_spectrum(decay, step, b_in, c_out, skip, sign, ft_ref, rate, lead):
    length = ft_ref.shape[0]
    blocks = length // LAG
    rate[...] = jnp.exp(step) * jnp.exp(decay)
    weight = (1.0 - jnp.exp(-rate[...])) * jnp.exp(-decay) * b_in * c_out
    for b in range(blocks):
        lead[b] = weight * jnp.exp(-(LAG * b) * rate[...])
    lanes = rate.shape[1]
    offs = lax.broadcasted_iota(jnp.int32, (LAG, lanes), 0).astype(F32)

    def state(i, totals):
        powers = jnp.exp(-offs * rate[pl.ds(i, 1)])
        return tuple(totals[b] + powers * lead[b, pl.ds(i, 1)] for b in range(blocks))

    zero = jnp.zeros((LAG, lanes), F32)
    totals = list(lax.fori_loop(0, rate.shape[0], state, (zero,) * blocks, unroll=2))
    at_zero = lax.broadcasted_iota(jnp.int32, (LAG, lanes), 0) == 0
    totals[0] = totals[0] + jnp.where(at_zero, skip, 0.0)
    kernel = jnp.concatenate(totals, axis=0)
    k_hat = dot(kernel.T.astype(BF), ft_ref[...], 1, 0) * (1.0 / length)
    return k_hat[:, :length], k_hat[:, length:] * sign


def fwd_kernel(
    n, m, first, res_ref, gain_ref, shift_ref, own_live_ref, own_mask_ref, sh_mx, sh_out, in_bias_ref,
    mix_bias_ref, out_bias_ref, ft_ref, f_ref, decay_ref, step_ref, b_ref, c_ref, skip_ref, sign_ref, *rest
):
    if first:
        sh_in, sh_next, *rest = rest
    else:
        w_in_ref, *rest = rest
    new_ref, g_out, mx_out, pre_out, u_out, y_out, pm_out, prod_out, kre_out, kim_out, w_mx_out, w_out_out, *rest = rest
    if first:
        w_in_out, next_out, mask_ref, *rest = rest
    else:
        mask_ref = own_live_ref
    (
        w_in_t, w_mx_t, g, mx, pre, u_sp, y, pm, prod, act, spec, y_hat, prod_f, prod_t,
        kre_ref, kim_ref, rate, lead, land_mx, land_out, w_out_t,
        own, mate_out, mate_in, sum_out, sum_in,
        send_a, recv_a, send_am, recv_am, send_b, recv_b, send_bm, recv_bm, send_c, recv_c, send_cm, recv_cm, save,
        send_gm, recv_gm, send_go, recv_go, *rest,
    ) = rest
    place = Place(n, m)
    d, c = place.d, place.c
    rows, width = res_ref.shape
    length = ft_ref.shape[0]
    hid = sh_mx.shape[1]
    ch2 = decay_ref.shape[1]
    ch = ch2 // 2

    place.greet()
    gather_mx = RowGather(place, sh_mx, land_mx, send_gm, recv_gm)
    gather_out = RowGather(place, sh_out, land_out, send_go, recv_go)
    start_a, own_a, fetch_a, finish_a = gather_tokens(place, g, rows, length, send_a, recv_a, send_am, recv_am)
    if first:
        land_in, land_next, send_gi, recv_gi, send_gn, recv_gn, send_mk, recv_mk = rest
        gather_in = RowGather(place, sh_in, land_in, send_gi, recv_gi)
        gather_next = RowGather(place, sh_next, land_next, send_gn, recv_gn)
        gather_in.start()

        def mask_peer(k):
            return place.to_dp(
                own_live_ref, mask_ref.at[d], send_mk.at[k], recv_mk.at[k], place.ahead(k)
            )

        for k in range(1, n):
            mask_peer(k).start()
        mask_ref[d] = own_live_ref[...]
    else:
        gather_mx.start()
        gather_out.start()
    base = d * length + c * rows
    xhat, _ = norm_stats(res_ref[...])
    g[pl.ds(pl.multiple_of(base, rows), rows)] = (xhat * gain_ref[...] + shift_ref[...]).astype(BF)
    start_a()
    for j in range(ch2 // 128):
        at = slice(128 * j, 128 * (j + 1))
        kre_ref[at], kim_ref[at] = kernel_spectrum(
            decay_ref[:, at], step_ref[:, at], b_ref[:, at], c_ref[:, at], skip_ref[:, at], sign_ref[at], ft_ref,
            rate, lead,
        )
    kre_out[...] = kre_ref[...]
    kim_out[...] = kim_ref[...]
    if first:
        w_in = gather_in.whole()
        gather_mx.start()
        gather_out.start()
        w_in_out[...] = w_in.astype(BF)
        for k in range(1, n):
            mask_peer(k).wait_recv()
    else:
        w_in = w_in_ref[...].astype(F32)
    w_in_t[...] = w_in.T.astype(BF)
    own_a()

    def chunk(owner, slot):
        at = pl.ds(pl.multiple_of((c * n + owner) * ch, ch), ch)
        return mx.at[at, pl.ds(pl.multiple_of(slot * length, length), length)]

    def peer_b(k, slot):
        part = chunk(d, slot)
        return place.to_dp(part, part, send_b.at[slot, k], recv_b.at[slot, k], place.ahead(k))

    def mate_b(k, slot):
        part = chunk(place.behind(k), slot)
        return place.to_mate(part, part, send_bm.at[slot, k], recv_bm.at[slot, k])

    def saves(slot, item):
        lanes = pl.ds(pl.multiple_of(slot * length, length), length)
        src, dst = (
            lambda: (g.at[lanes], g_out.at[lanes]),
            lambda: (u_sp.at[slot], u_out.at[slot]),
            lambda: (y.at[slot], y_out.at[slot]),
            lambda: (pre.at[slot], pre_out.at[slot]),
            lambda: (mx.at[:, lanes], mx_out.at[:, lanes]),
            lambda: (pm.at[slot], pm_out.at[slot]),
            lambda: (prod.at[:, lanes], prod_out.at[:, lanes]),
        )[item]()
        return pltpu.make_async_copy(src, dst, save.at[item, slot])

    def scan_slot(i, unused):
        slot = lax.select(i == 0, d, place.other(i - 1))

        @pl.when(i > 0)
        def _():
            fetch_a(lax.rem(d - slot + n, n))

        lanes = pl.ds(pl.multiple_of(slot * length, length), length)
        pre[slot] = dot(w_in_t[...], g[lanes], 1, 1)
        live = mask_ref[slot, 0:1]
        v = pre[slot, :ch2] + in_bias_ref[:ch2]
        pre[slot, :ch2] = v
        act[...] = (gelu_only(v) * live).astype(BF)
        pre[slot, ch2:] = pre[slot, ch2:] + in_bias_ref[ch2:]
        spec[...] = dot(act[...], ft_ref[...], 1, 0)
        u_re, u_im = spec[:, :length], spec[:, length:]
        k_re, k_im = kre_ref[...], kim_ref[...]
        u_sp[slot, :, :length] = u_re.astype(BF)
        u_sp[slot, :, length:] = u_im.astype(BF)
        y_hat[:, :length] = (k_re * u_re - k_im * u_im).astype(BF)
        y_hat[:, length:] = (k_re * u_im + k_im * u_re).astype(BF)
        y[slot] = dot(y_hat[...], f_ref[...], 1, 0)
        mine = pl.ds(pl.multiple_of((c * n + d) * ch, ch), ch)
        mx[mine, lanes] = (y[slot, :ch] * y[slot, ch:]).astype(BF)
        mate_b(0, slot).start()
        for k in range(1, n):
            peer_b(k, slot).start()
        for item in range(4):
            saves(slot, item).start()
        return unused

    lax.fori_loop(0, n, scan_slot, 0)
    w_mx = gather_mx.whole()
    w_mx_out[...] = w_mx.astype(BF)
    w_mx_t[...] = w_mx.T.astype(BF)
    w_out = gather_out.whole()
    w_out_t[...] = w_out.astype(BF)
    w_out_out[...] = w_out.T.astype(BF)
    if first:
        gather_next.start()

    to_mate, close, receive, finish_c = sum_to_owner(
        place, rows, mate_out, mate_in, sum_out, sum_in, own, send_cm, recv_cm, send_c, recv_c
    )

    def order(i):
        return lax.select(i == n - 1, d, place.other(i))

    def hidden_slot(i, unused):
        slot = order(i)
        lanes = pl.ds(pl.multiple_of(slot * length, length), length)
        for k in range(1, n):
            peer_b(k, slot).wait_recv()
            mate_b(k, slot).start()
        for k in range(n):
            mate_b(k, slot).wait_recv()
        pm[slot] = dot(w_mx_t[...], mx[:, lanes], 1, 0)

        v = pm[slot] + mix_bias_ref[...]
        pm[slot] = v
        product = gelu_only(v) * gelu_only(pre[slot, ch2:])
        prod_f[...] = product
        prod[:, lanes] = product.astype(BF)
        prod_t[...] = prod_f[...].T.astype(BF)
        for item in range(4, 7):
            saves(slot, item).start()
        theirs = pl.ds(pl.multiple_of((1 - c) * rows, rows), rows)
        ours = pl.ds(pl.multiple_of(c * rows, rows), rows)
        mate_out[slot] = dot(prod_t[theirs], w_out_t[...], 1, 1).astype(BF)
        to_mate(slot).start()

        @pl.when(i > 0)
        def _():
            close(order(i - 1), lax.rem(i - 1, 2))

        own[lax.rem(i, 2)] = dot(prod_t[ours], w_out_t[...], 1, 1)
        return unused

    lax.fori_loop(0, n, hidden_slot, 0)
    last = (n - 1) % 2
    close(d, last)
    receive()

    total = own[last]
    for k in range(1, n):
        total = total + sum_in[k].astype(F32)
    new_ref[...] = res_ref[...] + own_mask_ref[...] * (total + out_bias_ref[...])
    finish_a()
    finish_c()
    gather_mx.finish()
    gather_out.finish()
    if first:
        next_out[...] = gather_next.whole().astype(BF)
        gather_next.finish()
        gather_in.finish()
        for k in range(1, n):
            mask_peer(k).wait_send()

    def drain(slot, unused):
        for k in range(1, n):
            peer_b(k, slot).wait_send()
        for k in range(n):
            mate_b(k, slot).wait_send()
        for item in range(7):
            saves(slot, item).wait()
        return unused

    lax.fori_loop(0, n, drain, 0)


def bwd_kernel(
    n, m, later, grad_ref, res_ref, gain_ref, mask_ref, own_mask_ref, w_in_ref, w_mx_ref, w_out_ref, kre_ref,
    kim_ref, ft_ref, f_ref, g_in, mx_in, pre_in, u_in, y_in, pm_in, prod_in, *rest
):
    if later:
        late_part, *rest = rest
    (new_ref, gw_in_ref, red_mx_ref, red_out_ref, in_row_ref, mix_row_ref, norm_sum_ref, dk_ref, *rest) = rest
    if later:
        red_late_ref, *rest = rest
    (
        gb, g, mx, pre, u_sp, y, pm, prod, gpre, gpre_f, gpm, gact, spec, hat, turned,
        mix_sum, mix_mate, mix_own, mix_got, in_sum, mix_acc, part_mx, got_mx, part_out, got_out,
        own, mate_out, mate_in, sum_out, sum_in,
        send_a, recv_a, send_am, recv_am, send_b, recv_b, send_bm, recv_bm, send_c, recv_c, send_cm, recv_cm, load,
        send_rm, recv_rm, send_ro, recv_ro, *rest,
    ) = rest
    place = Place(n, m)
    d, c = place.d, place.c
    rows, width = res_ref.shape
    length = ft_ref.shape[0]
    hid = w_mx_ref.shape[1]
    ch2 = kre_ref.shape[0]
    ch = ch2 // 2
    half = n * ch

    def loads(slot, item):
        lanes = pl.ds(pl.multiple_of(slot * length, length), length)
        src, dst = (
            lambda: (pre_in.at[slot], pre.at[slot]),
            lambda: (pm_in.at[slot], pm.at[slot]),
            lambda: (y_in.at[slot], y.at[slot]),
            lambda: (u_in.at[slot], u_sp.at[slot]),
            lambda: (prod_in.at[:, lanes], prod.at[:, lanes]),
            lambda: (mx_in.at[:, lanes], mx.at[:, lanes]),
            lambda: (g_in.at[lanes], g.at[lanes]),
        )[item]()
        return pltpu.make_async_copy(src, dst, load.at[item, slot])

    for item in range(7):
        loads(d, item).start()

    def start_loads(i, unused):
        for item in range(7):
            loads(place.other(i), item).start()
        return unused

    lax.fori_loop(0, n - 1, start_loads, 0)

    place.greet()
    start_a, own_a, fetch_a, finish_a = gather_tokens(place, gb, rows, length, send_a, recv_a, send_am, recv_am)
    base = d * length + c * rows
    first = grad_ref[...] * own_mask_ref[...]
    gb[pl.ds(pl.multiple_of(base, rows), rows)] = first.astype(BF)
    start_a()
    sum_mx = RowSum(place, part_mx, got_mx, send_rm, recv_rm)
    sum_out_w = RowSum(place, part_out, got_out, send_ro, recv_ro)
    row_sums = [sum_mx, sum_out_w]
    if later:
        got_late, send_rl, recv_rl = rest
        sum_late = RowSum(place, late_part, got_late, send_rl, recv_rl)
        sum_late.start()
        row_sums.append(sum_late)
    norm_sum_ref[...] = jnp.zeros_like(norm_sum_ref)
    norm_sum_ref[2:3] = jnp.sum(first, axis=0, keepdims=True)
    in_sum[...] = jnp.zeros_like(in_sum)
    mix_acc[...] = jnp.zeros_like(mix_acc)
    dk_ref[...] = jnp.zeros_like(dk_ref)
    own_a()

    def mate_b(slot):
        return place.to_mate(mix_sum.at[slot], mix_mate.at[slot], send_bm.at[slot], recv_bm.at[slot])

    def peer_b(k, slot):
        q = place.ahead(k)
        part = mix_sum.at[slot, pl.ds(pl.multiple_of(q * ch, ch), ch)]
        return place.to_dp(part, mix_got.at[k, slot], send_b.at[slot, k], recv_b.at[slot, k], q)

    def hidden_slot(i, unused):
        slot = lax.select(i == 0, d, place.other(i - 1))

        @pl.when(i > 0)
        def _():
            fetch_a(lax.rem(d - slot + n, n))

        lanes = pl.ds(pl.multiple_of(slot * length, length), length)
        gact[...] = dot(w_out_ref[...], gb[lanes], 1, 1)
        for item in range(2):
            loads(slot, item).wait()
        gated, slope = gelu_parts(pm[slot])
        value, value_slope = gelu_parts(pre[slot, ch2:])
        now = gact[...]
        to_value = now * gated * value_slope
        to_mix = now * value * slope
        gpre[ch2:, lanes] = to_value.astype(BF)
        gpm[:, lanes] = to_mix.astype(BF)
        in_sum[ch2:] = in_sum[ch2:] + lane_sums(to_value)
        mix_acc[...] = mix_acc[...] + lane_sums(to_mix)
        theirs = pl.ds(pl.multiple_of((1 - c) * half, half), half)
        ours = pl.ds(pl.multiple_of(c * half, half), half)
        mix_sum[slot] = dot(w_mx_ref[theirs], gpm[:, lanes], 1, 0).astype(BF)
        mate_b(slot).start()
        mix_own[...] = dot(w_mx_ref[ours], gpm[:, lanes], 1, 0)
        mate_b(slot).wait()
        mix_sum[slot] = (mix_own[...] + mix_mate[slot].astype(F32)).astype(BF)
        for k in range(1, n):
            peer_b(k, slot).start()
        return unused

    lax.fori_loop(0, n, hidden_slot, 0)

    def wait_loads(slot, unused):
        for item in range(2, 7):
            loads(slot, item).wait()
        return unused

    lax.fori_loop(0, n, wait_loads, 0)
    share = mx.shape[0] // m

    def grad_mix(q, unused):
        part_mx[q] = dot(mx[pl.ds(pl.multiple_of(q * share, share), share)], gpm[...], 1, 1).astype(BF)
        return unused

    lax.fori_loop(0, m, grad_mix, 0)
    sum_mx.start()
    gw_out = dot(prod[...], gb[...], 1, 0).T
    part_out[...] = gw_out.reshape(m, width // m, hid).astype(BF)
    sum_out_w.start()

    to_mate, close, receive, finish_c = sum_to_owner(
        place, rows, mate_out, mate_in, sum_out, sum_in, own, send_cm, recv_cm, send_c, recv_c
    )

    def order(i):
        return lax.select(i == n - 1, d, place.other(i))

    def scan_slot(i, unused):
        slot = order(i)
        lanes = pl.ds(pl.multiple_of(slot * length, length), length)
        for k in range(1, n):
            peer_b(k, slot).wait_recv()
        total = mix_sum[slot, pl.ds(pl.multiple_of(d * ch, ch), ch)].astype(F32)
        for k in range(1, n):
            total = total + mix_got[k, slot].astype(F32)
        hat[:ch, :length] = (total * y[slot, ch:]).astype(BF)
        hat[ch:, :length] = (total * y[slot, :ch]).astype(BF)
        spec[...] = dot(hat[:, :length], ft_ref[...], 1, 0)
        g_re, g_im = spec[:, :length], spec[:, length:]
        k_re, k_im = kre_ref[...], kim_ref[...]
        hat[:, :length] = (k_re * g_re + k_im * g_im).astype(BF)
        hat[:, length:] = (k_re * g_im - k_im * g_re).astype(BF)
        u_re, u_im = u_sp[slot, :, :length].astype(F32), u_sp[slot, :, length:].astype(F32)
        dk_ref[:, :length] = dk_ref[:, :length] + (u_re * g_re + u_im * g_im)
        dk_ref[:, length:] = dk_ref[:, length:] + (u_re * g_im - u_im * g_re)
        spec[:, :length] = dot(hat[...], f_ref[...], 1, 0)
        live = mask_ref[slot, 0:1]
        _, slope = gelu_parts(pre[slot, :ch2])
        part = spec[:, :length] * slope * live
        gpre_f[...] = part
        gpre[:ch2, lanes] = part.astype(BF)
        in_sum[:ch2] = in_sum[:ch2] + lane_sums(part)
        turned[:, :ch2] = gpre_f[...].T.astype(BF)
        gpre_f[...] = gpre[ch2:, lanes].astype(F32)
        turned[:, ch2:] = gpre_f[...].T.astype(BF)
        theirs = pl.ds(pl.multiple_of((1 - c) * rows, rows), rows)
        ours = pl.ds(pl.multiple_of(c * rows, rows), rows)
        mate_out[slot] = dot(turned[theirs], w_in_ref[...], 1, 1).astype(BF)
        to_mate(slot).start()

        @pl.when(i > 0)
        def _():
            close(order(i - 1), lax.rem(i - 1, 2))

        own[lax.rem(i, 2)] = dot(turned[ours], w_in_ref[...], 1, 1)
        return unused

    lax.fori_loop(0, n, scan_slot, 0)
    last = (n - 1) % 2
    close(d, last)

    def grad_in(r):
        part = dot(gpre[r], g[...], 1, 0).T
        gw_in_ref[:, :, r] = part.reshape(m, width // m, part.shape[1]).astype(BF)

    over_rows(gpre.shape[0], 128, grad_in)
    in_row_ref[...] = as_row(in_sum[...])
    mix_row_ref[...] = as_row(mix_acc[...])
    if later:
        red_late_ref[...] = sum_late.total().astype(BF)
    receive()
    total = own[last]
    for k in range(1, n):
        total = total + sum_in[k].astype(F32)
    xhat, inv = norm_stats(res_ref[...])
    h = total * gain_ref[...]
    middle = jnp.mean(h, axis=1, keepdims=True)
    along = jnp.mean(h * xhat, axis=1, keepdims=True)
    new_ref[...] = grad_ref[...] + inv * (h - middle - xhat * along)
    norm_sum_ref[0:1] = jnp.sum(total * xhat, axis=0, keepdims=True)
    norm_sum_ref[1:2] = jnp.sum(total, axis=0, keepdims=True)
    red_mx_ref[...] = sum_mx.total().astype(BF)
    red_out_ref[...] = sum_out_w.total().astype(BF)
    finish_a()
    finish_c()
    for row_sum in row_sums:
        row_sum.finish()

    def drain(slot, unused):
        for k in range(1, n):
            peer_b(k, slot).wait_send()
        return unused

    lax.fori_loop(0, n, drain, 0)


def state_grads(dk_re, dk_im, sign, ft_ref, decay, step, b_in, c_out, lag_sums):
    length = ft_ref.shape[0]
    re = dk_re.astype(BF)
    im = (dk_im * sign).astype(BF)
    lag_sums[...] = (dot(ft_ref[:, :length], re, 1, 1) + dot(ft_ref[:, length:], im, 1, 1)) * (1.0 / length)
    rate = jnp.exp(step) * jnp.exp(decay)
    a = jnp.exp(-rate)

    def lag(i, carry):
        total, slope = carry
        row = lag_sums[pl.ds(length - 1 - i, 1)]
        return total * a + row, slope * a + total

    zero = jnp.zeros_like(a)
    total, slope = lax.fori_loop(0, length, lag, (zero, zero), unroll=4)
    inv_decay = jnp.exp(-decay)
    gain = (1.0 - a) * inv_decay
    b_disc = gain * b_in
    to_b = c_out * total
    to_rate = a * (to_b * inv_decay * b_in - (c_out * b_disc) * slope)
    through = to_rate * rate
    return (
        through - to_b * b_disc, to_b * gain, b_disc * total,
        jnp.sum(through, axis=0, keepdims=True), lag_sums[0:1],
    )


def finish_kernel(
    n, m, part_in, late_in, red_mx0, red_out0, red_mx1, red_out1, dk0, dk1, in0, in1, mix0, mix1, norm0, norm1,
    decay_ref, step_ref, b_ref, c_ref, sign_ref, ft_ref,
    all_in, all_mx, all_out, all_states, all_small, norm_ref,
    got_in, red_in0, states, part_s, got_s, red_s, full_s, lag_sums, small, row_small, dp_small, norm_own, norm_got,
    send_w, recv_w, keep_w, send_ri, recv_ri, send_rs, recv_rs, send_gs, recv_gs, send_sm, recv_sm,
    send_ds, recv_ds, keep_s, send_n, recv_n, send_st, recv_st, keep_st,
):
    place = Place(n, m)
    d, r = place.d, place.r
    ch2 = decay_ref.shape[2]
    states_n = decay_ref.shape[1]
    place.greet()
    sum_in = RowSum(place, part_in, got_in, send_ri, recv_ri)
    sum_in.start()

    def spread(item, src, out, layer):
        def remote(k):
            return place.to_dp(
                src, out.at[layer, d], send_w.at[item, k], recv_w.at[item, k], place.ahead(k)
            )

        def local():
            return pltpu.make_async_copy(src, out.at[layer, d], keep_w.at[item])

        def start():
            for k in range(1, n):
                remote(k).start()
            local().start()

        def wait():
            for k in range(1, n):
                remote(k).wait_recv()
                remote(k).wait_send()
            local().wait()

        return start, wait

    spreads = [
        spread(0, red_mx1, all_mx, 1), spread(1, red_out1, all_out, 1), spread(2, late_in, all_in, 1),
        spread(3, red_mx0, all_mx, 0), spread(4, red_out0, all_out, 0), spread(5, red_in0, all_in, 0),
    ]
    for start, _ in spreads[:5]:
        start()

    small[...] = jnp.zeros_like(small)
    for l, (dk, in_row, mix_row, norm) in enumerate(((dk0, in0, mix0, norm0), (dk1, in1, mix1, norm1))):
        small[l, 0:1] = in_row[0:1]
        small[l, 1:2, :ch2] = mix_row[0:1]
        small[l, 3:6] = norm[0:3]
        length = ft_ref.shape[0]
        g_decay, g_b, g_c, g_step, g_skip = state_grads(
            dk[:, :length], dk[:, length:], sign_ref[...], ft_ref, decay_ref[l], step_ref[l], b_ref[l], c_ref[l],
            lag_sums,
        )
        small[l, 1:2, ch2:] = g_step
        small[l, 2:3, :ch2] = g_skip
        for i, part in enumerate((g_decay, g_b, g_c)):
            states[pl.ds((3 * l + i) * states_n, states_n)] = part
    share = states.shape[0] // m
    for q in range(m):
        part_s[q] = states[q * share : (q + 1) * share].astype(BF)
    sum_s = RowSum(place, part_s, got_s, send_rs, recv_rs)
    sum_s.start()
    row_small[r] = small[...]

    def small_row(j):
        return place.to_row(row_small.at[r], row_small.at[r], send_sm.at[j], recv_sm.at[j], place.up(j))

    def each(work, count):
        def one(j, unused):
            work(j)
            return unused

        lax.fori_loop(1, count, one, 0)

    each(lambda j: small_row(j).start(), m)

    red_s[...] = sum_s.total().astype(BF)
    full_s[r] = red_s[...]

    def state_row(j):
        return place.to_row(full_s.at[r], full_s.at[r], send_gs.at[j], recv_gs.at[j], place.up(j))

    each(lambda j: state_row(j).start(), m)
    each(lambda j: small_row(j).wait_recv(), m)
    total = row_small[0]
    for q in range(1, m):
        total = total + row_small[q]
    dp_small[d] = total

    def small_dp(k):
        return place.to_dp(dp_small.at[d], dp_small.at[d], send_ds.at[k], recv_ds.at[k], place.ahead(k))

    for k in range(1, n):
        small_dp(k).start()
    red_in0[...] = sum_in.total().astype(BF)
    spreads[5][0]()
    each(lambda j: state_row(j).wait_recv(), m)

    def states_dp(k):
        return place.to_dp(full_s, all_states.at[d], send_st.at[k], recv_st.at[k], place.ahead(k))

    keep_states = pltpu.make_async_copy(full_s, all_states.at[d], keep_st)
    keep_states.start()
    for k in range(1, n):
        states_dp(k).start()
    for k in range(1, n):
        small_dp(k).wait_recv()
    total = dp_small[0]
    for q in range(1, n):
        total = total + dp_small[q]
    norm_own[...] = total
    swap = place.to_mate(norm_own, norm_got, send_n, recv_n)
    swap.start()
    all_small[...] = dp_small[...]
    swap.wait_recv()
    norm_ref[...] = norm_own[...] + norm_got[...]
    swap.wait_send()
    for _, wait in spreads:
        wait()
    for k in range(1, n):
        states_dp(k).wait_recv()
        states_dp(k).wait_send()
        small_dp(k).wait_send()
    keep_states.wait()
    each(lambda j: small_row(j).wait_send(), m)
    each(lambda j: state_row(j).wait_send(), m)
    sum_in.finish()
    sum_s.finish()


VM = pl.BlockSpec(memory_space=pltpu.VMEM)
ANY = pl.BlockSpec(memory_space=pl.ANY)


def shape(dims, dtype):
    return jax.ShapeDtypeStruct(tuple(dims), dtype)


def sem(*dims):
    return pltpu.SemaphoreType.DMA(dims)


def body(
    tokens_in, lengths, cotangent, norm_gain, norm_shift, w_fwd, w_bwd, w_value, bias_fwd, bias_bwd,
    bias_value, decay_log, step_log, b_input, c_output, skip_gain, w_mix, bias_mix, w_output, bias_output,
):
    n = lax.axis_size("dp")
    m = lax.axis_size("row")
    cols = lax.axis_size("col")
    d = lax.axis_index("dp")
    rows, width = tokens_in.shape
    length = rows * cols
    ch = w_fwd.shape[2] // n
    ch2 = 2 * ch
    hid = w_mix.shape[2] // n
    wide = ch2 + hid
    chans = n * cols * ch
    tokens = n * length
    matrix = transform_matrix(length)
    f_mat = jnp.asarray(matrix, BF)
    ft_mat = jnp.asarray(np.ascontiguousarray(matrix.T), BF)

    def mine(x, size, axis):
        return lax.dynamic_slice_in_dim(x, d * size, size, axis)

    shards, biases = [], []
    for l in range(LAYERS):
        shards.append((
            jnp.concatenate(
                (mine(w_fwd[l], ch, 1), mine(w_bwd[l], ch, 1), mine(w_value[l], hid, 1)), axis=1
            ).astype(BF),
            mine(w_mix[l], hid, 1).astype(BF),
            mine(w_output[l], hid, 0).astype(BF).T,
        ))
        in_bias = jnp.concatenate(
            (mine(bias_fwd[l], ch, 0), mine(bias_bwd[l], ch, 0), mine(bias_value[l], hid, 0))
        )[:, None]
        biases.append((in_bias, mine(bias_mix[l], hid, 0)[:, None], bias_output[l][None]))

    positions = jnp.arange(length, dtype=jnp.int32)
    live = (positions < lengths[0]).astype(F32)
    own_live = jnp.broadcast_to(live[None], (8, length))
    own_mask = lax.dynamic_slice_in_dim(live, lax.axis_index("col") * rows, rows, 0)[:, None]

    def states_first(x):
        part = mine(x, ch, 2)
        return part.transpose(0, 3, 1, 2).reshape(LAYERS, x.shape[3], ch2)

    def one_row(x):
        return mine(x, ch, 2).reshape(LAYERS, 1, ch2)

    decay_t, b_t, c_t = states_first(decay_log), states_first(b_input), states_first(c_output)
    step_t, skip_t = one_row(step_log), one_row(skip_gain)
    states = decay_t.shape[1]
    sign = jnp.where(jnp.arange(ch2) < ch, 1.0, -1.0).astype(F32)[:, None]
    comm = [
        sem(n), sem(n), sem(n), sem(n), sem(n, n), sem(n, n),
    ]
    sums = [
        pltpu.VMEM((2, rows, width), F32), pltpu.VMEM((n, rows, width), BF), pltpu.VMEM((n, rows, width), BF),
        pltpu.VMEM((n, rows, width), BF), pltpu.VMEM((n, rows, width), BF),
    ]
    saved_shapes = (
        shape((tokens, width), BF), shape((chans, tokens), BF), shape((n, wide, length), F32),
        shape((n, ch2, 2 * length), BF), shape((n, ch2, length), F32), shape((n, hid, length), F32),
        shape((hid, tokens), BF),
    )
    def fwd(first):
        table = shape((ch2, length), F32)
        ahead = shape((width, wide), BF)
        extra = (ahead, ahead, shape((n, 8, length), F32)) if first else ()
        lands = [(m, chans // m, hid), (m, width // m, hid)]
        return pl.pallas_call(
            functools.partial(fwd_kernel, n, m, first),
            out_shape=(
                shape((rows, width), F32), *saved_shapes, table, table, shape((chans, hid), BF),
                shape((hid, width), BF), *extra,
            ),
            in_specs=[VM] * (18 + 1 + first),
            out_specs=(VM, *([ANY] * 7), *([VM] * (4 + len(extra)))),
            scratch_shapes=[
                pltpu.VMEM((wide, width), BF), pltpu.VMEM((hid, chans), BF),
                *(pltpu.VMEM(s.shape, s.dtype) for s in saved_shapes),
                pltpu.VMEM((ch2, length), BF), pltpu.VMEM((ch2, 2 * length), F32),
                pltpu.VMEM((ch2, 2 * length), BF), pltpu.VMEM((hid, length), F32), pltpu.VMEM((length, hid), BF),
                pltpu.VMEM((ch2, length), F32), pltpu.VMEM((ch2, length), F32),
                pltpu.VMEM((states, 128), F32), pltpu.VMEM((length // LAG, states, 128), F32),
                *(pltpu.VMEM(s, BF) for s in lands), pltpu.VMEM((width, hid), BF),
                *sums, *comm, sem(n, n), sem(n, n), sem(n), sem(n), sem(n), sem(n), sem(7, n),
                sem(m), sem(m), sem(m), sem(m),
                *([pltpu.VMEM((m, width // m, wide), BF)] * 2 + [sem(m)] * 4 + [sem(n)] * 2 if first else []),
            ],
            compiler_params=pltpu.CompilerParams(
                collective_id=4 if first else 0, has_side_effects=True, vmem_limit_bytes=VMEM_LIMIT
            ),
            name="forward_block",
        )

    def bwd(later):
        late = (m, width // m, wide)
        out_shape = [
            shape((rows, width), F32), shape(late, BF), shape((chans // m, hid), BF), shape((width // m, hid), BF),
            shape((8, wide), F32), shape((8, hid), F32), shape((8, width), F32), shape((ch2, 2 * length), F32),
        ]
        if later:
            out_shape.append(shape(late[1:], BF))
        return pl.pallas_call(
            functools.partial(bwd_kernel, n, m, later),
            out_shape=tuple(out_shape),
            in_specs=[VM] * 12 + [ANY] * 7 + [VM] * later,
            out_specs=(VM,) * len(out_shape),
            scratch_shapes=[
                pltpu.VMEM((tokens, width), BF),
                *(pltpu.VMEM(s.shape, s.dtype) for s in saved_shapes),
                pltpu.VMEM((wide, tokens), BF), pltpu.VMEM((ch2, length), F32), pltpu.VMEM((hid, tokens), BF),
                pltpu.VMEM((hid, length), F32), pltpu.VMEM((ch2, 2 * length), F32),
                pltpu.VMEM((ch2, 2 * length), BF), pltpu.VMEM((length, wide), BF),
                pltpu.VMEM((n, n * ch, length), BF), pltpu.VMEM((n, n * ch, length), BF),
                pltpu.VMEM((n * ch, length), F32),
                pltpu.VMEM((n, n, ch, length), BF), pltpu.VMEM((wide, 128), F32), pltpu.VMEM((hid, 128), F32),
                *(pltpu.VMEM((m, chans // m, hid), BF),) * 2, *(pltpu.VMEM((m, width // m, hid), BF),) * 2,
                *sums, *comm, sem(n), sem(n), sem(n), sem(n), sem(n), sem(n), sem(7, n),
                sem(m), sem(m), sem(m), sem(m),
                *([pltpu.VMEM(late, BF), sem(m), sem(m)] if later else []),
            ],
            compiler_params=pltpu.CompilerParams(
                collective_id=1 + later, has_side_effects=True, vmem_limit_bytes=VMEM_LIMIT
            ),
            name="backward_block",
        )

    residual = tokens_in.astype(F32)
    stored = []
    for l in range(LAYERS):
        sh_in, sh_mx, sh_out = shards[l]
        first = l == 0
        given = (sh_in, shards[1][0]) if first else (w_next,)
        new, *made = fwd(first)(
            residual, norm_gain[l][None], norm_shift[l][None], own_live if first else mask, own_mask, sh_mx, sh_out,
            *biases[l], ft_mat, f_mat, decay_t[l], step_t[l], b_t[l], c_t[l], skip_t[l], sign, *given,
        )
        saved, (kre, kim, w_mx, w_out) = made[:7], made[7:11]
        if first:
            w_in, w_next, mask = made[11:]
        else:
            w_in = w_next
        stored.append((residual, saved, kre, kim, w_in, w_mx, w_out))
        residual = new
    tokens_out = residual.astype(BF)

    grad = cotangent.astype(F32)
    parts = [None] * LAYERS
    extra = ()
    for l in reversed(range(LAYERS)):
        resid_in, saved, kre, kim, w_in, w_mx, w_out = stored[l]
        grad, *parts[l] = bwd(l < LAYERS - 1)(
            grad, resid_in, norm_gain[l][None], mask, own_mask, w_in, w_mx, w_out, kre, kim, ft_mat,
            f_mat, *saved, *extra,
        )
        extra = (parts[l][0],)
    part_in, red_mx0, red_out0, in0, mix0, norm0, dk0, late_in = parts[0]
    _, red_mx1, red_out1, in1, mix1, norm1, dk1 = parts[1]
    lots = LAYERS * 3 * states
    all_in, all_mx, all_out, all_states, all_small, norms = pl.pallas_call(
        functools.partial(finish_kernel, n, m),
        out_shape=(
            shape((LAYERS, n, width // m, wide), BF), shape((LAYERS, n, chans // m, hid), BF),
            shape((LAYERS, n, width // m, hid), BF), shape((n, m, lots // m, ch2), BF),
            shape((n, LAYERS, 8, wide), F32), shape((LAYERS, 8, wide), F32),
        ),
        in_specs=[VM] * 20,
        out_specs=(ANY, ANY, ANY, ANY, VM, VM),
        scratch_shapes=[
            pltpu.VMEM((m, width // m, wide), BF), pltpu.VMEM((width // m, wide), BF), pltpu.VMEM((lots, ch2), F32),
            pltpu.VMEM((m, lots // m, ch2), BF), pltpu.VMEM((m, lots // m, ch2), BF),
            pltpu.VMEM((lots // m, ch2), BF), pltpu.VMEM((m, lots // m, ch2), BF), pltpu.VMEM((length, ch2), F32),
            pltpu.VMEM((LAYERS, 8, wide), F32), pltpu.VMEM((m, LAYERS, 8, wide), F32),
            pltpu.VMEM((n, LAYERS, 8, wide), F32), pltpu.VMEM((LAYERS, 8, wide), F32),
            pltpu.VMEM((LAYERS, 8, wide), F32),
            sem(6, n), sem(6, n), sem(6), sem(m), sem(m), sem(m), sem(m), sem(m), sem(m), sem(m), sem(m),
            sem(n), sem(n), sem(1), pltpu.SemaphoreType.DMA, pltpu.SemaphoreType.DMA, sem(n), sem(n),
            pltpu.SemaphoreType.DMA,
        ],
        compiler_params=pltpu.CompilerParams(
            collective_id=3, has_side_effects=True, vmem_limit_bytes=VMEM_LIMIT
        ),
        name="finish",
    )(
        part_in, late_in, red_mx0, red_out0, red_mx1, red_out1, dk0, dk1, in0, in1, mix0, mix1, norm0, norm1,
        decay_t, step_t, b_t, c_t, sign, ft_mat,
    )

    def columns(x):
        x = x.transpose(0, 2, 1, 3)
        return x.reshape(x.shape[0], x.shape[1], -1).astype(F32)

    def along(x):
        return x.transpose(1, 0, 2).reshape(LAYERS, -1)

    by_state = all_states.reshape(n, LAYERS, 3, states, 2, ch)
    by_state = by_state.transpose(2, 1, 4, 0, 5, 3).reshape(3, LAYERS, 2, n * ch, states).astype(F32)

    def per_direction(x):
        return x.reshape(n, LAYERS, 2, ch).transpose(1, 2, 0, 3).reshape(LAYERS, 2, n * ch)

    return (
        tokens_out, grad, norms[:, 3], norms[:, 4],
        columns(all_in[..., :ch]), columns(all_in[..., ch:ch2]), columns(all_in[..., ch2:]),
        along(all_small[:, :, 0, :ch]), along(all_small[:, :, 0, ch:ch2]), along(all_small[:, :, 0, ch2:]),
        by_state[0], per_direction(all_small[:, :, 1, ch2:]), by_state[1], by_state[2],
        per_direction(all_small[:, :, 2, :ch2]), columns(all_mx), along(all_small[:, :, 1, :hid]),
        all_out.transpose(0, 1, 3, 2).reshape(LAYERS, n * hid, width // m).astype(F32), norms[:, 5],
    )


def solution(mesh):
    tokens = P(("dp", "row", "col"), None)
    weight = P(None, "row", "col")
    bias = P(None, "col")
    state = P(None, None, "col", None)
    chan = P(None, None, "col")
    in_specs = (
        tokens, P(("dp", "row")), tokens, P(), P(), weight, weight, weight, bias, bias, bias,
        state, chan, state, state, chan, weight, bias, P(None, "col", "row"), P(),
    )
    out_specs = (
        tokens, tokens, P(), P(), weight, weight, weight, bias, bias, bias,
        state, chan, state, state, chan, weight, bias, P(None, "col", "row"), P(),
    )
    return jax.shard_map(body, mesh=mesh, in_specs=in_specs, out_specs=out_specs, check_vma=False)
```

```python
import functools

import jax
import jax.numpy as jnp
import numpy as np
from jax import lax
from jax.experimental import pallas as pl
from jax.experimental.pallas import tpu as pltpu
from jax.sharding import PartitionSpec as P

LAYERS = 2
EPS = 1e-05
LAG = 64
BF = jnp.bfloat16
F32 = jnp.float32
MESH = pl.DeviceIdType.MESH
VMEM_LIMIT = 60 * 1024 * 1024


def transform_matrix(length):
    k = np.arange(length)[:, None]
    t = np.arange(length)[None, :]
    angle = np.pi * (((2 * k + 1) * t) % (4 * length)) / (2 * length)
    return np.concatenate((np.cos(angle), -np.sin(angle)), axis=0)


def gelu_only(v):
    t = jnp.tanh(v * (0.7978845608 + 0.035677408 * v * v))
    return (0.5 * v) * (1.0 + t)


def gelu_parts(v):
    sq = v * v
    t = jnp.tanh(v * (0.7978845608 + 0.035677408 * sq))
    half = 0.5 + 0.5 * t
    slope = half + (v * half) * (1.0 - t) * (0.7978845608 + 0.107032225 * sq)
    return v * half, slope


def dot(a, b, ca, cb):
    return lax.dot_general(a, b, (((ca,), (cb,)), ((), ())), preferred_element_type=F32)


def over_rows(rows, step, work):
    def one(i, unused):
        work(pl.ds(pl.multiple_of(i * step, step), step))
        return unused

    lax.fori_loop(0, rows // step, one, 0)


def lane_sums(x):
    total = x[:, :128]
    for i in range(1, x.shape[1] // 128):
        total = total + x[:, 128 * i : 128 * (i + 1)]
    return total


def as_row(partial):
    return lax.dot_general(
        jnp.ones((8, 128), F32), partial, (((1,), (1,)), ((), ())), precision=lax.Precision.HIGHEST,
        preferred_element_type=F32,
    )


class Place:
    def __init__(self, n, m):
        self.n = n
        self.m = m
        self.d = lax.axis_index("dp")
        self.c = lax.axis_index("col")
        self.r = lax.axis_index("row")

    def greet(self):
        barrier = pltpu.get_barrier_semaphore()

        def hail(device):
            pl.semaphore_signal(barrier, inc=1, device_id=device, device_id_type=MESH)

        for k in range(1, self.n):
            hail({"dp": self.ahead(k)})
        hail({"col": 1 - self.c})

        def one(j, unused):
            hail({"row": self.up(j)})
            return unused

        lax.fori_loop(1, self.m, one, 0)
        pl.semaphore_wait(barrier, self.n + self.m - 1)

    def ahead(self, k):
        return lax.rem(self.d + k, self.n)

    def behind(self, k):
        return lax.rem(self.d - k + self.n, self.n)

    def near(self, k):
        return lax.rem(self.d + k, 2) + 2 * lax.rem(self.d // 2 + k // 2, 2)

    def apart(self, e):
        return lax.rem(self.d + e, 2) + 2 * lax.rem(self.d // 2 + e // 2, 2)

    def up(self, j):
        return lax.rem(self.r + j, self.m)

    def down(self, j):
        return lax.rem(self.r - j + self.m, self.m)

    def other(self, i):
        return i + (i + self.n - self.d) // self.n

    def to_dp(self, src, dst, send, recv, q):
        return pltpu.make_async_remote_copy(
            src, dst, send, recv, device_id={"dp": q}, device_id_type=MESH
        )

    def to_mate(self, src, dst, send, recv):
        return pltpu.make_async_remote_copy(
            src, dst, send, recv, device_id={"col": 1 - self.c}, device_id_type=MESH
        )

    def to_row(self, src, dst, send, recv, q):
        return pltpu.make_async_remote_copy(
            src, dst, send, recv, device_id={"row": q}, device_id_type=MESH
        )


class RowSum:
    def __init__(self, place, part, got, send, recv):
        self.place, self.part, self.got, self.send, self.recv = place, part, got, send, recv

    def copy(self, j):
        q = self.place.up(j)
        return self.place.to_row(self.part.at[q], self.got.at[j - 1], self.send.at[j], self.recv.at[j], q)

    def each(self, act):
        def one(j, unused):
            act(self.copy(j))
            return unused

        lax.fori_loop(1, self.place.m, one, 0)

    def start(self):
        self.each(lambda copy: copy.start())

    def total(self):
        self.each(lambda copy: copy.wait_recv())
        total = self.part[self.place.r].astype(F32)
        if self.place.m <= 4:
            for j in range(1, self.place.m):
                total = total + self.got[j - 1].astype(F32)
            return total
        return lax.fori_loop(1, self.place.m, lambda j, t: t + self.got[j - 1].astype(F32), total)

    def finish(self):
        self.each(lambda copy: copy.wait_send())


class Tokens:
    def __init__(self, place, buf, rows, length, sems):
        self.place, self.buf, self.rows, self.length = place, buf, rows, length
        self.send_p, self.recv_p, self.send_h, self.recv_h, self.send_m, self.recv_m = sems

    def region(self, slot, half=None):
        rows = self.rows // 2 if half is not None else self.rows
        start = slot * self.length + self.place.c * self.rows + (half or 0) * rows
        return self.buf.at[pl.ds(pl.multiple_of(start, rows), rows)]

    def peer(self, i):
        own = self.region(self.place.d)
        return self.place.to_dp(own, own, self.send_p.at[i], self.recv_p.at[i], self.place.near(i))

    def hop(self, i):
        part = self.region(self.place.near(3 - i), i - 1)
        return self.place.to_dp(part, part, self.send_h.at[i], self.recv_h.at[i], self.place.near(i))

    def mate(self, k):
        part = self.region(self.place.near(k))
        return self.place.to_mate(part, part, self.send_m.at[k], self.recv_m.at[k])

    def start(self):
        self.peer(1).start()
        self.peer(2).start()
        self.mate(0).start()

    def own(self):
        self.mate(0).wait_recv()

    def pass_on(self):
        for i in (1, 2):
            self.peer(i).wait_recv()
            self.hop(3 - i).start()
            self.mate(i).start()

    def fetch(self, k):
        @pl.when(k == 3)
        def _():
            self.hop(1).wait_recv()
            self.hop(2).wait_recv()
            self.mate(3).start()

        self.mate(k).wait_recv()

    def finish(self):
        for i in (1, 2):
            self.peer(i).wait_send()
            self.hop(i).wait_send()
        for k in range(4):
            self.mate(k).wait_send()


def norm_stats(residual):
    mean = jnp.mean(residual, axis=1, keepdims=True)
    centered = residual - mean
    variance = jnp.mean(centered * centered, axis=1, keepdims=True)
    inv = lax.rsqrt(variance + EPS)
    return centered * inv, inv


def sum_to_owner(place, rows, mate_out, mate_in, sum_out, sum_in, own, send_m, recv_m, send_p, recv_p):
    def to_mate(slot):
        return place.to_mate(mate_out.at[slot], mate_in.at[slot], send_m.at[slot], recv_m.at[slot])

    def to_owner(slot):
        k = lax.rem(slot - place.d + place.n, place.n)
        return place.to_dp(sum_out.at[slot], sum_in.at[k - 1], send_p.at[k], recv_p.at[k], slot)

    def close(slot, mine):
        to_mate(slot).wait_recv()

        own[mine] = own[mine] + mate_in[slot].astype(F32)

        @pl.when(slot != place.d)
        def _():
            sum_out[slot] = own[mine].astype(BF)
            to_owner(slot).start()

    def receive():
        def one(k, unused):
            to_owner(place.ahead(k)).wait_recv()
            return unused

        lax.fori_loop(1, place.n, one, 0)

    def finish():
        def one(k, unused):
            to_owner(place.ahead(k)).wait_send()
            return unused

        lax.fori_loop(1, place.n, one, 0)

        def two(s, unused):
            to_mate(s).wait_send()
            return unused

        lax.fori_loop(0, place.n, two, 0)

    return to_mate, close, receive, finish


class RowGather:
    def __init__(self, place, shard, land, send, recv):
        self.place, self.shard, self.land, self.send, self.recv = place, shard, land, send, recv

    def copy(self, j):
        place = self.place
        return place.to_row(self.shard, self.land.at[place.r], self.send.at[j], self.recv.at[j], place.up(j))

    def each(self, act):
        def one(j, unused):
            act(self.copy(j))
            return unused

        lax.fori_loop(1, self.place.m, one, 0)

    def start(self):
        self.each(lambda copy: copy.start())
        self.land[self.place.r] = self.shard[...]

    def whole(self):
        self.each(lambda copy: copy.wait_recv())
        m, rows, lanes = self.land.shape
        return self.land[...].astype(F32).reshape(m * rows, lanes)

    def finish(self):
        self.each(lambda copy: copy.wait_send())


def kernel_spectrum(decay, step, b_in, c_out, skip, sign, ft_ref, rate, lead):
    length = ft_ref.shape[0]
    blocks = length // LAG
    rate[...] = jnp.exp(step) * jnp.exp(decay)
    weight = (1.0 - jnp.exp(-rate[...])) * jnp.exp(-decay) * b_in * c_out
    for b in range(blocks):
        lead[b] = weight * jnp.exp(-(LAG * b) * rate[...])
    lanes = rate.shape[1]
    offs = lax.broadcasted_iota(jnp.int32, (LAG, lanes), 0).astype(F32)

    def state(i, totals):
        powers = jnp.exp(-offs * rate[pl.ds(i, 1)])
        return tuple(totals[b] + powers * lead[b, pl.ds(i, 1)] for b in range(blocks))

    zero = jnp.zeros((LAG, lanes), F32)
    totals = list(lax.fori_loop(0, rate.shape[0], state, (zero,) * blocks, unroll=2))
    at_zero = lax.broadcasted_iota(jnp.int32, (LAG, lanes), 0) == 0
    totals[0] = totals[0] + jnp.where(at_zero, skip, 0.0)
    kernel = jnp.concatenate(totals, axis=0)
    k_hat = dot(kernel.T.astype(BF), ft_ref[...], 1, 0) * (1.0 / length)
    return k_hat[:, :length], k_hat[:, length:] * sign


def direction_sign(ch, rows, lanes, start=0):
    at = lax.broadcasted_iota(jnp.int32, (rows, lanes), 0) + start
    return jnp.where(at < ch, 1.0, -1.0)


def fwd_kernel(
    n, m, layer, res_ref, gain_ref, shift_ref, own_live_ref, own_mask_ref, sh_v, sh_mx, sh_out, in_bias_ref,
    mix_bias_ref, out_bias_ref, ft_ref, f_ref, *rest
):
    first = layer == 0
    if first:
        sh_fb, sh_next, *rest = rest
        tables, next_tables, rest = rest[:4], rest[4:8], rest[8:]
    else:
        w_fb_ref, kre_ref, kim_ref, *rest = rest
    new_ref, g_out, mx_out, pre_out, u_out, y_out, pm_out, prod_out, w_in_out, w_mx_out, w_out_out, *rest = rest
    if first:
        next_out, mask_ref, kre_ref, kim_ref, kre_next, kim_next, *rest = rest
    else:
        mask_ref = own_live_ref
    (
        w_in_t, w_mx_t, g, mx, pre, u_sp, y, pm, prod, act, spec, y_hat, prod_f, prod_t,
        rate, lead, land_v, land_mx, land_out, w_out_t,
        own, mate_out, mate_in, sum_out, sum_in,
        send_a, recv_a, send_ah, recv_ah, send_am, recv_am, send_b, recv_b, send_bh, recv_bh, send_bm, recv_bm,
        send_c, recv_c, send_cm, recv_cm, save,
        send_gv, recv_gv, send_gm, recv_gm, send_go, recv_go, *rest,
    ) = rest
    place = Place(n, m)
    d, c = place.d, place.c
    rows, width = res_ref.shape
    length = ft_ref.shape[0]
    hid = sh_mx.shape[1]
    ch2 = kre_ref.shape[0]
    ch = ch2 // 2
    gain, shift, out_bias = (ref[layer : layer + 1] for ref in (gain_ref, shift_ref, out_bias_ref))

    place.greet()
    gather_v = RowGather(place, sh_v, land_v, send_gv, recv_gv)
    gather_mx = RowGather(place, sh_mx, land_mx, send_gm, recv_gm)
    gather_out = RowGather(place, sh_out, land_out, send_go, recv_go)
    later_weights = (gather_mx, gather_v, gather_out)
    gather_a = Tokens(place, g, rows, length, (send_a, recv_a, send_ah, recv_ah, send_am, recv_am))
    if first:
        land_fb, land_next, send_gi, recv_gi, send_gn, recv_gn, send_mk, recv_mk = rest
        gather_fb = RowGather(place, sh_fb, land_fb, send_gi, recv_gi)
        gather_next = RowGather(place, sh_next, land_next, send_gn, recv_gn)
        gather_fb.start()

        def mask_peer(k):
            return place.to_dp(
                own_live_ref, mask_ref.at[d], send_mk.at[k], recv_mk.at[k], place.ahead(k)
            )

        for k in range(1, n):
            mask_peer(k).start()
        mask_ref[d] = own_live_ref[...]
    else:
        for gather in later_weights:
            gather.start()
    base = d * length + c * rows
    xhat, _ = norm_stats(res_ref[...].astype(F32))
    g[pl.ds(pl.multiple_of(base, rows), rows)] = (xhat * gain + shift).astype(BF)
    gather_a.start()

    def spectra(given, re_ref, im_ref):
        decay_ref, b_ref, c_ref, row_ref = given
        for j in range(ch2 // 128):
            at = slice(128 * j, 128 * (j + 1))
            re_ref[at], im_ref[at] = kernel_spectrum(
                decay_ref[:, at], row_ref[0:1, at], b_ref[:, at], c_ref[:, at], row_ref[1:2, at],
                direction_sign(ch, 128, length, 128 * j), ft_ref, rate, lead,
            )

    if first:
        spectra(tables, kre_ref, kim_ref)
    if first:
        w_fb = gather_fb.whole()
        for gather in later_weights:
            gather.start()
        for k in range(1, n):
            mask_peer(k).wait_recv()
    else:
        w_fb = w_fb_ref[...].astype(F32)
    w_in_out[:, :ch2] = w_fb.astype(BF)
    w_in_t[:ch2] = w_fb.T.astype(BF)
    gather_a.own()

    def chunk(owner, slot):
        at = pl.ds(pl.multiple_of((c * n + owner) * ch, ch), ch)
        return mx.at[at, pl.ds(pl.multiple_of(slot * length, length), length)]

    def turn(k, j):
        return place.near(k ^ j)

    def half_chunk(owner, slot, half):
        at = pl.ds(pl.multiple_of((c * n + owner) * ch + half * (ch // 2), ch // 2), ch // 2)
        return mx.at[at, pl.ds(pl.multiple_of(slot * length, length), length)]

    def peer_b(i, j):
        part = chunk(d, turn(0, j))
        return place.to_dp(part, part, send_b.at[j, i], recv_b.at[j, i], place.near(i))

    def hop_b(i, j):
        part = half_chunk(place.near(3 - i), turn(3 - i, j), i - 1)
        return place.to_dp(part, part, send_bh.at[j, i], recv_bh.at[j, i], place.near(i))

    def mate_b(k, j):
        part = chunk(place.near(k), turn(k, j))
        return place.to_mate(part, part, send_bm.at[j, k], recv_bm.at[j, k])

    def saves(slot, item):
        lanes = pl.ds(pl.multiple_of(slot * length, length), length)
        src, dst = (
            lambda: (g.at[lanes], g_out.at[lanes]),
            lambda: (u_sp.at[slot], u_out.at[slot]),
            lambda: (y.at[slot], y_out.at[slot]),
            lambda: (pre.at[slot], pre_out.at[slot]),
            lambda: (mx.at[:, lanes], mx_out.at[:, lanes]),
            lambda: (pm.at[slot], pm_out.at[slot]),
            lambda: (prod.at[:, lanes], prod_out.at[:, lanes]),
        )[item]()
        return pltpu.make_async_copy(src, dst, save.at[item, slot])

    def scan_slot(i, unused):
        slot = place.near(i)

        @pl.when(i == 1)
        def _():
            gather_a.pass_on()

        @pl.when(i > 0)
        def _():
            gather_a.fetch(i)

        lanes = pl.ds(pl.multiple_of(slot * length, length), length)
        live = mask_ref[slot, 0:1]
        v = dot(w_in_t[:ch2], g[lanes], 1, 1) + in_bias_ref[:ch2]
        pre[slot, :ch2] = v
        act[...] = (gelu_only(v) * live).astype(BF)
        spec[...] = dot(act[...], ft_ref[...], 1, 0)
        u_re, u_im = spec[:, :length], spec[:, length:]
        k_re, k_im = kre_ref[...], kim_ref[...]
        u_sp[slot, :, :length] = u_re.astype(BF)
        u_sp[slot, :, length:] = u_im.astype(BF)
        y_hat[:, :length] = (k_re * u_re - k_im * u_im).astype(BF)
        y_hat[:, length:] = (k_re * u_im + k_im * u_re).astype(BF)
        both = dot(y_hat[...], f_ref[...], 1, 0)
        y[slot] = both.astype(BF)
        mine = pl.ds(pl.multiple_of((c * n + d) * ch, ch), ch)
        mx[mine, lanes] = (both[:ch] * both[ch:]).astype(BF)
        for j in range(n):

            @pl.when(i == j)
            def _():
                peer_b(1, j).start()
                peer_b(2, j).start()
                mate_b(0, j).start()

        for item in range(3):
            saves(slot, item).start()
        return unused

    lax.fori_loop(0, n, scan_slot, 0)
    if first:
        spectra(next_tables, kre_next, kim_next)
    w_mx = gather_mx.whole()
    w_mx_out[...] = w_mx.astype(BF)
    for block in range(2 * n):
        w_mx_t[block] = w_mx[block * ch : (block + 1) * ch].T.astype(BF)
    begun = set()

    def mix_in(k, j):
        owner, slot = place.near(k), turn(k, j)
        lanes = pl.ds(pl.multiple_of(slot * length, length), length)
        mate_b(k, j).wait_recv()
        total = None
        for side in range(2):
            rows_at = pl.ds(pl.multiple_of((side * n + owner) * ch, ch), ch)
            part = dot(w_mx_t[side * n + owner], mx[rows_at, lanes], 1, 0)
            total = part if total is None else total + part
        pm[slot] = (pm[slot] if k ^ j in begun else mix_bias_ref[...]) + total
        begun.add(k ^ j)

    def across(j):
        hop_b(1, j).wait_recv()
        hop_b(2, j).wait_recv()
        mate_b(3, j).start()
        mix_in(3, j)

    for j in range(n):
        for i in (1, 2):
            peer_b(i, j).wait_recv()
            hop_b(3 - i, j).start()
            mate_b(i, j).start()
        for k in range(3):
            mix_in(k, j)
        if j > 0:
            across(j - 1)
    across(n - 1)
    w_v = gather_v.whole()
    w_in_out[:, ch2:] = w_v.astype(BF)
    w_in_t[ch2:] = w_v.T.astype(BF)
    w_out = gather_out.whole()
    w_out_t[...] = w_out.astype(BF)
    w_out_out[...] = w_out.T.astype(BF)
    if first:
        gather_next.start()

    to_mate, close, receive, finish_c = sum_to_owner(
        place, rows, mate_out, mate_in, sum_out, sum_in, own, send_cm, recv_cm, send_c, recv_c
    )

    def order(i):
        return lax.select(i == n - 1, d, place.other(i))

    def hidden_slot(i, unused):
        slot = order(i)
        lanes = pl.ds(pl.multiple_of(slot * length, length), length)
        v = pm[slot]
        value = dot(w_in_t[ch2:], g[lanes], 1, 1) + in_bias_ref[ch2:]
        pre[slot, ch2:] = value
        product = gelu_only(v) * gelu_only(value)
        prod_f[...] = product
        prod[:, lanes] = product.astype(BF)
        prod_t[...] = prod_f[...].T.astype(BF)
        for item in range(3, 7):
            saves(slot, item).start()
        theirs = pl.ds(pl.multiple_of((1 - c) * rows, rows), rows)
        ours = pl.ds(pl.multiple_of(c * rows, rows), rows)
        mate_out[slot] = dot(prod_t[theirs], w_out_t[...], 1, 1).astype(BF)
        to_mate(slot).start()

        @pl.when(i > 0)
        def _():
            close(order(i - 1), lax.rem(i - 1, 2))

        own[lax.rem(i, 2)] = dot(prod_t[ours], w_out_t[...], 1, 1)
        return unused

    lax.fori_loop(0, n, hidden_slot, 0)
    last = (n - 1) % 2
    close(d, last)
    receive()

    total = own[last]
    for k in range(1, n):
        total = total + sum_in[k - 1].astype(F32)
    new_ref[...] = res_ref[...].astype(F32) + own_mask_ref[...] * (total + out_bias)
    gather_a.finish()
    finish_c()
    for gather in later_weights:
        gather.finish()
    if first:
        next_out[...] = gather_next.whole().astype(BF)
        gather_next.finish()
        gather_fb.finish()
        for k in range(1, n):
            mask_peer(k).wait_send()

    for j in range(n):
        for i in (1, 2):
            peer_b(i, j).wait_send()
            hop_b(i, j).wait_send()
        for k in range(n):
            mate_b(k, j).wait_send()

    def drain(slot, unused):
        for item in range(7):
            saves(slot, item).wait()
        return unused

    lax.fori_loop(0, n, drain, 0)


def bwd_kernel(
    n, m, layer, later, grad_ref, res_ref, gain_ref, mask_ref, own_mask_ref, w_in_ref, w_mx_ref, w_out_ref, kre_ref,
    kim_ref, ft_ref, f_ref, g_in, mx_in, pre_in, u_in, y_in, pm_in, prod_in, *rest
):
    if later:
        late_part, red_mx1, red_out1, late_dk, decay_ref, b_ref, c_ref, row_ref, *rest = rest
    (new_ref, gw_in_ref, red_mx_ref, red_out_ref, in_row_ref, mix_row_ref, norm_sum_ref, dk_ref, *rest) = rest
    if later:
        red_late_ref, states_ref, step_ref, all_mx, all_out, *rest = rest
    (
        gb, g, mx, pre, u_sp, y, pm, prod, gpre, gpre_f, gpm, spec, hat, turned,
        mix_sum, mix_mate, mix_own, mix_got, in_sum, mix_acc, part_mx, got_mx, part_out, got_out,
        own, mate_out, mate_in, sum_out, sum_in,
        send_a, recv_a, send_ah, recv_ah, send_am, recv_am, send_b, recv_b, send_bm, recv_bm, send_c, recv_c, send_cm, recv_cm, load,
        send_rm, recv_rm, send_ro, recv_ro, *rest,
    ) = rest
    place = Place(n, m)
    d, c = place.d, place.c
    rows, width = res_ref.shape
    length = ft_ref.shape[0]
    hid = w_mx_ref.shape[1]
    ch2 = kre_ref.shape[0]
    ch = ch2 // 2
    half = n * ch

    def loads(slot, item):
        lanes = pl.ds(pl.multiple_of(slot * length, length), length)
        src, dst = (
            lambda: (pre_in.at[slot], pre.at[slot]),
            lambda: (pm_in.at[slot], pm.at[slot]),
            lambda: (y_in.at[slot], y.at[slot]),
            lambda: (u_in.at[slot], u_sp.at[slot]),
            lambda: (prod_in.at[:, lanes], prod.at[:, lanes]),
            lambda: (mx_in.at[:, lanes], mx.at[:, lanes]),
            lambda: (g_in.at[lanes], g.at[lanes]),
        )[item]()
        return pltpu.make_async_copy(src, dst, load.at[item, slot])

    for item in range(7):
        loads(d, item).start()

    def start_loads(i, unused):
        for item in range(7):
            loads(place.other(i), item).start()
        return unused

    lax.fori_loop(0, n - 1, start_loads, 0)

    place.greet()
    gather_a = Tokens(place, gb, rows, length, (send_a, recv_a, send_ah, recv_ah, send_am, recv_am))
    base = d * length + c * rows
    gain = gain_ref[layer : layer + 1]
    first = grad_ref[...].astype(F32) * own_mask_ref[...]
    gb[pl.ds(pl.multiple_of(base, rows), rows)] = first.astype(BF)
    gather_a.start()
    sum_mx = RowSum(place, part_mx, got_mx, send_rm, recv_rm)
    sum_out_w = RowSum(place, part_out, got_out, send_ro, recv_ro)
    row_sums = [sum_mx, sum_out_w]
    if later:
        lag_sums, got_late, send_rl, recv_rl, *sems = rest
        sum_late = RowSum(place, late_part, got_late, send_rl, recv_rl)
        sum_late.start()
        row_sums.append(sum_late)
    norm_sum_ref[...] = jnp.zeros_like(norm_sum_ref)
    norm_sum_ref[2:3] = jnp.sum(first, axis=0, keepdims=True)
    in_sum[...] = jnp.zeros_like(in_sum)
    mix_acc[...] = jnp.zeros_like(mix_acc)
    dk_ref[...] = jnp.zeros_like(dk_ref)
    gather_a.own()

    def mate_b(slot):
        return place.to_mate(mix_sum.at[slot], mix_mate.at[slot], send_bm.at[slot], recv_bm.at[slot])

    def peer_b(k, slot):
        q = place.ahead(k)
        part = mix_sum.at[slot, pl.ds(pl.multiple_of(q * ch, ch), ch)]
        return place.to_dp(part, mix_got.at[k - 1, slot], send_b.at[slot, k], recv_b.at[slot, k], q)

    def hidden_slot(i, unused):
        slot = lax.select(i == 0, d, place.other(i - 1))

        @pl.when(i == 1)
        def _():
            gather_a.pass_on()

        @pl.when(i > 0)
        def _():
            gather_a.fetch(place.apart(slot))

        lanes = pl.ds(pl.multiple_of(slot * length, length), length)
        mix_own[:hid] = dot(w_out_ref[...], gb[lanes], 1, 1)
        for item in range(2):
            loads(slot, item).wait()
        gated, slope = gelu_parts(pm[slot])
        value, value_slope = gelu_parts(pre[slot, ch2:])
        now = mix_own[:hid]
        to_value = now * gated * value_slope
        to_mix = now * value * slope
        gpre[ch2:, lanes] = to_value.astype(BF)
        gpm[:, lanes] = to_mix.astype(BF)
        in_sum[ch2:] = in_sum[ch2:] + lane_sums(to_value)
        mix_acc[...] = mix_acc[...] + lane_sums(to_mix)
        theirs = pl.ds(pl.multiple_of((1 - c) * half, half), half)
        ours = pl.ds(pl.multiple_of(c * half, half), half)
        mix_sum[slot] = dot(w_mx_ref[theirs], gpm[:, lanes], 1, 0).astype(BF)
        mate_b(slot).start()
        mix_own[...] = dot(w_mx_ref[ours], gpm[:, lanes], 1, 0)
        mate_b(slot).wait()
        mix_sum[slot] = (mix_own[...] + mix_mate[slot].astype(F32)).astype(BF)
        for k in range(1, n):
            peer_b(k, slot).start()
        return unused

    lax.fori_loop(0, n, hidden_slot, 0)

    def wait_loads(slot, unused):
        for item in range(2, 7):
            loads(slot, item).wait()
        return unused

    lax.fori_loop(0, n, wait_loads, 0)
    share = mx.shape[0] // m

    def grad_mix(q, unused):
        part_mx[q] = dot(mx[pl.ds(pl.multiple_of(q * share, share), share)], gpm[...], 1, 1).astype(BF)
        return unused

    lax.fori_loop(0, m, grad_mix, 0)
    sum_mx.start()
    gw_out = dot(prod[...], gb[...], 1, 0).T
    part_out[...] = gw_out.reshape(m, width // m, hid).astype(BF)
    sum_out_w.start()
    spreads = []
    if later:
        grads = state_grads(
            late_dk[:, :length], late_dk[:, length:], direction_sign(ch, ch2, length), ft_ref, decay_ref[...],
            row_ref[0:1], b_ref[...], c_ref[...], lag_sums,
        )
        count = decay_ref.shape[0]
        for i in range(3):
            states_ref[i * count : (i + 1) * count] = grads[i]
        step_ref[...] = jnp.zeros_like(step_ref)
        step_ref[0:1] = grads[3]
        step_ref[1:2] = grads[4]
        spreads = [
            Spread(place, red_mx1, all_mx, sems, 0),
            Spread(place, red_out1, all_out, sems, 1),
        ]

    to_mate, close, receive, finish_c = sum_to_owner(
        place, rows, mate_out, mate_in, sum_out, sum_in, own, send_cm, recv_cm, send_c, recv_c
    )

    def order(i):
        return lax.select(i == n - 1, d, place.other(i))

    def scan_slot(i, unused):
        slot = order(i)
        lanes = pl.ds(pl.multiple_of(slot * length, length), length)
        for k in range(1, n):
            peer_b(k, slot).wait_recv()

        @pl.when(i == n - 2)
        def _():
            for each in spreads:
                each.start()

        total = mix_sum[slot, pl.ds(pl.multiple_of(d * ch, ch), ch)].astype(F32)
        for k in range(1, n):
            total = total + mix_got[k - 1, slot].astype(F32)
        hat[:ch, :length] = (total * y[slot, ch:].astype(F32)).astype(BF)
        hat[ch:, :length] = (total * y[slot, :ch].astype(F32)).astype(BF)
        spec[...] = dot(hat[:, :length], ft_ref[...], 1, 0)
        g_re, g_im = spec[:, :length], spec[:, length:]
        k_re, k_im = kre_ref[...], kim_ref[...]
        hat[:, :length] = (k_re * g_re + k_im * g_im).astype(BF)
        hat[:, length:] = (k_re * g_im - k_im * g_re).astype(BF)
        u_re, u_im = u_sp[slot, :, :length].astype(F32), u_sp[slot, :, length:].astype(F32)
        dk_ref[:, :length] = dk_ref[:, :length] + (u_re * g_re + u_im * g_im)
        dk_ref[:, length:] = dk_ref[:, length:] + (u_re * g_im - u_im * g_re)
        spec[:, :length] = dot(hat[...], f_ref[...], 1, 0)
        live = mask_ref[slot, 0:1]
        _, slope = gelu_parts(pre[slot, :ch2])
        part = spec[:, :length] * slope * live
        gpre_f[...] = part
        gpre[:ch2, lanes] = part.astype(BF)
        in_sum[:ch2] = in_sum[:ch2] + lane_sums(part)
        turned[:, :ch2] = gpre_f[...].T.astype(BF)
        gpre_f[...] = gpre[ch2:, lanes].astype(F32)
        turned[:, ch2:] = gpre_f[...].T.astype(BF)
        theirs = pl.ds(pl.multiple_of((1 - c) * rows, rows), rows)
        ours = pl.ds(pl.multiple_of(c * rows, rows), rows)
        mate_out[slot] = dot(turned[theirs], w_in_ref[...], 1, 1).astype(BF)
        to_mate(slot).start()

        @pl.when(i > 0)
        def _():
            close(order(i - 1), lax.rem(i - 1, 2))

        own[lax.rem(i, 2)] = dot(turned[ours], w_in_ref[...], 1, 1)
        return unused

    lax.fori_loop(0, n, scan_slot, 0)
    last = (n - 1) % 2
    close(d, last)

    def grad_in(r):
        part = dot(gpre[r], g[...], 1, 0).T
        gw_in_ref[:, :, r] = part.reshape(m, width // m, part.shape[1]).astype(BF)

    over_rows(gpre.shape[0], 128, grad_in)
    for each in spreads:
        each.pass_on()
    in_row_ref[...] = as_row(in_sum[...])
    mix_row_ref[...] = as_row(mix_acc[...])
    if later:
        red_late_ref[...] = sum_late.total().astype(BF)
    receive()
    total = own[last]
    for k in range(1, n):
        total = total + sum_in[k - 1].astype(F32)
    xhat, inv = norm_stats(res_ref[...].astype(F32))
    h = total * gain
    middle = jnp.mean(h, axis=1, keepdims=True)
    along = jnp.mean(h * xhat, axis=1, keepdims=True)
    new_ref[...] = grad_ref[...].astype(F32) + inv * (h - middle - xhat * along)
    norm_sum_ref[0:1] = jnp.sum(total * xhat, axis=0, keepdims=True)
    norm_sum_ref[1:2] = jnp.sum(total, axis=0, keepdims=True)
    red_mx_ref[...] = sum_mx.total().astype(BF)
    red_out_ref[...] = sum_out_w.total().astype(BF)
    gather_a.finish()
    finish_c()
    for row_sum in row_sums:
        row_sum.finish()
    for each in spreads:
        each.wait()

    def drain(slot, unused):
        for k in range(1, n):
            peer_b(k, slot).wait_send()
        return unused

    lax.fori_loop(0, n, drain, 0)


class Spread:
    def __init__(self, place, src, out, sems, item):
        self.place, self.src, self.out, self.item = place, src, out, item
        self.send, self.recv, self.send_h, self.recv_h, self.keep = sems
        rows = src.shape[0]
        half = rows // 2 if rows % 32 == 0 else rows
        self.pieces = [(i, start, half) for i, start in ((1, 0), (2, half)) if start < rows]

    def peer(self, i):
        place, item = self.place, self.item
        return place.to_dp(
            self.src, self.out.at[place.d], self.send.at[item, i], self.recv.at[item, i], place.near(i)
        )

    def hop(self, i, start, count):
        place, item = self.place, self.item
        part = self.out.at[place.near(3 - i), pl.ds(start, count)]
        return place.to_dp(part, part, self.send_h.at[item, i], self.recv_h.at[item, i], place.near(i))

    def local(self):
        return pltpu.make_async_copy(self.src, self.out.at[self.place.d], self.keep.at[self.item])

    def start(self):
        self.peer(1).start()
        self.peer(2).start()
        self.local().start()

    def pass_on(self):
        self.peer(1).wait_recv()
        self.peer(2).wait_recv()
        for piece in self.pieces:
            self.hop(*piece).start()

    def wait(self):
        for piece in self.pieces:
            self.hop(*piece).wait()
        self.peer(1).wait_send()
        self.peer(2).wait_send()
        self.local().wait()


def state_grads(dk_re, dk_im, sign, ft_ref, decay, step, b_in, c_out, lag_sums):
    length = ft_ref.shape[0]
    re = dk_re.astype(BF)
    im = (dk_im * sign).astype(BF)
    lag_sums[...] = (dot(ft_ref[:, :length], re, 1, 1) + dot(ft_ref[:, length:], im, 1, 1)) * (1.0 / length)
    rate = jnp.exp(step) * jnp.exp(decay)
    a = jnp.exp(-rate)

    def lag(i, carry):
        total, slope = carry
        row = lag_sums[pl.ds(length - 1 - i, 1)]
        return total * a + row, slope * a + total

    zero = jnp.zeros_like(a)
    total, slope = lax.fori_loop(0, length, lag, (zero, zero), unroll=4)
    inv_decay = jnp.exp(-decay)
    gain = (1.0 - a) * inv_decay
    b_disc = gain * b_in
    to_b = c_out * total
    to_rate = a * (to_b * inv_decay * b_in - (c_out * b_disc) * slope)
    through = to_rate * rate
    return (
        through - to_b * b_disc, to_b * gain, b_disc * total,
        jnp.sum(through, axis=0, keepdims=True), lag_sums[0:1],
    )


def finish_kernel(
    n, m, part_in, late_in, red_mx0, red_out0, dk0, in0, in1, mix0, mix1, norm0, norm1, states1, steps1,
    decay0, b0, c0, row0, ft_ref,
    all_in1, all_mx0, all_out0, all_in0, all_states, all_small, norm_ref,
    got_in, red_in0, states, part_s, got_s, red_s, full_s, lag_sums, small, row_small, dp_small, norm_own, norm_got,
    send_w, recv_w, send_wh, recv_wh, keep_w, send_ri, recv_ri, send_rs, recv_rs, send_gs, recv_gs, send_sm, recv_sm,
    send_ds, recv_ds, send_n, recv_n, send_st, recv_st, keep_st,
):
    place = Place(n, m)
    d, r = place.d, place.r
    states_n, ch2 = decay0.shape
    place.greet()
    sum_in = RowSum(place, part_in, got_in, send_ri, recv_ri)
    sum_in.start()
    spreads = [
        Spread(place, src, out, (send_w, recv_w, send_wh, recv_wh, keep_w), item)
        for item, (src, out) in enumerate(
            ((late_in, all_in1), (red_mx0, all_mx0), (red_out0, all_out0), (red_in0, all_in0))
        )
    ]
    for each in spreads[:3]:
        each.start()

    small[...] = jnp.zeros_like(small)
    for l, (in_row, mix_row, norm) in enumerate(((in0, mix0, norm0), (in1, mix1, norm1))):
        small[l, 0:1] = in_row[0:1]
        small[l, 1:2, :ch2] = mix_row[0:1]
        small[l, 3:6] = norm[0:3]
    length = ft_ref.shape[0]
    grads = state_grads(
        dk0[:, :length], dk0[:, length:], direction_sign(ch2 // 2, ch2, length), ft_ref, decay0[...], row0[0:1],
        b0[...], c0[...], lag_sums,
    )
    for i in range(3):
        states[pl.ds(i * states_n, states_n)] = grads[i]
    states[3 * states_n :] = states1[...]
    for l, (step, skip) in enumerate((grads[3:5], (steps1[0:1], steps1[1:2]))):
        small[l, 1:2, ch2:] = step
        small[l, 2:3, :ch2] = skip
    share = states.shape[0] // m
    for q in range(m):
        part_s[q] = states[q * share : (q + 1) * share].astype(BF)
    sum_s = RowSum(place, part_s, got_s, send_rs, recv_rs)
    sum_s.start()
    row_small[r] = small[...]

    def small_row(j):
        return place.to_row(row_small.at[r], row_small.at[r], send_sm.at[j], recv_sm.at[j], place.up(j))

    def repeat(work, count):
        def one(j, unused):
            work(j)
            return unused

        lax.fori_loop(1, count, one, 0)

    repeat(lambda j: small_row(j).start(), m)

    spreads[0].pass_on()
    spreads[1].pass_on()
    red_in0[...] = sum_in.total().astype(BF)
    spreads[3].start()
    spreads[2].pass_on()
    red_s[...] = sum_s.total().astype(BF)
    full_s[r] = red_s[...]

    def state_row(j):
        return place.to_row(full_s.at[r], full_s.at[r], send_gs.at[j], recv_gs.at[j], place.up(j))

    repeat(lambda j: state_row(j).start(), m)
    repeat(lambda j: small_row(j).wait_recv(), m)
    total = row_small[0]
    for q in range(1, m):
        total = total + row_small[q]
    dp_small[d] = total

    def small_dp(k):
        return place.to_dp(dp_small.at[d], dp_small.at[d], send_ds.at[k], recv_ds.at[k], place.ahead(k))

    for k in range(1, n):
        small_dp(k).start()
    repeat(lambda j: state_row(j).wait_recv(), m)

    def states_dp(k):
        return place.to_dp(full_s, all_states.at[d], send_st.at[k], recv_st.at[k], place.ahead(k))

    keep_states = pltpu.make_async_copy(full_s, all_states.at[d], keep_st)
    keep_states.start()
    for k in range(1, n):
        states_dp(k).start()
    for k in range(1, n):
        small_dp(k).wait_recv()
    total = dp_small[0]
    for q in range(1, n):
        total = total + dp_small[q]
    norm_own[...] = total
    swap = place.to_mate(norm_own, norm_got, send_n, recv_n)
    swap.start()
    all_small[...] = dp_small[...]
    swap.wait_recv()
    norm_ref[...] = norm_own[...] + norm_got[...]
    swap.wait_send()
    spreads[3].pass_on()
    for each in spreads:
        each.wait()
    for k in range(1, n):
        states_dp(k).wait_recv()
        states_dp(k).wait_send()
        small_dp(k).wait_send()
    keep_states.wait()
    repeat(lambda j: small_row(j).wait_send(), m)
    repeat(lambda j: state_row(j).wait_send(), m)
    sum_in.finish()
    sum_s.finish()


def prepare_kernel(
    n, lengths_ref, bias_fwd, bias_bwd, bias_value, bias_mix, step_ref, skip_ref, *rest
):
    d = lax.axis_index("dp")
    w_fwd, w_bwd, w_value, w_mix, w_out, decay, b_in, c_out, live_ref, mask_ref, *rest = rest
    per = 10
    outs = [rest[per * l : per * (l + 1)] for l in range(LAYERS)]
    win_f, win_b, win_v, win_m, win_o, win_d, win_i, win_c, load = rest[per * LAYERS :]
    ch = w_fwd.shape[2] // n
    hid = w_value.shape[2] // n
    size = win_f.shape[2]
    places = sorted({(k * ch) % 128 for k in range(n)})

    def window(width, wide):
        start = pl.multiple_of((d * width) // 128 * 128, 128)
        return pl.ds(start, wide)

    narrow, broad = window(ch, size), window(hid, hid)
    copies = [
        pltpu.make_async_copy(src.at[at], dst, load.at[i])
        for i, (src, at, dst) in enumerate((
            (w_fwd, (slice(None), slice(None), narrow), win_f), (w_bwd, (slice(None), slice(None), narrow), win_b),
            (decay, (slice(None), slice(None), slice(None), narrow), win_d),
            (b_in, (slice(None), slice(None), slice(None), narrow), win_i),
            (c_out, (slice(None), slice(None), slice(None), narrow), win_c),
            (w_value, (slice(None), slice(None), broad), win_v), (w_mix, (slice(None), slice(None), broad), win_m),
            (w_out, (slice(None), slice(None), broad), win_o),
        ))
    ]
    for copy in copies:
        copy.start()

    def pick(x):
        kept = x[..., places[0] : places[0] + ch]
        for place in places[1:]:
            kept = jnp.where(lax.rem(d * ch, 128) == place, x[..., place : place + ch], kept)
        return kept

    def cut(x, width):
        kept = x[:, :width]
        for k in range(1, n):
            kept = jnp.where(d == k, x[:, k * width : (k + 1) * width], kept)
        return kept

    def column(row):
        return jnp.broadcast_to(row, (8, row.shape[1])).T[:, :1]

    rows, length = mask_ref.shape[0], live_ref.shape[1]
    alive = lengths_ref[0]
    live_ref[...] = (lax.broadcasted_iota(jnp.int32, live_ref.shape, 1) < alive).astype(F32)
    at = lax.broadcasted_iota(jnp.int32, mask_ref.shape, 0) + lax.axis_index("col") * rows
    mask_ref[...] = (at < alive).astype(F32)
    for l in range(LAYERS):
        in_bias, mix_bias, row_ref = outs[l][4], outs[l][5], outs[l][9]
        one = slice(l, l + 1)
        in_bias[:ch] = column(cut(bias_fwd[one], ch))
        in_bias[ch : 2 * ch] = column(cut(bias_bwd[one], ch))
        in_bias[2 * ch :] = column(cut(bias_value[one], hid))
        mix_bias[...] = column(cut(bias_mix[one], hid))
        row_ref[...] = jnp.zeros_like(row_ref)
        for k in range(2):
            lanes = slice(k * ch, (k + 1) * ch)
            row_ref[0:1, lanes] = cut(step_ref[l, k : k + 1], ch)
            row_ref[1:2, lanes] = cut(skip_ref[l, k : k + 1], ch)
    for copy in copies:
        copy.wait()
    for l in range(LAYERS):
        fb_ref, v_ref, mx_ref, out_ref, _, _, decay_ref, b_ref, c_ref, _ = outs[l]
        fb_ref[:, :ch] = pick(win_f[l]).astype(BF)
        fb_ref[:, ch:] = pick(win_b[l]).astype(BF)
        v_ref[...] = win_v[l].astype(BF)
        mx_ref[...] = win_m[l].astype(BF)
        out_ref[...] = win_o[l].astype(BF)
        for k in range(2):
            lanes = slice(k * ch, (k + 1) * ch)
            decay_ref[:, lanes] = pick(win_d[l, k])
            b_ref[:, lanes] = pick(win_i[l, k])
            c_ref[:, lanes] = pick(win_c[l, k])


def assemble_kernel(
    n, in0, in1, mx0, mx1, out0, out1, states_ref, small_ref, norm_ref,
    gain, shift, wf, wb, wv, bf, bb, bv, decay, step, b_in, c_out, skip, wm, bm, wo, bo,
):
    l = pl.program_id(0)
    ch = wf.shape[2] // n
    hid = wv.shape[2] // n
    count = decay.shape[2]
    one = pl.ds(l, 1)
    for i, ref in ((3, gain), (4, shift), (5, bo)):
        ref[one] = norm_ref[one, i]
    for k in range(n):
        narrow, broad = slice(k * ch, (k + 1) * ch), slice(k * hid, (k + 1) * hid)
        for layer, (part_in, part_mx, part_out) in enumerate(((in0, mx0, out0), (in1, mx1, out1))):

            @pl.when(l == layer)
            def _():
                piece = part_in[k].astype(F32)
                wf[0, :, narrow] = piece[:, :ch]
                wb[0, :, narrow] = piece[:, ch : 2 * ch]
                wv[0, :, broad] = piece[:, 2 * ch :]
                wm[0, :, broad] = part_mx[k].astype(F32)
                wo[0, :, broad] = part_out[k].astype(F32)

        piece = states_ref[k].astype(F32)
        for i, ref in enumerate((decay, b_in, c_out)):
            for direction in range(2):
                lanes = slice(direction * ch, (direction + 1) * ch)
                ref[0, direction, :, narrow] = piece[i * count : (i + 1) * count, lanes]
        row = small_ref[k, one]
        bf[one, narrow] = row[:, 0, :ch]
        bb[one, narrow] = row[:, 0, ch : 2 * ch]
        bv[one, broad] = row[:, 0, 2 * ch :]
        bm[one, broad] = row[:, 1, :hid]
        for direction in range(2):
            start = direction * ch
            step[one, direction, narrow] = row[:, 1, hid + start : hid + start + ch]
            skip[one, direction, narrow] = row[:, 2, start : start + ch]


VM = pl.BlockSpec(memory_space=pltpu.VMEM)
ANY = pl.BlockSpec(memory_space=pl.ANY)


def shape(dims, dtype):
    return jax.ShapeDtypeStruct(tuple(dims), dtype)


def sem(*dims):
    return pltpu.SemaphoreType.DMA(dims)


def body(
    tokens_in, lengths, cotangent, norm_gain, norm_shift, w_fwd, w_bwd, w_value, bias_fwd, bias_bwd,
    bias_value, decay_log, step_log, b_input, c_output, skip_gain, w_mix, bias_mix, w_output, bias_output,
):
    n = lax.axis_size("dp")
    m = lax.axis_size("row")
    cols = lax.axis_size("col")
    rows, width = tokens_in.shape
    length = rows * cols
    ch = w_fwd.shape[2] // n
    ch2 = 2 * ch
    hid = w_mix.shape[2] // n
    wide = ch2 + hid
    chans = n * cols * ch
    tokens = n * length
    matrix = transform_matrix(length)
    f_mat = jnp.asarray(matrix, BF)
    ft_mat = jnp.asarray(np.ascontiguousarray(matrix.T), BF)
    states = decay_log.shape[3]
    share = w_fwd.shape[1]
    narrow = -(-(ch + max(k * ch % 128 for k in range(n))) // 128) * 128

    def turned(x):
        return jnp.swapaxes(x, -1, -2)

    per_layer = (
        shape((share, ch2), BF), shape((share, hid), BF), shape((w_mix.shape[1], hid), BF), shape((share, hid), BF),
        shape((wide, 1), F32), shape((hid, 1), F32), *[shape((states, ch2), F32)] * 3, shape((8, ch2), F32),
    )
    own_live, own_mask, *cuts = pl.pallas_call(
        functools.partial(prepare_kernel, n),
        out_shape=(shape((8, length), F32), shape((rows, 1), F32), *per_layer * LAYERS),
        in_specs=[pl.BlockSpec(memory_space=pltpu.SMEM)] + [VM] * 6 + [ANY] * 8,
        out_specs=(VM,) * (2 + len(per_layer) * LAYERS),
        scratch_shapes=[
            pltpu.VMEM((LAYERS, share, narrow), F32), pltpu.VMEM((LAYERS, share, narrow), F32),
            pltpu.VMEM((LAYERS, share, hid), F32), pltpu.VMEM((LAYERS, w_mix.shape[1], hid), F32),
            pltpu.VMEM((LAYERS, share, hid), F32), *[pltpu.VMEM((LAYERS, 2, states, narrow), F32)] * 3, sem(8),
        ],
        compiler_params=pltpu.CompilerParams(vmem_limit_bytes=VMEM_LIMIT),
        name="prepare",
    )(
        lengths, bias_fwd, bias_bwd, bias_value, bias_mix, step_log, skip_gain, w_fwd, w_bwd, w_value, w_mix,
        turned(w_output), turned(decay_log), turned(b_input), turned(c_output),
    )
    given = [cuts[len(per_layer) * l : len(per_layer) * (l + 1)] for l in range(LAYERS)]

    comm = [
        *[sem(n)] * 6, sem(n, n), sem(n, n),
    ]
    sums = [
        pltpu.VMEM((2, rows, width), F32), pltpu.VMEM((n, rows, width), BF), pltpu.VMEM((n, rows, width), BF),
        pltpu.VMEM((n, rows, width), BF), pltpu.VMEM((n - 1, rows, width), BF),
    ]
    saved_shapes = (
        shape((tokens, width), BF), shape((chans, tokens), BF), shape((n, wide, length), F32),
        shape((n, ch2, 2 * length), BF), shape((n, ch2, length), BF), shape((n, hid, length), F32),
        shape((hid, tokens), BF),
    )
    def fwd(layer):
        first = layer == 0
        table = shape((ch2, length), F32)
        extra = (shape((width, ch2), BF), shape((n, 8, length), F32), *[table] * 4) if first else ()
        lands = [(m, share, hid), (m, chans // m, hid), (m, share, hid)]
        return pl.pallas_call(
            functools.partial(fwd_kernel, n, m, layer),
            out_shape=(
                shape((rows, width), F32), *saved_shapes, shape((width, wide), BF),
                shape((chans, hid), BF), shape((hid, width), BF), *extra,
            ),
            in_specs=[VM] * (13 + (10 if first else 3)),
            out_specs=(VM, *([ANY] * 7), *([VM] * (3 + len(extra)))),
            scratch_shapes=[
                pltpu.VMEM((wide, width), BF), pltpu.VMEM((2 * n, hid, ch), BF),
                *(pltpu.VMEM(s.shape, s.dtype) for s in saved_shapes),
                pltpu.VMEM((ch2, length), BF), pltpu.VMEM((ch2, 2 * length), F32),
                pltpu.VMEM((ch2, 2 * length), BF), pltpu.VMEM((hid, length), F32), pltpu.VMEM((length, hid), BF),
                pltpu.VMEM((states, 128), F32), pltpu.VMEM((length // LAG, states, 128), F32),
                *(pltpu.VMEM(s, BF) for s in lands), pltpu.VMEM((width, hid), BF),
                *sums, *comm, *[sem(n, n)] * 4, *[sem(n)] * 4, sem(7, n),
                *[sem(m)] * 6,
                *([pltpu.VMEM((m, share, ch2), BF)] * 2 + [sem(m)] * 4 + [sem(n)] * 2 if first else []),
            ],
            compiler_params=pltpu.CompilerParams(
                collective_id=4 if first else 0, has_side_effects=True, vmem_limit_bytes=VMEM_LIMIT
            ),
            name="forward_block",
        )

    def bwd(layer):
        later = layer < LAYERS - 1
        late = (m, width // m, wide)
        out_shape = [
            shape((rows, width), F32), shape(late, BF), shape((chans // m, hid), BF), shape((width // m, hid), BF),
            shape((8, wide), F32), shape((8, hid), F32), shape((8, width), F32), shape((ch2, 2 * length), F32),
        ]
        if later:
            out_shape += [
                shape(late[1:], BF), shape((3 * states, ch2), F32), shape((8, ch2), F32),
                shape((n, chans // m, hid), BF), shape((n, share, hid), BF),
            ]
        return pl.pallas_call(
            functools.partial(bwd_kernel, n, m, layer, later),
            out_shape=tuple(out_shape),
            in_specs=[VM] * 12 + [ANY] * 7 + [VM] * (8 * later),
            out_specs=(*[VM] * (8 + 3 * later), *[ANY] * (2 * later)),
            scratch_shapes=[
                pltpu.VMEM((tokens, width), BF),
                *(pltpu.VMEM(s.shape, s.dtype) for s in saved_shapes),
                pltpu.VMEM((wide, tokens), BF), pltpu.VMEM((ch2, length), F32), pltpu.VMEM((hid, tokens), BF),
                pltpu.VMEM((ch2, 2 * length), F32), pltpu.VMEM((ch2, 2 * length), BF), pltpu.VMEM((length, wide), BF),
                pltpu.VMEM((n, n * ch, length), BF), pltpu.VMEM((n, n * ch, length), BF),
                pltpu.VMEM((n * ch, length), F32),
                pltpu.VMEM((n - 1, n, ch, length), BF), pltpu.VMEM((wide, 128), F32), pltpu.VMEM((hid, 128), F32),
                *(pltpu.VMEM((m - i, chans // m, hid), BF) for i in range(2)),
                *(pltpu.VMEM((m - i, width // m, hid), BF) for i in range(2)),
                *sums, *comm, sem(n), sem(n), sem(n), sem(n), sem(n), sem(n), sem(7, n),
                sem(m), sem(m), sem(m), sem(m),
                *([pltpu.VMEM((length, ch2), F32), pltpu.VMEM((m - 1, *late[1:]), BF), sem(m), sem(m), *[sem(2, n)] * 4, sem(2)]
                  if later else []),
            ],
            compiler_params=pltpu.CompilerParams(
                collective_id=1 + later, has_side_effects=True, vmem_limit_bytes=VMEM_LIMIT
            ),
            name="backward_block",
        )

    residual = tokens_in
    stored = []
    for l in range(LAYERS):
        sh_fb, sh_v, sh_mx, sh_out, in_bias, mix_bias, *tables = given[l]
        first = l == 0
        more = (sh_fb, given[1][0], *tables, *given[1][6:]) if first else (w_next, *spectrum)
        new, *made = fwd(l)(
            residual, norm_gain, norm_shift, own_live if first else mask, own_mask, sh_v, sh_mx, sh_out, in_bias,
            mix_bias, bias_output, ft_mat, f_mat, *more,
        )
        weights = made[7:10]
        if first:
            w_next, mask, *spectrum = made[10:]
            kernels = spectrum[:2], spectrum[2:]
            spectrum = spectrum[2:]
        stored.append((residual, made[:7], weights, kernels[l]))
        residual = new
    tokens_out = residual.astype(BF)

    grad = cotangent
    parts = [None] * LAYERS
    extra = ()
    for l in reversed(range(LAYERS)):
        resid_in, saved, weights, (kre, kim) = stored[l]
        grad, *parts[l] = bwd(l)(
            grad, resid_in, norm_gain, mask, own_mask, *weights, kre, kim, ft_mat, f_mat, *saved, *extra,
        )
        if l > 0:
            extra = (*parts[l][:3], parts[l][6], *given[l][6:])
    part_in, red_mx0, red_out0, in0, mix0, norm0, dk0, late_in, states1, steps1, all_mx1, all_out1 = parts[0]
    _, _, _, in1, mix1, norm1, _ = parts[1]
    lots = LAYERS * 3 * states
    all_in, all_mx, all_out = (n, share, wide), (n, chans // m, hid), (n, share, hid)
    all_in1, all_mx0, all_out0, all_in0, all_states, all_small, norms = pl.pallas_call(
        functools.partial(finish_kernel, n, m),
        out_shape=(
            shape(all_in, BF), shape(all_mx, BF), shape(all_out, BF), shape(all_in, BF),
            shape((n, m, lots // m, ch2), BF), shape((n, LAYERS, 8, wide), F32), shape((LAYERS, 8, wide), F32),
        ),
        in_specs=[VM] * 18,
        out_specs=(*[ANY] * 5, VM, VM),
        scratch_shapes=[
            pltpu.VMEM((m - 1, share, wide), BF), pltpu.VMEM((share, wide), BF), pltpu.VMEM((lots, ch2), F32),
            pltpu.VMEM((m, lots // m, ch2), BF), pltpu.VMEM((m - 1, lots // m, ch2), BF),
            pltpu.VMEM((lots // m, ch2), BF), pltpu.VMEM((m, lots // m, ch2), BF), pltpu.VMEM((length, ch2), F32),
            pltpu.VMEM((LAYERS, 8, wide), F32), pltpu.VMEM((m, LAYERS, 8, wide), F32),
            pltpu.VMEM((n, LAYERS, 8, wide), F32), pltpu.VMEM((LAYERS, 8, wide), F32),
            pltpu.VMEM((LAYERS, 8, wide), F32),
            *[sem(4, n)] * 4, sem(4), *[sem(m)] * 8,
            sem(n), sem(n), pltpu.SemaphoreType.DMA, pltpu.SemaphoreType.DMA, sem(n), sem(n),
            pltpu.SemaphoreType.DMA,
        ],
        compiler_params=pltpu.CompilerParams(
            collective_id=3, has_side_effects=True, vmem_limit_bytes=VMEM_LIMIT
        ),
        name="finish",
    )(
        part_in, late_in, red_mx0, red_out0, dk0, in0, in1, mix0, mix1, norm0, norm1, states1, steps1,
        *given[0][6:], ft_mat,
    )

    def fixed(dims):
        return pl.BlockSpec(tuple(dims), lambda l: (0,) * len(dims))

    def by_layer(dims):
        return pl.BlockSpec((1, *dims), lambda l: (l,) + (0,) * len(dims))

    chan, unit = n * ch, n * hid
    matrices = [(share, chan), (share, chan), (share, unit)]
    layouts = [
        (width,), (width,), *matrices, (chan,), (chan,), (unit,), (2, states, chan), (2, chan), (2, states, chan),
        (2, states, chan), (2, chan), (chans // m, unit), (unit,), (share, unit), (width,),
    ]
    small_out = {0, 1, 5, 6, 7, 9, 12, 14, 16}
    grads = list(pl.pallas_call(
        functools.partial(assemble_kernel, n),
        grid=(LAYERS,),
        out_shape=tuple(shape((LAYERS, *dims), F32) for dims in layouts),
        in_specs=[
            fixed(all_in), fixed(all_in), fixed(all_mx), fixed(all_mx), fixed(all_out), fixed(all_out),
            pl.BlockSpec((n, 3 * states, ch2), lambda l: (0, l, 0)), fixed((n, LAYERS, 8, wide)),
            fixed((LAYERS, 8, wide)),
        ],
        out_specs=tuple(
            fixed((LAYERS, *dims)) if i in small_out else by_layer(dims) for i, dims in enumerate(layouts)
        ),
        compiler_params=pltpu.CompilerParams(vmem_limit_bytes=VMEM_LIMIT),
        name="assemble",
    )(
        all_in0, all_in1, all_mx0, all_mx1, all_out0, all_out1, all_states.reshape(n, lots, ch2), all_small, norms,
    ))
    for i in (8, 10, 11, 15):
        grads[i] = turned(grads[i])
    return (tokens_out, grad, *grads)


def solution(mesh):
    tokens = P(("dp", "row", "col"), None)
    weight = P(None, "row", "col")
    bias = P(None, "col")
    state = P(None, None, "col", None)
    chan = P(None, None, "col")
    in_specs = (
        tokens, P(("dp", "row")), tokens, P(), P(), weight, weight, weight, bias, bias, bias,
        state, chan, state, state, chan, weight, bias, P(None, "col", "row"), P(),
    )
    out_specs = (
        tokens, tokens, P(), P(), weight, weight, weight, bias, bias, bias,
        state, chan, state, state, chan, weight, bias, P(None, "col", "row"), P(),
    )
    return jax.shard_map(body, mesh=mesh, in_specs=in_specs, out_specs=out_specs, check_vma=False)
```

```python
import functools

import jax
import jax.numpy as jnp
import numpy as np
from jax import lax
from jax.experimental import pallas as pl
from jax.experimental.pallas import tpu as pltpu
from jax.sharding import PartitionSpec as P

LAYERS = 2
EPS = 1e-05
LAG = 64
BF = jnp.bfloat16
F32 = jnp.float32
MESH = pl.DeviceIdType.MESH
VMEM_LIMIT = 60 * 1024 * 1024


def transform_matrix(length):
    k = np.arange(length)[:, None]
    t = np.arange(length)[None, :]
    angle = np.pi * (((2 * k + 1) * t) % (4 * length)) / (2 * length)
    return np.concatenate((np.cos(angle), -np.sin(angle)), axis=0)


def gelu_only(v):
    t = jnp.tanh(v * (0.7978845608 + 0.035677408 * v * v))
    return (0.5 * v) * (1.0 + t)


def gelu_parts(v):
    sq = v * v
    t = jnp.tanh(v * (0.7978845608 + 0.035677408 * sq))
    half = 0.5 + 0.5 * t
    slope = half + (v * half) * (1.0 - t) * (0.7978845608 + 0.107032225 * sq)
    return v * half, slope


def dot(a, b, ca, cb):
    return lax.dot_general(a, b, (((ca,), (cb,)), ((), ())), preferred_element_type=F32)


def over_rows(rows, step, work):
    def one(i, unused):
        work(pl.ds(pl.multiple_of(i * step, step), step))
        return unused

    lax.fori_loop(0, rows // step, one, 0)


def lane_sums(x):
    total = x[:, :128]
    for i in range(1, x.shape[1] // 128):
        total = total + x[:, 128 * i : 128 * (i + 1)]
    return total


def as_row(partial):
    return lax.dot_general(
        jnp.ones((8, 128), F32), partial, (((1,), (1,)), ((), ())), precision=lax.Precision.HIGHEST,
        preferred_element_type=F32,
    )


class Place:
    def __init__(self, n, m):
        self.n = n
        self.m = m
        self.d = lax.axis_index("dp")
        self.c = lax.axis_index("col")
        self.r = lax.axis_index("row")

    def greet(self):
        barrier = pltpu.get_barrier_semaphore()

        def hail(device):
            pl.semaphore_signal(barrier, inc=1, device_id=device, device_id_type=MESH)

        for k in range(1, self.n):
            hail({"dp": self.ahead(k)})
        hail({"col": 1 - self.c})

        def one(j, unused):
            hail({"row": self.up(j)})
            return unused

        lax.fori_loop(1, self.m, one, 0)
        pl.semaphore_wait(barrier, self.n + self.m - 1)

    def ahead(self, k):
        return lax.rem(self.d + k, self.n)

    def behind(self, k):
        return lax.rem(self.d - k + self.n, self.n)

    def near(self, k):
        return lax.rem(self.d + k, 2) + 2 * lax.rem(self.d // 2 + k // 2, 2)

    def apart(self, e):
        return lax.rem(self.d + e, 2) + 2 * lax.rem(self.d // 2 + e // 2, 2)

    def up(self, j):
        return lax.rem(self.r + j, self.m)

    def down(self, j):
        return lax.rem(self.r - j + self.m, self.m)

    def other(self, i):
        return i + (i + self.n - self.d) // self.n

    def to_dp(self, src, dst, send, recv, q):
        return pltpu.make_async_remote_copy(
            src, dst, send, recv, device_id={"dp": q}, device_id_type=MESH
        )

    def to_mate(self, src, dst, send, recv):
        return pltpu.make_async_remote_copy(
            src, dst, send, recv, device_id={"col": 1 - self.c}, device_id_type=MESH
        )

    def to_row(self, src, dst, send, recv, q):
        return pltpu.make_async_remote_copy(
            src, dst, send, recv, device_id={"row": q}, device_id_type=MESH
        )


class RowSum:
    def __init__(self, place, part, got, send, recv, hand=None):
        self.place, self.part, self.got, self.send, self.recv, self.hand = place, part, got, send, recv, hand
        self.line = place.m == 4 and hand is not None

    def copy(self, j):
        q = self.place.up(j)
        return self.place.to_row(self.part.at[q], self.got.at[j - 1], self.send.at[j], self.recv.at[j], q)

    def give(self):
        r = self.place.r
        return self.place.to_row(self.part.at[3 - r], self.hand, self.send.at[0], self.recv.at[0], 1 + r // 3)

    def sum_on(self):
        q = self.place.up(2)
        return self.place.to_row(self.hand, self.got.at[1], self.send.at[2], self.recv.at[2], q)

    def outer(self):
        return 1 + 2 * lax.rem(self.place.r, 2)

    def by_place(self, end, middle):
        r = self.place.r
        pl.when(r * (3 - r) == 0)(end)
        pl.when(r * (3 - r) > 0)(middle)

    def each(self, act):
        def one(j, unused):
            act(self.copy(j))
            return unused

        lax.fori_loop(1, self.place.m, one, 0)

    def start(self):
        if not self.line:
            self.each(lambda copy: copy.start())
            return

        def end():
            self.give().start()
            self.got[lax.rem(self.place.r, 2) * 2] = jnp.zeros(self.got.shape[1:], self.got.dtype)

        def middle():
            self.copy(1).start()
            self.copy(3).start()

        self.by_place(end, middle)

    def second(self):
        if self.line:

            def middle():
                self.give().wait_recv()
                mine = self.part[self.place.up(2)].astype(F32)
                self.hand[...] = (self.hand[...].astype(F32) + mine).astype(BF)
                self.sum_on().start()

            def end():
                self.copy(2).start()
                self.copy(self.outer()).start()

            self.by_place(end, middle)

    def total(self):
        if self.line:
            self.copy(2).wait_recv()
            pl.when(self.place.r > 0)(lambda: self.copy(1).wait_recv())
            pl.when(self.place.r < 3)(lambda: self.copy(3).wait_recv())
        else:
            self.each(lambda copy: copy.wait_recv())
        total = self.part[self.place.r].astype(F32)
        if self.place.m <= 4:
            for j in range(1, self.place.m):
                total = total + self.got[j - 1].astype(F32)
            return total
        return lax.fori_loop(1, self.place.m, lambda j, t: t + self.got[j - 1].astype(F32), total)

    def finish(self):
        if not self.line:
            self.each(lambda copy: copy.wait_send())
            return

        def end():
            self.give().wait_send()
            self.copy(2).wait_send()
            self.copy(self.outer()).wait_send()

        def middle():
            self.copy(1).wait_send()
            self.copy(3).wait_send()
            self.sum_on().wait_send()

        self.by_place(end, middle)


class Tokens:
    def __init__(self, place, buf, rows, length, sems):
        self.place, self.buf, self.rows, self.length = place, buf, rows, length
        self.send_p, self.recv_p, self.send_h, self.recv_h, self.send_m, self.recv_m = sems

    def region(self, slot, half=None):
        rows = self.rows // 2 if half is not None else self.rows
        start = slot * self.length + self.place.c * self.rows + (half or 0) * rows
        return self.buf.at[pl.ds(pl.multiple_of(start, rows), rows)]

    def peer(self, i):
        own = self.region(self.place.d)
        return self.place.to_dp(own, own, self.send_p.at[i], self.recv_p.at[i], self.place.near(i))

    def hop(self, i):
        part = self.region(self.place.near(3 - i), i - 1)
        return self.place.to_dp(part, part, self.send_h.at[i], self.recv_h.at[i], self.place.near(i))

    def mate(self, k):
        part = self.region(self.place.near(k))
        return self.place.to_mate(part, part, self.send_m.at[k], self.recv_m.at[k])

    def start(self):
        self.peer(1).start()
        self.peer(2).start()
        self.mate(0).start()

    def own(self):
        self.mate(0).wait_recv()

    def pass_on(self):
        for i in (1, 2):
            self.peer(i).wait_recv()
            self.hop(3 - i).start()
            self.mate(i).start()

    def fetch(self, k):
        @pl.when(k == 3)
        def _():
            self.hop(1).wait_recv()
            self.hop(2).wait_recv()
            self.mate(3).start()

        self.mate(k).wait_recv()

    def finish(self):
        for i in (1, 2):
            self.peer(i).wait_send()
            self.hop(i).wait_send()
        for k in range(4):
            self.mate(k).wait_send()


def norm_stats(residual):
    mean = jnp.mean(residual, axis=1, keepdims=True)
    centered = residual - mean
    variance = jnp.mean(centered * centered, axis=1, keepdims=True)
    inv = lax.rsqrt(variance + EPS)
    return centered * inv, inv


def sum_to_owner(place, rows, mate_out, mate_in, sum_out, sum_in, own, send_m, recv_m, send_p, recv_p):
    def to_mate(slot):
        return place.to_mate(mate_out.at[slot], mate_in.at[slot], send_m.at[slot], recv_m.at[slot])

    def to_owner(slot):
        k = lax.rem(slot - place.d + place.n, place.n)
        return place.to_dp(sum_out.at[slot], sum_in.at[k - 1], send_p.at[k], recv_p.at[k], slot)

    def close(slot, mine):
        to_mate(slot).wait_recv()

        own[mine] = own[mine] + mate_in[slot].astype(F32)

        @pl.when(slot != place.d)
        def _():
            sum_out[slot] = own[mine].astype(BF)
            to_owner(slot).start()

    def receive():
        def one(k, unused):
            to_owner(place.ahead(k)).wait_recv()
            return unused

        lax.fori_loop(1, place.n, one, 0)

    def finish():
        def one(k, unused):
            to_owner(place.ahead(k)).wait_send()
            return unused

        lax.fori_loop(1, place.n, one, 0)

        def two(s, unused):
            to_mate(s).wait_send()
            return unused

        lax.fori_loop(0, place.n, two, 0)

    return to_mate, close, receive, finish


class RowGather:
    def __init__(self, place, shard, land, send, recv):
        self.place, self.shard, self.land, self.send, self.recv = place, shard, land, send, recv
        self.line = place.m == 4

    def copy(self, j):
        place = self.place
        return place.to_row(self.shard, self.land.at[place.r], self.send.at[j], self.recv.at[j], place.up(j))

    def hop(self):
        place = self.place
        part = self.land.at[place.up(2)]
        return place.to_row(
            part, part, self.send.at[0], self.recv.at[self.inner()], lax.rem(3 * place.r + 1, place.m)
        )

    def outer(self):
        return 1 + 2 * lax.rem(self.place.r, 2)

    def inner(self):
        return lax.rem(2 * self.place.r + 3, self.place.m)

    def in_middle(self, act):
        r = self.place.r
        pl.when(r * (3 - r) > 0)(act)

    def each(self, act):
        def one(j, unused):
            act(self.copy(j))
            return unused

        lax.fori_loop(1, self.place.m, one, 0)

    def direct(self):
        self.line = False
        self.first()

    def first(self):
        if self.line:
            self.copy(2).start()
            self.copy(self.outer()).start()
        else:
            self.each(lambda copy: copy.start())
        self.land[self.place.r] = self.shard[...]

    def second(self):
        if self.line:
            self.copy(2).wait_recv()

            def act():
                self.hop().start()
                self.copy(self.inner()).start()

            self.in_middle(act)

    def whole(self):
        if self.line:
            self.copy(1).wait_recv()
            self.copy(3).wait_recv()
        else:
            self.each(lambda copy: copy.wait_recv())
        m, rows, lanes = self.land.shape
        return self.land[...].astype(F32).reshape(m * rows, lanes)

    def finish(self):
        if self.line:
            self.copy(2).wait_send()
            self.copy(self.outer()).wait_send()

            def act():
                self.hop().wait_send()
                self.copy(self.inner()).wait_send()

            self.in_middle(act)
        else:
            self.each(lambda copy: copy.wait_send())


def kernel_spectrum(decay, step, b_in, c_out, skip, sign, ft_ref, rate, lead):
    length = ft_ref.shape[0]
    blocks = length // LAG
    rate[...] = jnp.exp(step) * jnp.exp(decay)
    weight = (1.0 - jnp.exp(-rate[...])) * jnp.exp(-decay) * b_in * c_out
    for b in range(blocks):
        lead[b] = weight * jnp.exp(-(LAG * b) * rate[...])
    lanes = rate.shape[1]
    offs = lax.broadcasted_iota(jnp.int32, (LAG, lanes), 0).astype(F32)

    def state(i, totals):
        powers = jnp.exp(-offs * rate[pl.ds(i, 1)])
        return tuple(totals[b] + powers * lead[b, pl.ds(i, 1)] for b in range(blocks))

    zero = jnp.zeros((LAG, lanes), F32)
    totals = list(lax.fori_loop(0, rate.shape[0], state, (zero,) * blocks, unroll=2))
    at_zero = lax.broadcasted_iota(jnp.int32, (LAG, lanes), 0) == 0
    totals[0] = totals[0] + jnp.where(at_zero, skip, 0.0)
    kernel = jnp.concatenate(totals, axis=0)
    k_hat = dot(kernel.T.astype(BF), ft_ref[...], 1, 0) * (1.0 / length)
    return k_hat[:, :length], k_hat[:, length:] * sign


def direction_sign(ch, rows, lanes, start=0):
    at = lax.broadcasted_iota(jnp.int32, (rows, lanes), 0) + start
    return jnp.where(at < ch, 1.0, -1.0)


def fwd_kernel(
    n, m, layer, res_ref, gain_ref, shift_ref, own_live_ref, own_mask_ref, sh_v, sh_mx, sh_out, in_bias_ref,
    mix_bias_ref, out_bias_ref, ft_ref, f_ref, *rest
):
    first = layer == 0
    if first:
        sh_fb, sh_next, *rest = rest
        tables, next_tables, rest = rest[:4], rest[4:8], rest[8:]
    else:
        w_fb_ref, kre_ref, kim_ref, *rest = rest
    new_ref, g_out, mx_out, pre_out, u_out, y_out, pm_out, prod_out, w_in_out, w_mx_out, w_out_out, *rest = rest
    if first:
        next_out, mask_ref, kre_ref, kim_ref, kre_next, kim_next, *rest = rest
    else:
        mask_ref = own_live_ref
    (
        w_in_t, w_mx_t, g, mx, pre, u_sp, y, pm, prod, act, spec, y_hat, prod_f, prod_t,
        rate, lead, land_v, land_mx, land_out, w_out_t,
        own, mate_out, mate_in, sum_out, sum_in,
        send_a, recv_a, send_ah, recv_ah, send_am, recv_am, send_b, recv_b, send_bh, recv_bh, send_bm, recv_bm,
        send_c, recv_c, send_cm, recv_cm, save,
        send_gv, recv_gv, send_gm, recv_gm, send_go, recv_go, *rest,
    ) = rest
    place = Place(n, m)
    d, c = place.d, place.c
    rows, width = res_ref.shape
    length = ft_ref.shape[0]
    hid = sh_mx.shape[1]
    ch2 = kre_ref.shape[0]
    ch = ch2 // 2
    gain, shift, out_bias = (ref[layer : layer + 1] for ref in (gain_ref, shift_ref, out_bias_ref))

    place.greet()
    gather_v = RowGather(place, sh_v, land_v, send_gv, recv_gv)
    gather_mx = RowGather(place, sh_mx, land_mx, send_gm, recv_gm)
    gather_out = RowGather(place, sh_out, land_out, send_go, recv_go)
    later_weights = (gather_mx, gather_v, gather_out)
    gather_a = Tokens(place, g, rows, length, (send_a, recv_a, send_ah, recv_ah, send_am, recv_am))
    if first:
        land_fb, land_next, send_gi, recv_gi, send_gn, recv_gn, send_mk, recv_mk = rest
        gather_fb = RowGather(place, sh_fb, land_fb, send_gi, recv_gi)
        gather_next = RowGather(place, sh_next, land_next, send_gn, recv_gn)
        gather_fb.direct()

        def mask_peer(k):
            return place.to_dp(
                own_live_ref, mask_ref.at[d], send_mk.at[k], recv_mk.at[k], place.ahead(k)
            )

        for k in range(1, n):
            mask_peer(k).start()
        mask_ref[d] = own_live_ref[...]
    else:
        gather_mx.first()
    base = d * length + c * rows
    xhat, _ = norm_stats(res_ref[...].astype(F32))
    g[pl.ds(pl.multiple_of(base, rows), rows)] = (xhat * gain + shift).astype(BF)
    gather_a.start()

    def spectra(given, re_ref, im_ref):
        decay_ref, b_ref, c_ref, row_ref = given
        for j in range(ch2 // 128):
            at = slice(128 * j, 128 * (j + 1))
            re_ref[at], im_ref[at] = kernel_spectrum(
                decay_ref[:, at], row_ref[0:1, at], b_ref[:, at], c_ref[:, at], row_ref[1:2, at],
                direction_sign(ch, 128, length, 128 * j), ft_ref, rate, lead,
            )

    if first:
        spectra(tables, kre_ref, kim_ref)
    if first:
        w_fb = gather_fb.whole()
        gather_mx.first()
        for k in range(1, n):
            mask_peer(k).wait_recv()
    else:
        w_fb = w_fb_ref[...].astype(F32)
    w_in_out[:, :ch2] = w_fb.astype(BF)
    w_in_t[:ch2] = w_fb.T.astype(BF)
    gather_a.own()

    def chunk(owner, slot):
        at = pl.ds(pl.multiple_of((c * n + owner) * ch, ch), ch)
        return mx.at[at, pl.ds(pl.multiple_of(slot * length, length), length)]

    def turn(k, j):
        return place.near(k ^ j)

    def half_chunk(owner, slot, half):
        at = pl.ds(pl.multiple_of((c * n + owner) * ch + half * (ch // 2), ch // 2), ch // 2)
        return mx.at[at, pl.ds(pl.multiple_of(slot * length, length), length)]

    def peer_b(i, j):
        part = chunk(d, turn(0, j))
        return place.to_dp(part, part, send_b.at[j, i], recv_b.at[j, i], place.near(i))

    def hop_b(i, j):
        part = half_chunk(place.near(3 - i), turn(3 - i, j), i - 1)
        return place.to_dp(part, part, send_bh.at[j, i], recv_bh.at[j, i], place.near(i))

    def mate_b(k, j):
        part = chunk(place.near(k), turn(k, j))
        return place.to_mate(part, part, send_bm.at[j, k], recv_bm.at[j, k])

    def saves(slot, item):
        lanes = pl.ds(pl.multiple_of(slot * length, length), length)
        src, dst = (
            lambda: (g.at[lanes], g_out.at[lanes]),
            lambda: (u_sp.at[slot], u_out.at[slot]),
            lambda: (y.at[slot], y_out.at[slot]),
            lambda: (pre.at[slot], pre_out.at[slot]),
            lambda: (mx.at[:, lanes], mx_out.at[:, lanes]),
            lambda: (pm.at[slot], pm_out.at[slot]),
            lambda: (prod.at[:, lanes], prod_out.at[:, lanes]),
        )[item]()
        return pltpu.make_async_copy(src, dst, save.at[item, slot])

    def scan_slot(i, unused):
        slot = place.near(i)

        @pl.when(i == 1)
        def _():
            gather_a.pass_on()

        @pl.when(i > 0)
        def _():
            gather_a.fetch(i)

        @pl.when(i == (n - 1 if first else n - 2))
        def _():
            gather_mx.second()
            gather_v.first()

        lanes = pl.ds(pl.multiple_of(slot * length, length), length)
        live = mask_ref[slot, 0:1]
        v = dot(w_in_t[:ch2], g[lanes], 1, 1) + in_bias_ref[:ch2]
        pre[slot, :ch2] = v
        act[...] = (gelu_only(v) * live).astype(BF)
        spec[...] = dot(act[...], ft_ref[...], 1, 0)
        u_re, u_im = spec[:, :length], spec[:, length:]
        k_re, k_im = kre_ref[...], kim_ref[...]
        u_sp[slot, :, :length] = u_re.astype(BF)
        u_sp[slot, :, length:] = u_im.astype(BF)
        y_hat[:, :length] = (k_re * u_re - k_im * u_im).astype(BF)
        y_hat[:, length:] = (k_re * u_im + k_im * u_re).astype(BF)
        both = dot(y_hat[...], f_ref[...], 1, 0)
        y[slot] = both.astype(BF)
        mine = pl.ds(pl.multiple_of((c * n + d) * ch, ch), ch)
        mx[mine, lanes] = (both[:ch] * both[ch:]).astype(BF)
        for j in range(n):

            @pl.when(i == j)
            def _():
                peer_b(1, j).start()
                peer_b(2, j).start()
                mate_b(0, j).start()

        for item in range(3):
            saves(slot, item).start()
        return unused

    lax.fori_loop(0, n, scan_slot, 0)
    if first:
        spectra(next_tables, kre_next, kim_next)
    w_mx = gather_mx.whole()
    w_mx_out[...] = w_mx.astype(BF)
    for block in range(2 * n):
        w_mx_t[block] = w_mx[block * ch : (block + 1) * ch].T.astype(BF)
    begun = set()

    def mix_in(k, j):
        owner, slot = place.near(k), turn(k, j)
        lanes = pl.ds(pl.multiple_of(slot * length, length), length)
        mate_b(k, j).wait_recv()
        total = None
        for side in range(2):
            rows_at = pl.ds(pl.multiple_of((side * n + owner) * ch, ch), ch)
            part = dot(w_mx_t[side * n + owner], mx[rows_at, lanes], 1, 0)
            total = part if total is None else total + part
        pm[slot] = (pm[slot] if k ^ j in begun else mix_bias_ref[...]) + total
        begun.add(k ^ j)

    def across(j):
        hop_b(1, j).wait_recv()
        hop_b(2, j).wait_recv()
        mate_b(3, j).start()
        mix_in(3, j)

    for j in range(n):
        for i in (1, 2):
            peer_b(i, j).wait_recv()
            hop_b(3 - i, j).start()
            mate_b(i, j).start()
        for k in range(3):
            mix_in(k, j)
        if j == 0:
            gather_v.second()
            gather_out.first()
        if j == 2:
            gather_out.second()
            if first:
                gather_next.first()
        if j > 0:
            across(j - 1)
    across(n - 1)
    w_v = gather_v.whole()
    w_in_out[:, ch2:] = w_v.astype(BF)
    w_in_t[ch2:] = w_v.T.astype(BF)
    w_out = gather_out.whole()
    w_out_t[...] = w_out.astype(BF)
    w_out_out[...] = w_out.T.astype(BF)

    to_mate, close, receive, finish_c = sum_to_owner(
        place, rows, mate_out, mate_in, sum_out, sum_in, own, send_cm, recv_cm, send_c, recv_c
    )

    def order(i):
        return lax.select(i == n - 1, d, place.other(i))

    def hidden_slot(i, unused):
        slot = order(i)
        lanes = pl.ds(pl.multiple_of(slot * length, length), length)
        v = pm[slot]
        value = dot(w_in_t[ch2:], g[lanes], 1, 1) + in_bias_ref[ch2:]
        pre[slot, ch2:] = value
        product = gelu_only(v) * gelu_only(value)
        prod_f[...] = product
        prod[:, lanes] = product.astype(BF)
        prod_t[...] = prod_f[...].T.astype(BF)
        for item in range(3, 7):
            saves(slot, item).start()
        theirs = pl.ds(pl.multiple_of((1 - c) * rows, rows), rows)
        ours = pl.ds(pl.multiple_of(c * rows, rows), rows)
        mate_out[slot] = dot(prod_t[theirs], w_out_t[...], 1, 1).astype(BF)
        to_mate(slot).start()

        @pl.when(i > 0)
        def _():
            close(order(i - 1), lax.rem(i - 1, 2))

        own[lax.rem(i, 2)] = dot(prod_t[ours], w_out_t[...], 1, 1)
        return unused

    lax.fori_loop(0, n, hidden_slot, 0)
    if first:
        gather_next.second()
    last = (n - 1) % 2
    close(d, last)
    receive()

    total = own[last]
    for k in range(1, n):
        total = total + sum_in[k - 1].astype(F32)
    new_ref[...] = res_ref[...].astype(F32) + own_mask_ref[...] * (total + out_bias)
    gather_a.finish()
    finish_c()
    for gather in later_weights:
        gather.finish()
    if first:
        next_out[...] = gather_next.whole().astype(BF)
        gather_next.finish()
        gather_fb.finish()
        for k in range(1, n):
            mask_peer(k).wait_send()

    for j in range(n):
        for i in (1, 2):
            peer_b(i, j).wait_send()
            hop_b(i, j).wait_send()
        for k in range(n):
            mate_b(k, j).wait_send()

    def drain(slot, unused):
        for item in range(7):
            saves(slot, item).wait()
        return unused

    lax.fori_loop(0, n, drain, 0)


def bwd_kernel(
    n, m, layer, later, grad_ref, res_ref, gain_ref, mask_ref, own_mask_ref, w_in_ref, w_mx_ref, w_out_ref, kre_ref,
    kim_ref, ft_ref, f_ref, g_in, mx_in, pre_in, u_in, y_in, pm_in, prod_in, *rest
):
    if later:
        late_part, red_mx1, red_out1, *rest = rest
    (new_ref, gw_in_ref, red_mx_ref, red_out_ref, in_row_ref, mix_row_ref, norm_sum_ref, dk_ref, *rest) = rest
    if later:
        red_late_ref, all_mx, all_out, *rest = rest
    (
        gb, g, mx, pre, u_sp, y, pm, prod, gpre, gpre_f, gpm, spec, hat, turned,
        mix_sum, mix_mate, mix_own, mix_got, in_sum, mix_acc, part_mx, got_mx, hand_mx, part_out, got_out, hand_out,
        own, mate_out, mate_in, sum_out, sum_in,
        send_a, recv_a, send_ah, recv_ah, send_am, recv_am, send_b, recv_b, send_bm, recv_bm, send_c, recv_c, send_cm, recv_cm, load,
        send_rm, recv_rm, send_ro, recv_ro, *rest,
    ) = rest
    place = Place(n, m)
    d, c = place.d, place.c
    rows, width = res_ref.shape
    length = ft_ref.shape[0]
    hid = w_mx_ref.shape[1]
    ch2 = kre_ref.shape[0]
    ch = ch2 // 2
    half = n * ch

    def loads(slot, item):
        lanes = pl.ds(pl.multiple_of(slot * length, length), length)
        src, dst = (
            lambda: (pre_in.at[slot], pre.at[slot]),
            lambda: (pm_in.at[slot], pm.at[slot]),
            lambda: (y_in.at[slot], y.at[slot]),
            lambda: (u_in.at[slot], u_sp.at[slot]),
            lambda: (prod_in.at[:, lanes], prod.at[:, lanes]),
            lambda: (mx_in.at[:, lanes], mx.at[:, lanes]),
            lambda: (g_in.at[lanes], g.at[lanes]),
        )[item]()
        return pltpu.make_async_copy(src, dst, load.at[item, slot])

    for item in range(7):
        loads(d, item).start()

    def start_loads(i, unused):
        for item in range(7):
            loads(place.other(i), item).start()
        return unused

    lax.fori_loop(0, n - 1, start_loads, 0)

    place.greet()
    gather_a = Tokens(place, gb, rows, length, (send_a, recv_a, send_ah, recv_ah, send_am, recv_am))
    base = d * length + c * rows
    gain = gain_ref[layer : layer + 1]
    first = grad_ref[...].astype(F32) * own_mask_ref[...]
    gb[pl.ds(pl.multiple_of(base, rows), rows)] = first.astype(BF)
    gather_a.start()
    sum_mx = RowSum(place, part_mx, got_mx, send_rm, recv_rm, hand_mx)
    sum_out_w = RowSum(place, part_out, got_out, send_ro, recv_ro, hand_out)
    row_sums = [sum_mx, sum_out_w]
    if later:
        got_late, hand_late, send_rl, recv_rl, *sems = rest
        sum_late = RowSum(place, late_part, got_late, send_rl, recv_rl, hand_late)
        sum_late.start()
        row_sums.append(sum_late)
    norm_sum_ref[...] = jnp.zeros_like(norm_sum_ref)
    norm_sum_ref[2:3] = jnp.sum(first, axis=0, keepdims=True)
    in_sum[...] = jnp.zeros_like(in_sum)
    mix_acc[...] = jnp.zeros_like(mix_acc)
    dk_ref[...] = jnp.zeros_like(dk_ref)
    gather_a.own()

    def mate_b(slot):
        return place.to_mate(mix_sum.at[slot], mix_mate.at[slot], send_bm.at[slot], recv_bm.at[slot])

    def peer_b(k, slot):
        q = place.ahead(k)
        part = mix_sum.at[slot, pl.ds(pl.multiple_of(q * ch, ch), ch)]
        return place.to_dp(part, mix_got.at[k - 1, slot], send_b.at[slot, k], recv_b.at[slot, k], q)

    def hidden_slot(i, unused):
        slot = lax.select(i == 0, d, place.other(i - 1))

        @pl.when(i == 1)
        def _():
            gather_a.pass_on()

        @pl.when(i > 0)
        def _():
            gather_a.fetch(place.apart(slot))

        if later:
            pl.when(i == n - 2)(sum_late.second)


        lanes = pl.ds(pl.multiple_of(slot * length, length), length)
        mix_own[:hid] = dot(w_out_ref[...], gb[lanes], 1, 1)
        for item in range(2):
            loads(slot, item).wait()
        gated, slope = gelu_parts(pm[slot])
        value, value_slope = gelu_parts(pre[slot, ch2:])
        now = mix_own[:hid]
        to_value = now * gated * value_slope
        to_mix = now * value * slope
        gpre[ch2:, lanes] = to_value.astype(BF)
        gpm[:, lanes] = to_mix.astype(BF)
        in_sum[ch2:] = in_sum[ch2:] + lane_sums(to_value)
        mix_acc[...] = mix_acc[...] + lane_sums(to_mix)
        theirs = pl.ds(pl.multiple_of((1 - c) * half, half), half)
        ours = pl.ds(pl.multiple_of(c * half, half), half)
        mix_sum[slot] = dot(w_mx_ref[theirs], gpm[:, lanes], 1, 0).astype(BF)
        mate_b(slot).start()
        mix_own[...] = dot(w_mx_ref[ours], gpm[:, lanes], 1, 0)
        mate_b(slot).wait()
        mix_sum[slot] = (mix_own[...] + mix_mate[slot].astype(F32)).astype(BF)
        for k in range(1, n):
            peer_b(k, slot).start()
        return unused

    lax.fori_loop(0, n, hidden_slot, 0)

    def wait_loads(slot, unused):
        for item in range(2, 7):
            loads(slot, item).wait()
        return unused

    lax.fori_loop(0, n, wait_loads, 0)
    share = mx.shape[0] // m

    def grad_mix(q, unused):
        part_mx[q] = dot(mx[pl.ds(pl.multiple_of(q * share, share), share)], gpm[...], 1, 1).astype(BF)
        return unused

    lax.fori_loop(0, m, grad_mix, 0)
    sum_mx.start()
    gw_out = dot(prod[...], gb[...], 1, 0).T
    part_out[...] = gw_out.reshape(m, width // m, hid).astype(BF)
    sum_out_w.start()
    spreads = []
    if later:
        spreads = [
            Spread(place, red_mx1, all_mx, sems, 0),
            Spread(place, red_out1, all_out, sems, 1),
        ]

    to_mate, close, receive, finish_c = sum_to_owner(
        place, rows, mate_out, mate_in, sum_out, sum_in, own, send_cm, recv_cm, send_c, recv_c
    )

    def order(i):
        return lax.select(i == n - 1, d, place.other(i))

    def scan_slot(i, unused):
        slot = order(i)
        lanes = pl.ds(pl.multiple_of(slot * length, length), length)
        for k in range(1, n):
            peer_b(k, slot).wait_recv()

        @pl.when(i == n - 2)
        def _():
            for each in spreads:
                each.start()

        @pl.when(i == n - 2)
        def _():
            sum_mx.second()
            sum_out_w.second()

        total = mix_sum[slot, pl.ds(pl.multiple_of(d * ch, ch), ch)].astype(F32)
        for k in range(1, n):
            total = total + mix_got[k - 1, slot].astype(F32)
        hat[:ch, :length] = (total * y[slot, ch:].astype(F32)).astype(BF)
        hat[ch:, :length] = (total * y[slot, :ch].astype(F32)).astype(BF)
        spec[...] = dot(hat[:, :length], ft_ref[...], 1, 0)
        g_re, g_im = spec[:, :length], spec[:, length:]
        k_re, k_im = kre_ref[...], kim_ref[...]
        hat[:, :length] = (k_re * g_re + k_im * g_im).astype(BF)
        hat[:, length:] = (k_re * g_im - k_im * g_re).astype(BF)
        u_re, u_im = u_sp[slot, :, :length].astype(F32), u_sp[slot, :, length:].astype(F32)
        dk_ref[:, :length] = dk_ref[:, :length] + (u_re * g_re + u_im * g_im)
        dk_ref[:, length:] = dk_ref[:, length:] + (u_re * g_im - u_im * g_re)
        spec[:, :length] = dot(hat[...], f_ref[...], 1, 0)
        live = mask_ref[slot, 0:1]
        _, slope = gelu_parts(pre[slot, :ch2])
        part = spec[:, :length] * slope * live
        gpre_f[...] = part
        gpre[:ch2, lanes] = part.astype(BF)
        in_sum[:ch2] = in_sum[:ch2] + lane_sums(part)
        turned[:, :ch2] = gpre_f[...].T.astype(BF)
        gpre_f[...] = gpre[ch2:, lanes].astype(F32)
        turned[:, ch2:] = gpre_f[...].T.astype(BF)
        theirs = pl.ds(pl.multiple_of((1 - c) * rows, rows), rows)
        ours = pl.ds(pl.multiple_of(c * rows, rows), rows)
        mate_out[slot] = dot(turned[theirs], w_in_ref[...], 1, 1).astype(BF)
        to_mate(slot).start()

        @pl.when(i > 0)
        def _():
            close(order(i - 1), lax.rem(i - 1, 2))

        own[lax.rem(i, 2)] = dot(turned[ours], w_in_ref[...], 1, 1)
        return unused

    lax.fori_loop(0, n, scan_slot, 0)
    last = (n - 1) % 2
    close(d, last)

    def grad_in(r):
        part = dot(gpre[r], g[...], 1, 0).T
        gw_in_ref[:, :, r] = part.reshape(m, width // m, part.shape[1]).astype(BF)

    over_rows(gpre.shape[0], 128, grad_in)
    for each in spreads:
        each.pass_on()
    in_row_ref[...] = as_row(in_sum[...])
    mix_row_ref[...] = as_row(mix_acc[...])
    if later:
        red_late_ref[...] = sum_late.total().astype(BF)
    receive()
    total = own[last]
    for k in range(1, n):
        total = total + sum_in[k - 1].astype(F32)
    xhat, inv = norm_stats(res_ref[...].astype(F32))
    h = total * gain
    middle = jnp.mean(h, axis=1, keepdims=True)
    along = jnp.mean(h * xhat, axis=1, keepdims=True)
    new_ref[...] = grad_ref[...].astype(F32) + inv * (h - middle - xhat * along)
    norm_sum_ref[0:1] = jnp.sum(total * xhat, axis=0, keepdims=True)
    norm_sum_ref[1:2] = jnp.sum(total, axis=0, keepdims=True)
    red_mx_ref[...] = sum_mx.total().astype(BF)
    red_out_ref[...] = sum_out_w.total().astype(BF)
    gather_a.finish()
    finish_c()
    for row_sum in row_sums:
        row_sum.finish()
    for each in spreads:
        each.wait()

    def drain(slot, unused):
        for k in range(1, n):
            peer_b(k, slot).wait_send()
        return unused

    lax.fori_loop(0, n, drain, 0)


class Spread:
    def __init__(self, place, src, out, sems, item):
        self.place, self.src, self.out, self.item = place, src, out, item
        self.send, self.recv, self.send_h, self.recv_h, self.keep = sems
        rows = src.shape[0]
        whole = len(src.shape) == 2 and rows % 32 != 0
        half = rows if whole else rows // 2
        self.pieces = [(i, start, half) for i, start in ((1, 0), (2, half)) if start < rows]

    def peer(self, i):
        place, item = self.place, self.item
        return place.to_dp(
            self.src, self.out.at[place.d], self.send.at[item, i], self.recv.at[item, i], place.near(i)
        )

    def hop(self, i, start, count):
        place, item = self.place, self.item
        part = self.out.at[place.near(3 - i), pl.ds(start, count)]
        return place.to_dp(part, part, self.send_h.at[item, i], self.recv_h.at[item, i], place.near(i))

    def local(self):
        return pltpu.make_async_copy(self.src, self.out.at[self.place.d], self.keep.at[self.item])

    def start(self):
        self.peer(1).start()
        self.peer(2).start()
        self.local().start()

    def pass_on(self):
        self.peer(1).wait_recv()
        self.peer(2).wait_recv()
        for piece in self.pieces:
            self.hop(*piece).start()

    def wait(self):
        for piece in self.pieces:
            self.hop(*piece).wait()
        self.peer(1).wait_send()
        self.peer(2).wait_send()
        self.local().wait()


def state_grads(dk_re, dk_im, sign, ft_ref, decay, step, b_in, c_out, lag_sums):
    length = ft_ref.shape[0]
    re = dk_re.astype(BF)
    im = (dk_im * sign).astype(BF)
    lag_sums[...] = (dot(ft_ref[:, :length], re, 1, 1) + dot(ft_ref[:, length:], im, 1, 1)) * (1.0 / length)
    rate = jnp.exp(step) * jnp.exp(decay)
    a = jnp.exp(-rate)

    totals, slopes = [], []
    for lanes in (slice(0, 256), slice(256, a.shape[1])):
        base = a[:, lanes]

        def lag(i, carry, base=base, lanes=lanes):
            total, slope = carry
            row = lag_sums[pl.ds(length - 1 - i, 1)][:, lanes]
            return total * base + row, slope * base + total

        zero = jnp.zeros_like(base)
        total, slope = lax.fori_loop(0, length, lag, (zero, zero), unroll=4)
        totals.append(total)
        slopes.append(slope)
    total, slope = jnp.concatenate(totals, axis=1), jnp.concatenate(slopes, axis=1)
    inv_decay = jnp.exp(-decay)
    gain = (1.0 - a) * inv_decay
    b_disc = gain * b_in
    to_b = c_out * total
    to_rate = a * (to_b * inv_decay * b_in - (c_out * b_disc) * slope)
    through = to_rate * rate
    return (
        through - to_b * b_disc, to_b * gain, b_disc * total,
        jnp.sum(through, axis=0, keepdims=True), lag_sums[0:1],
    )


def finish_kernel(
    n, m, part_in, late_in, red_mx0, red_out0, dk0, dk1, in0, in1, mix0, mix1, norm0, norm1,
    decay0, b0, c0, row0, decay1, b1, c1, row1, ft_ref,
    all_in1, all_mx0, all_out0, all_in0, all_states, all_small, norm_ref,
    got_in, hand_in, red_in0, states, part_s, got_s, red_s, full_s, lag_sums, small, row_small, dp_small, norm_own, norm_got,
    send_w, recv_w, send_wh, recv_wh, keep_w, send_ri, recv_ri, send_rs, recv_rs, send_gs, recv_gs, send_sm, recv_sm,
    send_ds, recv_ds, send_n, recv_n,
):
    place = Place(n, m)
    d, r = place.d, place.r
    states_n, ch2 = decay0.shape
    place.greet()
    sum_in = RowSum(place, part_in, got_in, send_ri, recv_ri, hand_in)
    sum_in.start()
    spreads = [
        Spread(place, src, out, (send_w, recv_w, send_wh, recv_wh, keep_w), item)
        for item, (src, out) in enumerate(
            ((late_in, all_in1), (red_mx0, all_mx0), (red_out0, all_out0), (red_in0, all_in0), (full_s, all_states))
        )
    ]
    for each in spreads[:3]:
        each.start()

    small[...] = jnp.zeros_like(small)
    for l, (in_row, mix_row, norm) in enumerate(((in0, mix0, norm0), (in1, mix1, norm1))):
        small[l, 0:1] = in_row[0:1]
        small[l, 1:2, :ch2] = mix_row[0:1]
        small[l, 3:6] = norm[0:3]
    length = ft_ref.shape[0]
    for l, (dk, decay, b_in, c_out, row) in enumerate(((dk0, decay0, b0, c0, row0), (dk1, decay1, b1, c1, row1))):
        grads = state_grads(
            dk[:, :length], dk[:, length:], direction_sign(ch2 // 2, ch2, length), ft_ref, decay[...], row[0:1],
            b_in[...], c_out[...], lag_sums,
        )
        for i in range(3):
            states[pl.ds((3 * l + i) * states_n, states_n)] = grads[i]
        small[l, 1:2, ch2:] = grads[3]
        small[l, 2:3, :ch2] = grads[4]
        if l == 0:
            sum_in.second()
    share = states.shape[0] // m
    for q in range(m):
        part_s[q] = states[q * share : (q + 1) * share].astype(BF)
    sum_s = RowSum(place, part_s, got_s, send_rs, recv_rs)
    sum_s.start()
    row_small[r] = small[...]

    def small_row(j):
        return place.to_row(row_small.at[r], row_small.at[r], send_sm.at[j], recv_sm.at[j], place.up(j))

    def repeat(work, count):
        def one(j, unused):
            work(j)
            return unused

        lax.fori_loop(1, count, one, 0)

    repeat(lambda j: small_row(j).start(), m)

    spreads[0].pass_on()
    spreads[1].pass_on()
    red_in0[...] = sum_in.total().astype(BF)
    spreads[3].start()
    spreads[2].pass_on()
    red_s[...] = sum_s.total().astype(BF)
    full_s[r] = red_s[...]

    def state_row(j):
        return place.to_row(full_s.at[r], full_s.at[r], send_gs.at[j], recv_gs.at[j], place.up(j))

    repeat(lambda j: state_row(j).start(), m)
    repeat(lambda j: small_row(j).wait_recv(), m)
    total = row_small[0]
    for q in range(1, m):
        total = total + row_small[q]
    dp_small[d] = total

    def small_dp(k):
        return place.to_dp(dp_small.at[d], dp_small.at[d], send_ds.at[k], recv_ds.at[k], place.ahead(k))

    for k in range(1, n):
        small_dp(k).start()
    repeat(lambda j: state_row(j).wait_recv(), m)

    spreads[4].start()
    spreads[3].pass_on()
    for k in range(1, n):
        small_dp(k).wait_recv()
    total = dp_small[0]
    for q in range(1, n):
        total = total + dp_small[q]
    norm_own[...] = total
    swap = place.to_mate(norm_own, norm_got, send_n, recv_n)
    swap.start()
    all_small[...] = dp_small[...]
    swap.wait_recv()
    norm_ref[...] = norm_own[...] + norm_got[...]
    swap.wait_send()
    spreads[4].pass_on()
    for each in spreads:
        each.wait()
    for k in range(1, n):
        small_dp(k).wait_send()
    repeat(lambda j: small_row(j).wait_send(), m)
    repeat(lambda j: state_row(j).wait_send(), m)
    sum_in.finish()
    sum_s.finish()


def prepare_kernel(
    n, lengths_ref, bias_fwd, bias_bwd, bias_value, bias_mix, step_ref, skip_ref, *rest
):
    d = lax.axis_index("dp")
    w_fwd, w_bwd, w_value, w_mix, w_out, decay, b_in, c_out, live_ref, mask_ref, *rest = rest
    per = 10
    outs = [rest[per * l : per * (l + 1)] for l in range(LAYERS)]
    win_f, win_b, win_v, win_m, win_o, win_d, win_i, win_c, load = rest[per * LAYERS :]
    ch = w_fwd.shape[2] // n
    hid = w_value.shape[2] // n
    size = win_f.shape[2]
    places = sorted({(k * ch) % 128 for k in range(n)})

    def window(width, wide):
        start = pl.multiple_of((d * width) // 128 * 128, 128)
        return pl.ds(start, wide)

    narrow, broad = window(ch, size), window(hid, hid)
    copies = [
        pltpu.make_async_copy(src.at[at], dst, load.at[i])
        for i, (src, at, dst) in enumerate((
            (w_fwd, (slice(None), slice(None), narrow), win_f), (w_bwd, (slice(None), slice(None), narrow), win_b),
            (decay, (slice(None), slice(None), slice(None), narrow), win_d),
            (b_in, (slice(None), slice(None), slice(None), narrow), win_i),
            (c_out, (slice(None), slice(None), slice(None), narrow), win_c),
            (w_value, (slice(None), slice(None), broad), win_v), (w_mix, (slice(None), slice(None), broad), win_m),
            (w_out, (slice(None), slice(None), broad), win_o),
        ))
    ]
    for copy in copies:
        copy.start()

    def pick(x):
        kept = x[..., places[0] : places[0] + ch]
        for place in places[1:]:
            kept = jnp.where(lax.rem(d * ch, 128) == place, x[..., place : place + ch], kept)
        return kept

    def cut(x, width):
        kept = x[:, :width]
        for k in range(1, n):
            kept = jnp.where(d == k, x[:, k * width : (k + 1) * width], kept)
        return kept

    def column(row):
        return jnp.broadcast_to(row, (8, row.shape[1])).T[:, :1]

    rows, length = mask_ref.shape[0], live_ref.shape[1]
    alive = lengths_ref[0]
    live_ref[...] = (lax.broadcasted_iota(jnp.int32, live_ref.shape, 1) < alive).astype(F32)
    at = lax.broadcasted_iota(jnp.int32, mask_ref.shape, 0) + lax.axis_index("col") * rows
    mask_ref[...] = (at < alive).astype(F32)
    for l in range(LAYERS):
        in_bias, mix_bias, row_ref = outs[l][4], outs[l][5], outs[l][9]
        one = slice(l, l + 1)
        in_bias[:ch] = column(cut(bias_fwd[one], ch))
        in_bias[ch : 2 * ch] = column(cut(bias_bwd[one], ch))
        in_bias[2 * ch :] = column(cut(bias_value[one], hid))
        mix_bias[...] = column(cut(bias_mix[one], hid))
        row_ref[...] = jnp.zeros_like(row_ref)
        for k in range(2):
            lanes = slice(k * ch, (k + 1) * ch)
            row_ref[0:1, lanes] = cut(step_ref[l, k : k + 1], ch)
            row_ref[1:2, lanes] = cut(skip_ref[l, k : k + 1], ch)
    for copy in copies:
        copy.wait()
    for l in range(LAYERS):
        fb_ref, v_ref, mx_ref, out_ref, _, _, decay_ref, b_ref, c_ref, _ = outs[l]
        fb_ref[:, :ch] = pick(win_f[l]).astype(BF)
        fb_ref[:, ch:] = pick(win_b[l]).astype(BF)
        v_ref[...] = win_v[l].astype(BF)
        mx_ref[...] = win_m[l].astype(BF)
        out_ref[...] = win_o[l].astype(BF)
        for k in range(2):
            lanes = slice(k * ch, (k + 1) * ch)
            decay_ref[:, lanes] = pick(win_d[l, k])
            b_ref[:, lanes] = pick(win_i[l, k])
            c_ref[:, lanes] = pick(win_c[l, k])


def assemble_kernel(
    n, in0, in1, mx0, mx1, out0, out1, states_ref, small_ref, norm_ref,
    gain, shift, wf, wb, wv, bf, bb, bv, decay, step, b_in, c_out, skip, wm, bm, wo, bo,
):
    l = pl.program_id(0)
    ch = wf.shape[2] // n
    hid = wv.shape[2] // n
    count = decay.shape[2]
    one = pl.ds(l, 1)
    for i, ref in ((3, gain), (4, shift), (5, bo)):
        ref[one] = norm_ref[one, i]
    for k in range(n):
        narrow, broad = slice(k * ch, (k + 1) * ch), slice(k * hid, (k + 1) * hid)
        for layer, (part_in, part_mx, part_out) in enumerate(((in0, mx0, out0), (in1, mx1, out1))):

            @pl.when(l == layer)
            def _():
                piece = part_in[k].astype(F32)
                wf[0, :, narrow] = piece[:, :ch]
                wb[0, :, narrow] = piece[:, ch : 2 * ch]
                wv[0, :, broad] = piece[:, 2 * ch :]
                wm[0, :, broad] = part_mx[k].astype(F32)
                wo[0, :, broad] = part_out[k].astype(F32)

        piece = states_ref[k].astype(F32)
        for i, ref in enumerate((decay, b_in, c_out)):
            for direction in range(2):
                lanes = slice(direction * ch, (direction + 1) * ch)
                ref[0, direction, :, narrow] = piece[i * count : (i + 1) * count, lanes]
        row = small_ref[k, one]
        bf[one, narrow] = row[:, 0, :ch]
        bb[one, narrow] = row[:, 0, ch : 2 * ch]
        bv[one, broad] = row[:, 0, 2 * ch :]
        bm[one, broad] = row[:, 1, :hid]
        for direction in range(2):
            start = direction * ch
            step[one, direction, narrow] = row[:, 1, hid + start : hid + start + ch]
            skip[one, direction, narrow] = row[:, 2, start : start + ch]


VM = pl.BlockSpec(memory_space=pltpu.VMEM)
ANY = pl.BlockSpec(memory_space=pl.ANY)


def shape(dims, dtype):
    return jax.ShapeDtypeStruct(tuple(dims), dtype)


def sem(*dims):
    return pltpu.SemaphoreType.DMA(dims)


def body(
    tokens_in, lengths, cotangent, norm_gain, norm_shift, w_fwd, w_bwd, w_value, bias_fwd, bias_bwd,
    bias_value, decay_log, step_log, b_input, c_output, skip_gain, w_mix, bias_mix, w_output, bias_output,
):
    n = lax.axis_size("dp")
    m = lax.axis_size("row")
    cols = lax.axis_size("col")
    rows, width = tokens_in.shape
    length = rows * cols
    ch = w_fwd.shape[2] // n
    ch2 = 2 * ch
    hid = w_mix.shape[2] // n
    wide = ch2 + hid
    chans = n * cols * ch
    tokens = n * length
    matrix = transform_matrix(length)
    f_mat = jnp.asarray(matrix, BF)
    ft_mat = jnp.asarray(np.ascontiguousarray(matrix.T), BF)
    states = decay_log.shape[3]
    share = w_fwd.shape[1]
    narrow = -(-(ch + max(k * ch % 128 for k in range(n))) // 128) * 128

    def turned(x):
        return jnp.swapaxes(x, -1, -2)

    per_layer = (
        shape((share, ch2), BF), shape((share, hid), BF), shape((w_mix.shape[1], hid), BF), shape((share, hid), BF),
        shape((wide, 1), F32), shape((hid, 1), F32), *[shape((states, ch2), F32)] * 3, shape((8, ch2), F32),
    )
    own_live, own_mask, *cuts = pl.pallas_call(
        functools.partial(prepare_kernel, n),
        out_shape=(shape((8, length), F32), shape((rows, 1), F32), *per_layer * LAYERS),
        in_specs=[pl.BlockSpec(memory_space=pltpu.SMEM)] + [VM] * 6 + [ANY] * 8,
        out_specs=(VM,) * (2 + len(per_layer) * LAYERS),
        scratch_shapes=[
            pltpu.VMEM((LAYERS, share, narrow), F32), pltpu.VMEM((LAYERS, share, narrow), F32),
            pltpu.VMEM((LAYERS, share, hid), F32), pltpu.VMEM((LAYERS, w_mix.shape[1], hid), F32),
            pltpu.VMEM((LAYERS, share, hid), F32), *[pltpu.VMEM((LAYERS, 2, states, narrow), F32)] * 3, sem(8),
        ],
        compiler_params=pltpu.CompilerParams(vmem_limit_bytes=VMEM_LIMIT),
        name="prepare",
    )(
        lengths, bias_fwd, bias_bwd, bias_value, bias_mix, step_log, skip_gain, w_fwd, w_bwd, w_value, w_mix,
        turned(w_output), turned(decay_log), turned(b_input), turned(c_output),
    )
    given = [cuts[len(per_layer) * l : len(per_layer) * (l + 1)] for l in range(LAYERS)]

    comm = [
        *[sem(n)] * 6, sem(n, n), sem(n, n),
    ]
    sums = [
        pltpu.VMEM((2, rows, width), F32), pltpu.VMEM((n, rows, width), BF), pltpu.VMEM((n, rows, width), BF),
        pltpu.VMEM((n, rows, width), BF), pltpu.VMEM((n - 1, rows, width), BF),
    ]
    saved_shapes = (
        shape((tokens, width), BF), shape((chans, tokens), BF), shape((n, wide, length), F32),
        shape((n, ch2, 2 * length), BF), shape((n, ch2, length), BF), shape((n, hid, length), F32),
        shape((hid, tokens), BF),
    )
    def fwd(layer):
        first = layer == 0
        table = shape((ch2, length), F32)
        extra = (shape((width, ch2), BF), shape((n, 8, length), F32), *[table] * 4) if first else ()
        lands = [(m, share, hid), (m, chans // m, hid), (m, share, hid)]
        return pl.pallas_call(
            functools.partial(fwd_kernel, n, m, layer),
            out_shape=(
                shape((rows, width), F32), *saved_shapes, shape((width, wide), BF),
                shape((chans, hid), BF), shape((hid, width), BF), *extra,
            ),
            in_specs=[VM] * (13 + (10 if first else 3)),
            out_specs=(VM, *([ANY] * 7), *([VM] * (3 + len(extra)))),
            scratch_shapes=[
                pltpu.VMEM((wide, width), BF), pltpu.VMEM((2 * n, hid, ch), BF),
                *(pltpu.VMEM(s.shape, s.dtype) for s in saved_shapes),
                pltpu.VMEM((ch2, length), BF), pltpu.VMEM((ch2, 2 * length), F32),
                pltpu.VMEM((ch2, 2 * length), BF), pltpu.VMEM((hid, length), F32), pltpu.VMEM((length, hid), BF),
                pltpu.VMEM((states, 128), F32), pltpu.VMEM((length // LAG, states, 128), F32),
                *(pltpu.VMEM(s, BF) for s in lands), pltpu.VMEM((width, hid), BF),
                *sums, *comm, *[sem(n, n)] * 4, *[sem(n)] * 4, sem(7, n),
                *[sem(m)] * 6,
                *([pltpu.VMEM((m, share, ch2), BF)] * 2 + [sem(m)] * 4 + [sem(n)] * 2 if first else []),
            ],
            compiler_params=pltpu.CompilerParams(
                collective_id=4 if first else 0, has_side_effects=True, vmem_limit_bytes=VMEM_LIMIT
            ),
            name="forward_block",
        )

    def bwd(layer):
        later = layer < LAYERS - 1
        late = (m, width // m, wide)
        out_shape = [
            shape((rows, width), F32), shape(late, BF), shape((chans // m, hid), BF), shape((width // m, hid), BF),
            shape((8, wide), F32), shape((8, hid), F32), shape((8, width), F32), shape((ch2, 2 * length), F32),
        ]
        if later:
            out_shape += [
                shape(late[1:], BF),
                shape((n, chans // m, hid), BF), shape((n, share, hid), BF),
            ]
        return pl.pallas_call(
            functools.partial(bwd_kernel, n, m, layer, later),
            out_shape=tuple(out_shape),
            in_specs=[VM] * 12 + [ANY] * 7 + [VM] * (3 * later),
            out_specs=(*[VM] * (8 + later), *[ANY] * (2 * later)),
            scratch_shapes=[
                pltpu.VMEM((tokens, width), BF),
                *(pltpu.VMEM(s.shape, s.dtype) for s in saved_shapes),
                pltpu.VMEM((wide, tokens), BF), pltpu.VMEM((ch2, length), F32), pltpu.VMEM((hid, tokens), BF),
                pltpu.VMEM((ch2, 2 * length), F32), pltpu.VMEM((ch2, 2 * length), BF), pltpu.VMEM((length, wide), BF),
                pltpu.VMEM((n, n * ch, length), BF), pltpu.VMEM((n, n * ch, length), BF),
                pltpu.VMEM((n * ch, length), F32),
                pltpu.VMEM((n - 1, n, ch, length), BF), pltpu.VMEM((wide, 128), F32), pltpu.VMEM((hid, 128), F32),
                *(pltpu.VMEM((*size, share_rows, hid), BF) for share_rows in (chans // m, share)
                  for size in ((m,), (m - 1,), ())),
                *sums, *comm, sem(n), sem(n), sem(n), sem(n), sem(n), sem(n), sem(7, n),
                sem(m), sem(m), sem(m), sem(m),
                *([pltpu.VMEM((m - 1, *late[1:]), BF), pltpu.VMEM(late[1:], BF), sem(m), sem(m), *[sem(2, n)] * 4, sem(2)]
                  if later else []),
            ],
            compiler_params=pltpu.CompilerParams(
                collective_id=1 + later, has_side_effects=True, vmem_limit_bytes=VMEM_LIMIT
            ),
            name="backward_block",
        )

    residual = tokens_in
    stored = []
    for l in range(LAYERS):
        sh_fb, sh_v, sh_mx, sh_out, in_bias, mix_bias, *tables = given[l]
        first = l == 0
        more = (sh_fb, given[1][0], *tables, *given[1][6:]) if first else (w_next, *spectrum)
        new, *made = fwd(l)(
            residual, norm_gain, norm_shift, own_live if first else mask, own_mask, sh_v, sh_mx, sh_out, in_bias,
            mix_bias, bias_output, ft_mat, f_mat, *more,
        )
        weights = made[7:10]
        if first:
            w_next, mask, *spectrum = made[10:]
            kernels = spectrum[:2], spectrum[2:]
            spectrum = spectrum[2:]
        stored.append((residual, made[:7], weights, kernels[l]))
        residual = new
    tokens_out = residual.astype(BF)

    grad = cotangent
    parts = [None] * LAYERS
    extra = ()
    for l in reversed(range(LAYERS)):
        resid_in, saved, weights, (kre, kim) = stored[l]
        grad, *parts[l] = bwd(l)(
            grad, resid_in, norm_gain, mask, own_mask, *weights, kre, kim, ft_mat, f_mat, *saved, *extra,
        )
        if l > 0:
            extra = tuple(parts[l][:3])
    part_in, red_mx0, red_out0, in0, mix0, norm0, dk0, late_in, all_mx1, all_out1 = parts[0]
    _, _, _, in1, mix1, norm1, dk1 = parts[1]
    lots = LAYERS * 3 * states
    all_in, all_mx, all_out = (n, share, wide), (n, chans // m, hid), (n, share, hid)
    all_in1, all_mx0, all_out0, all_in0, all_states, all_small, norms = pl.pallas_call(
        functools.partial(finish_kernel, n, m),
        out_shape=(
            shape(all_in, BF), shape(all_mx, BF), shape(all_out, BF), shape(all_in, BF),
            shape((n, m, lots // m, ch2), BF), shape((n, LAYERS, 8, wide), F32), shape((LAYERS, 8, wide), F32),
        ),
        in_specs=[VM] * 21,
        out_specs=(*[ANY] * 5, VM, VM),
        scratch_shapes=[
            pltpu.VMEM((m - 1, share, wide), BF), pltpu.VMEM((share, wide), BF), pltpu.VMEM((share, wide), BF),
            pltpu.VMEM((lots, ch2), F32),
            pltpu.VMEM((m, lots // m, ch2), BF), pltpu.VMEM((m - 1, lots // m, ch2), BF),
            pltpu.VMEM((lots // m, ch2), BF), pltpu.VMEM((m, lots // m, ch2), BF), pltpu.VMEM((length, ch2), F32),
            pltpu.VMEM((LAYERS, 8, wide), F32), pltpu.VMEM((m, LAYERS, 8, wide), F32),
            pltpu.VMEM((n, LAYERS, 8, wide), F32), pltpu.VMEM((LAYERS, 8, wide), F32),
            pltpu.VMEM((LAYERS, 8, wide), F32),
            *[sem(5, n)] * 4, sem(5), *[sem(m)] * 8,
            sem(n), sem(n), pltpu.SemaphoreType.DMA, pltpu.SemaphoreType.DMA,
        ],
        compiler_params=pltpu.CompilerParams(
            collective_id=3, has_side_effects=True, vmem_limit_bytes=VMEM_LIMIT
        ),
        name="finish",
    )(
        part_in, late_in, red_mx0, red_out0, dk0, dk1, in0, in1, mix0, mix1, norm0, norm1,
        *given[0][6:], *given[1][6:], ft_mat,
    )

    def fixed(dims):
        return pl.BlockSpec(tuple(dims), lambda l: (0,) * len(dims))

    def by_layer(dims):
        return pl.BlockSpec((1, *dims), lambda l: (l,) + (0,) * len(dims))

    chan, unit = n * ch, n * hid
    matrices = [(share, chan), (share, chan), (share, unit)]
    layouts = [
        (width,), (width,), *matrices, (chan,), (chan,), (unit,), (2, states, chan), (2, chan), (2, states, chan),
        (2, states, chan), (2, chan), (chans // m, unit), (unit,), (share, unit), (width,),
    ]
    small_out = {0, 1, 5, 6, 7, 9, 12, 14, 16}
    grads = list(pl.pallas_call(
        functools.partial(assemble_kernel, n),
        grid=(LAYERS,),
        out_shape=tuple(shape((LAYERS, *dims), F32) for dims in layouts),
        in_specs=[
            fixed(all_in), fixed(all_in), fixed(all_mx), fixed(all_mx), fixed(all_out), fixed(all_out),
            pl.BlockSpec((n, 3 * states, ch2), lambda l: (0, l, 0)), fixed((n, LAYERS, 8, wide)),
            fixed((LAYERS, 8, wide)),
        ],
        out_specs=tuple(
            fixed((LAYERS, *dims)) if i in small_out else by_layer(dims) for i, dims in enumerate(layouts)
        ),
        compiler_params=pltpu.CompilerParams(vmem_limit_bytes=VMEM_LIMIT),
        name="assemble",
    )(
        all_in0, all_in1, all_mx0, all_mx1, all_out0, all_out1, all_states.reshape(n, lots, ch2), all_small, norms,
    ))
    for i in (8, 10, 11, 15):
        grads[i] = turned(grads[i])
    return (tokens_out, grad, *grads)


def solution(mesh):
    tokens = P(("dp", "row", "col"), None)
    weight = P(None, "row", "col")
    bias = P(None, "col")
    state = P(None, None, "col", None)
    chan = P(None, None, "col")
    in_specs = (
        tokens, P(("dp", "row")), tokens, P(), P(), weight, weight, weight, bias, bias, bias,
        state, chan, state, state, chan, weight, bias, P(None, "col", "row"), P(),
    )
    out_specs = (
        tokens, tokens, P(), P(), weight, weight, weight, bias, bias, bias,
        state, chan, state, state, chan, weight, bias, P(None, "col", "row"), P(),
    )
    return jax.shard_map(body, mesh=mesh, in_specs=in_specs, out_specs=out_specs, check_vma=False)
```

```python
import functools

import jax
import jax.numpy as jnp
import numpy as np
from jax import lax
from jax.experimental import pallas as pl
from jax.experimental.pallas import tpu as pltpu
from jax.sharding import PartitionSpec as P

LAYERS = 2
EPS = 1e-05
LAG = 64
BF = jnp.bfloat16
F32 = jnp.float32
MESH = pl.DeviceIdType.MESH
VMEM_LIMIT = 60 * 1024 * 1024


def transform_matrix(length):
    k = np.arange(length)[:, None]
    t = np.arange(length)[None, :]
    angle = np.pi * (((2 * k + 1) * t) % (4 * length)) / (2 * length)
    return np.concatenate((np.cos(angle), -np.sin(angle)), axis=0)


def gelu_only(v):
    t = jnp.tanh(v * (0.7978845608 + 0.035677408 * v * v))
    return (0.5 * v) * (1.0 + t)


def gelu_parts(v):
    sq = v * v
    t = jnp.tanh(v * (0.7978845608 + 0.035677408 * sq))
    half = 0.5 + 0.5 * t
    slope = half + (v * half) * (1.0 - t) * (0.7978845608 + 0.107032225 * sq)
    return v * half, slope


def dot(a, b, ca, cb):
    return lax.dot_general(a, b, (((ca,), (cb,)), ((), ())), preferred_element_type=F32)


def over_rows(rows, step, work):
    def one(i, unused):
        work(pl.ds(pl.multiple_of(i * step, step), step))
        return unused

    lax.fori_loop(0, rows // step, one, 0)


def lane_sums(x):
    total = x[:, :128]
    for i in range(1, x.shape[1] // 128):
        total = total + x[:, 128 * i : 128 * (i + 1)]
    return total


def as_row(partial):
    return lax.dot_general(
        jnp.ones((8, 128), F32), partial, (((1,), (1,)), ((), ())), precision=lax.Precision.HIGHEST,
        preferred_element_type=F32,
    )


class Place:
    def __init__(self, n, m):
        self.n = n
        self.m = m
        self.d = lax.axis_index("dp")
        self.c = lax.axis_index("col")
        self.r = lax.axis_index("row")

    def greet(self):
        barrier = pltpu.get_barrier_semaphore()

        def hail(device):
            pl.semaphore_signal(barrier, inc=1, device_id=device, device_id_type=MESH)

        for k in range(1, self.n):
            hail({"dp": self.ahead(k)})
        hail({"col": 1 - self.c})

        def one(j, unused):
            hail({"row": self.up(j)})
            return unused

        lax.fori_loop(1, self.m, one, 0)
        pl.semaphore_wait(barrier, self.n + self.m - 1)

    def ahead(self, k):
        return lax.rem(self.d + k, self.n)

    def behind(self, k):
        return lax.rem(self.d - k + self.n, self.n)

    def near(self, k):
        return lax.rem(self.d + k, 2) + 2 * lax.rem(self.d // 2 + k // 2, 2)

    def apart(self, e):
        return lax.rem(self.d + e, 2) + 2 * lax.rem(self.d // 2 + e // 2, 2)

    def up(self, j):
        return lax.rem(self.r + j, self.m)

    def down(self, j):
        return lax.rem(self.r - j + self.m, self.m)

    def other(self, i):
        return i + (i + self.n - self.d) // self.n

    def to_dp(self, src, dst, send, recv, q):
        return pltpu.make_async_remote_copy(
            src, dst, send, recv, device_id={"dp": q}, device_id_type=MESH
        )

    def to_mate(self, src, dst, send, recv):
        return pltpu.make_async_remote_copy(
            src, dst, send, recv, device_id={"col": 1 - self.c}, device_id_type=MESH
        )

    def to_row(self, src, dst, send, recv, q):
        return pltpu.make_async_remote_copy(
            src, dst, send, recv, device_id={"row": q}, device_id_type=MESH
        )


class RowSum:
    def __init__(self, place, part, got, send, recv, hand=None):
        self.place, self.part, self.got, self.send, self.recv, self.hand = place, part, got, send, recv, hand
        self.line = place.m == 4 and hand is not None

    def copy(self, j):
        q = self.place.up(j)
        return self.place.to_row(self.part.at[q], self.got.at[j - 1], self.send.at[j], self.recv.at[j], q)

    def give(self):
        r = self.place.r
        return self.place.to_row(self.part.at[3 - r], self.hand, self.send.at[0], self.recv.at[0], 1 + r // 3)

    def sum_on(self):
        q = self.place.up(2)
        return self.place.to_row(self.hand, self.got.at[1], self.send.at[2], self.recv.at[2], q)

    def outer(self):
        return 1 + 2 * lax.rem(self.place.r, 2)

    def by_place(self, end, middle):
        r = self.place.r
        pl.when(r * (3 - r) == 0)(end)
        pl.when(r * (3 - r) > 0)(middle)

    def each(self, act):
        def one(j, unused):
            act(self.copy(j))
            return unused

        lax.fori_loop(1, self.place.m, one, 0)

    def start(self):
        if not self.line:
            self.each(lambda copy: copy.start())
            return

        def end():
            self.give().start()
            self.got[lax.rem(self.place.r, 2) * 2] = jnp.zeros(self.got.shape[1:], self.got.dtype)

        def middle():
            self.copy(1).start()
            self.copy(3).start()

        self.by_place(end, middle)

    def second(self):
        if self.line:

            def middle():
                self.give().wait_recv()
                mine = self.part[self.place.up(2)].astype(F32)
                self.hand[...] = (self.hand[...].astype(F32) + mine).astype(BF)
                self.sum_on().start()

            def end():
                self.copy(2).start()
                self.copy(self.outer()).start()

            self.by_place(end, middle)

    def total(self):
        if self.line:
            self.copy(2).wait_recv()
            pl.when(self.place.r > 0)(lambda: self.copy(1).wait_recv())
            pl.when(self.place.r < 3)(lambda: self.copy(3).wait_recv())
        else:
            self.each(lambda copy: copy.wait_recv())
        total = self.part[self.place.r].astype(F32)
        if self.place.m <= 4:
            for j in range(1, self.place.m):
                total = total + self.got[j - 1].astype(F32)
            return total
        return lax.fori_loop(1, self.place.m, lambda j, t: t + self.got[j - 1].astype(F32), total)

    def finish(self):
        if not self.line:
            self.each(lambda copy: copy.wait_send())
            return

        def end():
            self.give().wait_send()
            self.copy(2).wait_send()
            self.copy(self.outer()).wait_send()

        def middle():
            self.copy(1).wait_send()
            self.copy(3).wait_send()
            self.sum_on().wait_send()

        self.by_place(end, middle)


class Tokens:
    def __init__(self, place, buf, rows, length, sems):
        self.place, self.buf, self.rows, self.length = place, buf, rows, length
        self.send_p, self.recv_p, self.send_h, self.recv_h, self.send_m, self.recv_m = sems

    def region(self, slot, half=None):
        rows = self.rows // 2 if half is not None else self.rows
        start = slot * self.length + self.place.c * self.rows + (half or 0) * rows
        return self.buf.at[pl.ds(pl.multiple_of(start, rows), rows)]

    def peer(self, i):
        own = self.region(self.place.d)
        return self.place.to_dp(own, own, self.send_p.at[i], self.recv_p.at[i], self.place.near(i))

    def hop(self, i):
        part = self.region(self.place.near(3 - i), i - 1)
        return self.place.to_dp(part, part, self.send_h.at[i], self.recv_h.at[i], self.place.near(i))

    def mate(self, k):
        part = self.region(self.place.near(k))
        return self.place.to_mate(part, part, self.send_m.at[k], self.recv_m.at[k])

    def start(self):
        self.peer(1).start()
        self.peer(2).start()
        self.mate(0).start()

    def own(self):
        self.mate(0).wait_recv()

    def pass_on(self):
        for i in (1, 2):
            self.peer(i).wait_recv()
            self.hop(3 - i).start()
            self.mate(i).start()

    def fetch(self, k):
        @pl.when(k == 3)
        def _():
            self.hop(1).wait_recv()
            self.hop(2).wait_recv()
            self.mate(3).start()

        self.mate(k).wait_recv()

    def finish(self):
        for i in (1, 2):
            self.peer(i).wait_send()
            self.hop(i).wait_send()
        for k in range(4):
            self.mate(k).wait_send()


def norm_stats(residual):
    mean = jnp.mean(residual, axis=1, keepdims=True)
    centered = residual - mean
    variance = jnp.mean(centered * centered, axis=1, keepdims=True)
    inv = lax.rsqrt(variance + EPS)
    return centered * inv, inv


def sum_to_owner(place, rows, mate_out, mate_in, sum_out, sum_in, own, send_m, recv_m, send_p, recv_p):
    def to_mate(slot):
        return place.to_mate(mate_out.at[slot], mate_in.at[slot], send_m.at[slot], recv_m.at[slot])

    def to_owner(slot):
        k = lax.rem(slot - place.d + place.n, place.n)
        return place.to_dp(sum_out.at[slot], sum_in.at[k - 1], send_p.at[k], recv_p.at[k], slot)

    def close(slot, mine):
        to_mate(slot).wait_recv()

        own[mine] = own[mine] + mate_in[slot].astype(F32)

        @pl.when(slot != place.d)
        def _():
            sum_out[slot] = own[mine].astype(BF)
            to_owner(slot).start()

    def receive():
        def one(k, unused):
            to_owner(place.ahead(k)).wait_recv()
            return unused

        lax.fori_loop(1, place.n, one, 0)

    def finish():
        def one(k, unused):
            to_owner(place.ahead(k)).wait_send()
            return unused

        lax.fori_loop(1, place.n, one, 0)

        def two(s, unused):
            to_mate(s).wait_send()
            return unused

        lax.fori_loop(0, place.n, two, 0)

    return to_mate, close, receive, finish


class RowGather:
    def __init__(self, place, shard, land, send, recv):
        self.place, self.shard, self.land, self.send, self.recv = place, shard, land, send, recv
        self.line = place.m == 4

    def copy(self, j):
        place = self.place
        return place.to_row(self.shard, self.land.at[place.r], self.send.at[j], self.recv.at[j], place.up(j))

    def hop(self):
        place = self.place
        part = self.land.at[place.up(2)]
        return place.to_row(
            part, part, self.send.at[0], self.recv.at[self.inner()], lax.rem(3 * place.r + 1, place.m)
        )

    def outer(self):
        return 1 + 2 * lax.rem(self.place.r, 2)

    def inner(self):
        return lax.rem(2 * self.place.r + 3, self.place.m)

    def in_middle(self, act):
        r = self.place.r
        pl.when(r * (3 - r) > 0)(act)

    def each(self, act):
        def one(j, unused):
            act(self.copy(j))
            return unused

        lax.fori_loop(1, self.place.m, one, 0)

    def direct(self):
        self.line = False
        self.first()

    def first(self):
        if self.line:
            self.copy(2).start()
            self.copy(self.outer()).start()
        else:
            self.each(lambda copy: copy.start())
        self.land[self.place.r] = self.shard[...]

    def second(self):
        if self.line:
            self.copy(2).wait_recv()

            def act():
                self.hop().start()
                self.copy(self.inner()).start()

            self.in_middle(act)

    def whole(self):
        if self.line:
            self.copy(1).wait_recv()
            self.copy(3).wait_recv()
        else:
            self.each(lambda copy: copy.wait_recv())
        m, rows, lanes = self.land.shape
        return self.land[...].astype(F32).reshape(m * rows, lanes)

    def finish(self):
        if self.line:
            self.copy(2).wait_send()
            self.copy(self.outer()).wait_send()

            def act():
                self.hop().wait_send()
                self.copy(self.inner()).wait_send()

            self.in_middle(act)
        else:
            self.each(lambda copy: copy.wait_send())


def kernel_spectrum(decay, step, b_in, c_out, skip, sign, ft_ref, rate, lead):
    length = ft_ref.shape[0]
    blocks = length // LAG
    rate[...] = jnp.exp(step) * jnp.exp(decay)
    weight = (1.0 - jnp.exp(-rate[...])) * jnp.exp(-decay) * b_in * c_out
    for b in range(blocks):
        lead[b] = weight * jnp.exp(-(LAG * b) * rate[...])
    lanes = rate.shape[1]
    offs = lax.broadcasted_iota(jnp.int32, (LAG, lanes), 0).astype(F32)

    def state(i, totals):
        powers = jnp.exp(-offs * rate[pl.ds(i, 1)])
        return tuple(totals[b] + powers * lead[b, pl.ds(i, 1)] for b in range(blocks))

    zero = jnp.zeros((LAG, lanes), F32)
    totals = list(lax.fori_loop(0, rate.shape[0], state, (zero,) * blocks, unroll=2))
    at_zero = lax.broadcasted_iota(jnp.int32, (LAG, lanes), 0) == 0
    totals[0] = totals[0] + jnp.where(at_zero, skip, 0.0)
    kernel = jnp.concatenate(totals, axis=0)
    k_hat = dot(kernel.T.astype(BF), ft_ref[...], 1, 0) * (1.0 / length)
    return k_hat[:, :length], k_hat[:, length:] * sign


def direction_sign(ch, rows, lanes, start=0):
    at = lax.broadcasted_iota(jnp.int32, (rows, lanes), 0) + start
    return jnp.where(at < ch, 1.0, -1.0)


def fwd_kernel(
    n, m, layer, res_ref, gain_ref, shift_ref, own_live_ref, own_mask_ref, sh_v, sh_mx, sh_out, in_bias_ref,
    mix_bias_ref, out_bias_ref, ft_ref, f_ref, *rest
):
    first = layer == 0
    if first:
        sh_fb, sh_next, sh_mx_next, *rest = rest
        tables, next_tables, rest = rest[:4], rest[4:8], rest[8:]
    else:
        w_fb_ref, kre_ref, kim_ref, *rest = rest
    new_ref, g_out, mx_out, pre_out, u_out, y_out, pm_out, prod_out, w_in_out, w_out_out, *rest = rest
    if first:
        w_mx_out, *rest = rest
        next_out, mx_next_out, mask_ref, kre_ref, kim_ref, kre_next, kim_next, *rest = rest
    else:
        mask_ref = own_live_ref
    (
        w_in_t, w_mx_t, g, mx, pre, u_sp, y, pm, prod, act, spec, y_hat, prod_f, prod_t,
        rate, lead, value_act, land_v, land_mx, land_out, w_out_t,
        own, mate_out, mate_in, sum_out, sum_in,
        send_a, recv_a, send_ah, recv_ah, send_am, recv_am, send_b, recv_b, send_bh, recv_bh, send_bm, recv_bm,
        send_c, recv_c, send_cm, recv_cm, save,
        send_gv, recv_gv, send_gm, recv_gm, send_go, recv_go, *rest,
    ) = rest
    place = Place(n, m)
    d, c = place.d, place.c
    rows, width = res_ref.shape
    length = ft_ref.shape[0]
    hid = sh_mx.shape[1]
    ch2 = kre_ref.shape[0]
    ch = ch2 // 2
    gain, shift, out_bias = (ref[layer : layer + 1] for ref in (gain_ref, shift_ref, out_bias_ref))

    place.greet()
    gather_v = RowGather(place, sh_v, land_v, send_gv, recv_gv)
    gather_out = RowGather(place, sh_out, land_out, send_go, recv_go)
    later_weights = (gather_v, gather_out)
    gather_a = Tokens(place, g, rows, length, (send_a, recv_a, send_ah, recv_ah, send_am, recv_am))
    if first:
        land_fb, land_next, land_mx_next, send_gi, recv_gi, send_gn, recv_gn, send_gx, recv_gx, send_mk, recv_mk = rest
        gather_mx = RowGather(place, sh_mx, land_mx, send_gm, recv_gm)
        gather_mx_next = RowGather(place, sh_mx_next, land_mx_next, send_gx, recv_gx)
        gather_fb = RowGather(place, sh_fb, land_fb, send_gi, recv_gi)
        gather_next = RowGather(place, sh_next, land_next, send_gn, recv_gn)
        gather_fb.direct()

        def mask_peer(k):
            return place.to_dp(
                own_live_ref, mask_ref.at[d], send_mk.at[k], recv_mk.at[k], place.ahead(k)
            )

        for k in range(1, n):
            mask_peer(k).start()
        mask_ref[d] = own_live_ref[...]
    else:
        gather_v.first()
    base = d * length + c * rows
    xhat, _ = norm_stats(res_ref[...].astype(F32))
    g[pl.ds(pl.multiple_of(base, rows), rows)] = (xhat * gain + shift).astype(BF)
    gather_a.start()

    def spectra(given, re_ref, im_ref):
        decay_ref, b_ref, c_ref, row_ref = given
        for j in range(ch2 // 128):
            at = slice(128 * j, 128 * (j + 1))
            re_ref[at], im_ref[at] = kernel_spectrum(
                decay_ref[:, at], row_ref[0:1, at], b_ref[:, at], c_ref[:, at], row_ref[1:2, at],
                direction_sign(ch, 128, length, 128 * j), ft_ref, rate, lead,
            )

    if first:
        spectra(tables, kre_ref, kim_ref)
    if first:
        w_fb = gather_fb.whole()
        gather_mx.first()
        for k in range(1, n):
            mask_peer(k).wait_recv()
    else:
        w_fb = w_fb_ref[...].astype(F32)
    w_in_out[:, :ch2] = w_fb.astype(BF)
    w_in_t[:ch2] = w_fb.T.astype(BF)
    gather_a.own()

    def chunk(owner, slot):
        at = pl.ds(pl.multiple_of((c * n + owner) * ch, ch), ch)
        return mx.at[at, pl.ds(pl.multiple_of(slot * length, length), length)]

    def turn(k, j):
        return place.near(k ^ j)

    def half_chunk(owner, slot, half):
        at = pl.ds(pl.multiple_of((c * n + owner) * ch + half * (ch // 2), ch // 2), ch // 2)
        return mx.at[at, pl.ds(pl.multiple_of(slot * length, length), length)]

    def peer_b(i, j):
        part = chunk(d, turn(0, j))
        return place.to_dp(part, part, send_b.at[j, i], recv_b.at[j, i], place.near(i))

    def hop_b(i, j):
        part = half_chunk(place.near(3 - i), turn(3 - i, j), i - 1)
        return place.to_dp(part, part, send_bh.at[j, i], recv_bh.at[j, i], place.near(i))

    def mate_b(k, j):
        part = chunk(place.near(k), turn(k, j))
        return place.to_mate(part, part, send_bm.at[j, k], recv_bm.at[j, k])

    def saves(slot, item):
        lanes = pl.ds(pl.multiple_of(slot * length, length), length)
        src, dst = (
            lambda: (g.at[lanes], g_out.at[lanes]),
            lambda: (u_sp.at[slot], u_out.at[slot]),
            lambda: (y.at[slot], y_out.at[slot]),
            lambda: (pre.at[slot], pre_out.at[slot]),
            lambda: (mx.at[:, lanes], mx_out.at[:, lanes]),
            lambda: (pm.at[slot], pm_out.at[slot]),
            lambda: (prod.at[:, lanes], prod_out.at[:, lanes]),
        )[item]()
        return pltpu.make_async_copy(src, dst, save.at[item, slot])

    def scan_slot(i, unused):
        slot = place.near(i)

        @pl.when(i == 1)
        def _():
            gather_a.pass_on()

        @pl.when(i > 0)
        def _():
            gather_a.fetch(i)

        if first:

            @pl.when(i == n - 1)
            def _():
                gather_mx.second()
                gather_v.first()

        else:

            @pl.when(i == n - 2)
            def _():
                gather_v.second()
                gather_out.first()

        lanes = pl.ds(pl.multiple_of(slot * length, length), length)
        live = mask_ref[slot, 0:1]
        v = dot(w_in_t[:ch2], g[lanes], 1, 1) + in_bias_ref[:ch2]
        pre[slot, :ch2] = v
        act[...] = (gelu_only(v) * live).astype(BF)
        spec[...] = dot(act[...], ft_ref[...], 1, 0)
        u_re, u_im = spec[:, :length], spec[:, length:]
        k_re, k_im = kre_ref[...], kim_ref[...]
        u_sp[slot, :, :length] = u_re.astype(BF)
        u_sp[slot, :, length:] = u_im.astype(BF)
        y_hat[:, :length] = (k_re * u_re - k_im * u_im).astype(BF)
        y_hat[:, length:] = (k_re * u_im + k_im * u_re).astype(BF)
        both = dot(y_hat[...], f_ref[...], 1, 0)
        y[slot] = both.astype(BF)
        mine = pl.ds(pl.multiple_of((c * n + d) * ch, ch), ch)
        mx[mine, lanes] = (both[:ch] * both[ch:]).astype(BF)
        for j in range(n):

            @pl.when(i == j)
            def _():
                peer_b(1, j).start()
                peer_b(2, j).start()
                mate_b(0, j).start()

        for item in range(3):
            saves(slot, item).start()
        return unused

    lax.fori_loop(0, n, scan_slot, 0)

    def pass_b(j):
        for i in (1, 2):
            peer_b(i, j).wait_recv()
            hop_b(3 - i, j).start()
            mate_b(i, j).start()

    pass_b(0)
    if first:
        spectra(next_tables, kre_next, kim_next)
    else:
        gather_out.second()
    pass_b(1)
    if first:
        w_mx = gather_mx.whole()
        w_mx_out[...] = w_mx.astype(BF)
    else:
        w_mx = sh_mx[...].astype(F32)
    for block in range(2 * n):
        w_mx_t[block] = w_mx[block * ch : (block + 1) * ch].T.astype(BF)
    def value_slot(slot, unused):
        tokens = pl.ds(pl.multiple_of(slot * length, length), length)
        value = dot(w_in_t[ch2:], g[tokens], 1, 1) + in_bias_ref[ch2:]
        pre[slot, ch2:] = value
        value_act[slot] = gelu_only(value)
        saves(slot, 3).start()
        return unused

    begun = set()

    def mix_in(k, j):
        owner, slot = place.near(k), turn(k, j)
        lanes = pl.ds(pl.multiple_of(slot * length, length), length)
        mate_b(k, j).wait_recv()
        total = None
        for side in range(2):
            rows_at = pl.ds(pl.multiple_of((side * n + owner) * ch, ch), ch)
            part = dot(w_mx_t[side * n + owner], mx[rows_at, lanes], 1, 0)
            total = part if total is None else total + part
        pm[slot] = (pm[slot] if k ^ j in begun else mix_bias_ref[...]) + total
        begun.add(k ^ j)

    def across(j):
        hop_b(1, j).wait_recv()
        hop_b(2, j).wait_recv()
        mate_b(3, j).start()
        mix_in(3, j)

    for j in range(n):
        for k in range(3):
            mix_in(k, j)
        if j + 2 < n:
            pass_b(j + 2)
        if j == 0 and first:
            gather_v.second()
            gather_out.first()
        if j == 2 and first:
            gather_out.second()
            gather_next.first()
        if j == n - 1:
            w_v = gather_v.whole()
            w_in_out[:, ch2:] = w_v.astype(BF)
            w_in_t[ch2:] = w_v.T.astype(BF)
            lax.fori_loop(0, n, value_slot, 0)
        if j > 0:
            across(j - 1)
    across(n - 1)
    w_out = gather_out.whole()
    w_out_t[...] = w_out.astype(BF)
    w_out_out[...] = w_out.T.astype(BF)

    to_mate, close, receive, finish_c = sum_to_owner(
        place, rows, mate_out, mate_in, sum_out, sum_in, own, send_cm, recv_cm, send_c, recv_c
    )

    def order(i):
        return lax.select(i == n - 1, d, place.other(i))

    def hidden_slot(i, unused):
        if first:

            @pl.when(i == 1)
            def _():
                gather_next.second()
                gather_mx_next.first()

        slot = order(i)
        lanes = pl.ds(pl.multiple_of(slot * length, length), length)
        v = pm[slot]
        product = gelu_only(v) * value_act[slot]
        prod_f[...] = product
        prod[:, lanes] = product.astype(BF)
        prod_t[...] = prod_f[...].T.astype(BF)
        for item in range(4, 7):
            saves(slot, item).start()
        theirs = pl.ds(pl.multiple_of((1 - c) * rows, rows), rows)
        ours = pl.ds(pl.multiple_of(c * rows, rows), rows)
        mate_out[slot] = dot(prod_t[theirs], w_out_t[...], 1, 1).astype(BF)
        to_mate(slot).start()

        @pl.when(i > 0)
        def _():
            close(order(i - 1), lax.rem(i - 1, 2))

        own[lax.rem(i, 2)] = dot(prod_t[ours], w_out_t[...], 1, 1)
        return unused

    lax.fori_loop(0, n, hidden_slot, 0)
    last = (n - 1) % 2
    close(d, last)
    if first:
        gather_mx_next.second()
    receive()

    total = own[last]
    for k in range(1, n):
        total = total + sum_in[k - 1].astype(F32)
    new_ref[...] = res_ref[...].astype(F32) + own_mask_ref[...] * (total + out_bias)
    gather_a.finish()
    finish_c()
    for gather in later_weights:
        gather.finish()
    if first:
        next_out[...] = gather_next.whole().astype(BF)
        mx_next_out[...] = gather_mx_next.whole().astype(BF)
        gather_mx.finish()
        gather_mx_next.finish()
        gather_next.finish()
        gather_fb.finish()
        for k in range(1, n):
            mask_peer(k).wait_send()

    for j in range(n):
        for i in (1, 2):
            peer_b(i, j).wait_send()
            hop_b(i, j).wait_send()
        for k in range(n):
            mate_b(k, j).wait_send()

    def drain(slot, unused):
        for item in range(7):
            saves(slot, item).wait()
        return unused

    lax.fori_loop(0, n, drain, 0)


def bwd_kernel(
    n, m, layer, later, grad_ref, res_ref, gain_ref, mask_ref, own_mask_ref, w_in_ref, w_mx_ref, w_out_ref, kre_ref,
    kim_ref, ft_ref, f_ref, g_in, mx_in, pre_in, u_in, y_in, pm_in, prod_in, *rest
):
    if later:
        late_part, red_mx1, red_out1, *rest = rest
    (new_ref, gw_in_ref, red_mx_ref, red_out_ref, in_row_ref, mix_row_ref, norm_sum_ref, dk_ref, *rest) = rest
    if later:
        red_late_ref, all_mx, all_out, *rest = rest
    (
        gb, g, mx, pre, u_sp, y, pm, prod, gpre, gpre_f, gpm, spec, hat, turned,
        mix_sum, mix_mate, mix_own, mix_got, in_sum, mix_acc, part_mx, got_mx, hand_mx, part_out, got_out, hand_out,
        own, mate_out, mate_in, sum_out, sum_in,
        send_a, recv_a, send_ah, recv_ah, send_am, recv_am, send_b, recv_b, send_bm, recv_bm, send_c, recv_c, send_cm, recv_cm, load,
        send_rm, recv_rm, send_ro, recv_ro, *rest,
    ) = rest
    place = Place(n, m)
    d, c = place.d, place.c
    rows, width = res_ref.shape
    length = ft_ref.shape[0]
    hid = w_mx_ref.shape[1]
    ch2 = kre_ref.shape[0]
    ch = ch2 // 2
    half = n * ch

    def loads(slot, item):
        lanes = pl.ds(pl.multiple_of(slot * length, length), length)
        src, dst = (
            lambda: (pre_in.at[slot], pre.at[slot]),
            lambda: (pm_in.at[slot], pm.at[slot]),
            lambda: (y_in.at[slot], y.at[slot]),
            lambda: (u_in.at[slot], u_sp.at[slot]),
            lambda: (prod_in.at[:, lanes], prod.at[:, lanes]),
            lambda: (mx_in.at[:, lanes], mx.at[:, lanes]),
            lambda: (g_in.at[lanes], g.at[lanes]),
        )[item]()
        return pltpu.make_async_copy(src, dst, load.at[item, slot])

    for item in range(7):
        loads(d, item).start()

    def start_loads(i, unused):
        for item in range(7):
            loads(place.other(i), item).start()
        return unused

    lax.fori_loop(0, n - 1, start_loads, 0)

    place.greet()
    gather_a = Tokens(place, gb, rows, length, (send_a, recv_a, send_ah, recv_ah, send_am, recv_am))
    base = d * length + c * rows
    gain = gain_ref[layer : layer + 1]
    first = grad_ref[...].astype(F32) * own_mask_ref[...]
    gb[pl.ds(pl.multiple_of(base, rows), rows)] = first.astype(BF)
    gather_a.start()
    sum_mx = RowSum(place, part_mx, got_mx, send_rm, recv_rm, hand_mx)
    sum_out_w = RowSum(place, part_out, got_out, send_ro, recv_ro, hand_out)
    row_sums = [sum_mx, sum_out_w]
    if later:
        got_late, hand_late, send_rl, recv_rl, *sems = rest
        sum_late = RowSum(place, late_part, got_late, send_rl, recv_rl, hand_late)
        sum_late.start()
        row_sums.append(sum_late)
    norm_sum_ref[...] = jnp.zeros_like(norm_sum_ref)
    norm_sum_ref[2:3] = jnp.sum(first, axis=0, keepdims=True)
    in_sum[...] = jnp.zeros_like(in_sum)
    mix_acc[...] = jnp.zeros_like(mix_acc)
    dk_ref[...] = jnp.zeros_like(dk_ref)
    gather_a.own()

    def mate_b(slot):
        return place.to_mate(mix_sum.at[slot], mix_mate.at[slot], send_bm.at[slot], recv_bm.at[slot])

    def peer_b(k, slot):
        q = place.ahead(k)
        part = mix_sum.at[slot, pl.ds(pl.multiple_of(q * ch, ch), ch)]
        return place.to_dp(part, mix_got.at[k - 1, slot], send_b.at[slot, k], recv_b.at[slot, k], q)

    def hidden_slot(i, unused):
        slot = lax.select(i == 0, d, place.other(i - 1))

        @pl.when(i == 1)
        def _():
            gather_a.pass_on()

        @pl.when(i > 0)
        def _():
            gather_a.fetch(place.apart(slot))

        if later:
            pl.when(i == n - 2)(sum_late.second)


        lanes = pl.ds(pl.multiple_of(slot * length, length), length)
        mix_own[:hid] = dot(w_out_ref[...], gb[lanes], 1, 1)
        for item in range(2):
            loads(slot, item).wait()
        gated, slope = gelu_parts(pm[slot])
        value, value_slope = gelu_parts(pre[slot, ch2:])
        now = mix_own[:hid]
        to_value = now * gated * value_slope
        to_mix = now * value * slope
        gpre[ch2:, lanes] = to_value.astype(BF)
        gpm[:, lanes] = to_mix.astype(BF)
        in_sum[ch2:] = in_sum[ch2:] + lane_sums(to_value)
        mix_acc[...] = mix_acc[...] + lane_sums(to_mix)
        theirs = pl.ds(pl.multiple_of((1 - c) * half, half), half)
        ours = pl.ds(pl.multiple_of(c * half, half), half)
        mix_sum[slot] = dot(w_mx_ref[theirs], gpm[:, lanes], 1, 0).astype(BF)
        mate_b(slot).start()
        mix_own[...] = dot(w_mx_ref[ours], gpm[:, lanes], 1, 0)
        mate_b(slot).wait()
        mix_sum[slot] = (mix_own[...] + mix_mate[slot].astype(F32)).astype(BF)
        for k in range(1, n):
            peer_b(k, slot).start()
        return unused

    lax.fori_loop(0, n, hidden_slot, 0)

    def wait_loads(slot, unused):
        for item in range(2, 7):
            loads(slot, item).wait()
        return unused

    lax.fori_loop(0, n, wait_loads, 0)
    share = mx.shape[0] // m

    def grad_mix(q, unused):
        part_mx[q] = dot(mx[pl.ds(pl.multiple_of(q * share, share), share)], gpm[...], 1, 1).astype(BF)
        return unused

    lax.fori_loop(0, m, grad_mix, 0)
    sum_mx.start()
    gw_out = dot(prod[...], gb[...], 1, 0).T
    part_out[...] = gw_out.reshape(m, width // m, hid).astype(BF)
    sum_out_w.start()
    spreads = []
    if later:
        spreads = [
            Spread(place, red_mx1, all_mx, sems, 0),
            Spread(place, red_out1, all_out, sems, 1),
        ]

    to_mate, close, receive, finish_c = sum_to_owner(
        place, rows, mate_out, mate_in, sum_out, sum_in, own, send_cm, recv_cm, send_c, recv_c
    )

    def order(i):
        return lax.select(i == n - 1, d, place.other(i))

    def scan_slot(i, unused):
        slot = order(i)
        lanes = pl.ds(pl.multiple_of(slot * length, length), length)
        for k in range(1, n):
            peer_b(k, slot).wait_recv()

        @pl.when(i == n - 2)
        def _():
            for each in spreads:
                each.start()

        @pl.when(i == n - 2)
        def _():
            sum_mx.second()
            sum_out_w.second()

        total = mix_sum[slot, pl.ds(pl.multiple_of(d * ch, ch), ch)].astype(F32)
        for k in range(1, n):
            total = total + mix_got[k - 1, slot].astype(F32)
        hat[:ch, :length] = (total * y[slot, ch:].astype(F32)).astype(BF)
        hat[ch:, :length] = (total * y[slot, :ch].astype(F32)).astype(BF)
        spec[...] = dot(hat[:, :length], ft_ref[...], 1, 0)
        g_re, g_im = spec[:, :length], spec[:, length:]
        k_re, k_im = kre_ref[...], kim_ref[...]
        hat[:, :length] = (k_re * g_re + k_im * g_im).astype(BF)
        hat[:, length:] = (k_re * g_im - k_im * g_re).astype(BF)
        u_re, u_im = u_sp[slot, :, :length].astype(F32), u_sp[slot, :, length:].astype(F32)
        dk_ref[:, :length] = dk_ref[:, :length] + (u_re * g_re + u_im * g_im)
        dk_ref[:, length:] = dk_ref[:, length:] + (u_re * g_im - u_im * g_re)
        spec[:, :length] = dot(hat[...], f_ref[...], 1, 0)
        live = mask_ref[slot, 0:1]
        _, slope = gelu_parts(pre[slot, :ch2])
        part = spec[:, :length] * slope * live
        gpre_f[...] = part
        gpre[:ch2, lanes] = part.astype(BF)
        in_sum[:ch2] = in_sum[:ch2] + lane_sums(part)
        turned[:, :ch2] = gpre_f[...].T.astype(BF)
        gpre_f[...] = gpre[ch2:, lanes].astype(F32)
        turned[:, ch2:] = gpre_f[...].T.astype(BF)
        theirs = pl.ds(pl.multiple_of((1 - c) * rows, rows), rows)
        ours = pl.ds(pl.multiple_of(c * rows, rows), rows)
        mate_out[slot] = dot(turned[theirs], w_in_ref[...], 1, 1).astype(BF)
        to_mate(slot).start()

        @pl.when(i > 0)
        def _():
            close(order(i - 1), lax.rem(i - 1, 2))

        own[lax.rem(i, 2)] = dot(turned[ours], w_in_ref[...], 1, 1)
        return unused

    lax.fori_loop(0, n, scan_slot, 0)
    last = (n - 1) % 2
    close(d, last)

    def grad_in(r):
        part = dot(gpre[r], g[...], 1, 0).T
        gw_in_ref[:, :, r] = part.reshape(m, width // m, part.shape[1]).astype(BF)

    over_rows(gpre.shape[0], 128, grad_in)
    for each in spreads:
        each.pass_on()
    in_row_ref[...] = as_row(in_sum[...])
    mix_row_ref[...] = as_row(mix_acc[...])
    if later:
        red_late_ref[...] = sum_late.total().astype(BF)
    receive()
    total = own[last]
    for k in range(1, n):
        total = total + sum_in[k - 1].astype(F32)
    xhat, inv = norm_stats(res_ref[...].astype(F32))
    h = total * gain
    middle = jnp.mean(h, axis=1, keepdims=True)
    along = jnp.mean(h * xhat, axis=1, keepdims=True)
    new_ref[...] = grad_ref[...].astype(F32) + inv * (h - middle - xhat * along)
    norm_sum_ref[0:1] = jnp.sum(total * xhat, axis=0, keepdims=True)
    norm_sum_ref[1:2] = jnp.sum(total, axis=0, keepdims=True)
    red_mx_ref[...] = sum_mx.total().astype(BF)
    red_out_ref[...] = sum_out_w.total().astype(BF)
    gather_a.finish()
    finish_c()
    for row_sum in row_sums:
        row_sum.finish()
    for each in spreads:
        each.wait()

    def drain(slot, unused):
        for k in range(1, n):
            peer_b(k, slot).wait_send()
        return unused

    lax.fori_loop(0, n, drain, 0)


class Spread:
    def __init__(self, place, src, out, sems, item):
        self.place, self.src, self.out, self.item = place, src, out, item
        self.send, self.recv, self.send_h, self.recv_h, self.keep = sems
        rows = src.shape[0]
        whole = len(src.shape) == 2 and rows % 32 != 0
        half = rows if whole else rows // 2
        self.pieces = [(i, start, half) for i, start in ((1, 0), (2, half)) if start < rows]

    def peer(self, i):
        place, item = self.place, self.item
        return place.to_dp(
            self.src, self.out.at[place.d], self.send.at[item, i], self.recv.at[item, i], place.near(i)
        )

    def hop(self, i, start, count):
        place, item = self.place, self.item
        part = self.out.at[place.near(3 - i), pl.ds(start, count)]
        return place.to_dp(part, part, self.send_h.at[item, i], self.recv_h.at[item, i], place.near(i))

    def local(self):
        return pltpu.make_async_copy(self.src, self.out.at[self.place.d], self.keep.at[self.item])

    def start(self):
        self.peer(1).start()
        self.peer(2).start()
        self.local().start()

    def pass_on(self):
        self.peer(1).wait_recv()
        self.peer(2).wait_recv()
        for piece in self.pieces:
            self.hop(*piece).start()

    def wait(self):
        for piece in self.pieces:
            self.hop(*piece).wait()
        self.peer(1).wait_send()
        self.peer(2).wait_send()
        self.local().wait()


def state_grads(dk_re, dk_im, sign, ft_ref, decay, step, b_in, c_out, lag_sums):
    length = ft_ref.shape[0]
    re = dk_re.astype(BF)
    im = (dk_im * sign).astype(BF)
    lag_sums[...] = (dot(ft_ref[:, :length], re, 1, 1) + dot(ft_ref[:, length:], im, 1, 1)) * (1.0 / length)
    rate = jnp.exp(step) * jnp.exp(decay)
    a = jnp.exp(-rate)

    totals, slopes = [], []
    for lanes in (slice(0, 256), slice(256, a.shape[1])):
        base = a[:, lanes]

        def lag(i, carry, base=base, lanes=lanes):
            total, slope = carry
            row = lag_sums[pl.ds(length - 1 - i, 1)][:, lanes]
            return total * base + row, slope * base + total

        zero = jnp.zeros_like(base)
        total, slope = lax.fori_loop(0, length, lag, (zero, zero), unroll=4)
        totals.append(total)
        slopes.append(slope)
    total, slope = jnp.concatenate(totals, axis=1), jnp.concatenate(slopes, axis=1)
    inv_decay = jnp.exp(-decay)
    gain = (1.0 - a) * inv_decay
    b_disc = gain * b_in
    to_b = c_out * total
    to_rate = a * (to_b * inv_decay * b_in - (c_out * b_disc) * slope)
    through = to_rate * rate
    return (
        through - to_b * b_disc, to_b * gain, b_disc * total,
        jnp.sum(through, axis=0, keepdims=True), lag_sums[0:1],
    )


def finish_kernel(
    n, m, part_in, late_in, red_mx0, red_out0, dk0, dk1, in0, in1, mix0, mix1, norm0, norm1,
    decay0, b0, c0, row0, decay1, b1, c1, row1, ft_ref,
    all_in1, all_mx0, all_out0, all_in0, all_states, all_small, norm_ref,
    got_in, hand_in, red_in0, states, part_s, got_s, red_s, full_s, lag_sums, small, row_small, dp_small, norm_own, norm_got,
    send_w, recv_w, send_wh, recv_wh, keep_w, send_ri, recv_ri, send_rs, recv_rs, send_gs, recv_gs, send_sm, recv_sm,
    send_ds, recv_ds, send_n, recv_n,
):
    place = Place(n, m)
    d, r = place.d, place.r
    states_n, ch2 = decay0.shape
    place.greet()
    sum_in = RowSum(place, part_in, got_in, send_ri, recv_ri, hand_in)
    sum_in.start()
    spreads = [
        Spread(place, src, out, (send_w, recv_w, send_wh, recv_wh, keep_w), item)
        for item, (src, out) in enumerate(
            ((late_in, all_in1), (red_mx0, all_mx0), (red_out0, all_out0), (red_in0, all_in0), (full_s, all_states))
        )
    ]
    for each in spreads[:3]:
        each.start()

    small[...] = jnp.zeros_like(small)
    for l, (in_row, mix_row, norm) in enumerate(((in0, mix0, norm0), (in1, mix1, norm1))):
        small[l, 0:1] = in_row[0:1]
        small[l, 1:2, :ch2] = mix_row[0:1]
        small[l, 3:6] = norm[0:3]
    length = ft_ref.shape[0]
    for l, (dk, decay, b_in, c_out, row) in enumerate(((dk0, decay0, b0, c0, row0), (dk1, decay1, b1, c1, row1))):
        grads = state_grads(
            dk[:, :length], dk[:, length:], direction_sign(ch2 // 2, ch2, length), ft_ref, decay[...], row[0:1],
            b_in[...], c_out[...], lag_sums,
        )
        for i in range(3):
            states[pl.ds((3 * l + i) * states_n, states_n)] = grads[i]
        small[l, 1:2, ch2:] = grads[3]
        small[l, 2:3, :ch2] = grads[4]
        if l == 0:
            sum_in.second()
    share = states.shape[0] // m
    for q in range(m):
        part_s[q] = states[q * share : (q + 1) * share].astype(BF)
    sum_s = RowSum(place, part_s, got_s, send_rs, recv_rs)
    sum_s.start()
    row_small[r] = small[...]

    def small_row(j):
        return place.to_row(row_small.at[r], row_small.at[r], send_sm.at[j], recv_sm.at[j], place.up(j))

    def repeat(work, count):
        def one(j, unused):
            work(j)
            return unused

        lax.fori_loop(1, count, one, 0)

    repeat(lambda j: small_row(j).start(), m)

    spreads[0].pass_on()
    spreads[1].pass_on()
    red_in0[...] = sum_in.total().astype(BF)
    spreads[3].start()
    spreads[2].pass_on()
    red_s[...] = sum_s.total().astype(BF)
    full_s[r] = red_s[...]

    def state_row(j):
        return place.to_row(full_s.at[r], full_s.at[r], send_gs.at[j], recv_gs.at[j], place.up(j))

    repeat(lambda j: state_row(j).start(), m)
    repeat(lambda j: small_row(j).wait_recv(), m)
    total = row_small[0]
    for q in range(1, m):
        total = total + row_small[q]
    dp_small[d] = total

    def small_dp(k):
        return place.to_dp(dp_small.at[d], dp_small.at[d], send_ds.at[k], recv_ds.at[k], place.ahead(k))

    for k in range(1, n):
        small_dp(k).start()
    repeat(lambda j: state_row(j).wait_recv(), m)

    spreads[4].start()
    spreads[3].pass_on()
    for k in range(1, n):
        small_dp(k).wait_recv()
    total = dp_small[0]
    for q in range(1, n):
        total = total + dp_small[q]
    norm_own[...] = total
    swap = place.to_mate(norm_own, norm_got, send_n, recv_n)
    swap.start()
    all_small[...] = dp_small[...]
    swap.wait_recv()
    norm_ref[...] = norm_own[...] + norm_got[...]
    swap.wait_send()
    spreads[4].pass_on()
    for each in spreads:
        each.wait()
    for k in range(1, n):
        small_dp(k).wait_send()
    repeat(lambda j: small_row(j).wait_send(), m)
    repeat(lambda j: state_row(j).wait_send(), m)
    sum_in.finish()
    sum_s.finish()


def prepare_kernel(
    n, lengths_ref, bias_fwd, bias_bwd, bias_value, bias_mix, step_ref, skip_ref, *rest
):
    d = lax.axis_index("dp")
    w_fwd, w_bwd, w_value, w_mix, w_out, decay, b_in, c_out, live_ref, mask_ref, *rest = rest
    per = 10
    outs = [rest[per * l : per * (l + 1)] for l in range(LAYERS)]
    win_f, win_b, win_v, win_m, win_o, win_d, win_i, win_c, load = rest[per * LAYERS :]
    ch = w_fwd.shape[2] // n
    hid = w_value.shape[2] // n
    size = win_f.shape[2]
    places = sorted({(k * ch) % 128 for k in range(n)})

    def window(width, wide):
        start = pl.multiple_of((d * width) // 128 * 128, 128)
        return pl.ds(start, wide)

    narrow, broad = window(ch, size), window(hid, hid)
    copies = [
        pltpu.make_async_copy(src.at[at], dst, load.at[i])
        for i, (src, at, dst) in enumerate((
            (w_fwd, (slice(None), slice(None), narrow), win_f), (w_bwd, (slice(None), slice(None), narrow), win_b),
            (decay, (slice(None), slice(None), slice(None), narrow), win_d),
            (b_in, (slice(None), slice(None), slice(None), narrow), win_i),
            (c_out, (slice(None), slice(None), slice(None), narrow), win_c),
            (w_value, (slice(None), slice(None), broad), win_v), (w_mix, (slice(None), slice(None), broad), win_m),
            (w_out, (slice(None), slice(None), broad), win_o),
        ))
    ]
    for copy in copies:
        copy.start()

    def pick(x):
        kept = x[..., places[0] : places[0] + ch]
        for place in places[1:]:
            kept = jnp.where(lax.rem(d * ch, 128) == place, x[..., place : place + ch], kept)
        return kept

    def cut(x, width):
        kept = x[:, :width]
        for k in range(1, n):
            kept = jnp.where(d == k, x[:, k * width : (k + 1) * width], kept)
        return kept

    def column(row):
        return jnp.broadcast_to(row, (8, row.shape[1])).T[:, :1]

    rows, length = mask_ref.shape[0], live_ref.shape[1]
    alive = lengths_ref[0]
    live_ref[...] = (lax.broadcasted_iota(jnp.int32, live_ref.shape, 1) < alive).astype(F32)
    at = lax.broadcasted_iota(jnp.int32, mask_ref.shape, 0) + lax.axis_index("col") * rows
    mask_ref[...] = (at < alive).astype(F32)
    for l in range(LAYERS):
        in_bias, mix_bias, row_ref = outs[l][4], outs[l][5], outs[l][9]
        one = slice(l, l + 1)
        in_bias[:ch] = column(cut(bias_fwd[one], ch))
        in_bias[ch : 2 * ch] = column(cut(bias_bwd[one], ch))
        in_bias[2 * ch :] = column(cut(bias_value[one], hid))
        mix_bias[...] = column(cut(bias_mix[one], hid))
        row_ref[...] = jnp.zeros_like(row_ref)
        for k in range(2):
            lanes = slice(k * ch, (k + 1) * ch)
            row_ref[0:1, lanes] = cut(step_ref[l, k : k + 1], ch)
            row_ref[1:2, lanes] = cut(skip_ref[l, k : k + 1], ch)
    for copy in copies:
        copy.wait()
    for l in range(LAYERS):
        fb_ref, v_ref, mx_ref, out_ref, _, _, decay_ref, b_ref, c_ref, _ = outs[l]
        fb_ref[:, :ch] = pick(win_f[l]).astype(BF)
        fb_ref[:, ch:] = pick(win_b[l]).astype(BF)
        v_ref[...] = win_v[l].astype(BF)
        mx_ref[...] = win_m[l].astype(BF)
        out_ref[...] = win_o[l].astype(BF)
        for k in range(2):
            lanes = slice(k * ch, (k + 1) * ch)
            decay_ref[:, lanes] = pick(win_d[l, k])
            b_ref[:, lanes] = pick(win_i[l, k])
            c_ref[:, lanes] = pick(win_c[l, k])


def assemble_kernel(
    n, in0, in1, mx0, mx1, out0, out1, states_ref, small_ref, norm_ref,
    gain, shift, wf, wb, wv, bf, bb, bv, decay, step, b_in, c_out, skip, wm, bm, wo, bo,
):
    l = pl.program_id(0)
    ch = wf.shape[2] // n
    hid = wv.shape[2] // n
    count = decay.shape[2]
    one = pl.ds(l, 1)
    for i, ref in ((3, gain), (4, shift), (5, bo)):
        ref[one] = norm_ref[one, i]
    for k in range(n):
        narrow, broad = slice(k * ch, (k + 1) * ch), slice(k * hid, (k + 1) * hid)
        for layer, (part_in, part_mx, part_out) in enumerate(((in0, mx0, out0), (in1, mx1, out1))):

            @pl.when(l == layer)
            def _():
                piece = part_in[k].astype(F32)
                wf[0, :, narrow] = piece[:, :ch]
                wb[0, :, narrow] = piece[:, ch : 2 * ch]
                wv[0, :, broad] = piece[:, 2 * ch :]
                wm[0, :, broad] = part_mx[k].astype(F32)
                wo[0, :, broad] = part_out[k].astype(F32)

        piece = states_ref[k].astype(F32)
        for i, ref in enumerate((decay, b_in, c_out)):
            for direction in range(2):
                lanes = slice(direction * ch, (direction + 1) * ch)
                ref[0, direction, :, narrow] = piece[i * count : (i + 1) * count, lanes]
        row = small_ref[k, one]
        bf[one, narrow] = row[:, 0, :ch]
        bb[one, narrow] = row[:, 0, ch : 2 * ch]
        bv[one, broad] = row[:, 0, 2 * ch :]
        bm[one, broad] = row[:, 1, :hid]
        for direction in range(2):
            start = direction * ch
            step[one, direction, narrow] = row[:, 1, hid + start : hid + start + ch]
            skip[one, direction, narrow] = row[:, 2, start : start + ch]


VM = pl.BlockSpec(memory_space=pltpu.VMEM)
ANY = pl.BlockSpec(memory_space=pl.ANY)


def shape(dims, dtype):
    return jax.ShapeDtypeStruct(tuple(dims), dtype)


def sem(*dims):
    return pltpu.SemaphoreType.DMA(dims)


def body(
    tokens_in, lengths, cotangent, norm_gain, norm_shift, w_fwd, w_bwd, w_value, bias_fwd, bias_bwd,
    bias_value, decay_log, step_log, b_input, c_output, skip_gain, w_mix, bias_mix, w_output, bias_output,
):
    n = lax.axis_size("dp")
    m = lax.axis_size("row")
    cols = lax.axis_size("col")
    rows, width = tokens_in.shape
    length = rows * cols
    ch = w_fwd.shape[2] // n
    ch2 = 2 * ch
    hid = w_mix.shape[2] // n
    wide = ch2 + hid
    chans = n * cols * ch
    tokens = n * length
    matrix = transform_matrix(length)
    f_mat = jnp.asarray(matrix, BF)
    ft_mat = jnp.asarray(np.ascontiguousarray(matrix.T), BF)
    states = decay_log.shape[3]
    share = w_fwd.shape[1]
    narrow = -(-(ch + max(k * ch % 128 for k in range(n))) // 128) * 128

    def turned(x):
        return jnp.swapaxes(x, -1, -2)

    per_layer = (
        shape((share, ch2), BF), shape((share, hid), BF), shape((w_mix.shape[1], hid), BF), shape((share, hid), BF),
        shape((wide, 1), F32), shape((hid, 1), F32), *[shape((states, ch2), F32)] * 3, shape((8, ch2), F32),
    )
    own_live, own_mask, *cuts = pl.pallas_call(
        functools.partial(prepare_kernel, n),
        out_shape=(shape((8, length), F32), shape((rows, 1), F32), *per_layer * LAYERS),
        in_specs=[pl.BlockSpec(memory_space=pltpu.SMEM)] + [VM] * 6 + [ANY] * 8,
        out_specs=(VM,) * (2 + len(per_layer) * LAYERS),
        scratch_shapes=[
            pltpu.VMEM((LAYERS, share, narrow), F32), pltpu.VMEM((LAYERS, share, narrow), F32),
            pltpu.VMEM((LAYERS, share, hid), F32), pltpu.VMEM((LAYERS, w_mix.shape[1], hid), F32),
            pltpu.VMEM((LAYERS, share, hid), F32), *[pltpu.VMEM((LAYERS, 2, states, narrow), F32)] * 3, sem(8),
        ],
        compiler_params=pltpu.CompilerParams(vmem_limit_bytes=VMEM_LIMIT),
        name="prepare",
    )(
        lengths, bias_fwd, bias_bwd, bias_value, bias_mix, step_log, skip_gain, w_fwd, w_bwd, w_value, w_mix,
        turned(w_output), turned(decay_log), turned(b_input), turned(c_output),
    )
    given = [cuts[len(per_layer) * l : len(per_layer) * (l + 1)] for l in range(LAYERS)]

    comm = [
        *[sem(n)] * 6, sem(n, n), sem(n, n),
    ]
    sums = [
        pltpu.VMEM((2, rows, width), F32), pltpu.VMEM((n, rows, width), BF), pltpu.VMEM((n, rows, width), BF),
        pltpu.VMEM((n, rows, width), BF), pltpu.VMEM((n - 1, rows, width), BF),
    ]
    saved_shapes = (
        shape((tokens, width), BF), shape((chans, tokens), BF), shape((n, wide, length), F32),
        shape((n, ch2, 2 * length), BF), shape((n, ch2, length), BF), shape((n, hid, length), F32),
        shape((hid, tokens), BF),
    )
    def fwd(layer):
        first = layer == 0
        table = shape((ch2, length), F32)
        mixing = shape((chans, hid), BF)
        extra = (mixing, shape((width, ch2), BF), mixing, shape((n, 8, length), F32), *[table] * 4) if first else ()
        lands = [(m, share, hid), (m, chans // m, hid), (m, share, hid)]
        return pl.pallas_call(
            functools.partial(fwd_kernel, n, m, layer),
            out_shape=(
                shape((rows, width), F32), *saved_shapes, shape((width, wide), BF),
                shape((hid, width), BF), *extra,
            ),
            in_specs=[VM] * (13 + (11 if first else 3)),
            out_specs=(VM, *([ANY] * 7), *([VM] * (2 + len(extra)))),
            scratch_shapes=[
                pltpu.VMEM((wide, width), BF), pltpu.VMEM((2 * n, hid, ch), BF),
                *(pltpu.VMEM(s.shape, s.dtype) for s in saved_shapes),
                pltpu.VMEM((ch2, length), BF), pltpu.VMEM((ch2, 2 * length), F32),
                pltpu.VMEM((ch2, 2 * length), BF), pltpu.VMEM((hid, length), F32), pltpu.VMEM((length, hid), BF),
                pltpu.VMEM((states, 128), F32), pltpu.VMEM((length // LAG, states, 128), F32),
                pltpu.VMEM((n, hid, length), F32),
                *(pltpu.VMEM(s, BF) for s in lands), pltpu.VMEM((width, hid), BF),
                *sums, *comm, *[sem(n, n)] * 4, *[sem(n)] * 4, sem(7, n),
                *[sem(m)] * 6,
                *([pltpu.VMEM((m, share, ch2), BF)] * 2 + [pltpu.VMEM(lands[1], BF)] + [sem(m)] * 6 + [sem(n)] * 2
                  if first else []),
            ],
            compiler_params=pltpu.CompilerParams(
                collective_id=4 if first else 0, has_side_effects=True, vmem_limit_bytes=VMEM_LIMIT
            ),
            name="forward_block",
        )

    def bwd(layer):
        later = layer < LAYERS - 1
        late = (m, width // m, wide)
        out_shape = [
            shape((rows, width), F32), shape(late, BF), shape((chans // m, hid), BF), shape((width // m, hid), BF),
            shape((8, wide), F32), shape((8, hid), F32), shape((8, width), F32), shape((ch2, 2 * length), F32),
        ]
        if later:
            out_shape += [
                shape(late[1:], BF),
                shape((n, chans // m, hid), BF), shape((n, share, hid), BF),
            ]
        return pl.pallas_call(
            functools.partial(bwd_kernel, n, m, layer, later),
            out_shape=tuple(out_shape),
            in_specs=[VM] * 12 + [ANY] * 7 + [VM] * (3 * later),
            out_specs=(*[VM] * (8 + later), *[ANY] * (2 * later)),
            scratch_shapes=[
                pltpu.VMEM((tokens, width), BF),
                *(pltpu.VMEM(s.shape, s.dtype) for s in saved_shapes),
                pltpu.VMEM((wide, tokens), BF), pltpu.VMEM((ch2, length), F32), pltpu.VMEM((hid, tokens), BF),
                pltpu.VMEM((ch2, 2 * length), F32), pltpu.VMEM((ch2, 2 * length), BF), pltpu.VMEM((length, wide), BF),
                pltpu.VMEM((n, n * ch, length), BF), pltpu.VMEM((n, n * ch, length), BF),
                pltpu.VMEM((n * ch, length), F32),
                pltpu.VMEM((n - 1, n, ch, length), BF), pltpu.VMEM((wide, 128), F32), pltpu.VMEM((hid, 128), F32),
                *(pltpu.VMEM((*size, share_rows, hid), BF) for share_rows in (chans // m, share)
                  for size in ((m,), (m - 1,), ())),
                *sums, *comm, sem(n), sem(n), sem(n), sem(n), sem(n), sem(n), sem(7, n),
                sem(m), sem(m), sem(m), sem(m),
                *([pltpu.VMEM((m - 1, *late[1:]), BF), pltpu.VMEM(late[1:], BF), sem(m), sem(m), *[sem(2, n)] * 4, sem(2)]
                  if later else []),
            ],
            compiler_params=pltpu.CompilerParams(
                collective_id=1 + later, has_side_effects=True, vmem_limit_bytes=VMEM_LIMIT
            ),
            name="backward_block",
        )

    residual = tokens_in
    stored = []
    for l in range(LAYERS):
        sh_fb, sh_v, sh_mx, sh_out, in_bias, mix_bias, *tables = given[l]
        first = l == 0
        more = (sh_fb, given[1][0], given[1][2], *tables, *given[1][6:]) if first else (w_next, *spectrum)
        new, *made = fwd(l)(
            residual, norm_gain, norm_shift, own_live if first else mask, own_mask, sh_v, sh_mx if first else mx_next, sh_out, in_bias,
            mix_bias, bias_output, ft_mat, f_mat, *more,
        )
        w_in, w_out = made[7:9]
        if first:
            w_mx, w_next, mx_next, mask, *spectrum = made[9:]
            kernels = spectrum[:2], spectrum[2:]
            spectrum = spectrum[2:]
        stored.append((residual, made[:7], (w_in, w_mx if first else mx_next, w_out), kernels[l]))
        residual = new
    tokens_out = residual.astype(BF)

    grad = cotangent
    parts = [None] * LAYERS
    extra = ()
    for l in reversed(range(LAYERS)):
        resid_in, saved, weights, (kre, kim) = stored[l]
        grad, *parts[l] = bwd(l)(
            grad, resid_in, norm_gain, mask, own_mask, *weights, kre, kim, ft_mat, f_mat, *saved, *extra,
        )
        if l > 0:
            extra = tuple(parts[l][:3])
    part_in, red_mx0, red_out0, in0, mix0, norm0, dk0, late_in, all_mx1, all_out1 = parts[0]
    _, _, _, in1, mix1, norm1, dk1 = parts[1]
    lots = LAYERS * 3 * states
    all_in, all_mx, all_out = (n, share, wide), (n, chans // m, hid), (n, share, hid)
    all_in1, all_mx0, all_out0, all_in0, all_states, all_small, norms = pl.pallas_call(
        functools.partial(finish_kernel, n, m),
        out_shape=(
            shape(all_in, BF), shape(all_mx, BF), shape(all_out, BF), shape(all_in, BF),
            shape((n, m, lots // m, ch2), BF), shape((n, LAYERS, 8, wide), F32), shape((LAYERS, 8, wide), F32),
        ),
        in_specs=[VM] * 21,
        out_specs=(*[ANY] * 5, VM, VM),
        scratch_shapes=[
            pltpu.VMEM((m - 1, share, wide), BF), pltpu.VMEM((share, wide), BF), pltpu.VMEM((share, wide), BF),
            pltpu.VMEM((lots, ch2), F32),
            pltpu.VMEM((m, lots // m, ch2), BF), pltpu.VMEM((m - 1, lots // m, ch2), BF),
            pltpu.VMEM((lots // m, ch2), BF), pltpu.VMEM((m, lots // m, ch2), BF), pltpu.VMEM((length, ch2), F32),
            pltpu.VMEM((LAYERS, 8, wide), F32), pltpu.VMEM((m, LAYERS, 8, wide), F32),
            pltpu.VMEM((n, LAYERS, 8, wide), F32), pltpu.VMEM((LAYERS, 8, wide), F32),
            pltpu.VMEM((LAYERS, 8, wide), F32),
            *[sem(5, n)] * 4, sem(5), *[sem(m)] * 8,
            sem(n), sem(n), pltpu.SemaphoreType.DMA, pltpu.SemaphoreType.DMA,
        ],
        compiler_params=pltpu.CompilerParams(
            collective_id=3, has_side_effects=True, vmem_limit_bytes=VMEM_LIMIT
        ),
        name="finish",
    )(
        part_in, late_in, red_mx0, red_out0, dk0, dk1, in0, in1, mix0, mix1, norm0, norm1,
        *given[0][6:], *given[1][6:], ft_mat,
    )

    def fixed(dims):
        return pl.BlockSpec(tuple(dims), lambda l: (0,) * len(dims))

    def by_layer(dims):
        return pl.BlockSpec((1, *dims), lambda l: (l,) + (0,) * len(dims))

    chan, unit = n * ch, n * hid
    matrices = [(share, chan), (share, chan), (share, unit)]
    layouts = [
        (width,), (width,), *matrices, (chan,), (chan,), (unit,), (2, states, chan), (2, chan), (2, states, chan),
        (2, states, chan), (2, chan), (chans // m, unit), (unit,), (share, unit), (width,),
    ]
    small_out = {0, 1, 5, 6, 7, 9, 12, 14, 16}
    grads = list(pl.pallas_call(
        functools.partial(assemble_kernel, n),
        grid=(LAYERS,),
        out_shape=tuple(shape((LAYERS, *dims), F32) for dims in layouts),
        in_specs=[
            fixed(all_in), fixed(all_in), fixed(all_mx), fixed(all_mx), fixed(all_out), fixed(all_out),
            pl.BlockSpec((n, 3 * states, ch2), lambda l: (0, l, 0)), fixed((n, LAYERS, 8, wide)),
            fixed((LAYERS, 8, wide)),
        ],
        out_specs=tuple(
            fixed((LAYERS, *dims)) if i in small_out else by_layer(dims) for i, dims in enumerate(layouts)
        ),
        compiler_params=pltpu.CompilerParams(vmem_limit_bytes=VMEM_LIMIT),
        name="assemble",
    )(
        all_in0, all_in1, all_mx0, all_mx1, all_out0, all_out1, all_states.reshape(n, lots, ch2), all_small, norms,
    ))
    for i in (8, 10, 11, 15):
        grads[i] = turned(grads[i])
    return (tokens_out, grad, *grads)


def solution(mesh):
    tokens = P(("dp", "row", "col"), None)
    weight = P(None, "row", "col")
    bias = P(None, "col")
    state = P(None, None, "col", None)
    chan = P(None, None, "col")
    in_specs = (
        tokens, P(("dp", "row")), tokens, P(), P(), weight, weight, weight, bias, bias, bias,
        state, chan, state, state, chan, weight, bias, P(None, "col", "row"), P(),
    )
    out_specs = (
        tokens, tokens, P(), P(), weight, weight, weight, bias, bias, bias,
        state, chan, state, state, chan, weight, bias, P(None, "col", "row"), P(),
    )
    return jax.shard_map(body, mesh=mesh, in_specs=in_specs, out_specs=out_specs, check_vma=False)
```

```python
import functools

import jax
import jax.numpy as jnp
import numpy as np
from jax import lax
from jax.experimental import pallas as pl
from jax.experimental.pallas import tpu as pltpu
from jax.sharding import PartitionSpec as P

LAYERS = 2
EPS = 1e-05
LAG = 64
BF = jnp.bfloat16
F32 = jnp.float32
MESH = pl.DeviceIdType.MESH
VMEM_LIMIT = 60 * 1024 * 1024


def transform_matrix(length):
    k = np.arange(length)[:, None]
    t = np.arange(length)[None, :]
    angle = np.pi * (((2 * k + 1) * t) % (4 * length)) / (2 * length)
    return np.concatenate((np.cos(angle), -np.sin(angle)), axis=0)


def gelu_only(v):
    t = jnp.tanh(v * (0.7978845608 + 0.035677408 * v * v))
    return (0.5 * v) * (1.0 + t)


def gelu_parts(v):
    sq = v * v
    t = jnp.tanh(v * (0.7978845608 + 0.035677408 * sq))
    half = 0.5 + 0.5 * t
    slope = half + (v * half) * (1.0 - t) * (0.7978845608 + 0.107032225 * sq)
    return v * half, slope


def dot(a, b, ca, cb):
    return lax.dot_general(a, b, (((ca,), (cb,)), ((), ())), preferred_element_type=F32)


def over_rows(rows, step, work):
    def one(i, unused):
        work(pl.ds(pl.multiple_of(i * step, step), step))
        return unused

    lax.fori_loop(0, rows // step, one, 0)


def lane_sums(x):
    total = x[:, :128]
    for i in range(1, x.shape[1] // 128):
        total = total + x[:, 128 * i : 128 * (i + 1)]
    return total


def as_row(partial):
    return lax.dot_general(
        jnp.ones((8, 128), F32), partial, (((1,), (1,)), ((), ())), precision=lax.Precision.HIGHEST,
        preferred_element_type=F32,
    )


class Place:
    def __init__(self, n, m):
        self.n = n
        self.m = m
        self.d = lax.axis_index("dp")
        self.c = lax.axis_index("col")
        self.r = lax.axis_index("row")

    def greet(self):
        barrier = pltpu.get_barrier_semaphore()

        def hail(device):
            pl.semaphore_signal(barrier, inc=1, device_id=device, device_id_type=MESH)

        for k in range(1, self.n):
            hail({"dp": self.ahead(k)})
        hail({"col": 1 - self.c})

        def one(j, unused):
            hail({"row": self.up(j)})
            return unused

        lax.fori_loop(1, self.m, one, 0)
        pl.semaphore_wait(barrier, self.n + self.m - 1)

    def ahead(self, k):
        return lax.rem(self.d + k, self.n)

    def behind(self, k):
        return lax.rem(self.d - k + self.n, self.n)

    def near(self, k):
        return lax.rem(self.d + k, 2) + 2 * lax.rem(self.d // 2 + k // 2, 2)

    def apart(self, e):
        return lax.rem(self.d + e, 2) + 2 * lax.rem(self.d // 2 + e // 2, 2)

    def up(self, j):
        return lax.rem(self.r + j, self.m)

    def down(self, j):
        return lax.rem(self.r - j + self.m, self.m)

    def other(self, i):
        return i + (i + self.n - self.d) // self.n

    def to_dp(self, src, dst, send, recv, q):
        return pltpu.make_async_remote_copy(
            src, dst, send, recv, device_id={"dp": q}, device_id_type=MESH
        )

    def to_mate(self, src, dst, send, recv):
        return pltpu.make_async_remote_copy(
            src, dst, send, recv, device_id={"col": 1 - self.c}, device_id_type=MESH
        )

    def to_row(self, src, dst, send, recv, q):
        return pltpu.make_async_remote_copy(
            src, dst, send, recv, device_id={"row": q}, device_id_type=MESH
        )


class RowSum:
    def __init__(self, place, part, got, send, recv, hand=None):
        self.place, self.part, self.got, self.send, self.recv, self.hand = place, part, got, send, recv, hand
        self.line = place.m == 4 and hand is not None

    def copy(self, j):
        q = self.place.up(j)
        return self.place.to_row(self.part.at[q], self.got.at[j - 1], self.send.at[j], self.recv.at[j], q)

    def give(self):
        r = self.place.r
        return self.place.to_row(self.part.at[3 - r], self.hand, self.send.at[0], self.recv.at[0], 1 + r // 3)

    def sum_on(self):
        q = self.place.up(2)
        return self.place.to_row(self.hand, self.got.at[1], self.send.at[2], self.recv.at[2], q)

    def outer(self):
        return 1 + 2 * lax.rem(self.place.r, 2)

    def by_place(self, end, middle):
        r = self.place.r
        pl.when(r * (3 - r) == 0)(end)
        pl.when(r * (3 - r) > 0)(middle)

    def each(self, act):
        def one(j, unused):
            act(self.copy(j))
            return unused

        lax.fori_loop(1, self.place.m, one, 0)

    def start(self):
        if not self.line:
            self.each(lambda copy: copy.start())
            return

        def end():
            self.give().start()
            self.got[lax.rem(self.place.r, 2) * 2] = jnp.zeros(self.got.shape[1:], self.got.dtype)

        def middle():
            self.copy(1).start()
            self.copy(3).start()

        self.by_place(end, middle)

    def second(self):
        if self.line:

            def middle():
                self.give().wait_recv()
                mine = self.part[self.place.up(2)].astype(F32)
                self.hand[...] = (self.hand[...].astype(F32) + mine).astype(BF)
                self.sum_on().start()

            def end():
                self.copy(2).start()
                self.copy(self.outer()).start()

            self.by_place(end, middle)

    def total(self):
        if self.line:
            self.copy(2).wait_recv()
            pl.when(self.place.r > 0)(lambda: self.copy(1).wait_recv())
            pl.when(self.place.r < 3)(lambda: self.copy(3).wait_recv())
        else:
            self.each(lambda copy: copy.wait_recv())
        total = self.part[self.place.r].astype(F32)
        if self.place.m <= 4:
            for j in range(1, self.place.m):
                total = total + self.got[j - 1].astype(F32)
            return total
        return lax.fori_loop(1, self.place.m, lambda j, t: t + self.got[j - 1].astype(F32), total)

    def finish(self):
        if not self.line:
            self.each(lambda copy: copy.wait_send())
            return

        def end():
            self.give().wait_send()
            self.copy(2).wait_send()
            self.copy(self.outer()).wait_send()

        def middle():
            self.copy(1).wait_send()
            self.copy(3).wait_send()
            self.sum_on().wait_send()

        self.by_place(end, middle)


class Tokens:
    def __init__(self, place, buf, rows, length, sems):
        self.place, self.buf, self.rows, self.length = place, buf, rows, length
        self.send_p, self.recv_p, self.send_h, self.recv_h, self.send_m, self.recv_m = sems

    def region(self, slot, half=None):
        rows = self.rows // 2 if half is not None else self.rows
        start = slot * self.length + self.place.c * self.rows + (half or 0) * rows
        return self.buf.at[pl.ds(pl.multiple_of(start, rows), rows)]

    def peer(self, i):
        own = self.region(self.place.d)
        return self.place.to_dp(own, own, self.send_p.at[i], self.recv_p.at[i], self.place.near(i))

    def hop(self, i):
        part = self.region(self.place.near(3 - i), i - 1)
        return self.place.to_dp(part, part, self.send_h.at[i], self.recv_h.at[i], self.place.near(i))

    def mate(self, k):
        part = self.region(self.place.near(k))
        return self.place.to_mate(part, part, self.send_m.at[k], self.recv_m.at[k])

    def start(self):
        self.peer(1).start()
        self.peer(2).start()
        self.mate(0).start()

    def own(self):
        self.mate(0).wait_recv()

    def pass_on(self):
        for i in (1, 2):
            self.peer(i).wait_recv()
            self.hop(3 - i).start()
            self.mate(i).start()

    def fetch(self, k):
        @pl.when(k == 3)
        def _():
            self.hop(1).wait_recv()
            self.hop(2).wait_recv()
            self.mate(3).start()

        self.mate(k).wait_recv()

    def finish(self):
        for i in (1, 2):
            self.peer(i).wait_send()
            self.hop(i).wait_send()
        for k in range(4):
            self.mate(k).wait_send()


def norm_stats(residual):
    mean = jnp.mean(residual, axis=1, keepdims=True)
    centered = residual - mean
    variance = jnp.mean(centered * centered, axis=1, keepdims=True)
    inv = lax.rsqrt(variance + EPS)
    return centered * inv, inv


def sum_to_owner(place, rows, mate_out, mate_in, sum_out, sum_in, own, send_m, recv_m, send_p, recv_p):
    def to_mate(slot):
        return place.to_mate(mate_out.at[slot], mate_in.at[slot], send_m.at[slot], recv_m.at[slot])

    def to_owner(slot):
        k = lax.rem(slot - place.d + place.n, place.n)
        return place.to_dp(sum_out.at[slot], sum_in.at[k - 1], send_p.at[k], recv_p.at[k], slot)

    def close(slot, mine):
        to_mate(slot).wait_recv()

        own[mine] = own[mine] + mate_in[slot].astype(F32)

        @pl.when(slot != place.d)
        def _():
            sum_out[slot] = own[mine].astype(BF)
            to_owner(slot).start()

    def receive():
        def one(k, unused):
            to_owner(place.ahead(k)).wait_recv()
            return unused

        lax.fori_loop(1, place.n, one, 0)

    def finish():
        def one(k, unused):
            to_owner(place.ahead(k)).wait_send()
            return unused

        lax.fori_loop(1, place.n, one, 0)

        def two(s, unused):
            to_mate(s).wait_send()
            return unused

        lax.fori_loop(0, place.n, two, 0)

    return to_mate, close, receive, finish


class RowGather:
    def __init__(self, place, shard, land, send, recv):
        self.place, self.shard, self.land, self.send, self.recv = place, shard, land, send, recv
        self.line = place.m == 4

    def copy(self, j):
        place = self.place
        return place.to_row(self.shard, self.land.at[place.r], self.send.at[j], self.recv.at[j], place.up(j))

    def hop(self):
        place = self.place
        part = self.land.at[place.up(2)]
        return place.to_row(
            part, part, self.send.at[0], self.recv.at[self.inner()], lax.rem(3 * place.r + 1, place.m)
        )

    def outer(self):
        return 1 + 2 * lax.rem(self.place.r, 2)

    def inner(self):
        return lax.rem(2 * self.place.r + 3, self.place.m)

    def in_middle(self, act):
        r = self.place.r
        pl.when(r * (3 - r) > 0)(act)

    def each(self, act):
        def one(j, unused):
            act(self.copy(j))
            return unused

        lax.fori_loop(1, self.place.m, one, 0)

    def direct(self):
        self.line = False
        self.first()

    def first(self):
        if self.line:
            self.copy(2).start()
            self.copy(self.outer()).start()
        else:
            self.each(lambda copy: copy.start())
        self.land[self.place.r] = self.shard[...]

    def second(self):
        if self.line:
            self.copy(2).wait_recv()

            def act():
                self.hop().start()
                self.copy(self.inner()).start()

            self.in_middle(act)

    def whole(self):
        if self.line:
            self.copy(1).wait_recv()
            self.copy(3).wait_recv()
        else:
            self.each(lambda copy: copy.wait_recv())
        m, rows, lanes = self.land.shape
        return self.land[...].astype(F32).reshape(m * rows, lanes)

    def finish(self):
        if self.line:
            self.copy(2).wait_send()
            self.copy(self.outer()).wait_send()

            def act():
                self.hop().wait_send()
                self.copy(self.inner()).wait_send()

            self.in_middle(act)
        else:
            self.each(lambda copy: copy.wait_send())


def kernel_spectrum(decay, step, b_in, c_out, skip, sign, ft_ref, rate, lead):
    length = ft_ref.shape[0]
    blocks = length // LAG
    rate[...] = jnp.exp(step) * jnp.exp(decay)
    weight = (1.0 - jnp.exp(-rate[...])) * jnp.exp(-decay) * b_in * c_out
    for b in range(blocks):
        lead[b] = weight * jnp.exp(-(LAG * b) * rate[...])
    lanes = rate.shape[1]
    offs = lax.broadcasted_iota(jnp.int32, (LAG, lanes), 0).astype(F32)

    def state(i, totals):
        powers = jnp.exp(-offs * rate[pl.ds(i, 1)])
        return tuple(totals[b] + powers * lead[b, pl.ds(i, 1)] for b in range(blocks))

    zero = jnp.zeros((LAG, lanes), F32)
    totals = list(lax.fori_loop(0, rate.shape[0], state, (zero,) * blocks, unroll=2))
    at_zero = lax.broadcasted_iota(jnp.int32, (LAG, lanes), 0) == 0
    totals[0] = totals[0] + jnp.where(at_zero, skip, 0.0)
    kernel = jnp.concatenate(totals, axis=0)
    k_hat = dot(kernel.T.astype(BF), ft_ref[...], 1, 0) * (1.0 / length)
    return k_hat[:, :length], k_hat[:, length:] * sign


def direction_sign(ch, rows, lanes, start=0):
    at = lax.broadcasted_iota(jnp.int32, (rows, lanes), 0) + start
    return jnp.where(at < ch, 1.0, -1.0)


def fwd_kernel(
    n, m, layer, res_ref, gain_ref, shift_ref, own_live_ref, own_mask_ref, sh_v, sh_mx, sh_out, in_bias_ref,
    mix_bias_ref, out_bias_ref, ft_ref, f_ref, *rest
):
    first = layer == 0
    if first:
        sh_fb, sh_next, sh_out_next, *rest = rest
        tables, next_tables, rest = rest[:4], rest[4:8], rest[8:]
    else:
        w_fb_ref, kre_ref, kim_ref, *rest = rest
    new_ref, g_out, mx_out, pre_out, u_out, y_out, pm_out, prod_out, w_in_out, w_out_out, w_mx_out, *rest = rest
    if first:
        next_out, out_next_out, mask_ref, kre_ref, kim_ref, kre_next, kim_next, *rest = rest
    else:
        mask_ref = own_live_ref
    (
        w_in_t, w_mx_t, g, mx, pre, u_sp, y, pm, prod, act, spec, y_hat, prod_f, prod_t,
        rate, lead, value_act, land_v, land_mx, land_out, w_out_t,
        own, mate_out, mate_in, sum_out, sum_in,
        send_a, recv_a, send_ah, recv_ah, send_am, recv_am, send_b, recv_b, send_bh, recv_bh, send_bm, recv_bm,
        send_c, recv_c, send_cm, recv_cm, save,
        send_gv, recv_gv, send_gm, recv_gm, send_go, recv_go, *rest,
    ) = rest
    place = Place(n, m)
    d, c = place.d, place.c
    rows, width = res_ref.shape
    length = ft_ref.shape[0]
    hid = sh_mx.shape[1]
    ch2 = kre_ref.shape[0]
    ch = ch2 // 2
    gain, shift, out_bias = (ref[layer : layer + 1] for ref in (gain_ref, shift_ref, out_bias_ref))

    place.greet()
    gather_v = RowGather(place, sh_v, land_v, send_gv, recv_gv)
    gather_mx = RowGather(place, sh_mx, land_mx, send_gm, recv_gm)
    later_weights = (gather_mx, gather_v)
    gather_a = Tokens(place, g, rows, length, (send_a, recv_a, send_ah, recv_ah, send_am, recv_am))
    if first:
        land_fb, land_next, land_out_next, send_gi, recv_gi, send_gn, recv_gn, send_gx, recv_gx, send_mk, recv_mk = rest
        gather_out = RowGather(place, sh_out, land_out, send_go, recv_go)
        gather_out_next = RowGather(place, sh_out_next, land_out_next, send_gx, recv_gx)
        gather_fb = RowGather(place, sh_fb, land_fb, send_gi, recv_gi)
        gather_next = RowGather(place, sh_next, land_next, send_gn, recv_gn)
        gather_fb.direct()

        def mask_peer(k):
            return place.to_dp(
                own_live_ref, mask_ref.at[d], send_mk.at[k], recv_mk.at[k], place.ahead(k)
            )

        for k in range(1, n):
            mask_peer(k).start()
        mask_ref[d] = own_live_ref[...]
    else:
        gather_mx.first()
    base = d * length + c * rows
    xhat, _ = norm_stats(res_ref[...].astype(F32))
    g[pl.ds(pl.multiple_of(base, rows), rows)] = (xhat * gain + shift).astype(BF)
    gather_a.start()

    def spectra(given, re_ref, im_ref):
        decay_ref, b_ref, c_ref, row_ref = given
        for j in range(ch2 // 128):
            at = slice(128 * j, 128 * (j + 1))
            re_ref[at], im_ref[at] = kernel_spectrum(
                decay_ref[:, at], row_ref[0:1, at], b_ref[:, at], c_ref[:, at], row_ref[1:2, at],
                direction_sign(ch, 128, length, 128 * j), ft_ref, rate, lead,
            )

    if first:
        spectra(tables, kre_ref, kim_ref)
    if first:
        w_fb = gather_fb.whole()
        gather_mx.first()
        for k in range(1, n):
            mask_peer(k).wait_recv()
    else:
        w_fb = w_fb_ref[...].astype(F32)
    w_in_out[:, :ch2] = w_fb.astype(BF)
    w_in_t[:ch2] = w_fb.T.astype(BF)
    gather_a.own()

    def chunk(owner, slot):
        at = pl.ds(pl.multiple_of((c * n + owner) * ch, ch), ch)
        return mx.at[at, pl.ds(pl.multiple_of(slot * length, length), length)]

    def turn(k, j):
        return place.near(k ^ j)

    def half_chunk(owner, slot, half):
        at = pl.ds(pl.multiple_of((c * n + owner) * ch + half * (ch // 2), ch // 2), ch // 2)
        return mx.at[at, pl.ds(pl.multiple_of(slot * length, length), length)]

    def peer_b(i, j):
        part = chunk(d, turn(0, j))
        return place.to_dp(part, part, send_b.at[j, i], recv_b.at[j, i], place.near(i))

    def hop_b(i, j):
        part = half_chunk(place.near(3 - i), turn(3 - i, j), i - 1)
        return place.to_dp(part, part, send_bh.at[j, i], recv_bh.at[j, i], place.near(i))

    def mate_b(k, j):
        part = chunk(place.near(k), turn(k, j))
        return place.to_mate(part, part, send_bm.at[j, k], recv_bm.at[j, k])

    def saves(slot, item):
        lanes = pl.ds(pl.multiple_of(slot * length, length), length)
        src, dst = (
            lambda: (g.at[lanes], g_out.at[lanes]),
            lambda: (u_sp.at[slot], u_out.at[slot]),
            lambda: (y.at[slot], y_out.at[slot]),
            lambda: (pre.at[slot], pre_out.at[slot]),
            lambda: (mx.at[:, lanes], mx_out.at[:, lanes]),
            lambda: (pm.at[slot], pm_out.at[slot]),
            lambda: (prod.at[:, lanes], prod_out.at[:, lanes]),
        )[item]()
        return pltpu.make_async_copy(src, dst, save.at[item, slot])

    def scan_slot(i, unused):
        slot = place.near(i)

        @pl.when(i == 1)
        def _():
            gather_a.pass_on()

        @pl.when(i > 0)
        def _():
            gather_a.fetch(i)

        @pl.when(i == (n - 1 if first else n - 2))
        def _():
            gather_mx.second()
            gather_v.first()

        lanes = pl.ds(pl.multiple_of(slot * length, length), length)
        live = mask_ref[slot, 0:1]
        v = dot(w_in_t[:ch2], g[lanes], 1, 1) + in_bias_ref[:ch2]
        pre[slot, :ch2] = v
        act[...] = (gelu_only(v) * live).astype(BF)
        spec[...] = dot(act[...], ft_ref[...], 1, 0)
        u_re, u_im = spec[:, :length], spec[:, length:]
        k_re, k_im = kre_ref[...], kim_ref[...]
        u_sp[slot, :, :length] = u_re.astype(BF)
        u_sp[slot, :, length:] = u_im.astype(BF)
        y_hat[:, :length] = (k_re * u_re - k_im * u_im).astype(BF)
        y_hat[:, length:] = (k_re * u_im + k_im * u_re).astype(BF)
        both = dot(y_hat[...], f_ref[...], 1, 0)
        y[slot] = both.astype(BF)
        mine = pl.ds(pl.multiple_of((c * n + d) * ch, ch), ch)
        mx[mine, lanes] = (both[:ch] * both[ch:]).astype(BF)
        for j in range(n):

            @pl.when(i == j)
            def _():
                peer_b(1, j).start()
                peer_b(2, j).start()
                mate_b(0, j).start()

        for item in range(3):
            saves(slot, item).start()
        return unused

    lax.fori_loop(0, n, scan_slot, 0)

    def pass_b(j):
        for i in (1, 2):
            peer_b(i, j).wait_recv()
            hop_b(3 - i, j).start()
            mate_b(i, j).start()

    pass_b(0)
    if first:
        spectra(next_tables, kre_next, kim_next)
    else:
        gather_v.second()
    pass_b(1)
    w_mx = gather_mx.whole()
    w_mx_out[...] = w_mx.astype(BF)
    for block in range(2 * n):
        w_mx_t[block] = w_mx[block * ch : (block + 1) * ch].T.astype(BF)
    def value_slot(slot, unused):
        tokens = pl.ds(pl.multiple_of(slot * length, length), length)
        value = dot(w_in_t[ch2:], g[tokens], 1, 1) + in_bias_ref[ch2:]
        pre[slot, ch2:] = value
        value_act[slot] = gelu_only(value)
        saves(slot, 3).start()
        return unused

    begun = set()

    def mix_in(k, j):
        owner, slot = place.near(k), turn(k, j)
        lanes = pl.ds(pl.multiple_of(slot * length, length), length)
        mate_b(k, j).wait_recv()
        total = None
        for side in range(2):
            rows_at = pl.ds(pl.multiple_of((side * n + owner) * ch, ch), ch)
            part = dot(w_mx_t[side * n + owner], mx[rows_at, lanes], 1, 0)
            total = part if total is None else total + part
        pm[slot] = (pm[slot] if k ^ j in begun else mix_bias_ref[...]) + total
        begun.add(k ^ j)

    def across(j):
        hop_b(1, j).wait_recv()
        hop_b(2, j).wait_recv()
        mate_b(3, j).start()
        mix_in(3, j)

    for j in range(n):
        for k in range(3):
            mix_in(k, j)
        if j + 2 < n:
            pass_b(j + 2)
        if j == 0 and first:
            gather_v.second()
            gather_out.first()
        if j == 2 and first:
            gather_out.second()
            gather_next.first()
        if j == n - 1:
            w_v = gather_v.whole()
            w_in_out[:, ch2:] = w_v.astype(BF)
            w_in_t[ch2:] = w_v.T.astype(BF)
            lax.fori_loop(0, n, value_slot, 0)
        if j > 0:
            across(j - 1)
    across(n - 1)
    w_out = gather_out.whole() if first else sh_out[...].astype(F32)
    w_out_t[...] = w_out.astype(BF)
    w_out_out[...] = w_out.T.astype(BF)

    to_mate, close, receive, finish_c = sum_to_owner(
        place, rows, mate_out, mate_in, sum_out, sum_in, own, send_cm, recv_cm, send_c, recv_c
    )

    def order(i):
        return lax.select(i == n - 1, d, place.other(i))

    def hidden_slot(i, unused):
        if first:

            @pl.when(i == 1)
            def _():
                gather_next.second()
                gather_out_next.first()

        slot = order(i)
        lanes = pl.ds(pl.multiple_of(slot * length, length), length)
        v = pm[slot]
        product = gelu_only(v) * value_act[slot]
        prod_f[...] = product
        prod[:, lanes] = product.astype(BF)
        prod_t[...] = prod_f[...].T.astype(BF)
        for item in range(4, 7):
            saves(slot, item).start()
        theirs = pl.ds(pl.multiple_of((1 - c) * rows, rows), rows)
        ours = pl.ds(pl.multiple_of(c * rows, rows), rows)
        mate_out[slot] = dot(prod_t[theirs], w_out_t[...], 1, 1).astype(BF)
        to_mate(slot).start()

        @pl.when(i > 0)
        def _():
            close(order(i - 1), lax.rem(i - 1, 2))

        own[lax.rem(i, 2)] = dot(prod_t[ours], w_out_t[...], 1, 1)
        return unused

    lax.fori_loop(0, n, hidden_slot, 0)
    last = (n - 1) % 2
    close(d, last)
    if first:
        gather_out_next.second()
    receive()

    total = own[last]
    for k in range(1, n):
        total = total + sum_in[k - 1].astype(F32)
    new_ref[...] = res_ref[...].astype(F32) + own_mask_ref[...] * (total + out_bias)
    gather_a.finish()
    finish_c()
    for gather in later_weights:
        gather.finish()
    if first:
        next_out[...] = gather_next.whole().astype(BF)
        out_next_out[...] = gather_out_next.whole().astype(BF)
        gather_out.finish()
        gather_out_next.finish()
        gather_next.finish()
        gather_fb.finish()
        for k in range(1, n):
            mask_peer(k).wait_send()

    for j in range(n):
        for i in (1, 2):
            peer_b(i, j).wait_send()
            hop_b(i, j).wait_send()
        for k in range(n):
            mate_b(k, j).wait_send()

    def drain(slot, unused):
        for item in range(7):
            saves(slot, item).wait()
        return unused

    lax.fori_loop(0, n, drain, 0)


def bwd_kernel(
    n, m, layer, later, grad_ref, res_ref, gain_ref, mask_ref, own_mask_ref, w_in_ref, w_mx_ref, w_out_ref, kre_ref,
    kim_ref, ft_ref, f_ref, g_in, mx_in, pre_in, u_in, y_in, pm_in, prod_in, *rest
):
    if later:
        late_part, red_mx1, red_out1, *rest = rest
    (new_ref, gw_in_ref, red_mx_ref, red_out_ref, in_row_ref, mix_row_ref, norm_sum_ref, dk_ref, *rest) = rest
    if later:
        red_late_ref, all_mx, all_out, *rest = rest
    (
        gb, g, mx, pre, u_sp, y, pm, prod, gpre, gpre_f, gpm, spec, hat, turned,
        mix_sum, mix_mate, mix_own, mix_got, in_sum, mix_acc, part_mx, got_mx, hand_mx, part_out, got_out, hand_out,
        own, mate_out, mate_in, sum_out, sum_in,
        send_a, recv_a, send_ah, recv_ah, send_am, recv_am, send_b, recv_b, send_bm, recv_bm, send_c, recv_c, send_cm, recv_cm, load,
        send_rm, recv_rm, send_ro, recv_ro, *rest,
    ) = rest
    place = Place(n, m)
    d, c = place.d, place.c
    rows, width = res_ref.shape
    length = ft_ref.shape[0]
    hid = w_mx_ref.shape[1]
    ch2 = kre_ref.shape[0]
    ch = ch2 // 2
    half = n * ch

    def loads(slot, item):
        lanes = pl.ds(pl.multiple_of(slot * length, length), length)
        src, dst = (
            lambda: (pre_in.at[slot], pre.at[slot]),
            lambda: (pm_in.at[slot], pm.at[slot]),
            lambda: (y_in.at[slot], y.at[slot]),
            lambda: (u_in.at[slot], u_sp.at[slot]),
            lambda: (prod_in.at[:, lanes], prod.at[:, lanes]),
            lambda: (mx_in.at[:, lanes], mx.at[:, lanes]),
            lambda: (g_in.at[lanes], g.at[lanes]),
        )[item]()
        return pltpu.make_async_copy(src, dst, load.at[item, slot])

    for item in range(7):
        loads(d, item).start()

    def start_loads(i, unused):
        for item in range(7):
            loads(place.other(i), item).start()
        return unused

    lax.fori_loop(0, n - 1, start_loads, 0)

    place.greet()
    gather_a = Tokens(place, gb, rows, length, (send_a, recv_a, send_ah, recv_ah, send_am, recv_am))
    base = d * length + c * rows
    gain = gain_ref[layer : layer + 1]
    first = grad_ref[...].astype(F32) * own_mask_ref[...]
    gb[pl.ds(pl.multiple_of(base, rows), rows)] = first.astype(BF)
    gather_a.start()
    sum_mx = RowSum(place, part_mx, got_mx, send_rm, recv_rm, hand_mx)
    sum_out_w = RowSum(place, part_out, got_out, send_ro, recv_ro, hand_out)
    row_sums = [sum_mx, sum_out_w]
    if later:
        got_late, hand_late, send_rl, recv_rl, *sems = rest
        sum_late = RowSum(place, late_part, got_late, send_rl, recv_rl, hand_late)
        sum_late.start()
        row_sums.append(sum_late)
    norm_sum_ref[...] = jnp.zeros_like(norm_sum_ref)
    norm_sum_ref[2:3] = jnp.sum(first, axis=0, keepdims=True)
    in_sum[...] = jnp.zeros_like(in_sum)
    mix_acc[...] = jnp.zeros_like(mix_acc)
    dk_ref[...] = jnp.zeros_like(dk_ref)
    gather_a.own()

    def mate_b(slot):
        return place.to_mate(mix_sum.at[slot], mix_mate.at[slot], send_bm.at[slot], recv_bm.at[slot])

    def peer_b(k, slot):
        q = place.ahead(k)
        part = mix_sum.at[slot, pl.ds(pl.multiple_of(q * ch, ch), ch)]
        return place.to_dp(part, mix_got.at[k - 1, slot], send_b.at[slot, k], recv_b.at[slot, k], q)

    def hidden_slot(i, unused):
        slot = lax.select(i == 0, d, place.other(i - 1))

        @pl.when(i == 1)
        def _():
            gather_a.pass_on()

        @pl.when(i > 0)
        def _():
            gather_a.fetch(place.apart(slot))

        if later:
            pl.when(i == n - 2)(sum_late.second)


        lanes = pl.ds(pl.multiple_of(slot * length, length), length)
        mix_own[:hid] = dot(w_out_ref[...], gb[lanes], 1, 1)
        for item in range(2):
            loads(slot, item).wait()
        gated, slope = gelu_parts(pm[slot])
        value, value_slope = gelu_parts(pre[slot, ch2:])
        now = mix_own[:hid]
        to_value = now * gated * value_slope
        to_mix = now * value * slope
        gpre[ch2:, lanes] = to_value.astype(BF)
        gpm[:, lanes] = to_mix.astype(BF)
        in_sum[ch2:] = in_sum[ch2:] + lane_sums(to_value)
        mix_acc[...] = mix_acc[...] + lane_sums(to_mix)
        theirs = pl.ds(pl.multiple_of((1 - c) * half, half), half)
        ours = pl.ds(pl.multiple_of(c * half, half), half)
        mix_sum[slot] = dot(w_mx_ref[theirs], gpm[:, lanes], 1, 0).astype(BF)
        mate_b(slot).start()
        mix_own[...] = dot(w_mx_ref[ours], gpm[:, lanes], 1, 0)
        mate_b(slot).wait()
        mix_sum[slot] = (mix_own[...] + mix_mate[slot].astype(F32)).astype(BF)
        for k in range(1, n):
            peer_b(k, slot).start()
        return unused

    lax.fori_loop(0, n, hidden_slot, 0)

    def wait_loads(slot, unused):
        for item in range(2, 7):
            loads(slot, item).wait()
        return unused

    lax.fori_loop(0, n, wait_loads, 0)
    share = mx.shape[0] // m

    def grad_mix(q, unused):
        part_mx[q] = dot(mx[pl.ds(pl.multiple_of(q * share, share), share)], gpm[...], 1, 1).astype(BF)
        return unused

    lax.fori_loop(0, m, grad_mix, 0)
    sum_mx.start()
    gw_out = dot(prod[...], gb[...], 1, 0).T
    part_out[...] = gw_out.reshape(m, width // m, hid).astype(BF)
    sum_out_w.start()
    spreads = []
    if later:
        spreads = [
            Spread(place, red_mx1, all_mx, sems, 0),
            Spread(place, red_out1, all_out, sems, 1),
        ]

    to_mate, close, receive, finish_c = sum_to_owner(
        place, rows, mate_out, mate_in, sum_out, sum_in, own, send_cm, recv_cm, send_c, recv_c
    )

    def order(i):
        return lax.select(i == n - 1, d, place.other(i))

    def scan_slot(i, unused):
        slot = order(i)
        lanes = pl.ds(pl.multiple_of(slot * length, length), length)
        for k in range(1, n):
            peer_b(k, slot).wait_recv()

        @pl.when(i == n - 2)
        def _():
            for each in spreads:
                each.start()

        @pl.when(i == n - 2)
        def _():
            sum_mx.second()
            sum_out_w.second()

        total = mix_sum[slot, pl.ds(pl.multiple_of(d * ch, ch), ch)].astype(F32)
        for k in range(1, n):
            total = total + mix_got[k - 1, slot].astype(F32)
        hat[:ch, :length] = (total * y[slot, ch:].astype(F32)).astype(BF)
        hat[ch:, :length] = (total * y[slot, :ch].astype(F32)).astype(BF)
        spec[...] = dot(hat[:, :length], ft_ref[...], 1, 0)
        g_re, g_im = spec[:, :length], spec[:, length:]
        k_re, k_im = kre_ref[...], kim_ref[...]
        hat[:, :length] = (k_re * g_re + k_im * g_im).astype(BF)
        hat[:, length:] = (k_re * g_im - k_im * g_re).astype(BF)
        u_re, u_im = u_sp[slot, :, :length].astype(F32), u_sp[slot, :, length:].astype(F32)
        dk_ref[:, :length] = dk_ref[:, :length] + (u_re * g_re + u_im * g_im)
        dk_ref[:, length:] = dk_ref[:, length:] + (u_re * g_im - u_im * g_re)
        spec[:, :length] = dot(hat[...], f_ref[...], 1, 0)
        live = mask_ref[slot, 0:1]
        _, slope = gelu_parts(pre[slot, :ch2])
        part = spec[:, :length] * slope * live
        gpre_f[...] = part
        gpre[:ch2, lanes] = part.astype(BF)
        in_sum[:ch2] = in_sum[:ch2] + lane_sums(part)
        turned[:, :ch2] = gpre_f[...].T.astype(BF)
        gpre_f[...] = gpre[ch2:, lanes].astype(F32)
        turned[:, ch2:] = gpre_f[...].T.astype(BF)
        theirs = pl.ds(pl.multiple_of((1 - c) * rows, rows), rows)
        ours = pl.ds(pl.multiple_of(c * rows, rows), rows)
        mate_out[slot] = dot(turned[theirs], w_in_ref[...], 1, 1).astype(BF)
        to_mate(slot).start()

        @pl.when(i > 0)
        def _():
            close(order(i - 1), lax.rem(i - 1, 2))

        own[lax.rem(i, 2)] = dot(turned[ours], w_in_ref[...], 1, 1)
        return unused

    lax.fori_loop(0, n, scan_slot, 0)
    last = (n - 1) % 2
    close(d, last)

    def grad_in(r):
        part = dot(gpre[r], g[...], 1, 0).T
        gw_in_ref[:, :, r] = part.reshape(m, width // m, part.shape[1]).astype(BF)

    over_rows(gpre.shape[0], 128, grad_in)
    for each in spreads:
        each.pass_on()
    in_row_ref[...] = as_row(in_sum[...])
    mix_row_ref[...] = as_row(mix_acc[...])
    if later:
        red_late_ref[...] = sum_late.total().astype(BF)
    receive()
    total = own[last]
    for k in range(1, n):
        total = total + sum_in[k - 1].astype(F32)
    xhat, inv = norm_stats(res_ref[...].astype(F32))
    h = total * gain
    middle = jnp.mean(h, axis=1, keepdims=True)
    along = jnp.mean(h * xhat, axis=1, keepdims=True)
    new_ref[...] = grad_ref[...].astype(F32) + inv * (h - middle - xhat * along)
    norm_sum_ref[0:1] = jnp.sum(total * xhat, axis=0, keepdims=True)
    norm_sum_ref[1:2] = jnp.sum(total, axis=0, keepdims=True)
    red_mx_ref[...] = sum_mx.total().astype(BF)
    red_out_ref[...] = sum_out_w.total().astype(BF)
    gather_a.finish()
    finish_c()
    for row_sum in row_sums:
        row_sum.finish()
    for each in spreads:
        each.wait()

    def drain(slot, unused):
        for k in range(1, n):
            peer_b(k, slot).wait_send()
        return unused

    lax.fori_loop(0, n, drain, 0)


class Spread:
    def __init__(self, place, src, out, sems, item):
        self.place, self.src, self.out, self.item = place, src, out, item
        self.send, self.recv, self.send_h, self.recv_h, self.keep = sems
        rows = src.shape[0]
        whole = len(src.shape) == 2 and rows % 32 != 0
        half = rows if whole else rows // 2
        self.pieces = [(i, start, half) for i, start in ((1, 0), (2, half)) if start < rows]

    def peer(self, i):
        place, item = self.place, self.item
        return place.to_dp(
            self.src, self.out.at[place.d], self.send.at[item, i], self.recv.at[item, i], place.near(i)
        )

    def hop(self, i, start, count):
        place, item = self.place, self.item
        part = self.out.at[place.near(3 - i), pl.ds(start, count)]
        return place.to_dp(part, part, self.send_h.at[item, i], self.recv_h.at[item, i], place.near(i))

    def local(self):
        return pltpu.make_async_copy(self.src, self.out.at[self.place.d], self.keep.at[self.item])

    def start(self):
        self.peer(1).start()
        self.peer(2).start()
        self.local().start()

    def pass_on(self):
        self.peer(1).wait_recv()
        self.peer(2).wait_recv()
        for piece in self.pieces:
            self.hop(*piece).start()

    def wait(self):
        for piece in self.pieces:
            self.hop(*piece).wait()
        self.peer(1).wait_send()
        self.peer(2).wait_send()
        self.local().wait()


def state_grads(dk_re, dk_im, sign, ft_ref, decay, step, b_in, c_out, lag_sums):
    length = ft_ref.shape[0]
    re = dk_re.astype(BF)
    im = (dk_im * sign).astype(BF)
    lag_sums[...] = (dot(ft_ref[:, :length], re, 1, 1) + dot(ft_ref[:, length:], im, 1, 1)) * (1.0 / length)
    rate = jnp.exp(step) * jnp.exp(decay)
    a = jnp.exp(-rate)

    totals, slopes = [], []
    for lanes in (slice(0, 256), slice(256, a.shape[1])):
        base = a[:, lanes]

        def lag(i, carry, base=base, lanes=lanes):
            total, slope = carry
            row = lag_sums[pl.ds(length - 1 - i, 1)][:, lanes]
            return total * base + row, slope * base + total

        zero = jnp.zeros_like(base)
        total, slope = lax.fori_loop(0, length, lag, (zero, zero), unroll=4)
        totals.append(total)
        slopes.append(slope)
    total, slope = jnp.concatenate(totals, axis=1), jnp.concatenate(slopes, axis=1)
    inv_decay = jnp.exp(-decay)
    gain = (1.0 - a) * inv_decay
    b_disc = gain * b_in
    to_b = c_out * total
    to_rate = a * (to_b * inv_decay * b_in - (c_out * b_disc) * slope)
    through = to_rate * rate
    return (
        through - to_b * b_disc, to_b * gain, b_disc * total,
        jnp.sum(through, axis=0, keepdims=True), lag_sums[0:1],
    )


def finish_kernel(
    n, m, part_in, late_in, red_mx0, red_out0, dk0, dk1, in0, in1, mix0, mix1, norm0, norm1,
    decay0, b0, c0, row0, decay1, b1, c1, row1, ft_ref,
    all_in1, all_mx0, all_out0, all_in0, all_states, all_small, norm_ref,
    got_in, hand_in, red_in0, states, part_s, got_s, red_s, full_s, lag_sums, small, row_small, dp_small, norm_own, norm_got,
    send_w, recv_w, send_wh, recv_wh, keep_w, send_ri, recv_ri, send_rs, recv_rs, send_gs, recv_gs, send_sm, recv_sm,
    send_ds, recv_ds, send_n, recv_n,
):
    place = Place(n, m)
    d, r = place.d, place.r
    states_n, ch2 = decay0.shape
    place.greet()
    sum_in = RowSum(place, part_in, got_in, send_ri, recv_ri, hand_in)
    sum_in.start()
    spreads = [
        Spread(place, src, out, (send_w, recv_w, send_wh, recv_wh, keep_w), item)
        for item, (src, out) in enumerate(
            ((late_in, all_in1), (red_mx0, all_mx0), (red_out0, all_out0), (red_in0, all_in0), (full_s, all_states))
        )
    ]
    for each in spreads[:3]:
        each.start()

    small[...] = jnp.zeros_like(small)
    for l, (in_row, mix_row, norm) in enumerate(((in0, mix0, norm0), (in1, mix1, norm1))):
        small[l, 0:1] = in_row[0:1]
        small[l, 1:2, :ch2] = mix_row[0:1]
        small[l, 3:6] = norm[0:3]
    length = ft_ref.shape[0]
    for l, (dk, decay, b_in, c_out, row) in enumerate(((dk0, decay0, b0, c0, row0), (dk1, decay1, b1, c1, row1))):
        grads = state_grads(
            dk[:, :length], dk[:, length:], direction_sign(ch2 // 2, ch2, length), ft_ref, decay[...], row[0:1],
            b_in[...], c_out[...], lag_sums,
        )
        for i in range(3):
            states[pl.ds((3 * l + i) * states_n, states_n)] = grads[i]
        small[l, 1:2, ch2:] = grads[3]
        small[l, 2:3, :ch2] = grads[4]
        if l == 0:
            sum_in.second()
            spreads[0].pass_on()
    spreads[1].pass_on()
    share = states.shape[0] // m
    for q in range(m):
        part_s[q] = states[q * share : (q + 1) * share].astype(BF)
    sum_s = RowSum(place, part_s, got_s, send_rs, recv_rs)
    sum_s.start()
    row_small[r] = small[...]

    def small_row(j):
        return place.to_row(row_small.at[r], row_small.at[r], send_sm.at[j], recv_sm.at[j], place.up(j))

    def repeat(work, count):
        def one(j, unused):
            work(j)
            return unused

        lax.fori_loop(1, count, one, 0)

    repeat(lambda j: small_row(j).start(), m)

    red_in0[...] = sum_in.total().astype(BF)
    spreads[3].start()
    spreads[2].pass_on()
    red_s[...] = sum_s.total().astype(BF)
    full_s[r] = red_s[...]

    def state_row(j):
        return place.to_row(full_s.at[r], full_s.at[r], send_gs.at[j], recv_gs.at[j], place.up(j))

    repeat(lambda j: state_row(j).start(), m)
    repeat(lambda j: small_row(j).wait_recv(), m)
    total = row_small[0]
    for q in range(1, m):
        total = total + row_small[q]
    dp_small[d] = total

    def small_dp(k):
        return place.to_dp(dp_small.at[d], dp_small.at[d], send_ds.at[k], recv_ds.at[k], place.ahead(k))

    for k in range(1, n):
        small_dp(k).start()
    repeat(lambda j: state_row(j).wait_recv(), m)

    spreads[4].start()
    spreads[3].pass_on()
    for k in range(1, n):
        small_dp(k).wait_recv()
    total = dp_small[0]
    for q in range(1, n):
        total = total + dp_small[q]
    norm_own[...] = total
    swap = place.to_mate(norm_own, norm_got, send_n, recv_n)
    swap.start()
    all_small[...] = dp_small[...]
    swap.wait_recv()
    norm_ref[...] = norm_own[...] + norm_got[...]
    swap.wait_send()
    spreads[4].pass_on()
    for each in spreads:
        each.wait()
    for k in range(1, n):
        small_dp(k).wait_send()
    repeat(lambda j: small_row(j).wait_send(), m)
    repeat(lambda j: state_row(j).wait_send(), m)
    sum_in.finish()
    sum_s.finish()


def prepare_kernel(
    n, lengths_ref, bias_fwd, bias_bwd, bias_value, bias_mix, step_ref, skip_ref, *rest
):
    d = lax.axis_index("dp")
    w_fwd, w_bwd, w_value, w_mix, w_out, decay, b_in, c_out, live_ref, mask_ref, *rest = rest
    per = 10
    outs = [rest[per * l : per * (l + 1)] for l in range(LAYERS)]
    win_f, win_b, win_v, win_m, win_o, win_d, win_i, win_c, load = rest[per * LAYERS :]
    ch = w_fwd.shape[2] // n
    hid = w_value.shape[2] // n
    size = win_f.shape[2]
    places = sorted({(k * ch) % 128 for k in range(n)})

    def window(width, wide):
        start = pl.multiple_of((d * width) // 128 * 128, 128)
        return pl.ds(start, wide)

    narrow, broad = window(ch, size), window(hid, hid)
    copies = [
        pltpu.make_async_copy(src.at[at], dst, load.at[i])
        for i, (src, at, dst) in enumerate((
            (w_fwd, (slice(None), slice(None), narrow), win_f), (w_bwd, (slice(None), slice(None), narrow), win_b),
            (decay, (slice(None), slice(None), slice(None), narrow), win_d),
            (b_in, (slice(None), slice(None), slice(None), narrow), win_i),
            (c_out, (slice(None), slice(None), slice(None), narrow), win_c),
            (w_value, (slice(None), slice(None), broad), win_v), (w_mix, (slice(None), slice(None), broad), win_m),
            (w_out, (slice(None), slice(None), broad), win_o),
        ))
    ]
    for copy in copies:
        copy.start()

    def pick(x):
        kept = x[..., places[0] : places[0] + ch]
        for place in places[1:]:
            kept = jnp.where(lax.rem(d * ch, 128) == place, x[..., place : place + ch], kept)
        return kept

    def cut(x, width):
        kept = x[:, :width]
        for k in range(1, n):
            kept = jnp.where(d == k, x[:, k * width : (k + 1) * width], kept)
        return kept

    def column(row):
        return jnp.broadcast_to(row, (8, row.shape[1])).T[:, :1]

    rows, length = mask_ref.shape[0], live_ref.shape[1]
    alive = lengths_ref[0]
    live_ref[...] = (lax.broadcasted_iota(jnp.int32, live_ref.shape, 1) < alive).astype(F32)
    at = lax.broadcasted_iota(jnp.int32, mask_ref.shape, 0) + lax.axis_index("col") * rows
    mask_ref[...] = (at < alive).astype(F32)
    for l in range(LAYERS):
        in_bias, mix_bias, row_ref = outs[l][4], outs[l][5], outs[l][9]
        one = slice(l, l + 1)
        in_bias[:ch] = column(cut(bias_fwd[one], ch))
        in_bias[ch : 2 * ch] = column(cut(bias_bwd[one], ch))
        in_bias[2 * ch :] = column(cut(bias_value[one], hid))
        mix_bias[...] = column(cut(bias_mix[one], hid))
        row_ref[...] = jnp.zeros_like(row_ref)
        for k in range(2):
            lanes = slice(k * ch, (k + 1) * ch)
            row_ref[0:1, lanes] = cut(step_ref[l, k : k + 1], ch)
            row_ref[1:2, lanes] = cut(skip_ref[l, k : k + 1], ch)
    for copy in copies:
        copy.wait()
    for l in range(LAYERS):
        fb_ref, v_ref, mx_ref, out_ref, _, _, decay_ref, b_ref, c_ref, _ = outs[l]
        fb_ref[:, :ch] = pick(win_f[l]).astype(BF)
        fb_ref[:, ch:] = pick(win_b[l]).astype(BF)
        v_ref[...] = win_v[l].astype(BF)
        mx_ref[...] = win_m[l].astype(BF)
        out_ref[...] = win_o[l].astype(BF)
        for k in range(2):
            lanes = slice(k * ch, (k + 1) * ch)
            decay_ref[:, lanes] = pick(win_d[l, k])
            b_ref[:, lanes] = pick(win_i[l, k])
            c_ref[:, lanes] = pick(win_c[l, k])


def assemble_kernel(
    n, in0, in1, mx0, mx1, out0, out1, states_ref, small_ref, norm_ref,
    gain, shift, wf, wb, wv, bf, bb, bv, decay, step, b_in, c_out, skip, wm, bm, wo, bo,
):
    l = pl.program_id(0)
    ch = wf.shape[2] // n
    hid = wv.shape[2] // n
    count = decay.shape[2]
    one = pl.ds(l, 1)
    for i, ref in ((3, gain), (4, shift), (5, bo)):
        ref[one] = norm_ref[one, i]
    for k in range(n):
        narrow, broad = slice(k * ch, (k + 1) * ch), slice(k * hid, (k + 1) * hid)
        for layer, (part_in, part_mx, part_out) in enumerate(((in0, mx0, out0), (in1, mx1, out1))):

            @pl.when(l == layer)
            def _():
                piece = part_in[k].astype(F32)
                wf[0, :, narrow] = piece[:, :ch]
                wb[0, :, narrow] = piece[:, ch : 2 * ch]
                wv[0, :, broad] = piece[:, 2 * ch :]
                wm[0, :, broad] = part_mx[k].astype(F32)
                wo[0, :, broad] = part_out[k].astype(F32)

        piece = states_ref[k].astype(F32)
        for i, ref in enumerate((decay, b_in, c_out)):
            for direction in range(2):
                lanes = slice(direction * ch, (direction + 1) * ch)
                ref[0, direction, :, narrow] = piece[i * count : (i + 1) * count, lanes]
        row = small_ref[k, one]
        bf[one, narrow] = row[:, 0, :ch]
        bb[one, narrow] = row[:, 0, ch : 2 * ch]
        bv[one, broad] = row[:, 0, 2 * ch :]
        bm[one, broad] = row[:, 1, :hid]
        for direction in range(2):
            start = direction * ch
            step[one, direction, narrow] = row[:, 1, hid + start : hid + start + ch]
            skip[one, direction, narrow] = row[:, 2, start : start + ch]


VM = pl.BlockSpec(memory_space=pltpu.VMEM)
ANY = pl.BlockSpec(memory_space=pl.ANY)


def shape(dims, dtype):
    return jax.ShapeDtypeStruct(tuple(dims), dtype)


def sem(*dims):
    return pltpu.SemaphoreType.DMA(dims)


def body(
    tokens_in, lengths, cotangent, norm_gain, norm_shift, w_fwd, w_bwd, w_value, bias_fwd, bias_bwd,
    bias_value, decay_log, step_log, b_input, c_output, skip_gain, w_mix, bias_mix, w_output, bias_output,
):
    n = lax.axis_size("dp")
    m = lax.axis_size("row")
    cols = lax.axis_size("col")
    rows, width = tokens_in.shape
    length = rows * cols
    ch = w_fwd.shape[2] // n
    ch2 = 2 * ch
    hid = w_mix.shape[2] // n
    wide = ch2 + hid
    chans = n * cols * ch
    tokens = n * length
    matrix = transform_matrix(length)
    f_mat = jnp.asarray(matrix, BF)
    ft_mat = jnp.asarray(np.ascontiguousarray(matrix.T), BF)
    states = decay_log.shape[3]
    share = w_fwd.shape[1]
    narrow = -(-(ch + max(k * ch % 128 for k in range(n))) // 128) * 128

    def turned(x):
        return jnp.swapaxes(x, -1, -2)

    per_layer = (
        shape((share, ch2), BF), shape((share, hid), BF), shape((w_mix.shape[1], hid), BF), shape((share, hid), BF),
        shape((wide, 1), F32), shape((hid, 1), F32), *[shape((states, ch2), F32)] * 3, shape((8, ch2), F32),
    )
    own_live, own_mask, *cuts = pl.pallas_call(
        functools.partial(prepare_kernel, n),
        out_shape=(shape((8, length), F32), shape((rows, 1), F32), *per_layer * LAYERS),
        in_specs=[pl.BlockSpec(memory_space=pltpu.SMEM)] + [VM] * 6 + [ANY] * 8,
        out_specs=(VM,) * (2 + len(per_layer) * LAYERS),
        scratch_shapes=[
            pltpu.VMEM((LAYERS, share, narrow), F32), pltpu.VMEM((LAYERS, share, narrow), F32),
            pltpu.VMEM((LAYERS, share, hid), F32), pltpu.VMEM((LAYERS, w_mix.shape[1], hid), F32),
            pltpu.VMEM((LAYERS, share, hid), F32), *[pltpu.VMEM((LAYERS, 2, states, narrow), F32)] * 3, sem(8),
        ],
        compiler_params=pltpu.CompilerParams(vmem_limit_bytes=VMEM_LIMIT),
        name="prepare",
    )(
        lengths, bias_fwd, bias_bwd, bias_value, bias_mix, step_log, skip_gain, w_fwd, w_bwd, w_value, w_mix,
        turned(w_output), turned(decay_log), turned(b_input), turned(c_output),
    )
    given = [cuts[len(per_layer) * l : len(per_layer) * (l + 1)] for l in range(LAYERS)]

    comm = [
        *[sem(n)] * 6, sem(n, n), sem(n, n),
    ]
    sums = [
        pltpu.VMEM((2, rows, width), F32), pltpu.VMEM((n, rows, width), BF), pltpu.VMEM((n, rows, width), BF),
        pltpu.VMEM((n, rows, width), BF), pltpu.VMEM((n - 1, rows, width), BF),
    ]
    saved_shapes = (
        shape((tokens, width), BF), shape((chans, tokens), BF), shape((n, wide, length), F32),
        shape((n, ch2, 2 * length), BF), shape((n, ch2, length), BF), shape((n, hid, length), F32),
        shape((hid, tokens), BF),
    )
    def fwd(layer):
        first = layer == 0
        table = shape((ch2, length), F32)
        ahead = shape((width, ch2), BF), shape((width, hid), BF)
        extra = (*ahead, shape((n, 8, length), F32), *[table] * 4) if first else ()
        lands = [(m, share, hid), (m, chans // m, hid), (m, share, hid)]
        return pl.pallas_call(
            functools.partial(fwd_kernel, n, m, layer),
            out_shape=(
                shape((rows, width), F32), *saved_shapes, shape((width, wide), BF),
                shape((hid, width), BF), shape((chans, hid), BF), *extra,
            ),
            in_specs=[VM] * (13 + (11 if first else 3)),
            out_specs=(VM, *([ANY] * 7), *([VM] * (3 + len(extra)))),
            scratch_shapes=[
                pltpu.VMEM((wide, width), BF), pltpu.VMEM((2 * n, hid, ch), BF),
                *(pltpu.VMEM(s.shape, s.dtype) for s in saved_shapes),
                pltpu.VMEM((ch2, length), BF), pltpu.VMEM((ch2, 2 * length), F32),
                pltpu.VMEM((ch2, 2 * length), BF), pltpu.VMEM((hid, length), F32), pltpu.VMEM((length, hid), BF),
                pltpu.VMEM((states, 128), F32), pltpu.VMEM((length // LAG, states, 128), F32),
                pltpu.VMEM((n, hid, length), F32),
                *(pltpu.VMEM(s, BF) for s in lands), pltpu.VMEM((width, hid), BF),
                *sums, *comm, *[sem(n, n)] * 4, *[sem(n)] * 4, sem(7, n),
                *[sem(m)] * 6,
                *([pltpu.VMEM((m, share, ch2), BF)] * 2 + [pltpu.VMEM(lands[2], BF)] + [sem(m)] * 6 + [sem(n)] * 2
                  if first else []),
            ],
            compiler_params=pltpu.CompilerParams(
                collective_id=4 if first else 0, has_side_effects=True, vmem_limit_bytes=VMEM_LIMIT
            ),
            name="forward_block",
        )

    def bwd(layer):
        later = layer < LAYERS - 1
        late = (m, width // m, wide)
        out_shape = [
            shape((rows, width), F32), shape(late, BF), shape((chans // m, hid), BF), shape((width // m, hid), BF),
            shape((8, wide), F32), shape((8, hid), F32), shape((8, width), F32), shape((ch2, 2 * length), F32),
        ]
        if later:
            out_shape += [
                shape(late[1:], BF),
                shape((n, chans // m, hid), BF), shape((n, share, hid), BF),
            ]
        return pl.pallas_call(
            functools.partial(bwd_kernel, n, m, layer, later),
            out_shape=tuple(out_shape),
            in_specs=[VM] * 12 + [ANY] * 7 + [VM] * (3 * later),
            out_specs=(*[VM] * (8 + later), *[ANY] * (2 * later)),
            scratch_shapes=[
                pltpu.VMEM((tokens, width), BF),
                *(pltpu.VMEM(s.shape, s.dtype) for s in saved_shapes),
                pltpu.VMEM((wide, tokens), BF), pltpu.VMEM((ch2, length), F32), pltpu.VMEM((hid, tokens), BF),
                pltpu.VMEM((ch2, 2 * length), F32), pltpu.VMEM((ch2, 2 * length), BF), pltpu.VMEM((length, wide), BF),
                pltpu.VMEM((n, n * ch, length), BF), pltpu.VMEM((n, n * ch, length), BF),
                pltpu.VMEM((n * ch, length), F32),
                pltpu.VMEM((n - 1, n, ch, length), BF), pltpu.VMEM((wide, 128), F32), pltpu.VMEM((hid, 128), F32),
                *(pltpu.VMEM((*size, share_rows, hid), BF) for share_rows in (chans // m, share)
                  for size in ((m,), (m - 1,), ())),
                *sums, *comm, sem(n), sem(n), sem(n), sem(n), sem(n), sem(n), sem(7, n),
                sem(m), sem(m), sem(m), sem(m),
                *([pltpu.VMEM((m - 1, *late[1:]), BF), pltpu.VMEM(late[1:], BF), sem(m), sem(m), *[sem(2, n)] * 4, sem(2)]
                  if later else []),
            ],
            compiler_params=pltpu.CompilerParams(
                collective_id=1 + later, has_side_effects=True, vmem_limit_bytes=VMEM_LIMIT
            ),
            name="backward_block",
        )

    residual = tokens_in
    stored = []
    for l in range(LAYERS):
        sh_fb, sh_v, sh_mx, sh_out, in_bias, mix_bias, *tables = given[l]
        first = l == 0
        more = (sh_fb, given[1][0], given[1][3], *tables, *given[1][6:]) if first else (w_next, *spectrum)
        new, *made = fwd(l)(
            residual, norm_gain, norm_shift, own_live if first else mask, own_mask, sh_v, sh_mx, sh_out if first else out_next, in_bias,
            mix_bias, bias_output, ft_mat, f_mat, *more,
        )
        w_in, w_out, w_mx = made[7:10]
        if first:
            w_next, out_next, mask, *spectrum = made[10:]
            kernels = spectrum[:2], spectrum[2:]
            spectrum = spectrum[2:]
        stored.append((residual, made[:7], (w_in, w_mx, w_out), kernels[l]))
        residual = new
    tokens_out = residual.astype(BF)

    grad = cotangent
    parts = [None] * LAYERS
    extra = ()
    for l in reversed(range(LAYERS)):
        resid_in, saved, weights, (kre, kim) = stored[l]
        grad, *parts[l] = bwd(l)(
            grad, resid_in, norm_gain, mask, own_mask, *weights, kre, kim, ft_mat, f_mat, *saved, *extra,
        )
        if l > 0:
            extra = tuple(parts[l][:3])
    part_in, red_mx0, red_out0, in0, mix0, norm0, dk0, late_in, all_mx1, all_out1 = parts[0]
    _, _, _, in1, mix1, norm1, dk1 = parts[1]
    lots = LAYERS * 3 * states
    all_in, all_mx, all_out = (n, share, wide), (n, chans // m, hid), (n, share, hid)
    all_in1, all_mx0, all_out0, all_in0, all_states, all_small, norms = pl.pallas_call(
        functools.partial(finish_kernel, n, m),
        out_shape=(
            shape(all_in, BF), shape(all_mx, BF), shape(all_out, BF), shape(all_in, BF),
            shape((n, m, lots // m, ch2), BF), shape((n, LAYERS, 8, wide), F32), shape((LAYERS, 8, wide), F32),
        ),
        in_specs=[VM] * 21,
        out_specs=(*[ANY] * 5, VM, VM),
        scratch_shapes=[
            pltpu.VMEM((m - 1, share, wide), BF), pltpu.VMEM((share, wide), BF), pltpu.VMEM((share, wide), BF),
            pltpu.VMEM((lots, ch2), F32),
            pltpu.VMEM((m, lots // m, ch2), BF), pltpu.VMEM((m - 1, lots // m, ch2), BF),
            pltpu.VMEM((lots // m, ch2), BF), pltpu.VMEM((m, lots // m, ch2), BF), pltpu.VMEM((length, ch2), F32),
            pltpu.VMEM((LAYERS, 8, wide), F32), pltpu.VMEM((m, LAYERS, 8, wide), F32),
            pltpu.VMEM((n, LAYERS, 8, wide), F32), pltpu.VMEM((LAYERS, 8, wide), F32),
            pltpu.VMEM((LAYERS, 8, wide), F32),
            *[sem(5, n)] * 4, sem(5), *[sem(m)] * 8,
            sem(n), sem(n), pltpu.SemaphoreType.DMA, pltpu.SemaphoreType.DMA,
        ],
        compiler_params=pltpu.CompilerParams(
            collective_id=3, has_side_effects=True, vmem_limit_bytes=VMEM_LIMIT
        ),
        name="finish",
    )(
        part_in, late_in, red_mx0, red_out0, dk0, dk1, in0, in1, mix0, mix1, norm0, norm1,
        *given[0][6:], *given[1][6:], ft_mat,
    )

    def fixed(dims):
        return pl.BlockSpec(tuple(dims), lambda l: (0,) * len(dims))

    def by_layer(dims):
        return pl.BlockSpec((1, *dims), lambda l: (l,) + (0,) * len(dims))

    chan, unit = n * ch, n * hid
    matrices = [(share, chan), (share, chan), (share, unit)]
    layouts = [
        (width,), (width,), *matrices, (chan,), (chan,), (unit,), (2, states, chan), (2, chan), (2, states, chan),
        (2, states, chan), (2, chan), (chans // m, unit), (unit,), (share, unit), (width,),
    ]
    small_out = {0, 1, 5, 6, 7, 9, 12, 14, 16}
    grads = list(pl.pallas_call(
        functools.partial(assemble_kernel, n),
        grid=(LAYERS,),
        out_shape=tuple(shape((LAYERS, *dims), F32) for dims in layouts),
        in_specs=[
            fixed(all_in), fixed(all_in), fixed(all_mx), fixed(all_mx), fixed(all_out), fixed(all_out),
            pl.BlockSpec((n, 3 * states, ch2), lambda l: (0, l, 0)), fixed((n, LAYERS, 8, wide)),
            fixed((LAYERS, 8, wide)),
        ],
        out_specs=tuple(
            fixed((LAYERS, *dims)) if i in small_out else by_layer(dims) for i, dims in enumerate(layouts)
        ),
        compiler_params=pltpu.CompilerParams(vmem_limit_bytes=VMEM_LIMIT),
        name="assemble",
    )(
        all_in0, all_in1, all_mx0, all_mx1, all_out0, all_out1, all_states.reshape(n, lots, ch2), all_small, norms,
    ))
    for i in (8, 10, 11, 15):
        grads[i] = turned(grads[i])
    return (tokens_out, grad, *grads)


def solution(mesh):
    tokens = P(("dp", "row", "col"), None)
    weight = P(None, "row", "col")
    bias = P(None, "col")
    state = P(None, None, "col", None)
    chan = P(None, None, "col")
    in_specs = (
        tokens, P(("dp", "row")), tokens, P(), P(), weight, weight, weight, bias, bias, bias,
        state, chan, state, state, chan, weight, bias, P(None, "col", "row"), P(),
    )
    out_specs = (
        tokens, tokens, P(), P(), weight, weight, weight, bias, bias, bias,
        state, chan, state, state, chan, weight, bias, P(None, "col", "row"), P(),
    )
    return jax.shard_map(body, mesh=mesh, in_specs=in_specs, out_specs=out_specs, check_vma=False)
```

```python
import functools

import jax
import jax.numpy as jnp
import numpy as np
from jax import lax
from jax.experimental import pallas as pl
from jax.experimental.pallas import tpu as pltpu
from jax.sharding import PartitionSpec as P

LAYERS = 2
EPS = 1e-05
LAG = 64
BF = jnp.bfloat16
F32 = jnp.float32
MESH = pl.DeviceIdType.MESH
VMEM_LIMIT = 60 * 1024 * 1024


def transform_matrix(length):
    k = np.arange(length)[:, None]
    t = np.arange(length)[None, :]
    angle = np.pi * (((2 * k + 1) * t) % (4 * length)) / (2 * length)
    return np.concatenate((np.cos(angle), -np.sin(angle)), axis=0)


def gelu_only(v):
    t = jnp.tanh(v * (0.7978845608 + 0.035677408 * v * v))
    return (0.5 * v) * (1.0 + t)


def gelu_parts(v):
    sq = v * v
    t = jnp.tanh(v * (0.7978845608 + 0.035677408 * sq))
    half = 0.5 + 0.5 * t
    slope = half + (v * half) * (1.0 - t) * (0.7978845608 + 0.107032225 * sq)
    return v * half, slope


def dot(a, b, ca, cb):
    return lax.dot_general(a, b, (((ca,), (cb,)), ((), ())), preferred_element_type=F32)


def over_rows(rows, step, work):
    def one(i, unused):
        work(pl.ds(pl.multiple_of(i * step, step), step))
        return unused

    lax.fori_loop(0, rows // step, one, 0)


def lane_sums(x):
    total = x[:, :128]
    for i in range(1, x.shape[1] // 128):
        total = total + x[:, 128 * i : 128 * (i + 1)]
    return total


def as_row(partial):
    return lax.dot_general(
        jnp.ones((8, 128), F32), partial, (((1,), (1,)), ((), ())), precision=lax.Precision.HIGHEST,
        preferred_element_type=F32,
    )


class Place:
    def __init__(self, n, m):
        self.n = n
        self.m = m
        self.d = lax.axis_index("dp")
        self.c = lax.axis_index("col")
        self.r = lax.axis_index("row")

    def greet(self):
        barrier = pltpu.get_barrier_semaphore()

        def hail(device):
            pl.semaphore_signal(barrier, inc=1, device_id=device, device_id_type=MESH)

        for k in range(1, self.n):
            hail({"dp": self.ahead(k)})
        hail({"col": 1 - self.c})

        def one(j, unused):
            hail({"row": self.up(j)})
            return unused

        lax.fori_loop(1, self.m, one, 0)
        pl.semaphore_wait(barrier, self.n + self.m - 1)

    def ahead(self, k):
        return lax.rem(self.d + k, self.n)

    def behind(self, k):
        return lax.rem(self.d - k + self.n, self.n)

    def near(self, k):
        return lax.rem(self.d + k, 2) + 2 * lax.rem(self.d // 2 + k // 2, 2)

    def apart(self, e):
        return lax.rem(self.d + e, 2) + 2 * lax.rem(self.d // 2 + e // 2, 2)

    def up(self, j):
        return lax.rem(self.r + j, self.m)

    def down(self, j):
        return lax.rem(self.r - j + self.m, self.m)

    def other(self, i):
        return i + (i + self.n - self.d) // self.n

    def to_dp(self, src, dst, send, recv, q):
        return pltpu.make_async_remote_copy(
            src, dst, send, recv, device_id={"dp": q}, device_id_type=MESH
        )

    def to_mate(self, src, dst, send, recv):
        return pltpu.make_async_remote_copy(
            src, dst, send, recv, device_id={"col": 1 - self.c}, device_id_type=MESH
        )

    def to_row(self, src, dst, send, recv, q):
        return pltpu.make_async_remote_copy(
            src, dst, send, recv, device_id={"row": q}, device_id_type=MESH
        )


class RowSum:
    def __init__(self, place, part, got, send, recv, hand=None):
        self.place, self.part, self.got, self.send, self.recv, self.hand = place, part, got, send, recv, hand
        self.line = place.m == 4 and hand is not None

    def copy(self, j):
        q = self.place.up(j)
        return self.place.to_row(self.part.at[q], self.got.at[j - 1], self.send.at[j], self.recv.at[j], q)

    def give(self):
        r = self.place.r
        return self.place.to_row(self.part.at[3 - r], self.hand, self.send.at[0], self.recv.at[0], 1 + r // 3)

    def sum_on(self):
        q = self.place.up(2)
        return self.place.to_row(self.hand, self.got.at[1], self.send.at[2], self.recv.at[2], q)

    def outer(self):
        return 1 + 2 * lax.rem(self.place.r, 2)

    def by_place(self, end, middle):
        r = self.place.r
        pl.when(r * (3 - r) == 0)(end)
        pl.when(r * (3 - r) > 0)(middle)

    def each(self, act):
        def one(j, unused):
            act(self.copy(j))
            return unused

        lax.fori_loop(1, self.place.m, one, 0)

    def start(self):
        if not self.line:
            self.each(lambda copy: copy.start())
            return

        def end():
            self.give().start()
            self.got[lax.rem(self.place.r, 2) * 2] = jnp.zeros(self.got.shape[1:], self.got.dtype)

        def middle():
            self.copy(1).start()
            self.copy(3).start()

        self.by_place(end, middle)

    def second(self):
        if self.line:

            def middle():
                self.give().wait_recv()
                mine = self.part[self.place.up(2)].astype(F32)
                self.hand[...] = (self.hand[...].astype(F32) + mine).astype(BF)
                self.sum_on().start()

            def end():
                self.copy(2).start()
                self.copy(self.outer()).start()

            self.by_place(end, middle)

    def total(self):
        if self.line:
            self.copy(2).wait_recv()
            pl.when(self.place.r > 0)(lambda: self.copy(1).wait_recv())
            pl.when(self.place.r < 3)(lambda: self.copy(3).wait_recv())
        else:
            self.each(lambda copy: copy.wait_recv())
        total = self.part[self.place.r].astype(F32)
        if self.place.m <= 4:
            for j in range(1, self.place.m):
                total = total + self.got[j - 1].astype(F32)
            return total
        return lax.fori_loop(1, self.place.m, lambda j, t: t + self.got[j - 1].astype(F32), total)

    def finish(self):
        if not self.line:
            self.each(lambda copy: copy.wait_send())
            return

        def end():
            self.give().wait_send()
            self.copy(2).wait_send()
            self.copy(self.outer()).wait_send()

        def middle():
            self.copy(1).wait_send()
            self.copy(3).wait_send()
            self.sum_on().wait_send()

        self.by_place(end, middle)


class Tokens:
    def __init__(self, place, buf, rows, length, sems):
        self.place, self.buf, self.rows, self.length = place, buf, rows, length
        self.send_p, self.recv_p, self.send_h, self.recv_h, self.send_m, self.recv_m = sems

    def region(self, slot, half=None):
        rows = self.rows // 2 if half is not None else self.rows
        start = slot * self.length + self.place.c * self.rows + (half or 0) * rows
        return self.buf.at[pl.ds(pl.multiple_of(start, rows), rows)]

    def peer(self, i):
        own = self.region(self.place.d)
        return self.place.to_dp(own, own, self.send_p.at[i], self.recv_p.at[i], self.place.near(i))

    def hop(self, i):
        part = self.region(self.place.near(3 - i), i - 1)
        return self.place.to_dp(part, part, self.send_h.at[i], self.recv_h.at[i], self.place.near(i))

    def mate(self, k):
        part = self.region(self.place.near(k))
        return self.place.to_mate(part, part, self.send_m.at[k], self.recv_m.at[k])

    def start(self):
        self.peer(1).start()
        self.peer(2).start()
        self.mate(0).start()

    def own(self):
        self.mate(0).wait_recv()

    def pass_on(self):
        for i in (1, 2):
            self.peer(i).wait_recv()
            self.hop(3 - i).start()
            self.mate(i).start()

    def fetch(self, k):
        @pl.when(k == 3)
        def _():
            self.hop(1).wait_recv()
            self.hop(2).wait_recv()
            self.mate(3).start()

        self.mate(k).wait_recv()

    def finish(self):
        for i in (1, 2):
            self.peer(i).wait_send()
            self.hop(i).wait_send()
        for k in range(4):
            self.mate(k).wait_send()


def norm_stats(residual):
    mean = jnp.mean(residual, axis=1, keepdims=True)
    centered = residual - mean
    variance = jnp.mean(centered * centered, axis=1, keepdims=True)
    inv = lax.rsqrt(variance + EPS)
    return centered * inv, inv


def sum_to_owner(place, rows, mate_out, mate_in, sum_out, sum_in, own, send_m, recv_m, send_p, recv_p):
    def to_mate(slot):
        return place.to_mate(mate_out.at[slot], mate_in.at[slot], send_m.at[slot], recv_m.at[slot])

    def to_owner(slot):
        k = lax.rem(slot - place.d + place.n, place.n)
        return place.to_dp(sum_out.at[slot], sum_in.at[k - 1], send_p.at[k], recv_p.at[k], slot)

    def close(slot, mine):
        to_mate(slot).wait_recv()

        own[mine] = own[mine] + mate_in[slot].astype(F32)

        @pl.when(slot != place.d)
        def _():
            sum_out[slot] = own[mine].astype(BF)
            to_owner(slot).start()

    def receive():
        def one(k, unused):
            to_owner(place.ahead(k)).wait_recv()
            return unused

        lax.fori_loop(1, place.n, one, 0)

    def finish():
        def one(k, unused):
            to_owner(place.ahead(k)).wait_send()
            return unused

        lax.fori_loop(1, place.n, one, 0)

        def two(s, unused):
            to_mate(s).wait_send()
            return unused

        lax.fori_loop(0, place.n, two, 0)

    return to_mate, close, receive, finish


class RowGather:
    def __init__(self, place, shard, land, send, recv):
        self.place, self.shard, self.land, self.send, self.recv = place, shard, land, send, recv
        self.line = place.m == 4

    def copy(self, j):
        place = self.place
        return place.to_row(self.shard, self.land.at[place.r], self.send.at[j], self.recv.at[j], place.up(j))

    def hop(self):
        place = self.place
        part = self.land.at[place.up(2)]
        return place.to_row(
            part, part, self.send.at[0], self.recv.at[self.inner()], lax.rem(3 * place.r + 1, place.m)
        )

    def outer(self):
        return 1 + 2 * lax.rem(self.place.r, 2)

    def inner(self):
        return lax.rem(2 * self.place.r + 3, self.place.m)

    def in_middle(self, act):
        r = self.place.r
        pl.when(r * (3 - r) > 0)(act)

    def each(self, act):
        def one(j, unused):
            act(self.copy(j))
            return unused

        lax.fori_loop(1, self.place.m, one, 0)

    def direct(self):
        self.line = False
        self.first()

    def first(self):
        if self.line:
            self.copy(2).start()
            self.copy(self.outer()).start()
        else:
            self.each(lambda copy: copy.start())
        self.land[self.place.r] = self.shard[...]

    def second(self):
        if self.line:
            self.copy(2).wait_recv()

            def act():
                self.hop().start()
                self.copy(self.inner()).start()

            self.in_middle(act)

    def whole(self):
        if self.line:
            self.copy(1).wait_recv()
            self.copy(3).wait_recv()
        else:
            self.each(lambda copy: copy.wait_recv())
        m, rows, lanes = self.land.shape
        return self.land[...].astype(F32).reshape(m * rows, lanes)

    def finish(self):
        if self.line:
            self.copy(2).wait_send()
            self.copy(self.outer()).wait_send()

            def act():
                self.hop().wait_send()
                self.copy(self.inner()).wait_send()

            self.in_middle(act)
        else:
            self.each(lambda copy: copy.wait_send())


def kernel_spectrum(decay, step, b_in, c_out, skip, sign, ft_ref, rate, lead):
    length = ft_ref.shape[0]
    blocks = length // LAG
    rate[...] = jnp.exp(step) * jnp.exp(decay)
    weight = (1.0 - jnp.exp(-rate[...])) * jnp.exp(-decay) * b_in * c_out
    for b in range(blocks):
        lead[b] = weight * jnp.exp(-(LAG * b) * rate[...])
    lanes = rate.shape[1]
    offs = lax.broadcasted_iota(jnp.int32, (LAG, lanes), 0).astype(F32)

    def state(i, totals):
        powers = jnp.exp(-offs * rate[pl.ds(i, 1)])
        return tuple(totals[b] + powers * lead[b, pl.ds(i, 1)] for b in range(blocks))

    zero = jnp.zeros((LAG, lanes), F32)
    totals = list(lax.fori_loop(0, rate.shape[0], state, (zero,) * blocks, unroll=2))
    at_zero = lax.broadcasted_iota(jnp.int32, (LAG, lanes), 0) == 0
    totals[0] = totals[0] + jnp.where(at_zero, skip, 0.0)
    kernel = jnp.concatenate(totals, axis=0)
    k_hat = dot(kernel.T.astype(BF), ft_ref[...], 1, 0) * (1.0 / length)
    return k_hat[:, :length], k_hat[:, length:] * sign


def direction_sign(ch, rows, lanes, start=0):
    at = lax.broadcasted_iota(jnp.int32, (rows, lanes), 0) + start
    return jnp.where(at < ch, 1.0, -1.0)


def fwd_kernel(
    n, m, layer, res_ref, gain_ref, shift_ref, own_live_ref, own_mask_ref, sh_v, sh_mx, sh_out, in_bias_ref,
    mix_bias_ref, out_bias_ref, ft_ref, f_ref, *rest
):
    first = layer == 0
    if first:
        sh_fb, sh_next, sh_out_next, *rest = rest
        tables, next_tables, rest = rest[:4], rest[4:8], rest[8:]
    else:
        w_fb_ref, kre_ref, kim_ref, *rest = rest
    new_ref, g_out, mx_out, pre_out, u_out, y_out, pm_out, prod_out, w_in_out, w_out_out, w_mx_out, *rest = rest
    if first:
        next_out, out_next_out, mask_ref, kre_ref, kim_ref, kre_next, kim_next, *rest = rest
    else:
        mask_ref = own_live_ref
    (
        w_in_t, w_mx_t, g, mx, pre, u_sp, y, pm, prod, act, spec, y_hat, prod_f, prod_t,
        rate, lead, value_act, land_v, land_mx, land_out, w_out_t,
        own, mate_out, mate_in, sum_out, sum_in,
        send_a, recv_a, send_ah, recv_ah, send_am, recv_am, send_b, recv_b, send_bh, recv_bh, send_bm, recv_bm,
        send_c, recv_c, send_cm, recv_cm, save,
        send_gv, recv_gv, send_gm, recv_gm, send_go, recv_go, *rest,
    ) = rest
    place = Place(n, m)
    d, c = place.d, place.c
    rows, width = res_ref.shape
    length = ft_ref.shape[0]
    hid = sh_mx.shape[1]
    ch2 = kre_ref.shape[0]
    ch = ch2 // 2
    gain, shift, out_bias = (ref[layer : layer + 1] for ref in (gain_ref, shift_ref, out_bias_ref))

    place.greet()
    gather_v = RowGather(place, sh_v, land_v, send_gv, recv_gv)
    gather_mx = RowGather(place, sh_mx, land_mx, send_gm, recv_gm)
    later_weights = (gather_mx, gather_v)
    gather_a = Tokens(place, g, rows, length, (send_a, recv_a, send_ah, recv_ah, send_am, recv_am))
    if first:
        land_fb, land_next, land_out_next, send_gi, recv_gi, send_gn, recv_gn, send_gx, recv_gx, send_mk, recv_mk = rest
        gather_out = RowGather(place, sh_out, land_out, send_go, recv_go)
        gather_out_next = RowGather(place, sh_out_next, land_out_next, send_gx, recv_gx)
        gather_fb = RowGather(place, sh_fb, land_fb, send_gi, recv_gi)
        gather_next = RowGather(place, sh_next, land_next, send_gn, recv_gn)
        gather_fb.direct()

        def mask_peer(k):
            return place.to_dp(
                own_live_ref, mask_ref.at[d], send_mk.at[k], recv_mk.at[k], place.ahead(k)
            )

        for k in range(1, n):
            mask_peer(k).start()
        mask_ref[d] = own_live_ref[...]
    else:
        gather_mx.first()
    base = d * length + c * rows
    xhat, _ = norm_stats(res_ref[...].astype(F32))
    g[pl.ds(pl.multiple_of(base, rows), rows)] = (xhat * gain + shift).astype(BF)
    gather_a.start()

    def spectra(given, re_ref, im_ref):
        decay_ref, b_ref, c_ref, row_ref = given
        for j in range(ch2 // 128):
            at = slice(128 * j, 128 * (j + 1))
            re_ref[at], im_ref[at] = kernel_spectrum(
                decay_ref[:, at], row_ref[0:1, at], b_ref[:, at], c_ref[:, at], row_ref[1:2, at],
                direction_sign(ch, 128, length, 128 * j), ft_ref, rate, lead,
            )

    if first:
        spectra(tables, kre_ref, kim_ref)
    if first:
        w_fb = gather_fb.whole()
        gather_mx.first()
        for k in range(1, n):
            mask_peer(k).wait_recv()
    else:
        w_fb = w_fb_ref[...].astype(F32)
    w_in_out[:, :ch2] = w_fb.astype(BF)
    w_in_t[:ch2] = w_fb.T.astype(BF)
    gather_a.own()

    def chunk(owner, slot):
        at = pl.ds(pl.multiple_of((c * n + owner) * ch, ch), ch)
        return mx.at[at, pl.ds(pl.multiple_of(slot * length, length), length)]

    def turn(k, j):
        return place.near(k ^ j)

    def half_chunk(owner, slot, half):
        at = pl.ds(pl.multiple_of((c * n + owner) * ch + half * (ch // 2), ch // 2), ch // 2)
        return mx.at[at, pl.ds(pl.multiple_of(slot * length, length), length)]

    def peer_b(i, j):
        part = chunk(d, turn(0, j))
        return place.to_dp(part, part, send_b.at[j, i], recv_b.at[j, i], place.near(i))

    def hop_b(i, j):
        part = half_chunk(place.near(3 - i), turn(3 - i, j), i - 1)
        return place.to_dp(part, part, send_bh.at[j, i], recv_bh.at[j, i], place.near(i))

    def mate_b(k, j):
        part = chunk(place.near(k), turn(k, j))
        return place.to_mate(part, part, send_bm.at[j, k], recv_bm.at[j, k])

    def saves(slot, item):
        lanes = pl.ds(pl.multiple_of(slot * length, length), length)
        src, dst = (
            lambda: (g.at[lanes], g_out.at[lanes]),
            lambda: (u_sp.at[slot], u_out.at[slot]),
            lambda: (y.at[slot], y_out.at[slot]),
            lambda: (pre.at[slot], pre_out.at[slot]),
            lambda: (mx.at[:, lanes], mx_out.at[:, lanes]),
            lambda: (pm.at[slot], pm_out.at[slot]),
            lambda: (prod.at[:, lanes], prod_out.at[:, lanes]),
        )[item]()
        return pltpu.make_async_copy(src, dst, save.at[item, slot])

    def scan_slot(i, unused):
        slot = place.near(i)

        @pl.when(i == 1)
        def _():
            gather_a.pass_on()

        @pl.when(i > 0)
        def _():
            gather_a.fetch(i)

        @pl.when(i == (n - 1 if first else n - 2))
        def _():
            gather_mx.second()
            gather_v.first()

        lanes = pl.ds(pl.multiple_of(slot * length, length), length)
        live = mask_ref[slot, 0:1]
        v = dot(w_in_t[:ch2], g[lanes], 1, 1) + in_bias_ref[:ch2]
        pre[slot, :ch2] = v
        act[...] = (gelu_only(v) * live).astype(BF)
        spec[...] = dot(act[...], ft_ref[...], 1, 0)
        u_re, u_im = spec[:, :length], spec[:, length:]
        k_re, k_im = kre_ref[...], kim_ref[...]
        u_sp[slot, :, :length] = u_re.astype(BF)
        u_sp[slot, :, length:] = u_im.astype(BF)
        y_hat[:, :length] = (k_re * u_re - k_im * u_im).astype(BF)
        y_hat[:, length:] = (k_re * u_im + k_im * u_re).astype(BF)
        both = dot(y_hat[...], f_ref[...], 1, 0)
        y[slot] = both.astype(BF)
        mine = pl.ds(pl.multiple_of((c * n + d) * ch, ch), ch)
        mx[mine, lanes] = (both[:ch] * both[ch:]).astype(BF)
        for j in range(n):

            @pl.when(i == j)
            def _():
                peer_b(1, j).start()
                peer_b(2, j).start()
                mate_b(0, j).start()

        for item in range(3):
            saves(slot, item).start()
        return unused

    lax.fori_loop(0, n, scan_slot, 0)

    def pass_b(j):
        for i in (1, 2):
            peer_b(i, j).wait_recv()
            hop_b(3 - i, j).start()
            mate_b(i, j).start()

    pass_b(0)
    if first:
        spectra(next_tables, kre_next, kim_next)
    else:
        gather_v.second()
    pass_b(1)
    w_mx = gather_mx.whole()
    w_mx_out[...] = w_mx.astype(BF)
    for block in range(2 * n):
        w_mx_t[block] = w_mx[block * ch : (block + 1) * ch].T.astype(BF)
    def value_slot(slot, unused):
        tokens = pl.ds(pl.multiple_of(slot * length, length), length)
        value = dot(w_in_t[ch2:], g[tokens], 1, 1) + in_bias_ref[ch2:]
        pre[slot, ch2:] = value
        value_act[slot] = gelu_only(value)
        saves(slot, 3).start()
        return unused

    begun = set()

    def mix_in(k, j):
        owner, slot = place.near(k), turn(k, j)
        lanes = pl.ds(pl.multiple_of(slot * length, length), length)
        mate_b(k, j).wait_recv()
        total = None
        for side in range(2):
            rows_at = pl.ds(pl.multiple_of((side * n + owner) * ch, ch), ch)
            part = dot(w_mx_t[side * n + owner], mx[rows_at, lanes], 1, 0)
            total = part if total is None else total + part
        pm[slot] = (pm[slot] if k ^ j in begun else mix_bias_ref[...]) + total
        begun.add(k ^ j)

    def across(j):
        hop_b(1, j).wait_recv()
        hop_b(2, j).wait_recv()
        mate_b(3, j).start()
        mix_in(3, j)

    for j in range(n):
        for k in range(3):
            mix_in(k, j)
        if j + 2 < n:
            pass_b(j + 2)
        if j == 0 and first:
            gather_v.second()
            gather_out.first()
        if j == 2 and first:
            gather_out.second()
            gather_next.first()
        if j == n - 1:
            w_v = gather_v.whole()
            w_in_out[:, ch2:] = w_v.astype(BF)
            w_in_t[ch2:] = w_v.T.astype(BF)
            lax.fori_loop(0, n, value_slot, 0)
        if j > 0:
            across(j - 1)
    across(n - 1)
    w_out = gather_out.whole() if first else sh_out[...].astype(F32)
    w_out_t[...] = w_out.astype(BF)
    w_out_out[...] = w_out.T.astype(BF)

    to_mate, close, receive, finish_c = sum_to_owner(
        place, rows, mate_out, mate_in, sum_out, sum_in, own, send_cm, recv_cm, send_c, recv_c
    )

    def order(i):
        return lax.select(i == n - 1, d, place.other(i))

    def hidden_slot(i, unused):
        if first:

            @pl.when(i == 1)
            def _():
                gather_next.second()
                gather_out_next.first()

        slot = order(i)
        lanes = pl.ds(pl.multiple_of(slot * length, length), length)
        v = pm[slot]
        product = gelu_only(v) * value_act[slot]
        prod_f[...] = product
        prod[:, lanes] = product.astype(BF)
        prod_t[...] = prod_f[...].T.astype(BF)
        for item in range(4, 7):
            saves(slot, item).start()
        theirs = pl.ds(pl.multiple_of((1 - c) * rows, rows), rows)
        ours = pl.ds(pl.multiple_of(c * rows, rows), rows)
        mate_out[slot] = dot(prod_t[theirs], w_out_t[...], 1, 1).astype(BF)
        to_mate(slot).start()

        @pl.when(i > 0)
        def _():
            close(order(i - 1), lax.rem(i - 1, 2))

        own[lax.rem(i, 2)] = dot(prod_t[ours], w_out_t[...], 1, 1)
        return unused

    lax.fori_loop(0, n, hidden_slot, 0)
    last = (n - 1) % 2
    close(d, last)
    if first:
        gather_out_next.second()
    receive()

    total = own[last]
    for k in range(1, n):
        total = total + sum_in[k - 1].astype(F32)
    new = res_ref[...].astype(F32) + own_mask_ref[...] * (total + out_bias)
    new_ref[...] = new.astype(new_ref.dtype)
    gather_a.finish()
    finish_c()
    for gather in later_weights:
        gather.finish()
    if first:
        next_out[...] = gather_next.whole().astype(BF)
        out_next_out[...] = gather_out_next.whole().astype(BF)
        gather_out.finish()
        gather_out_next.finish()
        gather_next.finish()
        gather_fb.finish()
        for k in range(1, n):
            mask_peer(k).wait_send()

    for j in range(n):
        for i in (1, 2):
            peer_b(i, j).wait_send()
            hop_b(i, j).wait_send()
        for k in range(n):
            mate_b(k, j).wait_send()

    def drain(slot, unused):
        for item in range(7):
            saves(slot, item).wait()
        return unused

    lax.fori_loop(0, n, drain, 0)


def bwd_kernel(
    n, m, layer, later, grad_ref, res_ref, gain_ref, mask_ref, own_mask_ref, w_in_ref, w_mx_ref, w_out_ref, kre_ref,
    kim_ref, ft_ref, f_ref, g_in, mx_in, pre_in, u_in, y_in, pm_in, prod_in, *rest
):
    if later:
        late_part, red_mx1, red_out1, *rest = rest
    (new_ref, gw_in_ref, red_mx_ref, red_out_ref, in_row_ref, mix_row_ref, norm_sum_ref, dk_ref, *rest) = rest
    if later:
        red_late_ref, all_mx, all_out, *rest = rest
    (
        gb, g, mx, pre, u_sp, y, pm, prod, gpre, gpre_f, gpm, spec, hat, turned,
        mix_sum, mix_mate, mix_own, mix_got, in_sum, mix_acc, part_mx, got_mx, hand_mx, part_out, got_out, hand_out,
        own, mate_out, mate_in, sum_out, sum_in,
        send_a, recv_a, send_ah, recv_ah, send_am, recv_am, send_b, recv_b, send_bm, recv_bm, send_c, recv_c, send_cm, recv_cm, load,
        send_rm, recv_rm, send_ro, recv_ro, *rest,
    ) = rest
    place = Place(n, m)
    d, c = place.d, place.c
    rows, width = res_ref.shape
    length = ft_ref.shape[0]
    hid = w_mx_ref.shape[1]
    ch2 = kre_ref.shape[0]
    ch = ch2 // 2
    half = n * ch

    def loads(slot, item):
        lanes = pl.ds(pl.multiple_of(slot * length, length), length)
        src, dst = (
            lambda: (pre_in.at[slot], pre.at[slot]),
            lambda: (pm_in.at[slot], pm.at[slot]),
            lambda: (y_in.at[slot], y.at[slot]),
            lambda: (u_in.at[slot], u_sp.at[slot]),
            lambda: (prod_in.at[:, lanes], prod.at[:, lanes]),
            lambda: (mx_in.at[:, lanes], mx.at[:, lanes]),
            lambda: (g_in.at[lanes], g.at[lanes]),
        )[item]()
        return pltpu.make_async_copy(src, dst, load.at[item, slot])

    for item in range(7):
        loads(d, item).start()

    def start_loads(i, unused):
        for item in range(7):
            loads(place.other(i), item).start()
        return unused

    lax.fori_loop(0, n - 1, start_loads, 0)

    place.greet()
    gather_a = Tokens(place, gb, rows, length, (send_a, recv_a, send_ah, recv_ah, send_am, recv_am))
    base = d * length + c * rows
    gain = gain_ref[layer : layer + 1]
    first = grad_ref[...].astype(F32) * own_mask_ref[...]
    gb[pl.ds(pl.multiple_of(base, rows), rows)] = first.astype(BF)
    gather_a.start()
    sum_mx = RowSum(place, part_mx, got_mx, send_rm, recv_rm, hand_mx)
    sum_out_w = RowSum(place, part_out, got_out, send_ro, recv_ro, hand_out)
    row_sums = [sum_mx, sum_out_w]
    if later:
        got_late, hand_late, send_rl, recv_rl, *sems = rest
        sum_late = RowSum(place, late_part, got_late, send_rl, recv_rl, hand_late)
        sum_late.start()
        row_sums.append(sum_late)
    norm_sum_ref[...] = jnp.zeros_like(norm_sum_ref)
    norm_sum_ref[2:3] = jnp.sum(first, axis=0, keepdims=True)
    in_sum[...] = jnp.zeros_like(in_sum)
    mix_acc[...] = jnp.zeros_like(mix_acc)
    dk_ref[...] = jnp.zeros_like(dk_ref)
    gather_a.own()

    def mate_b(slot):
        return place.to_mate(mix_sum.at[slot], mix_mate.at[slot], send_bm.at[slot], recv_bm.at[slot])

    def peer_b(k, slot):
        q = place.ahead(k)
        part = mix_sum.at[slot, pl.ds(pl.multiple_of(q * ch, ch), ch)]
        return place.to_dp(part, mix_got.at[k - 1, slot], send_b.at[slot, k], recv_b.at[slot, k], q)

    def hidden_slot(i, unused):
        slot = lax.select(i == 0, d, place.other(i - 1))

        @pl.when(i == 1)
        def _():
            gather_a.pass_on()

        @pl.when(i > 0)
        def _():
            gather_a.fetch(place.apart(slot))

        if later:
            pl.when(i == n - 2)(sum_late.second)


        lanes = pl.ds(pl.multiple_of(slot * length, length), length)
        mix_own[:hid] = dot(w_out_ref[...], gb[lanes], 1, 1)
        for item in range(2):
            loads(slot, item).wait()
        gated, slope = gelu_parts(pm[slot])
        value, value_slope = gelu_parts(pre[slot, ch2:])
        now = mix_own[:hid]
        to_value = now * gated * value_slope
        to_mix = now * value * slope
        gpre[ch2:, lanes] = to_value.astype(BF)
        gpm[:, lanes] = to_mix.astype(BF)
        in_sum[ch2:] = in_sum[ch2:] + lane_sums(to_value)
        mix_acc[...] = mix_acc[...] + lane_sums(to_mix)
        theirs = pl.ds(pl.multiple_of((1 - c) * half, half), half)
        ours = pl.ds(pl.multiple_of(c * half, half), half)
        mix_sum[slot] = dot(w_mx_ref[theirs], gpm[:, lanes], 1, 0).astype(BF)
        mate_b(slot).start()
        mix_own[...] = dot(w_mx_ref[ours], gpm[:, lanes], 1, 0)
        mate_b(slot).wait()
        mix_sum[slot] = (mix_own[...] + mix_mate[slot].astype(F32)).astype(BF)
        for k in range(1, n):
            peer_b(k, slot).start()
        return unused

    lax.fori_loop(0, n, hidden_slot, 0)

    def wait_loads(slot, unused):
        for item in range(2, 7):
            loads(slot, item).wait()
        return unused

    lax.fori_loop(0, n, wait_loads, 0)
    share = mx.shape[0] // m

    def grad_mix(q, unused):
        part_mx[q] = dot(mx[pl.ds(pl.multiple_of(q * share, share), share)], gpm[...], 1, 1).astype(BF)
        return unused

    lax.fori_loop(0, m, grad_mix, 0)
    sum_mx.start()
    gw_out = dot(prod[...], gb[...], 1, 0).T
    part_out[...] = gw_out.reshape(m, width // m, hid).astype(BF)
    sum_out_w.start()
    spreads = []
    if later:
        spreads = [
            Spread(place, red_mx1, all_mx, sems, 0),
            Spread(place, red_out1, all_out, sems, 1),
        ]

    to_mate, close, receive, finish_c = sum_to_owner(
        place, rows, mate_out, mate_in, sum_out, sum_in, own, send_cm, recv_cm, send_c, recv_c
    )

    def order(i):
        return lax.select(i == n - 1, d, place.other(i))

    def scan_slot(i, unused):
        slot = order(i)
        lanes = pl.ds(pl.multiple_of(slot * length, length), length)
        for k in range(1, n):
            peer_b(k, slot).wait_recv()

        @pl.when(i == n - 2)
        def _():
            for each in spreads:
                each.start()

        @pl.when(i == n - 2)
        def _():
            sum_mx.second()
            sum_out_w.second()

        total = mix_sum[slot, pl.ds(pl.multiple_of(d * ch, ch), ch)].astype(F32)
        for k in range(1, n):
            total = total + mix_got[k - 1, slot].astype(F32)
        hat[:ch, :length] = (total * y[slot, ch:].astype(F32)).astype(BF)
        hat[ch:, :length] = (total * y[slot, :ch].astype(F32)).astype(BF)
        spec[...] = dot(hat[:, :length], ft_ref[...], 1, 0)
        g_re, g_im = spec[:, :length], spec[:, length:]
        k_re, k_im = kre_ref[...], kim_ref[...]
        hat[:, :length] = (k_re * g_re + k_im * g_im).astype(BF)
        hat[:, length:] = (k_re * g_im - k_im * g_re).astype(BF)
        u_re, u_im = u_sp[slot, :, :length].astype(F32), u_sp[slot, :, length:].astype(F32)
        dk_ref[:, :length] = dk_ref[:, :length] + (u_re * g_re + u_im * g_im)
        dk_ref[:, length:] = dk_ref[:, length:] + (u_re * g_im - u_im * g_re)
        spec[:, :length] = dot(hat[...], f_ref[...], 1, 0)
        live = mask_ref[slot, 0:1]
        _, slope = gelu_parts(pre[slot, :ch2])
        part = spec[:, :length] * slope * live
        gpre_f[...] = part
        gpre[:ch2, lanes] = part.astype(BF)
        in_sum[:ch2] = in_sum[:ch2] + lane_sums(part)
        turned[:, :ch2] = gpre_f[...].T.astype(BF)
        gpre_f[...] = gpre[ch2:, lanes].astype(F32)
        turned[:, ch2:] = gpre_f[...].T.astype(BF)
        theirs = pl.ds(pl.multiple_of((1 - c) * rows, rows), rows)
        ours = pl.ds(pl.multiple_of(c * rows, rows), rows)
        mate_out[slot] = dot(turned[theirs], w_in_ref[...], 1, 1).astype(BF)
        to_mate(slot).start()

        @pl.when(i > 0)
        def _():
            close(order(i - 1), lax.rem(i - 1, 2))

        own[lax.rem(i, 2)] = dot(turned[ours], w_in_ref[...], 1, 1)
        return unused

    lax.fori_loop(0, n, scan_slot, 0)
    last = (n - 1) % 2
    close(d, last)

    def grad_in(r):
        part = dot(gpre[r], g[...], 1, 0).T
        gw_in_ref[:, :, r] = part.reshape(m, width // m, part.shape[1]).astype(BF)

    over_rows(gpre.shape[0], 128, grad_in)
    for each in spreads:
        each.pass_on()
    in_row_ref[...] = as_row(in_sum[...])
    mix_row_ref[...] = as_row(mix_acc[...])
    if later:
        red_late_ref[...] = sum_late.total().astype(BF)
    receive()
    total = own[last]
    for k in range(1, n):
        total = total + sum_in[k - 1].astype(F32)
    xhat, inv = norm_stats(res_ref[...].astype(F32))
    h = total * gain
    middle = jnp.mean(h, axis=1, keepdims=True)
    along = jnp.mean(h * xhat, axis=1, keepdims=True)
    new_ref[...] = grad_ref[...].astype(F32) + inv * (h - middle - xhat * along)
    norm_sum_ref[0:1] = jnp.sum(total * xhat, axis=0, keepdims=True)
    norm_sum_ref[1:2] = jnp.sum(total, axis=0, keepdims=True)
    red_mx_ref[...] = sum_mx.total().astype(BF)
    red_out_ref[...] = sum_out_w.total().astype(BF)
    gather_a.finish()
    finish_c()
    for row_sum in row_sums:
        row_sum.finish()
    for each in spreads:
        each.wait()

    def drain(slot, unused):
        for k in range(1, n):
            peer_b(k, slot).wait_send()
        return unused

    lax.fori_loop(0, n, drain, 0)


class Spread:
    def __init__(self, place, src, out, sems, item):
        self.place, self.src, self.out, self.item = place, src, out, item
        self.send, self.recv, self.send_h, self.recv_h, self.keep = sems
        rows = src.shape[0]
        whole = len(src.shape) == 2 and rows % 32 != 0
        half = rows if whole else rows // 2
        self.pieces = [(i, start, half) for i, start in ((1, 0), (2, half)) if start < rows]

    def peer(self, i):
        place, item = self.place, self.item
        return place.to_dp(
            self.src, self.out.at[place.d], self.send.at[item, i], self.recv.at[item, i], place.near(i)
        )

    def hop(self, i, start, count):
        place, item = self.place, self.item
        part = self.out.at[place.near(3 - i), pl.ds(start, count)]
        return place.to_dp(part, part, self.send_h.at[item, i], self.recv_h.at[item, i], place.near(i))

    def local(self):
        return pltpu.make_async_copy(self.src, self.out.at[self.place.d], self.keep.at[self.item])

    def start(self):
        self.peer(1).start()
        self.peer(2).start()
        self.local().start()

    def pass_on(self):
        self.peer(1).wait_recv()
        self.peer(2).wait_recv()
        for piece in self.pieces:
            self.hop(*piece).start()

    def wait(self):
        for piece in self.pieces:
            self.hop(*piece).wait()
        self.peer(1).wait_send()
        self.peer(2).wait_send()
        self.local().wait()


def state_grads(dk_re, dk_im, sign, ft_ref, decay, step, b_in, c_out, lag_sums):
    length = ft_ref.shape[0]
    re = dk_re.astype(BF)
    im = (dk_im * sign).astype(BF)
    lag_sums[...] = (dot(ft_ref[:, :length], re, 1, 1) + dot(ft_ref[:, length:], im, 1, 1)) * (1.0 / length)
    rate = jnp.exp(step) * jnp.exp(decay)
    a = jnp.exp(-rate)

    totals, slopes = [], []
    for lanes in (slice(0, 256), slice(256, a.shape[1])):
        base = a[:, lanes]

        def lag(i, carry, base=base, lanes=lanes):
            total, slope = carry
            row = lag_sums[pl.ds(length - 1 - i, 1)][:, lanes]
            return total * base + row, slope * base + total

        zero = jnp.zeros_like(base)
        total, slope = lax.fori_loop(0, length, lag, (zero, zero), unroll=4)
        totals.append(total)
        slopes.append(slope)
    total, slope = jnp.concatenate(totals, axis=1), jnp.concatenate(slopes, axis=1)
    inv_decay = jnp.exp(-decay)
    gain = (1.0 - a) * inv_decay
    b_disc = gain * b_in
    to_b = c_out * total
    to_rate = a * (to_b * inv_decay * b_in - (c_out * b_disc) * slope)
    through = to_rate * rate
    return (
        through - to_b * b_disc, to_b * gain, b_disc * total,
        jnp.sum(through, axis=0, keepdims=True), lag_sums[0:1],
    )


def finish_kernel(
    n, m, part_in, late_in, red_mx0, red_out0, dk0, dk1, in0, in1, mix0, mix1, norm0, norm1,
    decay0, b0, c0, row0, decay1, b1, c1, row1, ft_ref,
    all_in1, all_mx0, all_out0, all_in0, all_states, all_small, norm_ref,
    got_in, hand_in, red_in0, states, part_s, got_s, red_s, full_s, lag_sums, small, row_small, dp_small, norm_own, norm_got,
    send_w, recv_w, send_wh, recv_wh, keep_w, send_ri, recv_ri, send_rs, recv_rs, send_gs, recv_gs, send_sm, recv_sm,
    send_ds, recv_ds, send_n, recv_n,
):
    place = Place(n, m)
    d, r = place.d, place.r
    states_n, ch2 = decay0.shape
    place.greet()
    sum_in = RowSum(place, part_in, got_in, send_ri, recv_ri, hand_in)
    sum_in.start()
    spreads = [
        Spread(place, src, out, (send_w, recv_w, send_wh, recv_wh, keep_w), item)
        for item, (src, out) in enumerate(
            ((late_in, all_in1), (red_mx0, all_mx0), (red_out0, all_out0), (red_in0, all_in0), (full_s, all_states))
        )
    ]
    for each in spreads[:3]:
        each.start()

    small[...] = jnp.zeros_like(small)
    for l, (in_row, mix_row, norm) in enumerate(((in0, mix0, norm0), (in1, mix1, norm1))):
        small[l, 0:1] = in_row[0:1]
        small[l, 1:2, :ch2] = mix_row[0:1]
        small[l, 3:6] = norm[0:3]
    length = ft_ref.shape[0]
    for l, (dk, decay, b_in, c_out, row) in enumerate(((dk0, decay0, b0, c0, row0), (dk1, decay1, b1, c1, row1))):
        grads = state_grads(
            dk[:, :length], dk[:, length:], direction_sign(ch2 // 2, ch2, length), ft_ref, decay[...], row[0:1],
            b_in[...], c_out[...], lag_sums,
        )
        for i in range(3):
            states[pl.ds((3 * l + i) * states_n, states_n)] = grads[i]
        small[l, 1:2, ch2:] = grads[3]
        small[l, 2:3, :ch2] = grads[4]
        if l == 0:
            sum_in.second()
            spreads[0].pass_on()
    spreads[1].pass_on()
    share = states.shape[0] // m
    for q in range(m):
        part_s[q] = states[q * share : (q + 1) * share].astype(BF)
    sum_s = RowSum(place, part_s, got_s, send_rs, recv_rs)
    sum_s.start()
    row_small[r] = small[...]

    def small_row(j):
        return place.to_row(row_small.at[r], row_small.at[r], send_sm.at[j], recv_sm.at[j], place.up(j))

    def repeat(work, count):
        def one(j, unused):
            work(j)
            return unused

        lax.fori_loop(1, count, one, 0)

    repeat(lambda j: small_row(j).start(), m)

    red_in0[...] = sum_in.total().astype(BF)
    spreads[3].start()
    spreads[2].pass_on()
    red_s[...] = sum_s.total().astype(BF)
    full_s[r] = red_s[...]

    def state_row(j):
        return place.to_row(full_s.at[r], full_s.at[r], send_gs.at[j], recv_gs.at[j], place.up(j))

    repeat(lambda j: state_row(j).start(), m)
    repeat(lambda j: small_row(j).wait_recv(), m)
    total = row_small[0]
    for q in range(1, m):
        total = total + row_small[q]
    dp_small[d] = total

    def small_dp(k):
        return place.to_dp(dp_small.at[d], dp_small.at[d], send_ds.at[k], recv_ds.at[k], place.ahead(k))

    for k in range(1, n):
        small_dp(k).start()
    repeat(lambda j: state_row(j).wait_recv(), m)

    spreads[4].start()
    spreads[3].pass_on()
    for k in range(1, n):
        small_dp(k).wait_recv()
    total = dp_small[0]
    for q in range(1, n):
        total = total + dp_small[q]
    norm_own[...] = total
    swap = place.to_mate(norm_own, norm_got, send_n, recv_n)
    swap.start()
    all_small[...] = dp_small[...]
    swap.wait_recv()
    norm_ref[...] = norm_own[...] + norm_got[...]
    swap.wait_send()
    spreads[4].pass_on()
    for each in spreads:
        each.wait()
    for k in range(1, n):
        small_dp(k).wait_send()
    repeat(lambda j: small_row(j).wait_send(), m)
    repeat(lambda j: state_row(j).wait_send(), m)
    sum_in.finish()
    sum_s.finish()


def prepare_kernel(
    n, lengths_ref, bias_fwd, bias_bwd, bias_value, bias_mix, step_ref, skip_ref, *rest
):
    d = lax.axis_index("dp")
    w_fwd, w_bwd, w_value, w_mix, w_out, decay, b_in, c_out, live_ref, mask_ref, *rest = rest
    per = 10
    outs = [rest[per * l : per * (l + 1)] for l in range(LAYERS)]
    win_f, win_b, win_v, win_m, win_o, win_d, win_i, win_c, load = rest[per * LAYERS :]
    ch = w_fwd.shape[2] // n
    hid = w_value.shape[2] // n
    size = win_f.shape[2]
    places = sorted({(k * ch) % 128 for k in range(n)})

    def window(width, wide):
        start = pl.multiple_of((d * width) // 128 * 128, 128)
        return pl.ds(start, wide)

    narrow, broad = window(ch, size), window(hid, hid)
    copies = [
        pltpu.make_async_copy(src.at[at], dst, load.at[i])
        for i, (src, at, dst) in enumerate((
            (w_fwd, (slice(None), slice(None), narrow), win_f), (w_bwd, (slice(None), slice(None), narrow), win_b),
            (decay, (slice(None), slice(None), slice(None), narrow), win_d),
            (b_in, (slice(None), slice(None), slice(None), narrow), win_i),
            (c_out, (slice(None), slice(None), slice(None), narrow), win_c),
            (w_value, (slice(None), slice(None), broad), win_v), (w_mix, (slice(None), slice(None), broad), win_m),
            (w_out, (slice(None), slice(None), broad), win_o),
        ))
    ]
    for copy in copies:
        copy.start()

    def pick(x):
        kept = x[..., places[0] : places[0] + ch]
        for place in places[1:]:
            kept = jnp.where(lax.rem(d * ch, 128) == place, x[..., place : place + ch], kept)
        return kept

    def cut(x, width):
        kept = x[:, :width]
        for k in range(1, n):
            kept = jnp.where(d == k, x[:, k * width : (k + 1) * width], kept)
        return kept

    def column(row):
        return jnp.broadcast_to(row, (8, row.shape[1])).T[:, :1]

    rows, length = mask_ref.shape[0], live_ref.shape[1]
    alive = lengths_ref[0]
    live_ref[...] = (lax.broadcasted_iota(jnp.int32, live_ref.shape, 1) < alive).astype(F32)
    at = lax.broadcasted_iota(jnp.int32, mask_ref.shape, 0) + lax.axis_index("col") * rows
    mask_ref[...] = (at < alive).astype(F32)
    for l in range(LAYERS):
        in_bias, mix_bias, row_ref = outs[l][4], outs[l][5], outs[l][9]
        one = slice(l, l + 1)
        in_bias[:ch] = column(cut(bias_fwd[one], ch))
        in_bias[ch : 2 * ch] = column(cut(bias_bwd[one], ch))
        in_bias[2 * ch :] = column(cut(bias_value[one], hid))
        mix_bias[...] = column(cut(bias_mix[one], hid))
        row_ref[...] = jnp.zeros_like(row_ref)
        for k in range(2):
            lanes = slice(k * ch, (k + 1) * ch)
            row_ref[0:1, lanes] = cut(step_ref[l, k : k + 1], ch)
            row_ref[1:2, lanes] = cut(skip_ref[l, k : k + 1], ch)
    for copy in copies:
        copy.wait()
    for l in range(LAYERS):
        fb_ref, v_ref, mx_ref, out_ref, _, _, decay_ref, b_ref, c_ref, _ = outs[l]
        fb_ref[:, :ch] = pick(win_f[l]).astype(BF)
        fb_ref[:, ch:] = pick(win_b[l]).astype(BF)
        v_ref[...] = win_v[l].astype(BF)
        mx_ref[...] = win_m[l].astype(BF)
        out_ref[...] = win_o[l].astype(BF)
        for k in range(2):
            lanes = slice(k * ch, (k + 1) * ch)
            decay_ref[:, lanes] = pick(win_d[l, k])
            b_ref[:, lanes] = pick(win_i[l, k])
            c_ref[:, lanes] = pick(win_c[l, k])


def assemble_kernel(
    n, in0, in1, mx0, mx1, out0, out1, states_ref, small_ref, norm_ref,
    gain, shift, wf, wb, wv, bf, bb, bv, decay, step, b_in, c_out, skip, wm, bm, wo, bo,
):
    l = pl.program_id(0)
    ch = wf.shape[2] // n
    hid = wv.shape[2] // n
    count = decay.shape[2]
    one = pl.ds(l, 1)
    for i, ref in ((3, gain), (4, shift), (5, bo)):
        ref[one] = norm_ref[one, i]
    for k in range(n):
        narrow, broad = slice(k * ch, (k + 1) * ch), slice(k * hid, (k + 1) * hid)
        for layer, (part_in, part_mx, part_out) in enumerate(((in0, mx0, out0), (in1, mx1, out1))):

            @pl.when(l == layer)
            def _():
                piece = part_in[k].astype(F32)
                wf[0, :, narrow] = piece[:, :ch]
                wb[0, :, narrow] = piece[:, ch : 2 * ch]
                wv[0, :, broad] = piece[:, 2 * ch :]
                wm[0, :, broad] = part_mx[k].astype(F32)
                wo[0, :, broad] = part_out[k].astype(F32)

        piece = states_ref[k].astype(F32)
        for i, ref in enumerate((decay, b_in, c_out)):
            for direction in range(2):
                lanes = slice(direction * ch, (direction + 1) * ch)
                ref[0, direction, :, narrow] = piece[i * count : (i + 1) * count, lanes]
        row = small_ref[k, one]
        bf[one, narrow] = row[:, 0, :ch]
        bb[one, narrow] = row[:, 0, ch : 2 * ch]
        bv[one, broad] = row[:, 0, 2 * ch :]
        bm[one, broad] = row[:, 1, :hid]
        for direction in range(2):
            start = direction * ch
            step[one, direction, narrow] = row[:, 1, hid + start : hid + start + ch]
            skip[one, direction, narrow] = row[:, 2, start : start + ch]


VM = pl.BlockSpec(memory_space=pltpu.VMEM)
ANY = pl.BlockSpec(memory_space=pl.ANY)


def shape(dims, dtype):
    return jax.ShapeDtypeStruct(tuple(dims), dtype)


def sem(*dims):
    return pltpu.SemaphoreType.DMA(dims)


def body(
    tokens_in, lengths, cotangent, norm_gain, norm_shift, w_fwd, w_bwd, w_value, bias_fwd, bias_bwd,
    bias_value, decay_log, step_log, b_input, c_output, skip_gain, w_mix, bias_mix, w_output, bias_output,
):
    n = lax.axis_size("dp")
    m = lax.axis_size("row")
    cols = lax.axis_size("col")
    rows, width = tokens_in.shape
    length = rows * cols
    ch = w_fwd.shape[2] // n
    ch2 = 2 * ch
    hid = w_mix.shape[2] // n
    wide = ch2 + hid
    chans = n * cols * ch
    tokens = n * length
    matrix = transform_matrix(length)
    f_mat = jnp.asarray(matrix, BF)
    ft_mat = jnp.asarray(np.ascontiguousarray(matrix.T), BF)
    states = decay_log.shape[3]
    share = w_fwd.shape[1]
    narrow = -(-(ch + max(k * ch % 128 for k in range(n))) // 128) * 128

    def turned(x):
        return jnp.swapaxes(x, -1, -2)

    per_layer = (
        shape((share, ch2), BF), shape((share, hid), BF), shape((w_mix.shape[1], hid), BF), shape((share, hid), BF),
        shape((wide, 1), F32), shape((hid, 1), F32), *[shape((states, ch2), F32)] * 3, shape((8, ch2), F32),
    )
    own_live, own_mask, *cuts = pl.pallas_call(
        functools.partial(prepare_kernel, n),
        out_shape=(shape((8, length), F32), shape((rows, 1), F32), *per_layer * LAYERS),
        in_specs=[pl.BlockSpec(memory_space=pltpu.SMEM)] + [VM] * 6 + [ANY] * 8,
        out_specs=(VM,) * (2 + len(per_layer) * LAYERS),
        scratch_shapes=[
            pltpu.VMEM((LAYERS, share, narrow), F32), pltpu.VMEM((LAYERS, share, narrow), F32),
            pltpu.VMEM((LAYERS, share, hid), F32), pltpu.VMEM((LAYERS, w_mix.shape[1], hid), F32),
            pltpu.VMEM((LAYERS, share, hid), F32), *[pltpu.VMEM((LAYERS, 2, states, narrow), F32)] * 3, sem(8),
        ],
        compiler_params=pltpu.CompilerParams(vmem_limit_bytes=VMEM_LIMIT),
        name="prepare",
    )(
        lengths, bias_fwd, bias_bwd, bias_value, bias_mix, step_log, skip_gain, w_fwd, w_bwd, w_value, w_mix,
        turned(w_output), turned(decay_log), turned(b_input), turned(c_output),
    )
    given = [cuts[len(per_layer) * l : len(per_layer) * (l + 1)] for l in range(LAYERS)]

    comm = [
        *[sem(n)] * 6, sem(n, n), sem(n, n),
    ]
    sums = [
        pltpu.VMEM((2, rows, width), F32), pltpu.VMEM((n, rows, width), BF), pltpu.VMEM((n, rows, width), BF),
        pltpu.VMEM((n, rows, width), BF), pltpu.VMEM((n - 1, rows, width), BF),
    ]
    saved_shapes = (
        shape((tokens, width), BF), shape((chans, tokens), BF), shape((n, wide, length), F32),
        shape((n, ch2, 2 * length), BF), shape((n, ch2, length), BF), shape((n, hid, length), F32),
        shape((hid, tokens), BF),
    )
    def fwd(layer):
        first = layer == 0
        table = shape((ch2, length), F32)
        ahead = shape((width, ch2), BF), shape((width, hid), BF)
        extra = (*ahead, shape((n, 8, length), F32), *[table] * 4) if first else ()
        lands = [(m, share, hid), (m, chans // m, hid), (m, share, hid)]
        return pl.pallas_call(
            functools.partial(fwd_kernel, n, m, layer),
            out_shape=(
                shape((rows, width), BF if layer == LAYERS - 1 else F32), *saved_shapes, shape((width, wide), BF),
                shape((hid, width), BF), shape((chans, hid), BF), *extra,
            ),
            in_specs=[VM] * (13 + (11 if first else 3)),
            out_specs=(VM, *([ANY] * 7), *([VM] * (3 + len(extra)))),
            scratch_shapes=[
                pltpu.VMEM((wide, width), BF), pltpu.VMEM((2 * n, hid, ch), BF),
                *(pltpu.VMEM(s.shape, s.dtype) for s in saved_shapes),
                pltpu.VMEM((ch2, length), BF), pltpu.VMEM((ch2, 2 * length), F32),
                pltpu.VMEM((ch2, 2 * length), BF), pltpu.VMEM((hid, length), F32), pltpu.VMEM((length, hid), BF),
                pltpu.VMEM((states, 128), F32), pltpu.VMEM((length // LAG, states, 128), F32),
                pltpu.VMEM((n, hid, length), F32),
                *(pltpu.VMEM(s, BF) for s in lands), pltpu.VMEM((width, hid), BF),
                *sums, *comm, *[sem(n, n)] * 4, *[sem(n)] * 4, sem(7, n),
                *[sem(m)] * 6,
                *([pltpu.VMEM((m, share, ch2), BF)] * 2 + [pltpu.VMEM(lands[2], BF)] + [sem(m)] * 6 + [sem(n)] * 2
                  if first else []),
            ],
            compiler_params=pltpu.CompilerParams(
                collective_id=4 if first else 0, has_side_effects=True, vmem_limit_bytes=VMEM_LIMIT
            ),
            name="forward_block",
        )

    def bwd(layer):
        later = layer < LAYERS - 1
        late = (m, width // m, wide)
        out_shape = [
            shape((rows, width), F32), shape(late, BF), shape((chans // m, hid), BF), shape((width // m, hid), BF),
            shape((8, wide), F32), shape((8, hid), F32), shape((8, width), F32), shape((ch2, 2 * length), F32),
        ]
        if later:
            out_shape += [
                shape(late[1:], BF),
                shape((n, chans // m, hid), BF), shape((n, share, hid), BF),
            ]
        return pl.pallas_call(
            functools.partial(bwd_kernel, n, m, layer, later),
            out_shape=tuple(out_shape),
            in_specs=[VM] * 12 + [ANY] * 7 + [VM] * (3 * later),
            out_specs=(*[VM] * (8 + later), *[ANY] * (2 * later)),
            scratch_shapes=[
                pltpu.VMEM((tokens, width), BF),
                *(pltpu.VMEM(s.shape, s.dtype) for s in saved_shapes),
                pltpu.VMEM((wide, tokens), BF), pltpu.VMEM((ch2, length), F32), pltpu.VMEM((hid, tokens), BF),
                pltpu.VMEM((ch2, 2 * length), F32), pltpu.VMEM((ch2, 2 * length), BF), pltpu.VMEM((length, wide), BF),
                pltpu.VMEM((n, n * ch, length), BF), pltpu.VMEM((n, n * ch, length), BF),
                pltpu.VMEM((n * ch, length), F32),
                pltpu.VMEM((n - 1, n, ch, length), BF), pltpu.VMEM((wide, 128), F32), pltpu.VMEM((hid, 128), F32),
                *(pltpu.VMEM((*size, share_rows, hid), BF) for share_rows in (chans // m, share)
                  for size in ((m,), (m - 1,), ())),
                *sums, *comm, sem(n), sem(n), sem(n), sem(n), sem(n), sem(n), sem(7, n),
                sem(m), sem(m), sem(m), sem(m),
                *([pltpu.VMEM((m - 1, *late[1:]), BF), pltpu.VMEM(late[1:], BF), sem(m), sem(m), *[sem(2, n)] * 4, sem(2)]
                  if later else []),
            ],
            compiler_params=pltpu.CompilerParams(
                collective_id=1 + later, has_side_effects=True, vmem_limit_bytes=VMEM_LIMIT
            ),
            name="backward_block",
        )

    residual = tokens_in
    stored = []
    for l in range(LAYERS):
        sh_fb, sh_v, sh_mx, sh_out, in_bias, mix_bias, *tables = given[l]
        first = l == 0
        more = (sh_fb, given[1][0], given[1][3], *tables, *given[1][6:]) if first else (w_next, *spectrum)
        new, *made = fwd(l)(
            residual, norm_gain, norm_shift, own_live if first else mask, own_mask, sh_v, sh_mx, sh_out if first else out_next, in_bias,
            mix_bias, bias_output, ft_mat, f_mat, *more,
        )
        w_in, w_out, w_mx = made[7:10]
        if first:
            w_next, out_next, mask, *spectrum = made[10:]
            kernels = spectrum[:2], spectrum[2:]
            spectrum = spectrum[2:]
        stored.append((residual, made[:7], (w_in, w_mx, w_out), kernels[l]))
        residual = new
    tokens_out = residual

    grad = cotangent
    parts = [None] * LAYERS
    extra = ()
    for l in reversed(range(LAYERS)):
        resid_in, saved, weights, (kre, kim) = stored[l]
        grad, *parts[l] = bwd(l)(
            grad, resid_in, norm_gain, mask, own_mask, *weights, kre, kim, ft_mat, f_mat, *saved, *extra,
        )
        if l > 0:
            extra = tuple(parts[l][:3])
    part_in, red_mx0, red_out0, in0, mix0, norm0, dk0, late_in, all_mx1, all_out1 = parts[0]
    _, _, _, in1, mix1, norm1, dk1 = parts[1]
    lots = LAYERS * 3 * states
    all_in, all_mx, all_out = (n, share, wide), (n, chans // m, hid), (n, share, hid)
    all_in1, all_mx0, all_out0, all_in0, all_states, all_small, norms = pl.pallas_call(
        functools.partial(finish_kernel, n, m),
        out_shape=(
            shape(all_in, BF), shape(all_mx, BF), shape(all_out, BF), shape(all_in, BF),
            shape((n, m, lots // m, ch2), BF), shape((n, LAYERS, 8, wide), F32), shape((LAYERS, 8, wide), F32),
        ),
        in_specs=[VM] * 21,
        out_specs=(*[ANY] * 5, VM, VM),
        scratch_shapes=[
            pltpu.VMEM((m - 1, share, wide), BF), pltpu.VMEM((share, wide), BF), pltpu.VMEM((share, wide), BF),
            pltpu.VMEM((lots, ch2), F32),
            pltpu.VMEM((m, lots // m, ch2), BF), pltpu.VMEM((m - 1, lots // m, ch2), BF),
            pltpu.VMEM((lots // m, ch2), BF), pltpu.VMEM((m, lots // m, ch2), BF), pltpu.VMEM((length, ch2), F32),
            pltpu.VMEM((LAYERS, 8, wide), F32), pltpu.VMEM((m, LAYERS, 8, wide), F32),
            pltpu.VMEM((n, LAYERS, 8, wide), F32), pltpu.VMEM((LAYERS, 8, wide), F32),
            pltpu.VMEM((LAYERS, 8, wide), F32),
            *[sem(5, n)] * 4, sem(5), *[sem(m)] * 8,
            sem(n), sem(n), pltpu.SemaphoreType.DMA, pltpu.SemaphoreType.DMA,
        ],
        compiler_params=pltpu.CompilerParams(
            collective_id=3, has_side_effects=True, vmem_limit_bytes=VMEM_LIMIT
        ),
        name="finish",
    )(
        part_in, late_in, red_mx0, red_out0, dk0, dk1, in0, in1, mix0, mix1, norm0, norm1,
        *given[0][6:], *given[1][6:], ft_mat,
    )

    def fixed(dims):
        return pl.BlockSpec(tuple(dims), lambda l: (0,) * len(dims))

    def by_layer(dims):
        return pl.BlockSpec((1, *dims), lambda l: (l,) + (0,) * len(dims))

    chan, unit = n * ch, n * hid
    matrices = [(share, chan), (share, chan), (share, unit)]
    layouts = [
        (width,), (width,), *matrices, (chan,), (chan,), (unit,), (2, states, chan), (2, chan), (2, states, chan),
        (2, states, chan), (2, chan), (chans // m, unit), (unit,), (share, unit), (width,),
    ]
    small_out = {0, 1, 5, 6, 7, 9, 12, 14, 16}
    grads = list(pl.pallas_call(
        functools.partial(assemble_kernel, n),
        grid=(LAYERS,),
        out_shape=tuple(shape((LAYERS, *dims), F32) for dims in layouts),
        in_specs=[
            fixed(all_in), fixed(all_in), fixed(all_mx), fixed(all_mx), fixed(all_out), fixed(all_out),
            pl.BlockSpec((n, 3 * states, ch2), lambda l: (0, l, 0)), fixed((n, LAYERS, 8, wide)),
            fixed((LAYERS, 8, wide)),
        ],
        out_specs=tuple(
            fixed((LAYERS, *dims)) if i in small_out else by_layer(dims) for i, dims in enumerate(layouts)
        ),
        compiler_params=pltpu.CompilerParams(vmem_limit_bytes=VMEM_LIMIT),
        name="assemble",
    )(
        all_in0, all_in1, all_mx0, all_mx1, all_out0, all_out1, all_states.reshape(n, lots, ch2), all_small, norms,
    ))
    for i in (8, 10, 11, 15):
        grads[i] = turned(grads[i])
    return (tokens_out, grad, *grads)


def solution(mesh):
    tokens = P(("dp", "row", "col"), None)
    weight = P(None, "row", "col")
    bias = P(None, "col")
    state = P(None, None, "col", None)
    chan = P(None, None, "col")
    in_specs = (
        tokens, P(("dp", "row")), tokens, P(), P(), weight, weight, weight, bias, bias, bias,
        state, chan, state, state, chan, weight, bias, P(None, "col", "row"), P(),
    )
    out_specs = (
        tokens, tokens, P(), P(), weight, weight, weight, bias, bias, bias,
        state, chan, state, state, chan, weight, bias, P(None, "col", "row"), P(),
    )
    return jax.shard_map(body, mesh=mesh, in_specs=in_specs, out_specs=out_specs, check_vma=False)
```
